32 devices in a mesh: section: 2 (over x), batch: 16 (over z, y, core).
Axes of the slice: x: 2, y: 2, z: 4, core: 2. Of those that a mesh axis runs over, the one named last changes fastest.
Arguments:
- stream_in: bfloat16 [32, 128, 2, 768], P('batch'), may hold values from -6 to 6
- char_ids: int32 [32, 384], P('batch'), may hold values from 0 to 255
- char_lengths: int32 [32, 128], P('batch'), may hold values from 1 to 12, 384 in all within a row
- mask_pos: int32 [32, 19], P('batch'), may hold values from 0 to 127
- cotangent: bfloat16 [32, 19, 2, 768], P('batch'), may hold values from -6 to 6
- qkv_weight: bfloat16 [2, 768, 2304], P('section'), may hold values from -0.21875 to 0.21875
- query_value_bias: float32 [2, 2, 768], P('section'), may hold values from -1.25 to 1.25
- out_weight: bfloat16 [2, 768, 768], P('section'), may hold values from -1.75 to 1.75
- out_bias: float32 [2, 768], P('section'), may hold values from -1.25 to 1.25
- norm_gain: float32 [2, 4, 768], P('section'), may hold values from 0.5 to 1.5
- norm_bias: float32 [2, 4, 768], P('section'), may hold values from -1.25 to 1.25
- up_weight: bfloat16 [2, 768, 3072], P('section'), may hold values from -0.21875 to 0.21875
- up_bias: float32 [2, 3072], P('section'), may hold values from -1.25 to 1.25
- down_weight: bfloat16 [2, 3072, 768], P('section'), may hold values from -0.109375 to 0.109375
- down_bias: float32 [2, 768], P('section'), may hold values from -1.25 to 1.25
- char_table: bfloat16 [2, 256, 768], P('section'), may hold values from -6 to 6
- gru_input: bfloat16 [2, 768, 2304], P('section'), may hold values from -0.21875 to 0.21875
- gru_input_bias: float32 [2, 2304], P('section'), may hold values from -1.75 to 1.75
- gru_recur: bfloat16 [2, 384, 2304], P('section'), may hold values from -0.3125 to 0.3125
- gru_recur_bias: float32 [2, 2304], P('section'), may hold values from -1.75 to 1.75
- merge_weight: bfloat16 [2, 2, 768, 768], P('section'), may hold values from -0.21875 to 0.21875
- merge_bias: float32 [2, 2, 768], P('section'), may hold values from -1.25 to 1.25
- convolution_weight: bfloat16 [2, 3, 1536, 1536], P('section'), may hold values from -0.09375 to 0.09375
- conv_bias: float32 [2, 1536], P('section'), may hold values from -1.25 to 1.25
Outputs:
- section_ends: bfloat16 [2, 32, 128, 2, 768], P('section', 'batch')
- grad_qkv_weight: float32 [2, 768, 2304], P('section', None, 'batch')
- grad_query_value_bias: float32 [2, 2, 768], P('section', None, 'batch')
- grad_out_weight: float32 [2, 768, 768], P('section', None, 'batch')
- grad_out_bias: float32 [2, 768], P('section', 'batch')
- grad_norm_gain: float32 [2, 4, 768], P('section', None, 'batch')
- grad_norm_bias: float32 [2, 4, 768], P('section', None, 'batch')
- grad_up_weight: float32 [2, 768, 3072], P('section', None, 'batch')
- grad_up_bias: float32 [2, 3072], P('section', 'batch')
- grad_down_weight: float32 [2, 3072, 768], P('section', None, 'batch')
- grad_down_bias: float32 [2, 768], P('section', 'batch')
- grad_char_table: float32 [2, 256, 768], P('section', None, 'batch')
- grad_gru_input: float32 [2, 768, 2304], P('section', None, 'batch')
- grad_gru_input_bias: float32 [2, 2304], P('section', 'batch')
- grad_gru_recur: float32 [2, 384, 2304], P('section', None, 'batch')
- grad_gru_recur_bias: float32 [2, 2304], P('section', 'batch')
- grad_merge_weight: float32 [2, 2, 768, 768], P('section', None, None, 'batch')
- grad_merge_bias: float32 [2, 2, 768], P('section', None, 'batch')
- grad_conv_weight: float32 [2, 3, 1536, 1536], P('section', None, None, 'batch')
- convolution_bias_gradient: float32 [2, 1536], P('section', 'batch')
The draws below stay inside these ranges and needn't reach their ends.
Inputs may be any that keep to these rules, and one draw needn't show every extreme that they name: `char_lengths`: token t of a sequence owns the characters after those of tokens 0 to t - 1; the lengths of a sequence sum to 384, and some token has 12. `mask_pos`: positions may repeat.
All inputs are finite; a program needn't handle non-finite values.
Results may differ from the reference program's by a relative error of at most 0.019.
Values may be sent and summed in bfloat16 or wider, within the bound.
No kernel may reach another device: no remote copies, remote signals or barrier semaphores. Data moves between devices by JAX's collectives and lax.ppermute only.
A program may use at most 576 MiB of HBM per device.

```python
import math
import jax
import jax.numpy as jnp
import numpy as np
from jax import lax

D = 768
HEADS = 12
FF = 3072
GRU_H = 384
CHAR_VOCAB = 256
SEQ_LEN = 128
MOST_CHARS = 12
BLOCK_CH = 8
CHARS = 384
PICKS = 19
SEQS = 32
N_SECTION = 2


def place_ends(drawn, key, smallest, largest):
    place = [jax.random.randint(jax.random.fold_in(key, axis), (), 0, length) for axis, length in enumerate(drawn.shape)]
    widest = drawn.shape.index(max(drawn.shape))
    next_to = place[:widest] + [(place[widest] + 1) % drawn.shape[widest]] + place[widest + 1:]
    return drawn.at[tuple(place)].set(smallest).at[tuple(next_to)].set(largest)


def levels(stream_key, shape, shards, smallest, high):
    def one(dim, blocks):
        heights = jax.random.uniform(jax.random.fold_in(jax.random.fold_in(stream_key, 6), dim), (blocks,), jnp.float32, smallest / len(shards), high / len(shards))
        return jnp.repeat(jnp.exp(heights), shape[dim] // blocks).reshape((-1,) + (1,) * (len(shape) - dim - 1))

    level = one(*shards[0])
    for cut in shards[1:]:
        level = level * one(*cut)
    return level


def length_profile(number_of, total, bound, skew):
    portions = [(1 << 20) // math.isqrt(grade ** skew) + 1 for grade in range(2, number_of + 1)]
    surplus, counts = total - bound - (number_of - 1), [1] * (number_of - 1)
    while surplus > 0:
        movable = [i for i in range(number_of - 1) if counts[i] < bound]
        whole, remaining = sum([portions[i] for i in movable]), surplus
        for i in movable:
            addition = min(bound - counts[i], max(1, remaining * portions[i] // whole), surplus)
            counts[i] = counts[i] + addition
            surplus = surplus - addition
    return np.array([bound] + counts)


def uneven_parts(rng, amount, total, bound, lean):
    if amount == 2:
        one = jax.random.randint(rng, (), max(1, total - bound), min(bound, total - 1) + 1)
        return jnp.stack([one, total - one])
    sizes = jnp.asarray(length_profile(amount, total, bound, lean), jnp.int32)
    couples = (amount - 1) // 2
    source_of, taker = sizes[1:1 + 2 * couples:2], sizes[2:2 + 2 * couples:2]
    room = jnp.minimum(source_of - 1, bound - taker)
    shifted = jax.random.randint(jax.random.fold_in(rng, 1), (couples,), 0, 1 << 20) % (room + 1)
    sizes = sizes.at[1:1 + 2 * couples:2].set(source_of - shifted).at[2:2 + 2 * couples:2].set(taker + shifted)
    return sizes[jax.random.permutation(jax.random.fold_in(rng, 2), amount)]


def noise(own_key, shape, scale, reach, cuts=(), kind=jnp.bfloat16):
    result = jax.random.normal(own_key, shape, jnp.float32) * scale
    if len(cuts) > 0:
        result = levels(own_key, shape, cuts, -0.22, 0.18) * result
    return jnp.clip(result, min=-reach, max=reach).astype(kind)


def setup_inputs(seed: int = 0) -> dict:
    splits = jax.random.split(jax.random.key(seed), 25)
    stream_in = noise(splits[0], (SEQS, SEQ_LEN, 2, D), 1.0, 6.0, ((0, 16),))
    char_ids = place_ends(jax.random.randint(splits[1], (SEQS, CHARS), 0, CHAR_VOCAB), jax.random.fold_in(splits[1], 1), 0, CHAR_VOCAB - 1).astype(jnp.int32)
    char_lengths = jax.vmap(lambda own: uneven_parts(own, SEQ_LEN, CHARS, MOST_CHARS, 1))(jax.random.split(splits[2], SEQS)).reshape((SEQS, SEQ_LEN)).astype(jnp.int32)
    mask_pos = place_ends(jax.random.randint(splits[3], (SEQS, PICKS), 0, SEQ_LEN), jax.random.fold_in(splits[3], 1), 0, SEQ_LEN - 1).astype(jnp.int32)
    cotangent = noise(splits[4], (SEQS, PICKS, 2, D), 1.0, 6.0, ((0, 16),))
    qkv_weight = noise(splits[5], (N_SECTION, D, 3 * D), D ** -0.5, 0.21875, ((0, 2),))
    query_value_bias = noise(splits[6], (N_SECTION, 2, D), 0.2, 1.25, ((0, 2),), jnp.float32)
    out_weight = noise(splits[7], (N_SECTION, D, D), (D // 64) ** -0.5, 1.75, ((0, 2),))
    out_bias = noise(splits[8], (N_SECTION, D), 0.2, 1.25, ((0, 2),), jnp.float32)
    norm_gain = jnp.clip(1.0 + 0.1 * jax.random.normal(splits[9], (N_SECTION, 4, D), jnp.float32), 0.5, 1.5)
    norm_bias = noise(splits[10], (N_SECTION, 4, D), 0.2, 1.25, ((0, 2),), jnp.float32)
    up_weight = noise(splits[11], (N_SECTION, D, FF), D ** -0.5, 0.21875, ((0, 2),))
    up_bias = noise(splits[12], (N_SECTION, FF), 0.2, 1.25, ((0, 2),), jnp.float32)
    down_weight = noise(splits[13], (N_SECTION, FF, D), FF ** -0.5, 0.109375, ((0, 2),))
    down_bias = noise(splits[14], (N_SECTION, D), 0.2, 1.25, ((0, 2),), jnp.float32)
    char_table = noise(splits[15], (N_SECTION, CHAR_VOCAB, D), 1.0, 6.0, ((0, 2),))
    gru_input = noise(splits[16], (N_SECTION, D, 6 * GRU_H), D ** -0.5, 0.21875, ((0, 2),))
    gru_input_bias = noise(splits[17], (N_SECTION, 6 * GRU_H), 0.3, 1.75, ((0, 2),), jnp.float32)
    gru_recur = noise(splits[18], (N_SECTION, GRU_H, 6 * GRU_H), GRU_H ** -0.5, 0.3125, ((0, 2),))
    gru_recur_bias = noise(splits[19], (N_SECTION, 6 * GRU_H), 0.3, 1.75, ((0, 2),), jnp.float32)
    merge_weight = noise(splits[20], (N_SECTION, 2, D, D), D ** -0.5, 0.21875, ((0, 2),))
    merge_bias = noise(splits[21], (N_SECTION, 2, D), 0.2, 1.25, ((0, 2),), jnp.float32)
    convolution_weight = noise(splits[22], (N_SECTION, 3, 2 * D, 2 * D), (6 * D) ** -0.5, 0.09375, ((0, 2),))
    conv_bias = noise(splits[23], (N_SECTION, 2 * D), 0.2, 1.25, ((0, 2),), jnp.float32)
    return dict(stream_in=stream_in, char_ids=char_ids, char_lengths=char_lengths, mask_pos=mask_pos, cotangent=cotangent, qkv_weight=qkv_weight, query_value_bias=query_value_bias, out_weight=out_weight, out_bias=out_bias, norm_gain=norm_gain, norm_bias=norm_bias, up_weight=up_weight, up_bias=up_bias, down_weight=down_weight, down_bias=down_bias, char_table=char_table, gru_input=gru_input, gru_input_bias=gru_input_bias, gru_recur=gru_recur, gru_recur_bias=gru_recur_bias, merge_weight=merge_weight, merge_bias=merge_bias, convolution_weight=convolution_weight, conv_bias=conv_bias)


EPSILON = 1e-05
HIGHEST = lax.Precision.HIGHEST

@jax.custom_vjp
def low(v):
    return lax.optimization_barrier(v.astype(jnp.bfloat16)).astype(jnp.float32)

@jax.custom_vjp
def low_back(v):
    return v

def low_keep(v):
    return (low(v), None)

def low_pass(kept, grad):
    return (grad,)

def back_keep(v):
    return (v, None)

def back_low(kept, grad):
    return (low(grad),)
low.defvjp(low_keep, low_pass)
low_back.defvjp(back_keep, back_low)

def matmul(left_side, right_side):
    return jnp.matmul(left_side, right_side, precision=HIGHEST)

def linear(inputs, weight, bias):
    return low_back(matmul(low(inputs), weight)) + bias

def layer_normalize(values, norm_scale, norm_shift):
    row_mean = lax.optimization_barrier(jnp.mean(values, axis=-1, keepdims=True))
    centered = values - row_mean
    row_var = lax.optimization_barrier(jnp.mean(centered * centered, axis=-1, keepdims=True))
    return centered * lax.rsqrt(row_var + EPSILON) * norm_scale + norm_shift

def token_map(lengths, char_count):
    ends = jnp.cumsum(lengths, axis=-1)
    positions = jnp.arange(char_count, dtype=jnp.int32)
    return lax.optimization_barrier(jnp.sum((ends[..., None, :] <= positions[:, None]).astype(jnp.int32), axis=-1)).astype(jnp.int32)

def gru_cell(gate_step, gate_rec, previous):
    hidden = previous.shape[-1]
    reset_gate = jax.nn.sigmoid(gate_step[..., :hidden] + gate_rec[..., :hidden])
    update_gate = jax.nn.sigmoid(gate_step[..., hidden:2 * hidden] + gate_rec[..., hidden:2 * hidden])
    candidate = jnp.tanh(gate_step[..., 2 * hidden:] + reset_gate * gate_rec[..., 2 * hidden:])
    return (1.0 - update_gate) * candidate + update_gate * previous

def recur(gate_in, rec_weight, rec_bias):

    def advance(hidden_state, gate_step):
        gate_rec = low_back(matmul(low(hidden_state), rec_weight)) + rec_bias
        hidden_state = gru_cell(gate_step, gate_rec, hidden_state)
        return (hidden_state, hidden_state)
    start_state = jnp.zeros((gate_in.shape[0], rec_weight.shape[0]), jnp.float32)
    final_state, states = lax.scan(advance, start_state, jnp.swapaxes(gate_in, 0, 1))
    return jnp.swapaxes(states, 0, 1)

@jax.checkpoint
def attention(queries, key_rows, value_rows):
    head_shape = queries.shape[:2] + (HEADS, queries.shape[2] // HEADS)
    score_scale = (queries.shape[2] // HEADS) ** (-0.5)
    scores = low_back(jnp.einsum('sqhd,skhd->shqk', low(queries).reshape(head_shape), low(key_rows).reshape(head_shape), precision=HIGHEST) * score_scale)
    attn_prob = jax.nn.softmax(scores, axis=-1)
    attended = jnp.einsum('shqk,skhd->sqhd', low(attn_prob), low(value_rows).reshape(head_shape), precision=HIGHEST)
    return attended.reshape(queries.shape)

def segment_pool(state_rows, segment_ids):
    return jax.ops.segment_sum(state_rows, segment_ids, num_segments=SEQ_LEN)

def layer(stream, char_ids, char_lengths, weights):
    qkv_weight, query_value_bias, out_weight, out_bias, norm_gain, norm_bias, up_weight, up_bias, down_weight, down_bias, char_table, gru_input, gru_input_bias, gru_recur, gru_recur_bias, merge_weight, merge_bias, convolution_weight, conv_bias = weights
    groups, sequence_length, width = (stream.shape[0], stream.shape[1], stream.shape[3])
    subword = stream[:, :, 0]
    charside = stream[:, :, 1]
    projected = low_back(matmul(low(subword), qkv_weight))
    queries = projected[..., :width] + query_value_bias[0]
    key_rows = projected[..., width:2 * width]
    value_rows = projected[..., 2 * width:] + query_value_bias[1]
    attended = attention(queries, key_rows, value_rows)
    attn_branch = linear(low_back(attended), out_weight, out_bias)
    after_attn = layer_normalize(subword + attn_branch, norm_gain[0], norm_bias[0])
    up_act = jax.nn.gelu(linear(after_attn, up_weight, up_bias))
    after_ffn = layer_normalize(after_attn + linear(up_act, down_weight, down_bias), norm_gain[1], norm_bias[1])
    token_of = token_map(char_lengths, char_ids.shape[1])
    gathered = jnp.take_along_axis(charside, token_of[..., None], axis=1)
    embedded = jnp.take(char_table, char_ids, axis=0)
    char_in = low_back(gathered + embedded)
    gate_in = linear(char_in, gru_input, gru_input_bias)
    hidden = gru_recur.shape[0]
    blocked = gate_in.reshape(-1, BLOCK_CH, 6 * hidden)
    forward_states = recur(blocked[..., :3 * hidden], gru_recur[:, :3 * hidden], gru_recur_bias[:3 * hidden])
    backward_states = jnp.flip(recur(jnp.flip(blocked[..., 3 * hidden:], 1), gru_recur[:, 3 * hidden:], gru_recur_bias[3 * hidden:]), 1)
    char_states = jnp.concatenate([forward_states, backward_states], -1).reshape(groups, -1, width)
    pooled = jax.vmap(segment_pool)(char_states, token_of) / char_lengths[..., None].astype(jnp.float32)
    token_side = jax.nn.gelu(linear(after_ffn, merge_weight[0], merge_bias[0]))
    char_side = jax.nn.gelu(linear(pooled, merge_weight[1], merge_bias[1]))
    joined = low(jnp.concatenate([token_side, char_side], -1))
    padded_rows = jnp.pad(joined, ((0, 0), (1, 1), (0, 0)))
    conv_sum = matmul(padded_rows[:, 0:sequence_length], convolution_weight[0]) + matmul(padded_rows[:, 1:sequence_length + 1], convolution_weight[1]) + matmul(padded_rows[:, 2:sequence_length + 2], convolution_weight[2])
    conv_out = low_back(conv_sum) + conv_bias
    out_sub = layer_normalize(after_ffn + conv_out[..., :width], norm_gain[2], norm_bias[2])
    out_char = layer_normalize(pooled + conv_out[..., width:], norm_gain[3], norm_bias[3])
    return jnp.stack([out_sub, out_char], 2)

def run_group(params, stream, char_ids, char_lengths, positions, cotangent_rows):
    first_layer = tuple((param[0] for param in params))
    second_layer = tuple((param[1] for param in params))
    middle = low_back(low(layer(stream, char_ids, char_lengths, first_layer)))
    final = layer(middle, char_ids, char_lengths, second_layer)
    picked = jnp.take_along_axis(final, positions[:, :, None, None], axis=1)
    return (jnp.sum(picked * cotangent_rows), final)

def reference(stream_in, char_ids, char_lengths, mask_pos, cotangent, qkv_weight, query_value_bias, out_weight, out_bias, norm_gain, norm_bias, up_weight, up_bias, down_weight, down_bias, char_table, gru_input, gru_input_bias, gru_recur, gru_recur_bias, merge_weight, merge_bias, convolution_weight, conv_bias):
    params = tuple((param.astype(jnp.float32) for param in (qkv_weight, query_value_bias, out_weight, out_bias, norm_gain, norm_bias, up_weight, up_bias, down_weight, down_bias, char_table, gru_input, gru_input_bias, gru_recur, gru_recur_bias, merge_weight, merge_bias, convolution_weight, conv_bias)))
    group_size = 1
    while group_size * 2 * SEQ_LEN <= 4096 and SEQS % (group_size * 2) == 0:
        group_size = group_size * 2
    group_count = SEQS // group_size

    def split_groups(array):
        return array.reshape((group_count, group_size) + array.shape[1:])
    ids_groups = split_groups(char_ids)
    length_groups = split_groups(char_lengths)
    pos_groups = split_groups(mask_pos)
    cot_groups = split_groups(cotangent.astype(jnp.float32))
    group_fn = jax.checkpoint(run_group)

    def whole(stream, weights):

        def step_fn(loss_total, slices):
            part_loss, final = group_fn(weights, *slices)
            return (loss_total + part_loss, final)
        loss_total, finals = lax.scan(step_fn, jnp.zeros((), jnp.float32), (split_groups(stream), ids_groups, length_groups, pos_groups, cot_groups))
        return (loss_total, finals.reshape(stream.shape))
    loss_total, reverse_mapping, final = jax.vjp(whole, stream_in.astype(jnp.float32), params, has_aux=True)
    grad_stream, grad_params = reverse_mapping(jnp.ones((), jnp.float32))
    section_ends = jnp.stack([grad_stream.astype(jnp.bfloat16), final.astype(jnp.bfloat16)])
    return (section_ends, grad_params[0], grad_params[1], grad_params[2], grad_params[3], grad_params[4], grad_params[5], grad_params[6], grad_params[7], grad_params[8], grad_params[9], grad_params[10], grad_params[11], grad_params[12], grad_params[13], grad_params[14], grad_params[15], grad_params[16], grad_params[17], grad_params[18])
```

```python
import functools

import jax
import jax.numpy as jnp
from jax import lax
from jax.experimental import pallas as pl
from jax.experimental.pallas import tpu as pltpu
from jax.sharding import PartitionSpec as P

HEAD = 64
BLOCK_CH = 8
EPSILON = 1e-05
LOW = jnp.bfloat16
FULL = jnp.float32
VMEM_LIMIT = 58 * 1024 * 1024


def dot(left, right):
    return lax.dot_general(left, right, (((1,), (0,)), ((), ())), preferred_element_type=FULL)


def dot_nt(left, right):
    return lax.dot_general(left, right, (((1,), (1,)), ((), ())), preferred_element_type=FULL)


def dot_tn(left, right):
    return lax.dot_general(left, right, (((0,), (0,)), ((), ())), preferred_element_type=FULL)


def norm_parts(values):
    row_mean = jnp.mean(values, axis=-1, keepdims=True)
    centered = values - row_mean
    row_var = jnp.mean(centered * centered, axis=-1, keepdims=True)
    inverse = lax.rsqrt(row_var + EPSILON)
    return centered * inverse, inverse


def norm(values, gain, shift):
    return norm_parts(values)[0] * gain + shift


def norm_back(values, gain, grad):
    unit, inverse = norm_parts(values)
    scaled = grad * gain
    first = jnp.mean(scaled, axis=-1, keepdims=True)
    second = jnp.mean(scaled * unit, axis=-1, keepdims=True)
    return inverse * (scaled - first - unit * second), unit


GELU_A = 0.7978845608028654
GELU_B = 0.044715


def gelu(x):
    return 0.5 * x * (1.0 + jnp.tanh(GELU_A * (x + GELU_B * x * x * x)))


def gelu_slope(x):
    square = x * x
    bent = jnp.tanh(GELU_A * (x + GELU_B * square * x))
    return 0.5 * (1.0 + bent) + 0.5 * x * (1.0 - bent * bent) * (
        GELU_A * (1.0 + 3.0 * GELU_B * square)
    )


def sigmoid(x):
    return 0.5 * jnp.tanh(0.5 * x) + 0.5


def column_sum(values):
    return jnp.sum(values, axis=0, keepdims=True)


class Stream:
    def __init__(self, pairs, sems):
        self.copies = [
            pltpu.make_async_copy(src, dst, sems.at[i]) for i, (src, dst) in enumerate(pairs)
        ]
        for copy in self.copies:
            copy.start()
        self.waited = set()

    def need(self, *which):
        for i in which:
            if i not in self.waited:
                self.waited.add(i)
                self.copies[i].wait()


def chunks(src, dst, axis, size):
    total = src.shape[axis]
    parts = []
    for start in range(0, total, size):
        index = [slice(None)] * len(src.shape)
        index[axis] = pl.ds(start, min(size, total - start))
        parts.append((src.at[tuple(index)], dst.at[tuple(index)]))
    return parts


def any_spec():
    return pl.BlockSpec(memory_space=pl.ANY)


def vmem_spec():
    return pl.BlockSpec(memory_space=pltpu.VMEM)


def sds(shape, dtype):
    return jax.ShapeDtypeStruct(shape, dtype)


def call(kernel, outs, ins, streamed, scratch, name, flops, copies):
    moved = sum(a.size * a.dtype.itemsize for a in ins) + sum(
        o.size * o.dtype.itemsize for o in outs
    )
    return pl.pallas_call(
        kernel,
        out_shape=outs,
        in_specs=[any_spec() if i in streamed else vmem_spec() for i in range(len(ins))],
        out_specs=[vmem_spec() for _ in outs],
        scratch_shapes=list(scratch) + [pltpu.SemaphoreType.DMA((copies,))],
        compiler_params=pltpu.CompilerParams(vmem_limit_bytes=VMEM_LIMIT),
        cost_estimate=pl.CostEstimate(flops=flops, bytes_accessed=moved, transcendentals=0),
        name=name,
    )(*ins)


def sub_forward_kernel(seqs, save, s_ref, qkv_hbm, qvb_ref, out_hbm, outb_ref, gain_ref, shift_ref,
                       up_hbm, upb_ref, down_hbm, downb_ref, *rest):
    if save:
        (after_ref, qkv_ref, prob_ref, att_ref, res1_ref, first_ref, pre_ref, act_ref, res2_ref,
         wqkv, wout, wup, wdown, sems) = rest
    else:
        after_ref, wqkv, wout, wup, wdown, qkv_ref, att_ref, sems = rest
    width = s_ref.shape[1]
    wide = wup.shape[1]
    length = s_ref.shape[0] // seqs
    w = Stream(chunks(qkv_hbm, wqkv, 1, width) + chunks(out_hbm, wout, 1, width)
               + chunks(up_hbm, wup, 1, width) + chunks(down_hbm, wdown, 0, width), sems)
    for part in range(3):
        w.need(part)
        cols = slice(part * width, (part + 1) * width)
        y = dot(s_ref[...], wqkv[:, cols])
        if part == 0:
            y = (y + qvb_ref[0:1, :]) * HEAD ** -0.5
        elif part == 2:
            y = y + qvb_ref[1:2, :]
        qkv_ref[:, cols] = y.astype(LOW)
    lanes = lax.broadcasted_iota(jnp.int32, (length, 2 * HEAD), 1)
    even = lanes < HEAD
    for seq in range(seqs):
        rows = slice(seq * length, (seq + 1) * length)
        for pair in range(width // (2 * HEAD)):
            lo = pair * 2 * HEAD
            q = qkv_ref[rows, lo:lo + 2 * HEAD]
            k = qkv_ref[rows, width + lo:width + lo + 2 * HEAD]
            v = qkv_ref[rows, 2 * width + lo:2 * width + lo + 2 * HEAD]
            zero = jnp.zeros_like(q)
            probs = []
            for half in range(2):
                mask = even if half == 0 else ~even
                scores = dot_nt(jnp.where(mask, q, zero), k)
                peak = jnp.max(scores, axis=-1, keepdims=True)
                e = jnp.exp(scores - peak)
                prob = (e / jnp.sum(e, axis=-1, keepdims=True)).astype(LOW)
                probs.append(prob)
                if save:
                    at = (seq * (width // HEAD) + 2 * pair + half) * length
                    prob_ref[at:at + length, :] = prob
            both = jnp.concatenate(probs, axis=1)
            vv = jnp.concatenate([jnp.where(even, v, zero), jnp.where(even, zero, v)], axis=0)
            att_ref[rows, lo:lo + 2 * HEAD] = dot(both, vv).astype(LOW)
    w.need(3)
    res1 = s_ref[...].astype(FULL) + dot(att_ref[...], wout[...]) + outb_ref[...]
    after = norm(res1, gain_ref[0:1, :], shift_ref[0:1, :])
    low = after.astype(LOW)
    if save:
        res1_ref[...] = res1
        first_ref[...] = low
    total = after + downb_ref[...]
    for part in range(wide // width):
        cols = slice(part * width, (part + 1) * width)
        w.need(4 + part)
        pre = dot(low, wup[:, cols]) + upb_ref[:, cols]
        act = gelu(pre).astype(LOW)
        if save:
            pre_ref[:, cols] = pre
            act_ref[:, cols] = act
        w.need(4 + wide // width + part)
        total = total + dot(act, wdown[cols, :])
    if save:
        res2_ref[...] = total
    after_ref[...] = norm(total, gain_ref[1:2, :], shift_ref[1:2, :])


def sub_forward(seqs, save, s, qkv_w, qvb, out_w, out_b, gain, shift, up_w, up_b, down_w, down_b):
    rows, width = s.shape
    wide = up_w.shape[1]
    length = rows // seqs
    outs = [sds((rows, width), FULL)]
    scratch = [pltpu.VMEM(a.shape, LOW) for a in (qkv_w, out_w, up_w, down_w)]
    saved = [sds((rows, 3 * width), LOW), sds((seqs * (width // HEAD) * length, length), LOW),
             sds((rows, width), LOW), sds((rows, width), FULL), sds((rows, width), LOW),
             sds((rows, wide), FULL), sds((rows, wide), LOW), sds((rows, width), FULL)]
    if save:
        outs = outs + saved
    else:
        scratch = scratch + [pltpu.VMEM(saved[0].shape, LOW), pltpu.VMEM(saved[2].shape, LOW)]
    copies = 4 + 2 * (wide // width)
    return call(functools.partial(sub_forward_kernel, seqs, save), outs,
                [s, qkv_w, qvb, out_w, out_b, gain, shift, up_w, up_b, down_w, down_b],
                {1, 3, 7, 9}, scratch, "sub_forward",
                2 * rows * (qkv_w.size + out_w.size + up_w.size + down_w.size), copies)


def gru_forward_kernel(save, c_ref, tokc_ref, tokr_ref, idc_ref, count_ref, table_hbm, win_hbm,
                       bin_ref, wrec_hbm, brec_ref, *rest):
    if save:
        (pooled_ref, charin_ref, r_ref, z_ref, n_ref, rn_ref, state_ref, prev_ref,
         table, win, wrec, gate, low_state, sems) = rest
    else:
        pooled_ref, table, win, wrec, gate, low_state, charin_ref, sems = rest
    rows, width = c_ref.shape
    count = tokc_ref.shape[0]
    hidden = wrec.shape[0]
    w = Stream([(table_hbm, table)] + chunks(win_hbm, win, 1, width)
               + chunks(wrec_hbm, wrec, 1, 3 * hidden), sems)
    token = (tokc_ref[...] == lax.broadcasted_iota(jnp.int32, (count, rows), 1))
    ident = (idc_ref[...] == lax.broadcasted_iota(jnp.int32, (count, table.shape[0]), 1))
    w.need(0)
    x = dot(token.astype(FULL).astype(LOW), c_ref[...]) + dot(ident.astype(FULL).astype(LOW), table[...])
    charin_ref[...] = x.astype(LOW)
    for part in range(3):
        w.need(1 + part)
        cols = slice(part * width, (part + 1) * width)
        gate[:, cols] = dot(charin_ref[...], win[:, cols]) + bin_ref[:, cols]
    lanes = count // BLOCK_CH
    state = [None, None]
    for turn in range(BLOCK_CH):
        for way in range(2):
            at = turn if way == 0 else BLOCK_CH - 1 - turn
            here = slice(at * lanes, (at + 1) * lanes)
            base = way * 3 * hidden
            out = slice(way * hidden, (way + 1) * hidden)
            bias = brec_ref[:, base:base + 3 * hidden]
            g = gate[here, base:base + 3 * hidden]
            if turn == 0:
                rec_n = jnp.broadcast_to(bias[:, 2 * hidden:], (lanes, hidden))
                rz = g[:, :2 * hidden] + bias[:, :2 * hidden]
                if save:
                    prev_ref[here, out] = jnp.zeros((lanes, hidden), LOW)
            else:
                w.need(4 + way)
                low = state[way].astype(LOW)
                if save:
                    prev_ref[here, out] = low
                rec = dot(low, wrec[:, base:base + 3 * hidden]) + bias
                rec_n = rec[:, 2 * hidden:]
                rz = g[:, :2 * hidden] + rec[:, :2 * hidden]
            rz = sigmoid(rz)
            r, z = rz[:, :hidden], rz[:, hidden:]
            n = jnp.tanh(g[:, 2 * hidden:] + r * rec_n)
            new = (1.0 - z) * n
            if turn > 0:
                new = new + z * state[way]
            state[way] = new
            low_state[here, out] = new.astype(LOW)
            if save:
                r_ref[here, out] = r
                z_ref[here, out] = z
                n_ref[here, out] = n
                rn_ref[here, out] = rec_n
                state_ref[here, out] = new
    spread = (tokr_ref[...] == lax.broadcasted_iota(jnp.int32, (rows, count), 0))
    pooled = dot(spread.astype(FULL).astype(LOW), low_state[...])
    pooled_ref[...] = pooled / count_ref[...]


def gru_forward(save, c, tokc, tokr, idc, counts, table, win, bin_, wrec, brec):
    rows, width = c.shape
    count = tokc.shape[0]
    outs = [sds((rows, width), FULL)]
    scratch = [pltpu.VMEM(a.shape, LOW) for a in (table, win, wrec)]
    scratch = scratch + [pltpu.VMEM((count, win.shape[1]), FULL), pltpu.VMEM((count, width), LOW)]
    if save:
        outs = outs + [sds((count, width), LOW)] + [sds((count, width), FULL)] * 5
        outs = outs + [sds((count, width), LOW)]
    else:
        scratch = scratch + [pltpu.VMEM((count, width), LOW)]
    return call(functools.partial(gru_forward_kernel, save), outs,
                [c, tokc, tokr, idc, counts, table, win, bin_, wrec, brec],
                {5, 6, 8}, scratch, "gru_forward",
                2 * count * (win.size + wrec.size) + 2 * count * width * (2 * rows + table.shape[0]), 6)


def shift_rows(values, by, length):
    rows, width = values.shape
    zero = jnp.zeros((1, width), values.dtype)
    pos = lax.broadcasted_iota(jnp.int32, (rows, 1), 0) % length
    if by == 1:
        moved = jnp.concatenate([zero, values[:-1]], axis=0)
        return jnp.where(pos == 0, 0.0, moved)
    moved = jnp.concatenate([values[1:], zero], axis=0)
    return jnp.where(pos == length - 1, 0.0, moved)


def merge_forward_kernel(length, save, after_ref, pooled_ref, mw_hbm, mb_ref, cw_hbm, cb_ref,
                         gain_ref, shift_ref, *rest):
    if save:
        (sub_ref, char_ref, pre_ref, joined_ref, second_ref, poollow_ref, res3_ref, res4_ref,
         mw, cw, sems) = rest
    else:
        sub_ref, char_ref, mw, cw, sems = rest
    width = after_ref.shape[1]
    w = Stream(chunks(mw_hbm, mw, 0, 1) + chunks(cw_hbm, cw, 0, 1), sems)
    halves = []
    for side in range(2):
        w.need(side)
        cols = slice(side * width, (side + 1) * width)
        low = (after_ref if side == 0 else pooled_ref)[...].astype(LOW)
        pre = dot(low, mw[side]) + mb_ref[side:side + 1, :]
        if save:
            (second_ref if side == 0 else poollow_ref)[...] = low
            pre_ref[:, cols] = pre
        halves.append(gelu(pre))
    joined = jnp.concatenate(halves, axis=1)
    if save:
        joined_ref[...] = joined.astype(LOW)
    total = cb_ref[...]
    for k in range(3):
        moved = joined if k == 1 else shift_rows(joined, 1 - k, length)
        w.need(2 + k)
        total = total + dot(moved.astype(LOW), cw[k])
    res3 = after_ref[...] + total[:, :width]
    res4 = pooled_ref[...] + total[:, width:]
    if save:
        res3_ref[...] = res3
        res4_ref[...] = res4
    sub_ref[...] = norm(res3, gain_ref[2:3, :], shift_ref[2:3, :]).astype(LOW)
    char_ref[...] = norm(res4, gain_ref[3:4, :], shift_ref[3:4, :]).astype(LOW)


def merge_forward(length, save, after, pooled, mw, mb, cw, cb, gain, shift):
    rows, width = after.shape
    outs = [sds((rows, width), LOW)] * 2
    scratch = [pltpu.VMEM(mw.shape, LOW), pltpu.VMEM(cw.shape, LOW)]
    if save:
        outs = outs + [sds((rows, 2 * width), FULL), sds((rows, 2 * width), LOW),
                       sds((rows, width), LOW), sds((rows, width), LOW),
                       sds((rows, width), FULL), sds((rows, width), FULL)]
    return call(functools.partial(merge_forward_kernel, length, save), outs,
                [after, pooled, mw, mb, cw, cb, gain, shift], {2, 4}, scratch, "merge_forward",
                2 * rows * (mw.size + cw.size), 5)


def merge_backward_kernel(length, full, gsub_ref, gchar_ref, res3_ref, res4_ref, pre_ref, mw_hbm, cw_hbm,
                          gain_ref, dsecond_ref, dpooled_ref, *rest):
    if full:
        dconv_ref, dpre_ref, small_ref, mw, cw, sems = rest
    else:
        mw, cw, sems = rest
    width = res3_ref.shape[1]
    w = Stream(chunks(cw_hbm, cw, 0, 1) + chunks(mw_hbm, mw, 0, 1), sems)
    grads = [gsub_ref[...], gchar_ref[...]]
    d_res = []
    for side in range(2):
        d, unit = norm_back((res3_ref, res4_ref)[side][...], gain_ref[2 + side:3 + side, :], grads[side])
        d_res.append(d)
        if full:
            cols = slice(side * width, (side + 1) * width)
            small_ref[2:3, cols] = column_sum(grads[side] * unit)
            small_ref[3:4, cols] = column_sum(grads[side])
            small_ref[0:1, cols] = column_sum(d)
    d_conv = jnp.concatenate(d_res, axis=1)
    if full:
        dconv_ref[...] = d_conv.astype(LOW)
        small_ref[4:8, :] = jnp.zeros((4, 2 * width), FULL)
    total = None
    for k in range(3):
        moved = d_conv if k == 1 else shift_rows(d_conv, k - 1, length)
        w.need(k)
        term = dot_nt(moved.astype(LOW), cw[k])
        total = term if total is None else total + term
    d_pre = total * gelu_slope(pre_ref[...])
    d_low = d_pre.astype(LOW)
    if full:
        dpre_ref[...] = d_low
        small_ref[1:2, :] = column_sum(d_pre)
    for side in range(2):
        w.need(3 + side)
        (dsecond_ref if side == 0 else dpooled_ref)[...] = d_res[side] + dot_nt(
            d_low[:, side * width:(side + 1) * width], mw[side])


def merge_backward(length, full, gsub, gchar, res3, res4, pre, mw, cw, gain):
    rows, width = res3.shape
    outs = [sds((rows, width), FULL)] * 2
    if full:
        outs = outs + [sds((rows, 2 * width), LOW)] * 2 + [sds((8, 2 * width), FULL)]
    scratch = [pltpu.VMEM(mw.shape, LOW), pltpu.VMEM(cw.shape, LOW)]
    return call(functools.partial(merge_backward_kernel, length, full), outs,
                [gsub, gchar, res3, res4, pre, mw, cw, gain], {5, 6}, scratch, "merge_backward",
                2 * rows * (mw.size + cw.size), 5)


def sub_backward_kernel(seqs, full, dsecond_ref, res2_ref, pre_ref, res1_ref, qkv_ref, prob_ref,
                        qkv_hbm, out_hbm, up_hbm, down_hbm, gain_ref, dsub_ref, *rest):
    if full:
        (ddown_ref, dup_ref, dbranch_ref, dproj_ref, small_ref,
         wqkv, wout, wup, wdown, datt, sems) = rest
    else:
        wqkv, wout, wup, wdown, datt, dproj_ref, sems = rest
    rows, width = dsub_ref.shape
    wide = wup.shape[1]
    length = rows // seqs
    parts = wide // width
    w = Stream(chunks(down_hbm, wdown, 0, width) + chunks(up_hbm, wup, 1, width)
               + chunks(out_hbm, wout, 1, width) + chunks(qkv_hbm, wqkv, 1, width), sems)
    d_second = dsecond_ref[...]
    d_res2, unit = norm_back(res2_ref[...], gain_ref[1:2, :], d_second)
    d_low = d_res2.astype(LOW)
    if full:
        ddown_ref[...] = d_low
        small_ref[1:2, 0:width] = column_sum(d_res2)
        small_ref[1:2, 3 * width:4 * width] = column_sum(d_second * unit)
        small_ref[2:3, width:2 * width] = column_sum(d_second)
        small_ref[3:8, :] = jnp.zeros((5, wide), FULL)
    d_first = d_res2
    for part in range(parts):
        cols = slice(part * width, (part + 1) * width)
        w.need(part)
        d_up = dot_nt(d_low, wdown[cols, :]) * gelu_slope(pre_ref[:, cols])
        up_low = d_up.astype(LOW)
        if full:
            dup_ref[:, cols] = up_low
            small_ref[0:1, cols] = column_sum(d_up)
        w.need(parts + part)
        d_first = d_first + dot_nt(up_low, wup[:, cols])
    d_res1, unit = norm_back(res1_ref[...], gain_ref[0:1, :], d_first)
    branch_low = d_res1.astype(LOW)
    if full:
        dbranch_ref[...] = branch_low
        small_ref[1:2, width:2 * width] = column_sum(d_res1)
        small_ref[1:2, 2 * width:3 * width] = column_sum(d_first * unit)
        small_ref[2:3, 0:width] = column_sum(d_first)
    w.need(2 * parts)
    datt[...] = dot_nt(branch_low, wout[...]).astype(LOW)
    even = lax.broadcasted_iota(jnp.int32, (length, 2 * HEAD), 1) < HEAD
    scale = HEAD ** -0.5
    sums = [[], []]
    for pair in range(width // (2 * HEAD)):
        lo = pair * 2 * HEAD
        totals = [0.0, 0.0]
        for seq in range(seqs):
            at_rows = slice(seq * length, (seq + 1) * length)
            q = qkv_ref[at_rows, lo:lo + 2 * HEAD]
            k = qkv_ref[at_rows, width + lo:width + lo + 2 * HEAD]
            v = qkv_ref[at_rows, 2 * width + lo:2 * width + lo + 2 * HEAD]
            da = datt[at_rows, lo:lo + 2 * HEAD]
            zero = jnp.zeros_like(q)

            def halves(x):
                return jnp.where(even, x, zero), jnp.where(even, zero, x)

            da_h = halves(da)
            probs, d_scores = [], []
            for half in range(2):
                at = (seq * (width // HEAD) + 2 * pair + half) * length
                prob = prob_ref[at:at + length, :]
                d_prob = dot_nt(da_h[half], v)
                wide_prob = prob.astype(FULL)
                weighted = wide_prob * d_prob
                d_score = weighted - wide_prob * jnp.sum(weighted, axis=-1, keepdims=True)
                probs.append(prob)
                d_scores.append(d_score.astype(LOW))
            d_v = dot_tn(jnp.concatenate(probs, axis=0), jnp.concatenate(da_h, axis=0))
            d_q = dot(jnp.concatenate(d_scores, axis=1), jnp.concatenate(halves(k), axis=0)) * scale
            d_k = dot_tn(jnp.concatenate(d_scores, axis=0), jnp.concatenate(halves(q), axis=0))
            dproj_ref[at_rows, lo:lo + 2 * HEAD] = d_q.astype(LOW)
            dproj_ref[at_rows, width + lo:width + lo + 2 * HEAD] = d_k.astype(LOW)
            dproj_ref[at_rows, 2 * width + lo:2 * width + lo + 2 * HEAD] = d_v.astype(LOW)
            if full:
                totals[0] = totals[0] + column_sum(d_q)
                totals[1] = totals[1] + column_sum(d_v)
        if full:
            small_ref[2:3, 2 * width + lo:2 * width + lo + 2 * HEAD] = totals[0]
            small_ref[2:3, 3 * width + lo:3 * width + lo + 2 * HEAD] = totals[1]
    total = d_res1
    for part in range(3):
        cols = slice(part * width, (part + 1) * width)
        w.need(2 * parts + 1 + part)
        total = total + dot_nt(dproj_ref[:, cols], wqkv[:, cols])
    dsub_ref[...] = total.astype(LOW)


def sub_backward(seqs, full, dsecond, res2, pre, res1, qkv, prob, qkv_w, out_w, up_w, down_w, gain):
    rows, width = res2.shape
    wide = up_w.shape[1]
    outs = [sds((rows, width), LOW)]
    scratch = [pltpu.VMEM(a.shape, LOW) for a in (qkv_w, out_w, up_w, down_w)]
    scratch = scratch + [pltpu.VMEM((rows, width), LOW)]
    if full:
        outs = outs + [sds((rows, width), LOW), sds((rows, wide), LOW), sds((rows, width), LOW),
                       sds((rows, 3 * width), LOW), sds((8, wide), FULL)]
    else:
        scratch = scratch + [pltpu.VMEM((rows, 3 * width), LOW)]
    return call(functools.partial(sub_backward_kernel, seqs, full), outs,
                [dsecond, res2, pre, res1, qkv, prob, qkv_w, out_w, up_w, down_w, gain],
                {6, 7, 8, 9}, scratch, "sub_backward",
                2 * rows * (qkv_w.size + out_w.size + up_w.size + down_w.size),
                4 + 2 * (wide // width))


def gru_backward_kernel(full, dpooled_ref, count_ref, tokc_ref, tokr_ref, r_ref, z_ref, n_ref, rn_ref,
                        state_ref, win_hbm, wrec_hbm, dchar_ref, *rest):
    if full:
        dgate_ref, drecn_ref, dcharin_ref, small_ref, dstate, win, wrec, sems = rest
    else:
        dstate, win, wrec, dgate_ref, sems = rest
    rows, width = dpooled_ref.shape
    count = tokc_ref.shape[0]
    hidden = wrec.shape[0]
    lanes = count // BLOCK_CH
    w = Stream(chunks(wrec_hbm, wrec, 1, 3 * hidden) + chunks(win_hbm, win, 1, width), sems)
    share = (dpooled_ref[...] / count_ref[...]).astype(LOW)
    token = (tokc_ref[...] == lax.broadcasted_iota(jnp.int32, (count, rows), 1))
    dstate[...] = dot(token.astype(FULL).astype(LOW), share)
    carry = [None, None]
    sums = [[None] * 4, [None] * 4]
    for turn in reversed(range(BLOCK_CH)):
        for way in range(2):
            at = turn if way == 0 else BLOCK_CH - 1 - turn
            before = at - 1 if way == 0 else at + 1
            here = slice(at * lanes, (at + 1) * lanes)
            base = way * 3 * hidden
            out = slice(way * hidden, (way + 1) * hidden)
            d_h = dstate[here, out]
            if carry[way] is not None:
                d_h = d_h + carry[way]
            r, z, n, rec_n = r_ref[here, out], z_ref[here, out], n_ref[here, out], rn_ref[here, out]
            d_n = d_h * (1.0 - z) * (1.0 - n * n)
            if turn > 0:
                prev = state_ref[before * lanes:(before + 1) * lanes, out]
                d_z = d_h * (prev - n) * (z * (1.0 - z))
            else:
                d_z = d_h * (-n) * (z * (1.0 - z))
            d_r = d_n * rec_n * (r * (1.0 - r))
            d_rec_n = d_n * r
            pieces = (d_r, d_z, d_n, d_rec_n)
            if full:
                for i, piece in enumerate(pieces):
                    one = column_sum(piece)
                    sums[way][i] = one if sums[way][i] is None else sums[way][i] + one
                drecn_ref[here, out] = d_rec_n.astype(LOW)
            low_r, low_z = d_r.astype(LOW), d_z.astype(LOW)
            dgate_ref[here, base:base + hidden] = low_r
            dgate_ref[here, base + hidden:base + 2 * hidden] = low_z
            dgate_ref[here, base + 2 * hidden:base + 3 * hidden] = d_n.astype(LOW)
            if turn > 0:
                w.need(way)
                d_rec = jnp.concatenate([low_r, low_z, d_rec_n.astype(LOW)], axis=1)
                carry[way] = d_h * z + dot_nt(d_rec, wrec[:, base:base + 3 * hidden])
    w.need(0, 1)
    if full:
        small_ref[2:8, :] = jnp.zeros((6, 6 * hidden), FULL)
        for way in range(2):
            base = way * 3 * hidden
            for i in range(3):
                at = slice(base + i * hidden, base + (i + 1) * hidden)
                small_ref[0:1, at] = sums[way][i]
                small_ref[1:2, at] = sums[way][i if i < 2 else 3]
    total = None
    for part in range(3):
        cols = slice(part * width, (part + 1) * width)
        w.need(2 + part)
        term = dot_nt(dgate_ref[:, cols], win[:, cols])
        total = term if total is None else total + term
    low = total.astype(LOW)
    if full:
        dcharin_ref[...] = low
    spread = (tokr_ref[...] == lax.broadcasted_iota(jnp.int32, (rows, count), 0))
    dchar_ref[...] = dot(spread.astype(FULL).astype(LOW), low).astype(LOW)


def gru_backward(full, dpooled, counts, tokc, tokr, r, z, n, rn, state, win, wrec):
    rows, width = dpooled.shape
    count = tokc.shape[0]
    wide = win.shape[1]
    outs = [sds((rows, width), LOW)]
    scratch = [pltpu.VMEM((count, width), FULL), pltpu.VMEM(win.shape, LOW), pltpu.VMEM(wrec.shape, LOW)]
    if full:
        outs = outs + [sds((count, wide), LOW), sds((count, width), LOW), sds((count, width), LOW),
                       sds((8, wide), FULL)]
    else:
        scratch = scratch + [pltpu.VMEM((count, wide), LOW)]
    return call(functools.partial(gru_backward_kernel, full), outs,
                [dpooled, counts, tokc, tokr, r, z, n, rn, state, win, wrec], {9, 10}, scratch,
                "gru_backward", 2 * count * (win.size + wrec.size) + 4 * count * rows * width, 5)


def in_blocks(values):
    return values.reshape(-1, BLOCK_CH).T.reshape(-1)


def layer_forward(seqs, save, sub, char, places, weights):
    (qkv_w, qvb, out_w, out_b, gain, shift, up_w, up_b, down_w, down_b, table, win, bin_, wrec,
     brec, mw, mb, cw, cb) = weights
    tokc, tokr, idc, counts = places
    first = sub_forward(seqs, save, sub, qkv_w, qvb, out_w, out_b, gain, shift, up_w, up_b,
                        down_w, down_b)
    second = gru_forward(save, char, tokc, tokr, idc, counts, table, win, bin_, wrec, brec)
    third = merge_forward(sub.shape[0] // seqs, save, first[0], second[0], mw, mb, cw, cb, gain,
                          shift)
    return first, second, third


def spread_cotangent(cotangent, positions, length):
    seqs, picks = positions.shape
    chosen = (positions[:, :, None] == jnp.arange(length, dtype=jnp.int32)).astype(LOW)
    grid = lax.dot_general(chosen, cotangent.reshape(seqs, picks, -1), (((1,), (1,)), ((0,), (0,))),
                           preferred_element_type=FULL)
    grid = grid.reshape(seqs * length, 2, -1)
    return grid[:, 0], grid[:, 1]


def sum_shares(whole, order):
    count = lax.axis_size("batch")
    bits = count.bit_length() - 1
    index = lax.axis_index("batch")
    held = whole.reshape((2,) * bits + whole.shape[1:])
    for bit in order:
        axis = bits - 1 - bit
        mine = (index >> bit) & 1
        keep = lax.dynamic_slice_in_dim(held, mine, 1, axis)
        give = lax.dynamic_slice_in_dim(held, 1 - mine, 1, axis)
        route = [(i, i ^ (1 << bit)) for i in range(count)]
        got = lax.ppermute(give, "batch", route)
        held = (keep.astype(FULL) + got.astype(FULL)).astype(LOW)
    return held.reshape(whole.shape[1:])


def body(stream_in, char_ids, char_lengths, mask_pos, cotangent, *params):
    weights = tuple(p.reshape(p.shape[1:]) if p.ndim > 2 else p for p in params)
    (qkv_w, qvb, out_w, out_b, gain, shift, up_w, up_b, down_w, down_b, table, win, bin_, wrec,
     brec, mw, mb, cw, cb) = weights
    section = lax.axis_index("section")
    sections = lax.axis_size("section")
    batch = lax.axis_size("batch")
    seqs, length, _, width = stream_in.shape
    rows = seqs * length
    hidden = wrec.shape[0]
    ends = jnp.cumsum(char_lengths, axis=-1)
    spots = jnp.arange(char_ids.shape[1], dtype=jnp.int32)
    token_of = jnp.sum((ends[:, None, :] <= spots[:, None]).astype(jnp.int32), axis=-1)
    token_of = in_blocks(token_of + length * jnp.arange(seqs, dtype=jnp.int32)[:, None])
    places = (token_of[:, None], token_of[None, :], in_blocks(char_ids)[:, None],
              char_lengths.reshape(-1, 1).astype(FULL))
    streams = stream_in.transpose(2, 0, 1, 3).reshape(2, rows, width)
    sub, char = streams[0], streams[1]

    def onward(pair):
        route = [(i, i + 1) for i in range(sections - 1)]
        a = lax.ppermute(pair[0], "section", route)
        a, b = lax.optimization_barrier((a, pair[1]))
        return a, lax.ppermute(b, "section", route)

    def back(value):
        return lax.ppermute(value, "section", [(i + 1, i) for i in range(sections - 1)])

    first, second, third = layer_forward(seqs, False, sub, char, places, weights)
    got = onward((third[0], third[1]))
    sub = jnp.where(section == 0, sub, got[0])
    char = jnp.where(section == 0, char, got[1])
    first, second, third = layer_forward(seqs, True, sub, char, places, weights)
    _, qkv, prob, att, res1, first_low, pre, act, res2 = first
    _, charin, r, z, n, rn, state, prev = second
    out_sub, out_char, mpre, joined, second_low, pooled_low, res3, res4 = third
    joined_all = lax.all_gather(joined, "batch")
    tokc, tokr, idc, counts = places
    grid = spread_cotangent(cotangent, mask_pos, length)

    d_second, d_pooled = merge_backward(length, False, grid[0], grid[1], res3, res4, mpre, mw, cw, gain)
    d_sub, = sub_backward(seqs, False, d_second, res2, pre, res1, qkv, prob, qkv_w, out_w, up_w,
                          down_w, gain)
    d_char, = gru_backward(False, d_pooled, counts, tokc, tokr, r, z, n, rn, state, win, wrec)
    last = section == sections - 1
    g_sub = jnp.where(last, grid[0], back(d_sub).astype(FULL))
    g_char = jnp.where(last, grid[1], back(d_char).astype(FULL))

    d_second, d_pooled, d_conv, d_mpre, small1 = merge_backward(
        length, True, g_sub, g_char, res3, res4, mpre, mw, cw, gain)
    d_sub, d_down, d_up, d_branch, d_proj, small2 = sub_backward(
        seqs, True, d_second, res2, pre, res1, qkv, prob, qkv_w, out_w, up_w, down_w, gain)
    d_char, d_gate, d_recn, d_charin, small3 = gru_backward(
        True, d_pooled, counts, tokc, tokr, r, z, n, rn, state, win, wrec)

    bits = list(range(batch.bit_length() - 1))

    def share(d_y, x):
        grad = dot_tn(d_y, x).astype(LOW)
        return sum_shares(grad.reshape(batch, -1, grad.shape[1]), bits)

    def placed(total):
        return total.T.astype(FULL)[None]

    g_merge = jnp.stack([placed(share(d_mpre[:, i * width:(i + 1) * width], x))
                         for i, x in enumerate((second_low, pooled_low))], 1)
    g_down = placed(share(d_down, act))
    g_up = placed(share(d_up, first_low))
    g_out = placed(share(d_branch, att))
    g_qkv = placed(share(d_proj, sub))
    g_win = placed(share(d_gate, charin))
    recs = []
    for way in range(2):
        base = way * 3 * hidden
        d_rec = jnp.concatenate([d_gate[:, base:base + 2 * hidden],
                                 d_recn[:, way * hidden:(way + 1) * hidden]], 1)
        recs.append(dot_tn(d_rec, prev[:, way * hidden:(way + 1) * hidden]))
    grad = jnp.concatenate(recs, 0).astype(LOW)
    g_rec = placed(sum_shares(grad.reshape(batch, -1, hidden), bits))
    ident = (in_blocks(char_ids)[:, None] == jnp.arange(table.shape[0], dtype=jnp.int32)).astype(LOW)
    g_table = placed(share(d_charin, ident))

    d_cols = d_conv.T.reshape(batch, -1, rows)
    d_cols = lax.all_to_all(d_cols, "batch", 0, 0, tiled=True)
    cols = d_cols.shape[1]
    d_cols = d_cols.reshape(batch, cols, seqs, length)
    none = jnp.zeros((batch, cols, seqs, 1), LOW)
    moved = jnp.stack([jnp.concatenate([d_cols[..., 1:], none], -1), d_cols,
                       jnp.concatenate([none, d_cols[..., :-1]], -1)], 1).reshape(batch, 3 * cols, rows)
    g_conv = lax.dot_general(joined_all, moved, (((0, 1), (0, 2)), ((), ())), preferred_element_type=FULL)
    g_conv = g_conv.reshape(2 * width, 3, cols).transpose(1, 0, 2)[None]

    small = lax.psum(jnp.concatenate([small1, small2, small3], 1), "batch")
    b = lax.axis_index("batch")
    at2, at3 = 2 * width, 2 * width + small2.shape[1]

    def piece(row, start, size):
        part = size // batch
        return lax.dynamic_slice(small, (row, start + b * part), (1, part))

    def pieces(*wanted):
        return jnp.concatenate([piece(*one) for one in wanted], 0)[None]

    ends_out = jnp.where(section == 0, jnp.stack([d_sub, d_char], 1), jnp.stack([out_sub, out_char], 1))
    return (
        ends_out.reshape(1, seqs, length, 2, width),
        g_qkv,
        pieces((2, at2 + 2 * width, width), (2, at2 + 3 * width, width)),
        g_out,
        piece(1, at2 + width, width),
        pieces((1, at2 + 2 * width, width), (1, at2 + 3 * width, width), (2, 0, width), (2, width, width)),
        pieces((2, at2, width), (2, at2 + width, width), (3, 0, width), (3, width, width)),
        g_up,
        piece(0, at2, small2.shape[1]),
        g_down,
        piece(1, at2, width),
        g_table,
        g_win,
        piece(0, at3, small3.shape[1]),
        g_rec,
        piece(1, at3, small3.shape[1]),
        g_merge,
        pieces((1, 0, width), (1, width, width)),
        g_conv,
        piece(0, 0, 2 * width),
    )


def solution(mesh):
    by = P("batch")
    part = P("section")

    def columns(rank):
        return P(*(["section"] + [None] * (rank - 2) + ["batch"]))

    return jax.shard_map(
        body,
        mesh=mesh,
        in_specs=(by,) * 5 + (part,) * 19,
        out_specs=(P("section", "batch"),) + tuple(
            columns(rank) for rank in (3, 3, 3, 2, 3, 3, 3, 2, 3, 2, 3, 3, 2, 3, 2, 4, 3, 4, 2)),
        check_vma=False,
    )
```

```python
import functools
import math

import jax
import jax.numpy as jnp
from jax import lax
from jax.experimental import pallas as pl
from jax.experimental.pallas import tpu as pltpu
from jax.sharding import PartitionSpec as P

HEAD = 64
BLOCK_CH = 8
EPSILON = 1e-05
LOW = jnp.bfloat16
FULL = jnp.float32
VMEM_LIMIT = 58 * 1024 * 1024


def dot(left, right):
    return lax.dot_general(left, right, (((1,), (0,)), ((), ())), preferred_element_type=FULL)


def dot_nt(left, right):
    return lax.dot_general(left, right, (((1,), (1,)), ((), ())), preferred_element_type=FULL)


def dot_tn(left, right):
    return lax.dot_general(left, right, (((0,), (0,)), ((), ())), preferred_element_type=FULL)


def norm_parts(values):
    row_mean = jnp.mean(values, axis=-1, keepdims=True)
    centered = values - row_mean
    row_var = jnp.mean(centered * centered, axis=-1, keepdims=True)
    inverse = lax.rsqrt(row_var + EPSILON)
    return centered * inverse, inverse


def norm(values, gain, shift):
    return norm_parts(values)[0] * gain + shift


def norm_back(values, gain, grad):
    unit, inverse = norm_parts(values)
    scaled = grad * gain
    first = jnp.mean(scaled, axis=-1, keepdims=True)
    second = jnp.mean(scaled * unit, axis=-1, keepdims=True)
    return inverse * (scaled - first - unit * second), unit


GELU_A = 0.7978845608028654
GELU_B = 0.044715


def gelu(x):
    return 0.5 * x * (1.0 + jnp.tanh(GELU_A * (x + GELU_B * x * x * x)))


def gelu_slope(x):
    square = x * x
    bent = jnp.tanh(GELU_A * (x + GELU_B * square * x))
    return 0.5 * (1.0 + bent) + 0.5 * x * (1.0 - bent * bent) * (
        GELU_A * (1.0 + 3.0 * GELU_B * square)
    )


def sigmoid(x):
    return 0.5 * jnp.tanh(0.5 * x) + 0.5


def column_sum(values):
    return jnp.sum(values, axis=0, keepdims=True)


class Stream:
    def __init__(self, pairs, sems):
        self.copies = [
            pltpu.make_async_copy(src, dst, sems.at[i]) for i, (src, dst) in enumerate(pairs)
        ]
        for copy in self.copies:
            copy.start()
        self.waited = set()

    def need(self, *which):
        for i in which:
            if i not in self.waited:
                self.waited.add(i)
                self.copies[i].wait()


def chunks(src, dst, axis, size):
    total = src.shape[axis]
    parts = []
    for start in range(0, total, size):
        index = [slice(None)] * len(src.shape)
        index[axis] = pl.ds(start, min(size, total - start))
        parts.append((src.at[tuple(index)], dst.at[tuple(index)]))
    return parts


def fill(out, near, terms):
    lead, chunk, columns = out.shape
    part = [term[9] for term in terms if term[8] > 0]
    if part:
        out[:, :, part[0]:] = jnp.zeros((lead, chunk, columns - part[0]), LOW)
    for d_y, base, height, start, stop, x, first, last, row, column in terms:
        d = jnp.concatenate([
            d_y[pl.ds(pl.multiple_of(base + (2 * i + near) * height, 16), height), :]
            for i in range(start, stop)], axis=0)
        step = min(last - first, 768)
        for at in range(first, last, step):
            value = dot(d, x[:, at:at + step]).astype(LOW)
            lanes = slice(column + at - first, column + at - first + step)
            out[start:stop, row:row + height, lanes] = value.reshape(stop - start, height, step)


def fill_plain(shape, near, terms):
    out = jnp.zeros(shape, LOW)
    for d_y, base, height, start, stop, x, first, last, row, column in terms:
        count = stop - start
        d = d_y[base + 2 * start * height:base + 2 * stop * height].reshape(count, 2, height, -1)
        d = lax.dynamic_slice_in_dim(d, near, 1, 1).reshape(count * height, -1)
        value = dot(d, x[:, first:last]).astype(LOW).reshape(count, height, last - first)
        out = lax.dynamic_update_slice(out, value, (start, row, column))
    return out


def named(plan, d_ys, xs):
    return [(d_ys[d],) + rest[:4] + (xs[rest[4]],) + rest[5:] for d, *rest in map(tuple, plan)
            for rest in [tuple(rest)]]


class Blocks:
    def __init__(self, bits, count, plans, d_shapes, xs):
        self.bits, self.count, self.plans, self.d_shapes, self.xs = bits, count, plans, d_shapes, xs
        self.inside = all(plan[0] % 16 == 0 for plan in plans)

    def shapes(self):
        return [sds((self.count, plan[0], plan[1]), LOW) for plan in self.plans]

    def outs(self):
        return self.shapes() * 2 if self.inside else [sds(shape, LOW) for shape in self.d_shapes]

    def scratch(self):
        return [pltpu.VMEM(shape, LOW) for shape in self.d_shapes] if self.inside else []

    def inputs(self):
        return [self.bits] + (self.xs if self.inside else [])

    def split(self, refs):
        if not self.inside:
            return refs[:len(self.d_shapes)], lambda bits_ref, xs: None
        results, d_ys = refs[:2 * len(self.plans)], refs[2 * len(self.plans):]

        def make(bits_ref, xs):
            near = bits_ref[0]
            for own in range(2):
                for i, plan in enumerate(self.plans):
                    fill(results[own * len(self.plans) + i], near if own else 1 - near,
                         named(plan[2], d_ys, xs))

        return d_ys, make

    def finish(self, results):
        if self.inside:
            return results[:len(self.plans)], results[len(self.plans):]
        near = self.bits[0]
        return tuple([fill_plain(shape.shape, which, named(plan[2], results, self.xs))
                      for shape, plan in zip(self.shapes(), self.plans)] for which in (1 - near, near))


def any_spec():
    return pl.BlockSpec(memory_space=pl.ANY)


def vmem_spec():
    return pl.BlockSpec(memory_space=pltpu.VMEM)


def sds(shape, dtype):
    return jax.ShapeDtypeStruct(shape, dtype)


def call(kernel, outs, ins, streamed, scratch, name, flops, copies, blocks=None):
    if blocks is not None:
        ins, outs = list(ins) + blocks.inputs(), list(outs) + blocks.outs()
        scratch = blocks.scratch() + list(scratch)
        scalar = len(ins) - len(blocks.inputs())
    else:
        scalar = -1
    moved = sum(a.size * a.dtype.itemsize for a in ins) + sum(
        o.size * o.dtype.itemsize for o in outs
    )
    return pl.pallas_call(
        kernel,
        out_shape=outs,
        in_specs=[any_spec() if i in streamed else pl.BlockSpec(memory_space=pltpu.SMEM) if i == scalar
                  else vmem_spec() for i in range(len(ins))],
        out_specs=[vmem_spec() for _ in outs],
        scratch_shapes=list(scratch) + [pltpu.SemaphoreType.DMA((copies,))],
        compiler_params=pltpu.CompilerParams(vmem_limit_bytes=VMEM_LIMIT),
        cost_estimate=pl.CostEstimate(flops=flops, bytes_accessed=moved, transcendentals=0),
        name=name,
    )(*ins)


def sub_forward_kernel(seqs, save, s_ref, qkv_hbm, qvb_ref, out_hbm, outb_ref, gain_ref, shift_ref,
                       up_hbm, upb_ref, down_hbm, downb_ref, *rest):
    if save:
        (after_ref, qkv_ref, prob_ref, att_ref, res1_ref, first_ref, pre_ref, act_ref, res2_ref,
         wqkv, wout, wup, wdown, sems) = rest
    else:
        after_ref, wqkv, wout, wup, wdown, qkv_ref, att_ref, sems = rest
    width = s_ref.shape[1]
    wide = wup.shape[1]
    length = s_ref.shape[0] // seqs
    w = Stream(chunks(qkv_hbm, wqkv, 1, width) + chunks(out_hbm, wout, 1, width)
               + chunks(up_hbm, wup, 1, width) + chunks(down_hbm, wdown, 0, width), sems)
    for part in range(3):
        w.need(part)
        cols = slice(part * width, (part + 1) * width)
        y = dot(s_ref[...], wqkv[:, cols])
        if part == 0:
            y = (y + qvb_ref[0:1, :]) * HEAD ** -0.5
        elif part == 2:
            y = y + qvb_ref[1:2, :]
        qkv_ref[:, cols] = y.astype(LOW)
    lanes = lax.broadcasted_iota(jnp.int32, (length, 2 * HEAD), 1)
    even = lanes < HEAD
    for seq in range(seqs):
        rows = slice(seq * length, (seq + 1) * length)
        for pair in range(width // (2 * HEAD)):
            lo = pair * 2 * HEAD
            q = qkv_ref[rows, lo:lo + 2 * HEAD]
            k = qkv_ref[rows, width + lo:width + lo + 2 * HEAD]
            v = qkv_ref[rows, 2 * width + lo:2 * width + lo + 2 * HEAD]
            zero = jnp.zeros_like(q)
            probs = []
            for half in range(2):
                mask = even if half == 0 else ~even
                scores = dot_nt(jnp.where(mask, q, zero), k)
                peak = jnp.max(scores, axis=-1, keepdims=True)
                e = jnp.exp(scores - peak)
                prob = (e / jnp.sum(e, axis=-1, keepdims=True)).astype(LOW)
                probs.append(prob)
                if save:
                    at = (seq * (width // HEAD) + 2 * pair + half) * length
                    prob_ref[at:at + length, :] = prob
            both = jnp.concatenate(probs, axis=1)
            vv = jnp.concatenate([jnp.where(even, v, zero), jnp.where(even, zero, v)], axis=0)
            att_ref[rows, lo:lo + 2 * HEAD] = dot(both, vv).astype(LOW)
    w.need(3)
    res1 = s_ref[...].astype(FULL) + dot(att_ref[...], wout[...]) + outb_ref[...]
    after = norm(res1, gain_ref[0:1, :], shift_ref[0:1, :])
    low = after.astype(LOW)
    if save:
        res1_ref[...] = res1
        first_ref[...] = low
    total = after + downb_ref[...]
    for part in range(wide // width):
        cols = slice(part * width, (part + 1) * width)
        w.need(4 + part)
        pre = dot(low, wup[:, cols]) + upb_ref[:, cols]
        act = gelu(pre).astype(LOW)
        if save:
            pre_ref[:, cols] = pre
            act_ref[:, cols] = act
        w.need(4 + wide // width + part)
        total = total + dot(act, wdown[cols, :])
    if save:
        res2_ref[...] = total
    after_ref[...] = norm(total, gain_ref[1:2, :], shift_ref[1:2, :])


def sub_forward(seqs, save, s, qkv_w, qvb, out_w, out_b, gain, shift, up_w, up_b, down_w, down_b):
    rows, width = s.shape
    wide = up_w.shape[1]
    length = rows // seqs
    outs = [sds((rows, width), FULL)]
    scratch = [pltpu.VMEM(a.shape, LOW) for a in (qkv_w, out_w, up_w, down_w)]
    saved = [sds((rows, 3 * width), LOW), sds((seqs * (width // HEAD) * length, length), LOW),
             sds((rows, width), LOW), sds((rows, width), FULL), sds((rows, width), LOW),
             sds((rows, wide), FULL), sds((rows, wide), LOW), sds((rows, width), FULL)]
    if save:
        outs = outs + saved
    else:
        scratch = scratch + [pltpu.VMEM(saved[0].shape, LOW), pltpu.VMEM(saved[2].shape, LOW)]
    copies = 4 + 2 * (wide // width)
    return call(functools.partial(sub_forward_kernel, seqs, save), outs,
                [s, qkv_w, qvb, out_w, out_b, gain, shift, up_w, up_b, down_w, down_b],
                {1, 3, 7, 9}, scratch, "sub_forward",
                2 * rows * (qkv_w.size + out_w.size + up_w.size + down_w.size), copies)


def gru_forward_kernel(save, c_ref, tokc_ref, tokr_ref, idc_ref, count_ref, table_hbm, win_hbm,
                       bin_ref, wrec_hbm, brec_ref, *rest):
    if save:
        (pooled_ref, charin_ref, r_ref, z_ref, n_ref, rn_ref, state_ref, prev_ref,
         table, win, wrec, gate, low_state, sems) = rest
    else:
        pooled_ref, table, win, wrec, gate, low_state, charin_ref, sems = rest
    rows, width = c_ref.shape
    count = tokc_ref.shape[0]
    hidden = wrec.shape[0]
    w = Stream([(table_hbm, table)] + chunks(win_hbm, win, 1, width)
               + chunks(wrec_hbm, wrec, 1, 3 * hidden), sems)
    token = (tokc_ref[...] == lax.broadcasted_iota(jnp.int32, (count, rows), 1))
    ident = (idc_ref[...] == lax.broadcasted_iota(jnp.int32, (count, table.shape[0]), 1))
    w.need(0)
    x = dot(token.astype(FULL).astype(LOW), c_ref[...]) + dot(ident.astype(FULL).astype(LOW), table[...])
    charin_ref[...] = x.astype(LOW)
    for part in range(3):
        w.need(1 + part)
        cols = slice(part * width, (part + 1) * width)
        gate[:, cols] = dot(charin_ref[...], win[:, cols]) + bin_ref[:, cols]
    lanes = count // BLOCK_CH
    state = [None, None]
    for turn in range(BLOCK_CH):
        for way in range(2):
            at = turn if way == 0 else BLOCK_CH - 1 - turn
            here = slice(at * lanes, (at + 1) * lanes)
            base = way * 3 * hidden
            out = slice(way * hidden, (way + 1) * hidden)
            bias = brec_ref[:, base:base + 3 * hidden]
            g = gate[here, base:base + 3 * hidden]
            if turn == 0:
                rec_n = jnp.broadcast_to(bias[:, 2 * hidden:], (lanes, hidden))
                rz = g[:, :2 * hidden] + bias[:, :2 * hidden]
                if save:
                    prev_ref[here, out] = jnp.zeros((lanes, hidden), LOW)
            else:
                w.need(4 + way)
                low = state[way].astype(LOW)
                if save:
                    prev_ref[here, out] = low
                rec = dot(low, wrec[:, base:base + 3 * hidden]) + bias
                rec_n = rec[:, 2 * hidden:]
                rz = g[:, :2 * hidden] + rec[:, :2 * hidden]
            rz = sigmoid(rz)
            r, z = rz[:, :hidden], rz[:, hidden:]
            n = jnp.tanh(g[:, 2 * hidden:] + r * rec_n)
            new = (1.0 - z) * n
            if turn > 0:
                new = new + z * state[way]
            state[way] = new
            low_state[here, out] = new.astype(LOW)
            if save:
                r_ref[here, out] = r
                z_ref[here, out] = z
                n_ref[here, out] = n
                rn_ref[here, out] = rec_n
                state_ref[here, out] = new
    spread = (tokr_ref[...] == lax.broadcasted_iota(jnp.int32, (rows, count), 0))
    pooled = dot(spread.astype(FULL).astype(LOW), low_state[...])
    pooled_ref[...] = pooled / count_ref[...]


def gru_forward(save, c, tokc, tokr, idc, counts, table, win, bin_, wrec, brec):
    rows, width = c.shape
    count = tokc.shape[0]
    outs = [sds((rows, width), FULL)]
    scratch = [pltpu.VMEM(a.shape, LOW) for a in (table, win, wrec)]
    scratch = scratch + [pltpu.VMEM((count, win.shape[1]), FULL), pltpu.VMEM((count, width), LOW)]
    if save:
        outs = outs + [sds((count, width), LOW)] + [sds((count, width), FULL)] * 5
        outs = outs + [sds((count, width), LOW)]
    else:
        scratch = scratch + [pltpu.VMEM((count, width), LOW)]
    return call(functools.partial(gru_forward_kernel, save), outs,
                [c, tokc, tokr, idc, counts, table, win, bin_, wrec, brec],
                {5, 6, 8}, scratch, "gru_forward",
                2 * count * (win.size + wrec.size) + 2 * count * width * (2 * rows + table.shape[0]), 6)


def shift_rows(values, by, length):
    rows, width = values.shape
    zero = jnp.zeros((1, width), values.dtype)
    pos = lax.broadcasted_iota(jnp.int32, (rows, 1), 0) % length
    if by == 1:
        moved = jnp.concatenate([zero, values[:-1]], axis=0)
        return jnp.where(pos == 0, 0.0, moved)
    moved = jnp.concatenate([values[1:], zero], axis=0)
    return jnp.where(pos == length - 1, 0.0, moved)


def merge_forward_kernel(length, save, after_ref, pooled_ref, mw_hbm, mb_ref, cw_hbm, cb_ref,
                         gain_ref, shift_ref, *rest):
    if save:
        (sub_ref, char_ref, pre_ref, joined_ref, second_ref, poollow_ref, res3_ref, res4_ref,
         mw, cw, sems) = rest
    else:
        sub_ref, char_ref, mw, cw, sems = rest
    width = after_ref.shape[1]
    w = Stream(chunks(mw_hbm, mw, 0, 1) + chunks(cw_hbm, cw, 0, 1), sems)
    halves = []
    for side in range(2):
        w.need(side)
        cols = slice(side * width, (side + 1) * width)
        low = (after_ref if side == 0 else pooled_ref)[...].astype(LOW)
        pre = dot(low, mw[side]) + mb_ref[side:side + 1, :]
        if save:
            (second_ref if side == 0 else poollow_ref)[...] = low
            pre_ref[:, cols] = pre
        halves.append(gelu(pre))
    joined = jnp.concatenate(halves, axis=1)
    if save:
        joined_ref[...] = joined.astype(LOW)
    total = cb_ref[...]
    for k in range(3):
        moved = joined if k == 1 else shift_rows(joined, 1 - k, length)
        w.need(2 + k)
        total = total + dot(moved.astype(LOW), cw[k])
    res3 = after_ref[...] + total[:, :width]
    res4 = pooled_ref[...] + total[:, width:]
    if save:
        res3_ref[...] = res3
        res4_ref[...] = res4
    sub_ref[...] = norm(res3, gain_ref[2:3, :], shift_ref[2:3, :]).astype(LOW)
    char_ref[...] = norm(res4, gain_ref[3:4, :], shift_ref[3:4, :]).astype(LOW)


def merge_forward(length, save, after, pooled, mw, mb, cw, cb, gain, shift):
    rows, width = after.shape
    outs = [sds((rows, width), LOW)] * 2
    scratch = [pltpu.VMEM(mw.shape, LOW), pltpu.VMEM(cw.shape, LOW)]
    if save:
        outs = outs + [sds((rows, 2 * width), FULL), sds((rows, 2 * width), LOW),
                       sds((rows, width), LOW), sds((rows, width), LOW),
                       sds((rows, width), FULL), sds((rows, width), FULL)]
    return call(functools.partial(merge_forward_kernel, length, save), outs,
                [after, pooled, mw, mb, cw, cb, gain, shift], {2, 4}, scratch, "merge_forward",
                2 * rows * (mw.size + cw.size), 5)


def merge_backward_kernel(length, full, gsub_ref, gchar_ref, res3_ref, res4_ref, pre_ref, mw_hbm, cw_hbm,
                          gain_ref, *rest):
    if full:
        xs, rest = rest[:len(full.inputs())], rest[len(full.inputs()):]
        dsecond_ref, dpooled_ref, dconv_ref, small_ref, *rest, mw, cw, sems = rest
        (dpre_ref,), make = full.split(rest)
    else:
        dsecond_ref, dpooled_ref, mw, cw, sems = rest
    width = res3_ref.shape[1]
    w = Stream(chunks(cw_hbm, cw, 0, 1) + chunks(mw_hbm, mw, 0, 1), sems)
    grads = [gsub_ref[...], gchar_ref[...]]
    d_res = []
    for side in range(2):
        d, unit = norm_back((res3_ref, res4_ref)[side][...], gain_ref[2 + side:3 + side, :], grads[side])
        d_res.append(d)
        if full:
            small_ref[4 + side:5 + side, :] = column_sum(grads[side] * unit)
            small_ref[6 + side:7 + side, :] = column_sum(grads[side])
            small_ref[side:side + 1, :] = column_sum(d)
    d_conv = jnp.concatenate(d_res, axis=1)
    if full:
        dconv_ref[...] = d_conv.astype(LOW).T
    total = None
    for k in range(3):
        moved = d_conv if k == 1 else shift_rows(d_conv, k - 1, length)
        w.need(k)
        term = dot_nt(moved.astype(LOW), cw[k])
        total = term if total is None else total + term
    d_pre = total * gelu_slope(pre_ref[...])
    d_low = d_pre.astype(LOW)
    if full:
        dpre_ref[...] = d_low.T
        for side in range(2):
            small_ref[2 + side:3 + side, :] = column_sum(d_pre[:, side * width:(side + 1) * width])
    for side in range(2):
        w.need(3 + side)
        (dsecond_ref if side == 0 else dpooled_ref)[...] = d_res[side] + dot_nt(
            d_low[:, side * width:(side + 1) * width], mw[side])
    if full:
        make(xs[0], xs[1:])


def merge_backward(length, full, gsub, gchar, res3, res4, pre, mw, cw, gain):
    rows, width = res3.shape
    outs = [sds((rows, width), FULL)] * 2
    if full:
        outs = outs + [sds((2 * width, rows), LOW), sds((8, width), FULL)]
    scratch = [pltpu.VMEM(mw.shape, LOW), pltpu.VMEM(cw.shape, LOW)]
    return call(functools.partial(merge_backward_kernel, length, full), outs,
                [gsub, gchar, res3, res4, pre, mw, cw, gain], {5, 6}, scratch, "merge_backward",
                2 * rows * (mw.size + cw.size), 5, full)


def ffn_backward_kernel(full, dsecond_ref, res2_ref, pre_ref, res1_ref, up_hbm, down_hbm, gain_ref, *rest):
    if full:
        xs, rest = rest[:len(full.inputs())], rest[len(full.inputs()):]
        dres1_ref, small_ref, *rest, wup, wdown, sems = rest
        (ddown_ref, dup_ref, dbranch_ref), make = full.split(rest)
    else:
        dres1_ref, wup, wdown, sems = rest
    rows, width = dres1_ref.shape
    wide = wup.shape[1]
    parts = wide // width
    w = Stream(chunks(down_hbm, wdown, 0, width) + chunks(up_hbm, wup, 1, width), sems)
    d_second = dsecond_ref[...]
    d_res2, unit = norm_back(res2_ref[...], gain_ref[1:2, :], d_second)
    d_low = d_res2.astype(LOW)
    if full:
        ddown_ref[...] = d_low.T
        small_ref[parts:parts + 1, :] = column_sum(d_res2)
        small_ref[parts + 3:parts + 4, :] = column_sum(d_second * unit)
        small_ref[parts + 5:parts + 6, :] = column_sum(d_second)
        small_ref[parts + 6:16, :] = jnp.zeros((10 - parts, width), FULL)
    d_first = d_res2
    for part in range(parts):
        cols = slice(part * width, (part + 1) * width)
        w.need(part)
        d_up = dot_nt(d_low, wdown[cols, :]) * gelu_slope(pre_ref[:, cols])
        up_low = d_up.astype(LOW)
        if full:
            dup_ref[cols, :] = up_low.T
            small_ref[part:part + 1, :] = column_sum(d_up)
        w.need(parts + part)
        d_first = d_first + dot_nt(up_low, wup[:, cols])
    d_res1, unit = norm_back(res1_ref[...], gain_ref[0:1, :], d_first)
    dres1_ref[...] = d_res1
    if full:
        dbranch_ref[...] = d_res1.astype(LOW).T
        small_ref[parts + 1:parts + 2, :] = column_sum(d_res1)
        small_ref[parts + 2:parts + 3, :] = column_sum(d_first * unit)
        small_ref[parts + 4:parts + 5, :] = column_sum(d_first)
        make(xs[0], xs[1:])


def ffn_backward(full, dsecond, res2, pre, res1, up_w, down_w, gain):
    rows, width = res2.shape
    wide = up_w.shape[1]
    outs = [sds((rows, width), FULL)]
    scratch = [pltpu.VMEM(a.shape, LOW) for a in (up_w, down_w)]
    if full:
        outs = outs + [sds((16, width), FULL)]
    return call(functools.partial(ffn_backward_kernel, full), outs,
                [dsecond, res2, pre, res1, up_w, down_w, gain], {4, 5}, scratch, "ffn_backward",
                2 * rows * (up_w.size + down_w.size), 2 * (wide // width), full)


def attention_backward_kernel(seqs, full, dres1_ref, qkv_ref, prob_ref, qkv_hbm, out_hbm, *rest):
    if full:
        xs, rest = rest[:len(full.inputs())], rest[len(full.inputs()):]
        dsub_ref, small_ref, *rest, wqkv, wout, datt, dproj_ref, sems = rest
        (dprojt_ref,), make = full.split(rest)
    else:
        dsub_ref, wqkv, wout, datt, dproj_ref, sems = rest
    rows, width = dsub_ref.shape
    length = rows // seqs
    w = Stream(chunks(out_hbm, wout, 1, width) + chunks(qkv_hbm, wqkv, 1, width), sems)
    w.need(0)
    datt[...] = dot_nt(dres1_ref[...].astype(LOW), wout[...]).astype(LOW)
    even = lax.broadcasted_iota(jnp.int32, (length, 2 * HEAD), 1) < HEAD
    scale = HEAD ** -0.5
    for pair in range(width // (2 * HEAD)):
        lo = pair * 2 * HEAD
        totals = [0.0, 0.0]
        for seq in range(seqs):
            at_rows = slice(seq * length, (seq + 1) * length)
            q = qkv_ref[at_rows, lo:lo + 2 * HEAD]
            k = qkv_ref[at_rows, width + lo:width + lo + 2 * HEAD]
            v = qkv_ref[at_rows, 2 * width + lo:2 * width + lo + 2 * HEAD]
            da = datt[at_rows, lo:lo + 2 * HEAD]
            zero = jnp.zeros_like(q)

            def halves(x):
                return jnp.where(even, x, zero), jnp.where(even, zero, x)

            da_h = halves(da)
            probs, d_scores = [], []
            for half in range(2):
                at = (seq * (width // HEAD) + 2 * pair + half) * length
                prob = prob_ref[at:at + length, :]
                d_prob = dot_nt(da_h[half], v)
                wide_prob = prob.astype(FULL)
                weighted = wide_prob * d_prob
                d_score = weighted - wide_prob * jnp.sum(weighted, axis=-1, keepdims=True)
                probs.append(prob)
                d_scores.append(d_score.astype(LOW))
            d_v = dot_tn(jnp.concatenate(probs, axis=0), jnp.concatenate(da_h, axis=0))
            d_q = dot(jnp.concatenate(d_scores, axis=1), jnp.concatenate(halves(k), axis=0)) * scale
            d_k = dot_tn(jnp.concatenate(d_scores, axis=0), jnp.concatenate(halves(q), axis=0))
            dproj_ref[at_rows, lo:lo + 2 * HEAD] = d_q.astype(LOW)
            dproj_ref[at_rows, width + lo:width + lo + 2 * HEAD] = d_k.astype(LOW)
            dproj_ref[at_rows, 2 * width + lo:2 * width + lo + 2 * HEAD] = d_v.astype(LOW)
            if full:
                totals[0] = totals[0] + column_sum(d_q)
                totals[1] = totals[1] + column_sum(d_v)
        if full:
            small_ref[0:1, lo:lo + 2 * HEAD] = totals[0]
            small_ref[1:2, lo:lo + 2 * HEAD] = totals[1]
    total = dres1_ref[...]
    for part in range(3):
        cols = slice(part * width, (part + 1) * width)
        if full:
            dprojt_ref[cols, :] = dproj_ref[:, cols].T
        w.need(1 + part)
        total = total + dot_nt(dproj_ref[:, cols], wqkv[:, cols])
    dsub_ref[...] = total.astype(LOW)
    if full:
        small_ref[2:8, :] = jnp.zeros((6, width), FULL)
        make(xs[0], xs[1:])


def attention_backward(seqs, full, dres1, qkv, prob, qkv_w, out_w):
    rows, width = dres1.shape
    outs = [sds((rows, width), LOW)]
    scratch = [pltpu.VMEM(a.shape, LOW) for a in (qkv_w, out_w)]
    scratch = scratch + [pltpu.VMEM((rows, width), LOW), pltpu.VMEM((rows, 3 * width), LOW)]
    if full:
        outs = outs + [sds((8, width), FULL)]
    return call(functools.partial(attention_backward_kernel, seqs, full), outs,
                [dres1, qkv, prob, qkv_w, out_w], {3, 4}, scratch, "attention_backward",
                2 * rows * (qkv_w.size + out_w.size), 4, full)


def gru_backward_kernel(full, dpooled_ref, count_ref, tokc_ref, tokr_ref, r_ref, z_ref, n_ref, rn_ref,
                        state_ref, win_hbm, wrec_hbm, *rest):
    if full:
        xs, rest = rest[:len(full.inputs())], rest[len(full.inputs()):]
        dchar_ref, small_ref, *rest, dstate, win, wrec, dgate_ref, drecn_ref, sems = rest
        (dgatet_ref, drect_ref, dchart_ref), make = full.split(rest)
    else:
        dchar_ref, dstate, win, wrec, dgate_ref, sems = rest
    rows, width = dpooled_ref.shape
    count = tokc_ref.shape[0]
    hidden = wrec.shape[0]
    lanes = count // BLOCK_CH
    w = Stream(chunks(wrec_hbm, wrec, 1, 3 * hidden) + chunks(win_hbm, win, 1, width), sems)
    share = (dpooled_ref[...] / count_ref[...]).astype(LOW)
    token = (tokc_ref[...] == lax.broadcasted_iota(jnp.int32, (count, rows), 1))
    dstate[...] = dot(token.astype(FULL).astype(LOW), share)
    carry = [None, None]
    sums = [[None] * 4, [None] * 4]
    for turn in reversed(range(BLOCK_CH)):
        for way in range(2):
            at = turn if way == 0 else BLOCK_CH - 1 - turn
            before = at - 1 if way == 0 else at + 1
            here = slice(at * lanes, (at + 1) * lanes)
            base = way * 3 * hidden
            out = slice(way * hidden, (way + 1) * hidden)
            d_h = dstate[here, out]
            if carry[way] is not None:
                d_h = d_h + carry[way]
            r, z, n, rec_n = r_ref[here, out], z_ref[here, out], n_ref[here, out], rn_ref[here, out]
            d_n = d_h * (1.0 - z) * (1.0 - n * n)
            if turn > 0:
                prev = state_ref[before * lanes:(before + 1) * lanes, out]
                d_z = d_h * (prev - n) * (z * (1.0 - z))
            else:
                d_z = d_h * (-n) * (z * (1.0 - z))
            d_r = d_n * rec_n * (r * (1.0 - r))
            d_rec_n = d_n * r
            pieces = (d_r, d_z, d_n, d_rec_n)
            if full:
                for i, piece in enumerate(pieces):
                    one = column_sum(piece)
                    sums[way][i] = one if sums[way][i] is None else sums[way][i] + one
                drecn_ref[here, out] = d_rec_n.astype(LOW)
            low_r, low_z = d_r.astype(LOW), d_z.astype(LOW)
            dgate_ref[here, base:base + hidden] = low_r
            dgate_ref[here, base + hidden:base + 2 * hidden] = low_z
            dgate_ref[here, base + 2 * hidden:base + 3 * hidden] = d_n.astype(LOW)
            if turn > 0:
                w.need(way)
                d_rec = jnp.concatenate([low_r, low_z, d_rec_n.astype(LOW)], axis=1)
                carry[way] = d_h * z + dot_nt(d_rec, wrec[:, base:base + 3 * hidden])
    w.need(0, 1)
    if full:
        for way in range(2):
            for i in range(3):
                at = slice((3 * way + i) * hidden, (3 * way + i + 1) * hidden)
                turned = dgate_ref[:, at].T
                dgatet_ref[at, :] = turned
                drect_ref[at, :] = turned if i < 2 else drecn_ref[:, way * hidden:(way + 1) * hidden].T
        small_ref[6:8, :] = jnp.zeros((2, width), FULL)
        for kind in range(2):
            line = [sums[way][i if i < 2 or kind == 0 else 3] for way in range(2) for i in range(3)]
            for i in range(3):
                small_ref[3 * kind + i:3 * kind + i + 1, :] = jnp.concatenate(line[2 * i:2 * i + 2], axis=1)
    total = None
    for part in range(3):
        cols = slice(part * width, (part + 1) * width)
        w.need(2 + part)
        term = dot_nt(dgate_ref[:, cols], win[:, cols])
        total = term if total is None else total + term
    low = total.astype(LOW)
    if full:
        dchart_ref[...] = low.T
    spread = (tokr_ref[...] == lax.broadcasted_iota(jnp.int32, (rows, count), 0))
    dchar_ref[...] = dot(spread.astype(FULL).astype(LOW), low).astype(LOW)
    if full:
        make(xs[0], xs[1:])


def gru_backward(full, dpooled, counts, tokc, tokr, r, z, n, rn, state, win, wrec):
    rows, width = dpooled.shape
    count = tokc.shape[0]
    wide = win.shape[1]
    outs = [sds((rows, width), LOW)]
    scratch = [pltpu.VMEM((count, width), FULL), pltpu.VMEM(win.shape, LOW), pltpu.VMEM(wrec.shape, LOW),
               pltpu.VMEM((count, wide), LOW)]
    if full:
        outs = outs + [sds((8, width), FULL)]
        scratch = scratch + [pltpu.VMEM((count, width), LOW)]
    return call(functools.partial(gru_backward_kernel, full), outs,
                [dpooled, counts, tokc, tokr, r, z, n, rn, state, win, wrec], {9, 10}, scratch,
                "gru_backward", 2 * count * (win.size + wrec.size) + 4 * count * rows * width, 5, full)


def conv_grad_kernel(length, joined_ref, d_ref, out_ref):
    sources, cols, rows = d_ref.shape
    pos = lax.broadcasted_iota(jnp.int32, (cols, rows), 1) % length
    moved = [[], [], []]
    for i in range(sources):
        d = d_ref[i].astype(FULL)
        moved[0].append(jnp.where(pos == length - 1, 0.0, pltpu.roll(d, rows - 1, 1)).astype(LOW))
        moved[1].append(d_ref[i])
        moved[2].append(jnp.where(pos == 0, 0.0, pltpu.roll(d, 1, 1)).astype(LOW))
    moved = jnp.concatenate([jnp.concatenate(one, axis=1) for one in moved], axis=0)
    width = joined_ref.shape[2]
    step = width // 2
    for at in range(0, width, step):
        joined = jnp.concatenate([joined_ref[i, :, at:at + step] for i in range(sources)], axis=0)
        term = dot(moved, joined)

        @pl.when(pl.program_id(0) == 0)
        def _():
            for k in range(3):
                out_ref[k, :, at:at + step] = term[k * cols:(k + 1) * cols]

        @pl.when(pl.program_id(0) > 0)
        def _():
            for k in range(3):
                out_ref[k, :, at:at + step] += term[k * cols:(k + 1) * cols]


def conv_grad(length, joined_all, d_cols):
    sources, rows, width = joined_all.shape
    cols = d_cols.shape[1]
    once = 4
    return pl.pallas_call(
        functools.partial(conv_grad_kernel, length),
        grid=(sources // once,),
        in_specs=[pl.BlockSpec((once, rows, width), lambda i: (i, 0, 0)),
                  pl.BlockSpec((once, cols, rows), lambda i: (i, 0, 0))],
        out_specs=pl.BlockSpec((3, cols, width), lambda i: (0, 0, 0)),
        out_shape=sds((3, cols, width), FULL),
        compiler_params=pltpu.CompilerParams(vmem_limit_bytes=VMEM_LIMIT),
        cost_estimate=pl.CostEstimate(flops=6 * sources * rows * width * cols,
                                      bytes_accessed=2 * joined_all.size, transcendentals=0),
        name="conv_grad",
    )(joined_all, d_cols)


def in_blocks(values):
    return values.reshape(-1, BLOCK_CH).T.reshape(-1)


def layer_forward(seqs, save, sub, char, places, weights):
    (qkv_w, qvb, out_w, out_b, gain, shift, up_w, up_b, down_w, down_b, table, win, bin_, wrec,
     brec, mw, mb, cw, cb) = weights
    tokc, tokr, idc, counts = places
    first = sub_forward(seqs, save, sub, qkv_w, qvb, out_w, out_b, gain, shift, up_w, up_b,
                        down_w, down_b)
    second = gru_forward(save, char, tokc, tokr, idc, counts, table, win, bin_, wrec, brec)
    third = merge_forward(sub.shape[0] // seqs, save, first[0], second[0], mw, mb, cw, cb, gain,
                          shift)
    return first, second, third


def spread_cotangent(cotangent, positions, length):
    seqs, picks = positions.shape
    chosen = (positions[:, :, None] == jnp.arange(length, dtype=jnp.int32)).astype(LOW)
    grid = lax.dot_general(chosen, cotangent.reshape(seqs, picks, -1), (((1,), (1,)), ((0,), (0,))),
                           preferred_element_type=FULL)
    grid = grid.reshape(seqs * length, 2, -1)
    return grid[:, 0], grid[:, 1]


def together(*values):
    return lax.optimization_barrier(values)


def sync(values, *marks):
    fields = [getattr(share, name) for share, name in marks]
    values, fields = lax.optimization_barrier((values, fields))
    for (share, name), field in zip(marks, fields):
        setattr(share, name, field)
    return values


def swap(value, bit):
    count = lax.axis_size("batch")
    return lax.ppermute(value, "batch", [(i, i ^ (1 << bit)) for i in range(count)])


def combine_kernel(plan, bits_ref, *refs):
    count = sum(len(sources) for sources in plan)
    sources, outs = refs[:count], refs[count:count + len(plan)]
    held, sems = refs[count + len(plan):-1], refs[-1]
    flat = [picks for item in plan for picks in item]
    copies = []
    for i, picks in enumerate(flat):
        index = tuple(
            slice(None) if pick is None else bits_ref[pick[0]] if pick[1] else 1 - bits_ref[pick[0]]
            for pick in picks)
        copies.append(pltpu.make_async_copy(sources[i].at[index], held[i], sems.at[i]))
    for copy in copies:
        copy.start()
    at = 0
    for item, out in zip(plan, outs):
        total = None
        for _ in item:
            copies[at].wait()
            term = held[at][...].astype(FULL)
            total = term if total is None else total + term
            at = at + 1
        out[...] = total.astype(out.dtype)


def combine(bits, items):
    plan = [[picks for _, picks in sources] for sources, _ in items]
    arrays = [array for sources, _ in items for array, _ in sources]
    shapes = []
    for sources, _ in items:
        for array, picks in sources:
            lead = [size for size, pick in zip(array.shape, picks) if pick is None]
            shapes.append(tuple(lead) + array.shape[len(picks):])
    outs, at = [], 0
    for sources, dtype in items:
        outs.append(sds(shapes[at], dtype))
        at = at + len(sources)
    moved = sum(2 * math.prod(shape) for shape in shapes) + sum(
        out.size * out.dtype.itemsize for out in outs)
    return pl.pallas_call(
        functools.partial(combine_kernel, plan),
        out_shape=outs,
        in_specs=[pl.BlockSpec(memory_space=pltpu.SMEM)] + [any_spec() for _ in arrays],
        out_specs=[vmem_spec() for _ in outs],
        scratch_shapes=[pltpu.VMEM(shape, LOW) for shape in shapes]
        + [pltpu.SemaphoreType.DMA((len(arrays),))],
        compiler_params=pltpu.CompilerParams(vmem_limit_bytes=VMEM_LIMIT),
        cost_estimate=pl.CostEstimate(flops=0, bytes_accessed=moved, transcendentals=0),
        name="combine",
    )(bits, *arrays)


class Share:
    def __init__(self, order, give, kept):
        self.bits = lax.axis_size("batch").bit_length() - 1
        self.order = order
        self.give, self.kept = self.shaped(give), self.shaped(kept)
        self.gots = []

    def shaped(self, value):
        return value.reshape((2,) * (self.bits - 1) + value.shape[1:])

    def item(self):
        turn = len(self.gots)
        sources = []
        for age, array in enumerate([self.kept] + self.gots):
            passed = self.order[:max(age, 1)]
            left = [bit for bit in reversed(range(self.bits)) if bit not in passed]
            picks = []
            for bit in left:
                if bit in self.order[:turn]:
                    picks.append((bit, True))
                elif turn < self.bits and bit == self.order[turn]:
                    picks.append((bit, False))
                else:
                    picks.append(None)
            sources.append((array, picks))
        return sources, LOW if turn < self.bits else FULL

    def finished(self):
        return len(self.gots) == self.bits

    def send(self):
        bit = self.order[len(self.gots)]
        count = lax.axis_size("batch")
        self.got = lax.ppermute(self.give, "batch", [(i, i ^ (1 << bit)) for i in range(count)])

    def land(self):
        self.gots = self.gots + [self.got]


class Flow:
    def __init__(self):
        self.index = lax.axis_index("batch")
        count = lax.axis_size("batch").bit_length() - 1
        self.bits = jnp.stack([(self.index >> bit) & 1 for bit in range(count)]).astype(jnp.int32)

    def prepare(self, *shares):
        outs = combine(self.bits, [s.item() for s in shares])
        for s, out in zip(shares, outs):
            if s.finished():
                s.total = out
            else:
                s.give = out

    def send(self, *shares):
        for s in shares:
            s.send()

    def slot(self, enter, moving=(), prepare=(), values=(), work=None):
        self.send(*enter)
        if moving or prepare:
            self.prepare(*moving, *prepare)
        going = [s for s in moving if not s.finished()]
        done = [s for s in moving if s.finished()]
        self.send(*going)
        if work is not None:
            made = [s.give for s in going + list(prepare)] + [s.total for s in done]
            values = work(lax.optimization_barrier((values, made))[0])
        return self.land(values, list(enter) + going, done, prepare)

    def land(self, values, sent, done=(), prepared=()):
        values = sync(values, *[(s, "total") for s in done], *[(s, "got") for s in sent],
                      *[(s, "give") for s in prepared])
        for s in sent:
            s.land()
        return values


def placed(block):
    return block.T[None]


def body(stream_in, char_ids, char_lengths, mask_pos, cotangent, *params):
    weights = tuple(p.reshape(p.shape[1:]) if p.ndim > 2 else p for p in params)
    (qkv_w, qvb, out_w, out_b, gain, shift, up_w, up_b, down_w, down_b, table, win, bin_, wrec,
     brec, mw, mb, cw, cb) = weights
    section = lax.axis_index("section")
    sections = lax.axis_size("section")
    batch = lax.axis_size("batch")
    seqs, length, _, width = stream_in.shape
    rows = seqs * length
    count = seqs * char_ids.shape[1]
    hidden = wrec.shape[0]
    ends = jnp.cumsum(char_lengths, axis=-1)
    spots = jnp.arange(char_ids.shape[1], dtype=jnp.int32)
    token_of = jnp.sum((ends[:, None, :] <= spots[:, None]).astype(jnp.int32), axis=-1)
    token_of = in_blocks(token_of + length * jnp.arange(seqs, dtype=jnp.int32)[:, None])
    places = (token_of[:, None], token_of[None, :], in_blocks(char_ids)[:, None],
              char_lengths.reshape(-1, 1).astype(FULL))
    streams = stream_in.transpose(2, 0, 1, 3).reshape(2, rows, width)
    sub, char = streams[0], streams[1]
    ident = (in_blocks(char_ids)[:, None] == jnp.arange(table.shape[0], dtype=jnp.int32)).astype(LOW)

    def onward(pair):
        route = [(i, i + 1) for i in range(sections - 1)]
        a = lax.ppermute(pair[0], "section", route)
        a, b = lax.optimization_barrier((a, pair[1]))
        return a, lax.ppermute(b, "section", route)

    def back(value):
        return lax.ppermute(value, "section", [(i + 1, i) for i in range(sections - 1)])

    first, second, third = layer_forward(seqs, False, sub, char, places, weights)
    got = onward((third[0], third[1]))
    sub = jnp.where(section == 0, sub, got[0])
    char = jnp.where(section == 0, char, got[1])
    first, second, third = layer_forward(seqs, True, sub, char, places, weights)
    _, qkv, prob, att, res1, first_low, pre, act, res2 = first
    _, charin, r, z, n, rn, state, prev = second
    out_sub, out_char, mpre, joined, second_low, pooled_low, res3, res4 = third
    joined_all = lax.all_gather(joined, "batch")
    tokc, tokr, idc, counts = places
    grid = spread_cotangent(cotangent, mask_pos, length)

    d_second, d_pooled = merge_backward(length, None, grid[0], grid[1], res3, res4, mpre, mw, cw, gain)
    d_res1, = ffn_backward(None, d_second, res2, pre, res1, up_w, down_w, gain)
    d_sub, = attention_backward(seqs, None, d_res1, qkv, prob, qkv_w, out_w)
    d_char, = gru_backward(None, d_pooled, counts, tokc, tokr, r, z, n, rn, state, win, wrec)
    last = section == sections - 1
    g_sub = jnp.where(last, grid[0], back(d_sub).astype(FULL))
    g_char = jnp.where(last, grid[1], back(d_char).astype(FULL))

    flow = Flow()
    wide, lead = act.shape[1], batch // 2
    chunk, tall = width // batch, 3 * width // batch
    early, late = tuple(range(batch.bit_length() - 1)), (0,) + tuple(range(2, batch.bit_length() - 1)) + (1,)

    def split(outs, count, blocks, order):
        gives, kepts = blocks.finish(outs[count:])
        return list(outs[:count]), [Share(order, give, kept) for give, kept in zip(gives, kepts)]

    blocks = Blocks(flow.bits, lead, [(chunk, 2 * width, [
        (0, 0, chunk, 0, lead, 0, 0, width, 0, 0), (0, width, chunk, 0, lead, 1, 0, width, 0, width)])],
        [(2 * width, rows)], [second_low, pooled_low])
    (d_second, d_pooled, d_conv, small1), (merges,) = split(merge_backward(
        length, blocks, g_sub, g_char, res3, res4, mpre, mw, cw, gain), 4, blocks, late)
    d_conv = d_conv.reshape(batch, -1, rows)

    half, up_chunk = wide // 2, wide // batch
    blocks = Blocks(flow.bits, lead, [
        (chunk, half, [(0, 0, chunk, 0, lead, 0, 0, half, 0, 0)]),
        (chunk, half + width, [(0, 0, chunk, 0, lead, 0, half, wide, 0, 0),
                               (2, 0, chunk, 0, lead, 1, 0, width, 0, half)]),
        (up_chunk, width // 2, [(1, 0, up_chunk, 0, lead, 2, 0, width // 2, 0, 0)]),
        (up_chunk, width // 2, [(1, 0, up_chunk, 0, lead, 2, width // 2, width, 0, 0)])],
        [(width, rows), (wide, rows), (width, rows)], [act, att, first_low])
    flow.send(merges)
    outs = flow.land(ffn_backward(blocks, d_second, res2, pre, res1, up_w, down_w, gain), [merges])
    (d_res1, small2), (down, down_out, up, up_more) = split(outs, 2, blocks, early)

    flow.send(down, down_out, up, up_more)
    d_cols = lax.all_to_all(d_conv, "batch", 0, 0, tiled=True)
    flow.land((), [down, down_out])
    flow.prepare(down, merges, down_out)
    d_pooled = flow.land(d_pooled, (), (), [down, merges, down_out])
    flow.send(down, merges)
    spot, few = width + hidden, table.shape[0] // 2
    blocks = Blocks(flow.bits, lead, [(tall, spot + few, [
        (0, 0, tall, 0, lead, 0, 0, width, 0, 0),
        (1, 0, tall, 0, lead // 2, 1, 0, hidden, 0, width),
        (1, 0, tall, lead // 2, lead, 1, hidden, 2 * hidden, 0, width),
        (2, 0, chunk, 0, lead, 2, 0, few, 0, spot),
        (2, 0, chunk, 0, lead, 2, few, 2 * few, chunk, spot)])],
        [(3 * width, count), (3 * width, count), (width, count)], [charin, prev, ident])
    outs, d_cols = flow.land(
        (gru_backward(blocks, d_pooled, counts, tokc, tokr, r, z, n, rn, state, win, wrec), d_cols),
        [down, merges, up, up_more])
    (d_char, small4), (chars,) = split(outs, 2, blocks, early)

    flow.send(down_out, chars)
    flow.prepare(merges, down, up)
    d_res1 = flow.land(d_res1, (), (), [merges, down, up])
    flow.send(merges, down)
    blocks = Blocks(flow.bits, lead, [(tall, width, [(0, 0, tall, 0, lead, 0, 0, width, 0, 0)])],
                    [(3 * width, rows)], [sub])
    outs, joined_all = flow.land(
        (attention_backward(seqs, blocks, d_res1, qkv, prob, qkv_w, out_w), joined_all),
        [down_out, chars, merges, down])
    (d_sub, small3), (heads,) = split(outs, 2, blocks, late)

    small = jnp.concatenate([small1, small2, small3, small4], 0)
    flow.send(heads)
    flow.slot([up], [merges, down, down_out], [chars, up_more])
    flow.land((), [heads])
    small = lax.all_gather(small, "batch")
    everything = [heads, up, down, down_out, merges, chars, up_more]

    def under_way(*entering):
        return [s for s in everything if s not in entering and not hasattr(s, "total")]

    conv = flow.slot([chars], under_way(chars, up_more), (), (joined_all, d_cols),
                     lambda held: conv_grad(length, *held))

    def ends_of(held):
        d_sub, d_char, out_sub, out_char = held
        ends = jnp.where(section == 0, jnp.stack([d_sub, d_char], 1), jnp.stack([out_sub, out_char], 1))
        return ends.reshape(1, seqs, length, 2, width)

    ends_out = flow.slot([up_more], under_way(up_more), (), (d_sub, d_char, out_sub, out_char), ends_of)
    while under_way():
        if all(s.finished() for s in under_way()):
            flow.prepare(*under_way())
        else:
            flow.slot([], under_way())

    small = jnp.sum(small.reshape(batch, -1, width), 0)
    b = lax.axis_index("batch")

    def pieces(*which):
        part = width // batch
        mine = lax.dynamic_slice_in_dim(small, b * part, part, 1)
        return jnp.concatenate([mine[i:i + 1] for i in which], 0)

    def piece(start, count):
        part = count * width // batch
        line = small[start:start + count].reshape(1, count * width)
        return lax.dynamic_slice_in_dim(line, b * part, part, 1)

    return (
        ends_out,
        placed(heads.total),
        pieces(24, 25)[None],
        placed(down_out.total[:, half:]),
        pieces(13),
        pieces(14, 15, 4, 5)[None],
        pieces(16, 17, 6, 7)[None],
        placed(jnp.concatenate([up.total, up_more.total], 1)),
        piece(8, 4),
        placed(jnp.concatenate([down.total, down_out.total[:, :half]], 1)),
        pieces(12),
        placed(jnp.concatenate([chars.total[:chunk, spot:], chars.total[chunk:2 * chunk, spot:]], 1)),
        placed(chars.total[:, :width]),
        piece(32, 3),
        placed(chars.total[:, width:spot]),
        piece(35, 3),
        merges.total.reshape(chunk, 2, width).transpose(1, 2, 0)[None],
        pieces(2, 3)[None],
        conv.transpose(0, 2, 1)[None],
        piece(0, 2),
    )


def solution(mesh):
    by = P("batch")
    part = P("section")

    def columns(rank):
        return P(*(["section"] + [None] * (rank - 2) + ["batch"]))

    return jax.shard_map(
        body,
        mesh=mesh,
        in_specs=(by,) * 5 + (part,) * 19,
        out_specs=(P("section", "batch"),) + tuple(
            columns(rank) for rank in (3, 3, 3, 2, 3, 3, 3, 2, 3, 2, 3, 3, 2, 3, 2, 4, 3, 4, 2)),
        check_vma=False,
    )
```

```python
import functools
import math

import jax
import jax.numpy as jnp
from jax import lax
from jax.experimental import pallas as pl
from jax.experimental.pallas import tpu as pltpu
from jax.sharding import PartitionSpec as P

HEAD = 64
BLOCK_CH = 8
EPSILON = 1e-05
LOW = jnp.bfloat16
FULL = jnp.float32
VMEM_LIMIT = 63 * 1024 * 1024


def dot(left, right):
    return lax.dot_general(left, right, (((1,), (0,)), ((), ())), preferred_element_type=FULL)


def dot_nt(left, right):
    return lax.dot_general(left, right, (((1,), (1,)), ((), ())), preferred_element_type=FULL)


def dot_tn(left, right):
    return lax.dot_general(left, right, (((0,), (0,)), ((), ())), preferred_element_type=FULL)


def norm_parts(values):
    row_mean = jnp.mean(values, axis=-1, keepdims=True)
    centered = values - row_mean
    row_var = jnp.mean(centered * centered, axis=-1, keepdims=True)
    inverse = lax.rsqrt(row_var + EPSILON)
    return centered * inverse, inverse


def norm(values, gain, shift):
    return norm_parts(values)[0] * gain + shift


def norm_back(values, gain, grad):
    unit, inverse = norm_parts(values)
    scaled = grad * gain
    first = jnp.mean(scaled, axis=-1, keepdims=True)
    second = jnp.mean(scaled * unit, axis=-1, keepdims=True)
    return inverse * (scaled - first - unit * second), unit


GELU_A = 0.7978845608028654
GELU_B = 0.044715


def gelu(x):
    return 0.5 * x * (1.0 + jnp.tanh(GELU_A * (x + GELU_B * x * x * x)))


def gelu_slope(x):
    square = x * x
    bent = jnp.tanh(GELU_A * (x + GELU_B * square * x))
    return 0.5 * (1.0 + bent) + 0.5 * x * (1.0 - bent * bent) * (
        GELU_A * (1.0 + 3.0 * GELU_B * square)
    )


def sigmoid(x):
    return 0.5 * jnp.tanh(0.5 * x) + 0.5


def column_sum(values):
    return jnp.sum(values, axis=0, keepdims=True)


class Stream:
    def __init__(self, pairs, sems):
        self.copies = [
            pltpu.make_async_copy(src, dst, sems.at[i]) for i, (src, dst) in enumerate(pairs)
        ]
        for copy in self.copies:
            copy.start()
        self.waited = set()

    def need(self, *which):
        for i in which:
            if i not in self.waited:
                self.waited.add(i)
                self.copies[i].wait()


def chunks(src, dst, axis, size):
    total = src.shape[axis]
    parts = []
    for start in range(0, total, size):
        index = [slice(None)] * len(src.shape)
        index[axis] = pl.ds(start, min(size, total - start))
        parts.append((src.at[tuple(index)], dst.at[tuple(index)]))
    return parts


def fill(out, near, terms):
    lead, chunk, columns = out.shape
    part = [term[9] for term in terms if term[8] > 0]
    if part:
        out[:, :, part[0]:] = jnp.zeros((lead, chunk, columns - part[0]), LOW)
    for d_y, base, height, start, stop, x, first, last, row, column in terms:
        d = jnp.concatenate([
            d_y[pl.ds(pl.multiple_of(base + (2 * i + near) * height, 16), height), :]
            for i in range(start, stop)], axis=0)
        step = min(last - first, 768)
        for at in range(first, last, step):
            value = dot(d, x[:, at:at + step]).astype(LOW)
            lanes = slice(column + at - first, column + at - first + step)
            out[start:stop, row:row + height, lanes] = value.reshape(stop - start, height, step)


def fill_plain(shape, near, terms):
    out = jnp.zeros(shape, LOW)
    for d_y, base, height, start, stop, x, first, last, row, column in terms:
        count = stop - start
        d = d_y[base + 2 * start * height:base + 2 * stop * height].reshape(count, 2, height, -1)
        d = lax.dynamic_slice_in_dim(d, near, 1, 1).reshape(count * height, -1)
        value = dot(d, x[:, first:last]).astype(LOW).reshape(count, height, last - first)
        out = lax.dynamic_update_slice(out, value, (start, row, column))
    return out


def named(plan, d_ys, xs):
    return [(d_ys[d],) + rest[:4] + (xs[rest[4]],) + rest[5:] for d, *rest in map(tuple, plan)
            for rest in [tuple(rest)]]


class Blocks:
    def __init__(self, bits, count, plans, d_shapes, xs):
        self.bits, self.count, self.plans, self.d_shapes, self.xs = bits, count, plans, d_shapes, xs
        self.inside = all(plan[0] % 16 == 0 for plan in plans)

    def shapes(self):
        return [sds((self.count, plan[0], plan[1]), LOW) for plan in self.plans]

    def outs(self):
        return self.shapes() * 2 if self.inside else [sds(shape, LOW) for shape in self.d_shapes]

    def scratch(self):
        return [pltpu.VMEM(shape, LOW) for shape in self.d_shapes] if self.inside else []

    def inputs(self):
        return [self.bits] + (self.xs if self.inside else [])

    def split(self, refs):
        if not self.inside:
            return refs[:len(self.d_shapes)], lambda bits_ref, xs: None
        results, d_ys = refs[:2 * len(self.plans)], refs[2 * len(self.plans):]

        def make(bits_ref, xs):
            near = bits_ref[0]
            for own in range(2):
                for i, plan in enumerate(self.plans):
                    fill(results[own * len(self.plans) + i], near if own else 1 - near,
                         named(plan[2], d_ys, xs))

        return d_ys, make

    def finish(self, results):
        if self.inside:
            return results[:len(self.plans)], results[len(self.plans):]
        near = self.bits[0]
        return tuple([fill_plain(shape.shape, which, named(plan[2], results, self.xs))
                      for shape, plan in zip(self.shapes(), self.plans)] for which in (1 - near, near))


def any_spec():
    return pl.BlockSpec(memory_space=pl.ANY)


def vmem_spec():
    return pl.BlockSpec(memory_space=pltpu.VMEM)


def sds(shape, dtype):
    return jax.ShapeDtypeStruct(shape, dtype)


def call(kernel, outs, ins, streamed, scratch, name, flops, copies, blocks=None):
    if blocks is not None:
        ins, outs = list(ins) + blocks.inputs(), list(outs) + blocks.outs()
        scratch = blocks.scratch() + list(scratch)
        scalar = len(ins) - len(blocks.inputs())
    else:
        scalar = -1
    moved = sum(a.size * a.dtype.itemsize for a in ins) + sum(
        o.size * o.dtype.itemsize for o in outs
    )
    return pl.pallas_call(
        kernel,
        out_shape=outs,
        in_specs=[any_spec() if i in streamed else pl.BlockSpec(memory_space=pltpu.SMEM) if i == scalar
                  else vmem_spec() for i in range(len(ins))],
        out_specs=[vmem_spec() for _ in outs],
        scratch_shapes=list(scratch) + [pltpu.SemaphoreType.DMA((copies,))],
        compiler_params=pltpu.CompilerParams(vmem_limit_bytes=VMEM_LIMIT),
        cost_estimate=pl.CostEstimate(flops=flops, bytes_accessed=moved, transcendentals=0),
        name=name,
    )(*ins)


def sub_forward_kernel(seqs, save, s_ref, qkv_hbm, qvb_ref, out_hbm, outb_ref, gain_ref, shift_ref,
                       up_hbm, upb_ref, down_hbm, downb_ref, *rest):
    if save:
        (after_ref, qkv_ref, prob_ref, att_ref, res1_ref, first_ref, pre_ref, act_ref, res2_ref,
         wqkv, wout, wup, wdown, sems) = rest
    else:
        after_ref, wqkv, wout, wup, wdown, qkv_ref, att_ref, sems = rest
    width = s_ref.shape[1]
    wide = wup.shape[1]
    length = s_ref.shape[0] // seqs
    w = Stream(chunks(qkv_hbm, wqkv, 1, width) + chunks(out_hbm, wout, 1, width)
               + chunks(up_hbm, wup, 1, width) + chunks(down_hbm, wdown, 0, width), sems)
    for part in range(3):
        w.need(part)
        cols = slice(part * width, (part + 1) * width)
        y = dot(s_ref[...], wqkv[:, cols])
        if part == 0:
            y = (y + qvb_ref[0:1, :]) * HEAD ** -0.5
        elif part == 2:
            y = y + qvb_ref[1:2, :]
        qkv_ref[:, cols] = y.astype(LOW)
    lanes = lax.broadcasted_iota(jnp.int32, (length, 2 * HEAD), 1)
    even = lanes < HEAD
    for seq in range(seqs):
        rows = slice(seq * length, (seq + 1) * length)
        for pair in range(width // (2 * HEAD)):
            lo = pair * 2 * HEAD
            q = qkv_ref[rows, lo:lo + 2 * HEAD]
            k = qkv_ref[rows, width + lo:width + lo + 2 * HEAD]
            v = qkv_ref[rows, 2 * width + lo:2 * width + lo + 2 * HEAD]
            zero = jnp.zeros_like(q)
            probs = []
            for half in range(2):
                mask = even if half == 0 else ~even
                scores = dot_nt(jnp.where(mask, q, zero), k)
                peak = jnp.max(scores, axis=-1, keepdims=True)
                e = jnp.exp(scores - peak)
                prob = (e / jnp.sum(e, axis=-1, keepdims=True)).astype(LOW)
                probs.append(prob)
                if save:
                    at = (seq * (width // HEAD) + 2 * pair + half) * length
                    prob_ref[at:at + length, :] = prob
            both = jnp.concatenate(probs, axis=1)
            vv = jnp.concatenate([jnp.where(even, v, zero), jnp.where(even, zero, v)], axis=0)
            att_ref[rows, lo:lo + 2 * HEAD] = dot(both, vv).astype(LOW)
    w.need(3)
    res1 = s_ref[...].astype(FULL) + dot(att_ref[...], wout[...]) + outb_ref[...]
    after = norm(res1, gain_ref[0:1, :], shift_ref[0:1, :])
    low = after.astype(LOW)
    if save:
        res1_ref[...] = res1
        first_ref[...] = low
    total = after + downb_ref[...]
    for part in range(wide // width):
        cols = slice(part * width, (part + 1) * width)
        w.need(4 + part)
        pre = dot(low, wup[:, cols]) + upb_ref[:, cols]
        act = gelu(pre).astype(LOW)
        if save:
            pre_ref[:, cols] = pre
            act_ref[:, cols] = act
        w.need(4 + wide // width + part)
        total = total + dot(act, wdown[cols, :])
    if save:
        res2_ref[...] = total
    after_ref[...] = norm(total, gain_ref[1:2, :], shift_ref[1:2, :])


def sub_forward(seqs, save, s, qkv_w, qvb, out_w, out_b, gain, shift, up_w, up_b, down_w, down_b):
    rows, width = s.shape
    wide = up_w.shape[1]
    length = rows // seqs
    outs = [sds((rows, width), FULL)]
    scratch = [pltpu.VMEM(a.shape, LOW) for a in (qkv_w, out_w, up_w, down_w)]
    saved = [sds((rows, 3 * width), LOW), sds((seqs * (width // HEAD) * length, length), LOW),
             sds((rows, width), LOW), sds((rows, width), FULL), sds((rows, width), LOW),
             sds((rows, wide), FULL), sds((rows, wide), LOW), sds((rows, width), FULL)]
    if save:
        outs = outs + saved
    else:
        scratch = scratch + [pltpu.VMEM(saved[0].shape, LOW), pltpu.VMEM(saved[2].shape, LOW)]
    copies = 4 + 2 * (wide // width)
    return call(functools.partial(sub_forward_kernel, seqs, save), outs,
                [s, qkv_w, qvb, out_w, out_b, gain, shift, up_w, up_b, down_w, down_b],
                {1, 3, 7, 9}, scratch, "sub_forward",
                2 * rows * (qkv_w.size + out_w.size + up_w.size + down_w.size), copies)


def gru_forward_kernel(save, c_ref, tokc_ref, tokr_ref, idc_ref, count_ref, table_hbm, win_hbm,
                       bin_ref, wrec_hbm, brec_ref, *rest):
    if save:
        (pooled_ref, charin_ref, r_ref, z_ref, n_ref, rn_ref, state_ref, prev_ref,
         table, win, wrec, gate, low_state, sems) = rest
    else:
        pooled_ref, table, win, wrec, gate, low_state, charin_ref, sems = rest
    rows, width = c_ref.shape
    count = tokc_ref.shape[0]
    hidden = wrec.shape[0]
    w = Stream([(table_hbm, table)] + chunks(win_hbm, win, 1, width)
               + chunks(wrec_hbm, wrec, 1, 3 * hidden), sems)
    token = (tokc_ref[...] == lax.broadcasted_iota(jnp.int32, (count, rows), 1))
    ident = (idc_ref[...] == lax.broadcasted_iota(jnp.int32, (count, table.shape[0]), 1))
    w.need(0)
    x = dot(token.astype(FULL).astype(LOW), c_ref[...]) + dot(ident.astype(FULL).astype(LOW), table[...])
    charin_ref[...] = x.astype(LOW)
    for part in range(3):
        w.need(1 + part)
        cols = slice(part * width, (part + 1) * width)
        gate[:, cols] = dot(charin_ref[...], win[:, cols]) + bin_ref[:, cols]
    lanes = count // BLOCK_CH
    state = [None, None]
    for turn in range(BLOCK_CH):
        for way in range(2):
            at = turn if way == 0 else BLOCK_CH - 1 - turn
            here = slice(at * lanes, (at + 1) * lanes)
            base = way * 3 * hidden
            out = slice(way * hidden, (way + 1) * hidden)
            bias = brec_ref[:, base:base + 3 * hidden]
            g = gate[here, base:base + 3 * hidden]
            if turn == 0:
                rec_n = jnp.broadcast_to(bias[:, 2 * hidden:], (lanes, hidden))
                rz = g[:, :2 * hidden] + bias[:, :2 * hidden]
                if save:
                    prev_ref[here, out] = jnp.zeros((lanes, hidden), LOW)
            else:
                w.need(4 + way)
                low = state[way].astype(LOW)
                if save:
                    prev_ref[here, out] = low
                rec = dot(low, wrec[:, base:base + 3 * hidden]) + bias
                rec_n = rec[:, 2 * hidden:]
                rz = g[:, :2 * hidden] + rec[:, :2 * hidden]
            rz = sigmoid(rz)
            r, z = rz[:, :hidden], rz[:, hidden:]
            n = jnp.tanh(g[:, 2 * hidden:] + r * rec_n)
            new = (1.0 - z) * n
            if turn > 0:
                new = new + z * state[way]
            state[way] = new
            low_state[here, out] = new.astype(LOW)
            if save:
                r_ref[here, out] = r
                z_ref[here, out] = z
                n_ref[here, out] = n
                rn_ref[here, out] = rec_n
                state_ref[here, out] = new
    spread = (tokr_ref[...] == lax.broadcasted_iota(jnp.int32, (rows, count), 0))
    pooled = dot(spread.astype(FULL).astype(LOW), low_state[...])
    pooled_ref[...] = pooled / count_ref[...]


def gru_forward(save, c, tokc, tokr, idc, counts, table, win, bin_, wrec, brec):
    rows, width = c.shape
    count = tokc.shape[0]
    outs = [sds((rows, width), FULL)]
    scratch = [pltpu.VMEM(a.shape, LOW) for a in (table, win, wrec)]
    scratch = scratch + [pltpu.VMEM((count, win.shape[1]), FULL), pltpu.VMEM((count, width), LOW)]
    if save:
        outs = outs + [sds((count, width), LOW)] + [sds((count, width), FULL)] * 5
        outs = outs + [sds((count, width), LOW)]
    else:
        scratch = scratch + [pltpu.VMEM((count, width), LOW)]
    return call(functools.partial(gru_forward_kernel, save), outs,
                [c, tokc, tokr, idc, counts, table, win, bin_, wrec, brec],
                {5, 6, 8}, scratch, "gru_forward",
                2 * count * (win.size + wrec.size) + 2 * count * width * (2 * rows + table.shape[0]), 6)


def shift_rows(values, by, length):
    rows, width = values.shape
    zero = jnp.zeros((1, width), values.dtype)
    pos = lax.broadcasted_iota(jnp.int32, (rows, 1), 0) % length
    if by == 1:
        moved = jnp.concatenate([zero, values[:-1]], axis=0)
        return jnp.where(pos == 0, 0.0, moved)
    moved = jnp.concatenate([values[1:], zero], axis=0)
    return jnp.where(pos == length - 1, 0.0, moved)


def merge_forward_kernel(length, save, after_ref, pooled_ref, mw_hbm, mb_ref, cw_hbm, cb_ref,
                         gain_ref, shift_ref, *rest):
    if save:
        (sub_ref, char_ref, pre_ref, joined_ref, second_ref, poollow_ref, res3_ref, res4_ref,
         mw, cw, sems) = rest
    else:
        sub_ref, char_ref, mw, cw, sems = rest
    width = after_ref.shape[1]
    w = Stream(chunks(mw_hbm, mw, 0, 1) + chunks(cw_hbm, cw, 0, 1), sems)
    halves = []
    for side in range(2):
        w.need(side)
        cols = slice(side * width, (side + 1) * width)
        low = (after_ref if side == 0 else pooled_ref)[...].astype(LOW)
        pre = dot(low, mw[side]) + mb_ref[side:side + 1, :]
        if save:
            (second_ref if side == 0 else poollow_ref)[...] = low
            pre_ref[:, cols] = pre
        halves.append(gelu(pre))
    joined = jnp.concatenate(halves, axis=1)
    if save:
        joined_ref[...] = joined.astype(LOW)
    total = cb_ref[...]
    for k in range(3):
        moved = joined if k == 1 else shift_rows(joined, 1 - k, length)
        w.need(2 + k)
        total = total + dot(moved.astype(LOW), cw[k])
    res3 = after_ref[...] + total[:, :width]
    res4 = pooled_ref[...] + total[:, width:]
    if save:
        res3_ref[...] = res3
        res4_ref[...] = res4
    sub_ref[...] = norm(res3, gain_ref[2:3, :], shift_ref[2:3, :]).astype(LOW)
    char_ref[...] = norm(res4, gain_ref[3:4, :], shift_ref[3:4, :]).astype(LOW)


def merge_forward(length, save, after, pooled, mw, mb, cw, cb, gain, shift):
    rows, width = after.shape
    outs = [sds((rows, width), LOW)] * 2
    scratch = [pltpu.VMEM(mw.shape, LOW), pltpu.VMEM(cw.shape, LOW)]
    if save:
        outs = outs + [sds((rows, 2 * width), FULL), sds((rows, 2 * width), LOW),
                       sds((rows, width), LOW), sds((rows, width), LOW),
                       sds((rows, width), FULL), sds((rows, width), FULL)]
    return call(functools.partial(merge_forward_kernel, length, save), outs,
                [after, pooled, mw, mb, cw, cb, gain, shift], {2, 4}, scratch, "merge_forward",
                2 * rows * (mw.size + cw.size), 5)


def merge_backward_kernel(length, full, gsub_ref, gchar_ref, res3_ref, res4_ref, pre_ref, mw_hbm, cw_hbm,
                          gain_ref, res2_ref, *rest):
    if full:
        xs, rest = rest[:len(full.inputs())], rest[len(full.inputs()):]
        dres2_ref, dpooled_ref, dconv_ref, small_ref, *rest, mw, cw, sems = rest
        (dpre_ref, ddown_ref), make = full.split(rest)
    else:
        dres2_ref, dpooled_ref, mw, cw, sems = rest
    width = res3_ref.shape[1]
    w = Stream(chunks(cw_hbm, cw, 0, 1) + chunks(mw_hbm, mw, 0, 1), sems)
    grads = [gsub_ref[...], gchar_ref[...]]
    d_res = []
    for side in range(2):
        d, unit = norm_back((res3_ref, res4_ref)[side][...], gain_ref[2 + side:3 + side, :], grads[side])
        d_res.append(d)
        if full:
            small_ref[4 + side:5 + side, :] = column_sum(grads[side] * unit)
            small_ref[6 + side:7 + side, :] = column_sum(grads[side])
            small_ref[side:side + 1, :] = column_sum(d)
    d_conv = jnp.concatenate(d_res, axis=1)
    if full:
        dconv_ref[...] = d_conv.astype(LOW).T
    total = None
    for k in range(3):
        moved = d_conv if k == 1 else shift_rows(d_conv, k - 1, length)
        w.need(k)
        term = dot_nt(moved.astype(LOW), cw[k])
        total = term if total is None else total + term
    d_pre = total * gelu_slope(pre_ref[...])
    d_low = d_pre.astype(LOW)
    if full:
        dpre_ref[...] = d_low.T
        for side in range(2):
            small_ref[2 + side:3 + side, :] = column_sum(d_pre[:, side * width:(side + 1) * width])
    w.need(3)
    d_second = d_res[0] + dot_nt(d_low[:, :width], mw[0])
    d_res2, unit = norm_back(res2_ref[...], gain_ref[1:2, :], d_second)
    dres2_ref[...] = d_res2
    w.need(4)
    dpooled_ref[...] = d_res[1] + dot_nt(d_low[:, width:], mw[1])
    if full:
        ddown_ref[...] = d_res2.astype(LOW).T
        small_ref[8:9, :] = column_sum(d_res2)
        small_ref[9:10, :] = column_sum(d_second * unit)
        small_ref[10:11, :] = column_sum(d_second)
        small_ref[11:16, :] = jnp.zeros((5, width), FULL)
        make(xs[0], xs[1:])


def merge_backward(length, full, gsub, gchar, res3, res4, pre, mw, cw, gain, res2):
    rows, width = res3.shape
    outs = [sds((rows, width), FULL)] * 2
    if full:
        outs = outs + [sds((2 * width, rows), LOW), sds((16, width), FULL)]
    scratch = [pltpu.VMEM(mw.shape, LOW), pltpu.VMEM(cw.shape, LOW)]
    return call(functools.partial(merge_backward_kernel, length, full), outs,
                [gsub, gchar, res3, res4, pre, mw, cw, gain, res2], {5, 6}, scratch, "merge_backward",
                2 * rows * (mw.size + cw.size), 5, full)


def ffn_backward_kernel(full, dres2_ref, pre_ref, res1_ref, up_hbm, down_hbm, gain_ref, *rest):
    if full:
        xs, rest = rest[:len(full.inputs())], rest[len(full.inputs()):]
        dres1_ref, small_ref, *rest, wup, wdown, sems = rest
        (dup_ref,), make = full.split(rest)
    else:
        dres1_ref, wup, wdown, sems = rest
    rows, width = dres1_ref.shape
    wide = wup.shape[1]
    parts = wide // width
    w = Stream(chunks(down_hbm, wdown, 0, width) + chunks(up_hbm, wup, 1, width), sems)
    d_res2 = dres2_ref[...]
    d_low = d_res2.astype(LOW)
    d_first = d_res2
    for part in range(parts):
        cols = slice(part * width, (part + 1) * width)
        w.need(part)
        d_up = dot_nt(d_low, wdown[cols, :]) * gelu_slope(pre_ref[:, cols])
        up_low = d_up.astype(LOW)
        if full:
            dup_ref[cols, :] = up_low.T
            small_ref[part:part + 1, :] = column_sum(d_up)
        w.need(parts + part)
        d_first = d_first + dot_nt(up_low, wup[:, cols])
    d_res1, unit = norm_back(res1_ref[...], gain_ref[0:1, :], d_first)
    dres1_ref[...] = d_res1
    if full:
        small_ref[parts:parts + 1, :] = column_sum(d_res1)
        small_ref[parts + 1:parts + 2, :] = column_sum(d_first * unit)
        small_ref[parts + 2:parts + 3, :] = column_sum(d_first)
        small_ref[parts + 3:, :] = jnp.zeros((small_ref.shape[0] - parts - 3, width), FULL)
        make(xs[0], xs[1:])


def ffn_backward(full, dres2, pre, res1, up_w, down_w, gain):
    rows, width = res1.shape
    wide = up_w.shape[1]
    outs = [sds((rows, width), FULL)]
    scratch = [pltpu.VMEM(a.shape, LOW) for a in (up_w, down_w)]
    if full:
        outs = outs + [sds((8, width), FULL)]
    return call(functools.partial(ffn_backward_kernel, full), outs,
                [dres2, pre, res1, up_w, down_w, gain], {3, 4}, scratch, "ffn_backward",
                2 * rows * (up_w.size + down_w.size), 2 * (wide // width), full)


def attention_backward_kernel(seqs, full, dres1_ref, qkv_ref, prob_ref, qkv_hbm, out_hbm, *rest):
    if full:
        xs, rest = rest[:len(full.inputs())], rest[len(full.inputs()):]
        dsub_ref, small_ref, *rest, wqkv, wout, datt, dproj_ref, sems = rest
        (dprojt_ref, dbranch_ref), make = full.split(rest)
    else:
        dsub_ref, wqkv, wout, datt, dproj_ref, sems = rest
    rows, width = dsub_ref.shape
    length = rows // seqs
    w = Stream(chunks(out_hbm, wout, 1, width) + chunks(qkv_hbm, wqkv, 1, width), sems)
    w.need(0)
    branch_low = dres1_ref[...].astype(LOW)
    datt[...] = dot_nt(branch_low, wout[...]).astype(LOW)
    if full:
        dbranch_ref[...] = branch_low.T
    even = lax.broadcasted_iota(jnp.int32, (length, 2 * HEAD), 1) < HEAD
    scale = HEAD ** -0.5
    for pair in range(width // (2 * HEAD)):
        lo = pair * 2 * HEAD
        totals = [0.0, 0.0]
        for seq in range(seqs):
            at_rows = slice(seq * length, (seq + 1) * length)
            q = qkv_ref[at_rows, lo:lo + 2 * HEAD]
            k = qkv_ref[at_rows, width + lo:width + lo + 2 * HEAD]
            v = qkv_ref[at_rows, 2 * width + lo:2 * width + lo + 2 * HEAD]
            da = datt[at_rows, lo:lo + 2 * HEAD]
            zero = jnp.zeros_like(q)

            def halves(x):
                return jnp.where(even, x, zero), jnp.where(even, zero, x)

            da_h = halves(da)
            probs, d_scores = [], []
            for half in range(2):
                at = (seq * (width // HEAD) + 2 * pair + half) * length
                prob = prob_ref[at:at + length, :]
                d_prob = dot_nt(da_h[half], v)
                wide_prob = prob.astype(FULL)
                weighted = wide_prob * d_prob
                d_score = weighted - wide_prob * jnp.sum(weighted, axis=-1, keepdims=True)
                probs.append(prob)
                d_scores.append(d_score.astype(LOW))
            d_v = dot_tn(jnp.concatenate(probs, axis=0), jnp.concatenate(da_h, axis=0))
            d_q = dot(jnp.concatenate(d_scores, axis=1), jnp.concatenate(halves(k), axis=0)) * scale
            d_k = dot_tn(jnp.concatenate(d_scores, axis=0), jnp.concatenate(halves(q), axis=0))
            dproj_ref[at_rows, lo:lo + 2 * HEAD] = d_q.astype(LOW)
            dproj_ref[at_rows, width + lo:width + lo + 2 * HEAD] = d_k.astype(LOW)
            dproj_ref[at_rows, 2 * width + lo:2 * width + lo + 2 * HEAD] = d_v.astype(LOW)
            if full:
                totals[0] = totals[0] + column_sum(d_q)
                totals[1] = totals[1] + column_sum(d_v)
        if full:
            small_ref[0:1, lo:lo + 2 * HEAD] = totals[0]
            small_ref[1:2, lo:lo + 2 * HEAD] = totals[1]
    total = dres1_ref[...]
    for part in range(3):
        cols = slice(part * width, (part + 1) * width)
        if full:
            dprojt_ref[cols, :] = dproj_ref[:, cols].T
        w.need(1 + part)
        total = total + dot_nt(dproj_ref[:, cols], wqkv[:, cols])
    dsub_ref[...] = total.astype(LOW)
    if full:
        small_ref[2:8, :] = jnp.zeros((6, width), FULL)
        make(xs[0], xs[1:])


def attention_backward(seqs, full, dres1, qkv, prob, qkv_w, out_w):
    rows, width = dres1.shape
    outs = [sds((rows, width), LOW)]
    scratch = [pltpu.VMEM(a.shape, LOW) for a in (qkv_w, out_w)]
    scratch = scratch + [pltpu.VMEM((rows, width), LOW), pltpu.VMEM((rows, 3 * width), LOW)]
    if full:
        outs = outs + [sds((8, width), FULL)]
    return call(functools.partial(attention_backward_kernel, seqs, full), outs,
                [dres1, qkv, prob, qkv_w, out_w], {3, 4}, scratch, "attention_backward",
                2 * rows * (qkv_w.size + out_w.size), 4, full)


def gru_backward_kernel(full, dpooled_ref, count_ref, tokc_ref, tokr_ref, r_ref, z_ref, n_ref, rn_ref,
                        state_ref, win_hbm, wrec_hbm, *rest):
    if full:
        xs, rest = rest[:len(full.inputs())], rest[len(full.inputs()):]
        dchar_ref, small_ref, *rest, dstate, win, wrec, dgate_ref, drecn_ref, sems = rest
        (dgatet_ref, drect_ref, dchart_ref), make = full.split(rest)
    else:
        dchar_ref, dstate, win, wrec, dgate_ref, sems = rest
    rows, width = dpooled_ref.shape
    count = tokc_ref.shape[0]
    hidden = wrec.shape[0]
    lanes = count // BLOCK_CH
    w = Stream(chunks(wrec_hbm, wrec, 1, 3 * hidden) + chunks(win_hbm, win, 1, width), sems)
    share = (dpooled_ref[...] / count_ref[...]).astype(LOW)
    token = (tokc_ref[...] == lax.broadcasted_iota(jnp.int32, (count, rows), 1))
    dstate[...] = dot(token.astype(FULL).astype(LOW), share)
    carry = [None, None]
    sums = [[None] * 4, [None] * 4]
    for turn in reversed(range(BLOCK_CH)):
        for way in range(2):
            at = turn if way == 0 else BLOCK_CH - 1 - turn
            before = at - 1 if way == 0 else at + 1
            here = slice(at * lanes, (at + 1) * lanes)
            base = way * 3 * hidden
            out = slice(way * hidden, (way + 1) * hidden)
            d_h = dstate[here, out]
            if carry[way] is not None:
                d_h = d_h + carry[way]
            r, z, n, rec_n = r_ref[here, out], z_ref[here, out], n_ref[here, out], rn_ref[here, out]
            d_n = d_h * (1.0 - z) * (1.0 - n * n)
            if turn > 0:
                prev = state_ref[before * lanes:(before + 1) * lanes, out]
                d_z = d_h * (prev - n) * (z * (1.0 - z))
            else:
                d_z = d_h * (-n) * (z * (1.0 - z))
            d_r = d_n * rec_n * (r * (1.0 - r))
            d_rec_n = d_n * r
            pieces = (d_r, d_z, d_n, d_rec_n)
            if full:
                for i, piece in enumerate(pieces):
                    one = column_sum(piece)
                    sums[way][i] = one if sums[way][i] is None else sums[way][i] + one
                drecn_ref[here, out] = d_rec_n.astype(LOW)
            low_r, low_z = d_r.astype(LOW), d_z.astype(LOW)
            dgate_ref[here, base:base + hidden] = low_r
            dgate_ref[here, base + hidden:base + 2 * hidden] = low_z
            dgate_ref[here, base + 2 * hidden:base + 3 * hidden] = d_n.astype(LOW)
            if turn > 0:
                w.need(way)
                d_rec = jnp.concatenate([low_r, low_z, d_rec_n.astype(LOW)], axis=1)
                carry[way] = d_h * z + dot_nt(d_rec, wrec[:, base:base + 3 * hidden])
    w.need(0, 1)
    if full:
        for way in range(2):
            for i in range(3):
                at = slice((3 * way + i) * hidden, (3 * way + i + 1) * hidden)
                turned = dgate_ref[:, at].T
                dgatet_ref[at, :] = turned
                drect_ref[at, :] = turned if i < 2 else drecn_ref[:, way * hidden:(way + 1) * hidden].T
        small_ref[6:8, :] = jnp.zeros((2, width), FULL)
        for kind in range(2):
            line = [sums[way][i if i < 2 or kind == 0 else 3] for way in range(2) for i in range(3)]
            for i in range(3):
                small_ref[3 * kind + i:3 * kind + i + 1, :] = jnp.concatenate(line[2 * i:2 * i + 2], axis=1)
    total = None
    for part in range(3):
        cols = slice(part * width, (part + 1) * width)
        w.need(2 + part)
        term = dot_nt(dgate_ref[:, cols], win[:, cols])
        total = term if total is None else total + term
    low = total.astype(LOW)
    if full:
        dchart_ref[...] = low.T
    spread = (tokr_ref[...] == lax.broadcasted_iota(jnp.int32, (rows, count), 0))
    dchar_ref[...] = dot(spread.astype(FULL).astype(LOW), low).astype(LOW)
    if full:
        make(xs[0], xs[1:])


def gru_backward(full, dpooled, counts, tokc, tokr, r, z, n, rn, state, win, wrec):
    rows, width = dpooled.shape
    count = tokc.shape[0]
    wide = win.shape[1]
    outs = [sds((rows, width), LOW)]
    scratch = [pltpu.VMEM((count, width), FULL), pltpu.VMEM(win.shape, LOW), pltpu.VMEM(wrec.shape, LOW),
               pltpu.VMEM((count, wide), LOW)]
    if full:
        outs = outs + [sds((8, width), FULL)]
        scratch = scratch + [pltpu.VMEM((count, width), LOW)]
    return call(functools.partial(gru_backward_kernel, full), outs,
                [dpooled, counts, tokc, tokr, r, z, n, rn, state, win, wrec], {9, 10}, scratch,
                "gru_backward", 2 * count * (win.size + wrec.size) + 4 * count * rows * width, 5, full)


def conv_grad_kernel(length, joined_ref, d_ref, out_ref):
    sources, cols, rows = d_ref.shape
    pos = lax.broadcasted_iota(jnp.int32, (cols, rows), 1) % length
    moved = [[], [], []]
    for i in range(sources):
        d = d_ref[i].astype(FULL)
        moved[0].append(jnp.where(pos == length - 1, 0.0, pltpu.roll(d, rows - 1, 1)).astype(LOW))
        moved[1].append(d_ref[i])
        moved[2].append(jnp.where(pos == 0, 0.0, pltpu.roll(d, 1, 1)).astype(LOW))
    moved = jnp.concatenate([jnp.concatenate(one, axis=1) for one in moved], axis=0)
    width = joined_ref.shape[2]
    step = width // 2
    for at in range(0, width, step):
        joined = jnp.concatenate([joined_ref[i, :, at:at + step] for i in range(sources)], axis=0)
        term = dot(moved, joined)

        @pl.when(pl.program_id(0) == 0)
        def _():
            for k in range(3):
                out_ref[k, :, at:at + step] = term[k * cols:(k + 1) * cols]

        @pl.when(pl.program_id(0) > 0)
        def _():
            for k in range(3):
                out_ref[k, :, at:at + step] += term[k * cols:(k + 1) * cols]


def conv_grad(length, joined_all, d_cols):
    sources, rows, width = joined_all.shape
    cols = d_cols.shape[1]
    once = 4
    return pl.pallas_call(
        functools.partial(conv_grad_kernel, length),
        grid=(sources // once,),
        in_specs=[pl.BlockSpec((once, rows, width), lambda i: (i, 0, 0)),
                  pl.BlockSpec((once, cols, rows), lambda i: (i, 0, 0))],
        out_specs=pl.BlockSpec((3, cols, width), lambda i: (0, 0, 0)),
        out_shape=sds((3, cols, width), FULL),
        compiler_params=pltpu.CompilerParams(vmem_limit_bytes=VMEM_LIMIT),
        cost_estimate=pl.CostEstimate(flops=6 * sources * rows * width * cols,
                                      bytes_accessed=2 * joined_all.size, transcendentals=0),
        name="conv_grad",
    )(joined_all, d_cols)


def in_blocks(values):
    return values.reshape(-1, BLOCK_CH).T.reshape(-1)


def layer_forward(seqs, save, sub, char, places, weights):
    (qkv_w, qvb, out_w, out_b, gain, shift, up_w, up_b, down_w, down_b, table, win, bin_, wrec,
     brec, mw, mb, cw, cb) = weights
    tokc, tokr, idc, counts = places
    first = sub_forward(seqs, save, sub, qkv_w, qvb, out_w, out_b, gain, shift, up_w, up_b,
                        down_w, down_b)
    second = gru_forward(save, char, tokc, tokr, idc, counts, table, win, bin_, wrec, brec)
    third = merge_forward(sub.shape[0] // seqs, save, first[0], second[0], mw, mb, cw, cb, gain,
                          shift)
    return first, second, third


def spread_cotangent(cotangent, positions, length):
    seqs, picks = positions.shape
    chosen = (positions[:, :, None] == jnp.arange(length, dtype=jnp.int32)).astype(LOW)
    grid = lax.dot_general(chosen, cotangent.reshape(seqs, picks, -1), (((1,), (1,)), ((0,), (0,))),
                           preferred_element_type=FULL)
    grid = grid.reshape(seqs * length, 2, -1)
    return grid[:, 0], grid[:, 1]


def together(*values):
    return lax.optimization_barrier(values)


def sync(values, *marks):
    fields = [getattr(share, name) for share, name in marks]
    values, fields = lax.optimization_barrier((values, fields))
    for (share, name), field in zip(marks, fields):
        setattr(share, name, field)
    return values


def swap(value, bit):
    count = lax.axis_size("batch")
    return lax.ppermute(value, "batch", [(i, i ^ (1 << bit)) for i in range(count)])


def combine_kernel(plan, count, bits_ref, *refs):
    flat = [source for parts in plan for _, _, _, sources in parts for source in sources]
    sources, outs = refs[:count], refs[count:count + len(plan)]
    held, sems = refs[count + len(plan):-1], refs[-1]
    copies = []
    for i, (at, columns, picks) in enumerate(flat):
        index = tuple(
            slice(None) if pick is None else bits_ref[pick[0]] if pick[1] else 1 - bits_ref[pick[0]]
            for pick in picks)
        if columns is not None:
            index = index + (slice(None), pl.ds(columns[0], columns[1] - columns[0]))
        copies.append(pltpu.make_async_copy(sources[at].at[index], held[i], sems.at[i]))
    for copy in copies:
        copy.start()
    at = 0
    for parts, out in zip(plan, outs):
        for row, column, windows, sources in parts:
            total = None
            for _ in sources:
                copies[at].wait()
                term = held[at][...].astype(FULL)
                total = term if total is None else total + term
                at = at + 1
            total = total.astype(out.dtype)
            if windows is None:
                out[..., column:column + total.shape[-1]] = total
                continue
            for (top, height, left, wide), (to_row, to_column) in windows:
                out[to_row:to_row + height, to_column:to_column + wide] = (
                    total[top:top + height, left:left + wide])


def combine(bits, items):
    plan, arrays, shapes, dtypes, outs = [], [], [], [], []
    for parts, shape, dtype in items:
        planned, column = [], 0
        for windows, sources in parts:
            listed = []
            for array, columns, picks in sources:
                place = next((i for i, other in enumerate(arrays) if other is array), len(arrays))
                if place == len(arrays):
                    arrays.append(array)
                listed.append((place, columns, picks))
                lead = tuple(size for size, pick in zip(array.shape, picks) if pick is None)
                tail = array.shape[len(picks):]
                if columns is not None:
                    tail = tail[:-1] + (columns[1] - columns[0],)
                shapes.append(lead + tail)
                dtypes.append(array.dtype)
            planned.append((0, column, windows, listed))
            column = column + shapes[-1][-1]
        plan.append(planned)
        outs.append(sds(shapes[-1][:-1] + (column,) if shape is None else shape, dtype))
    return pl.pallas_call(
        functools.partial(combine_kernel, plan, len(arrays)),
        out_shape=outs,
        in_specs=[pl.BlockSpec(memory_space=pltpu.SMEM)] + [any_spec() for _ in arrays],
        out_specs=[vmem_spec() for _ in outs],
        scratch_shapes=[pltpu.VMEM(shape, dtype) for shape, dtype in zip(shapes, dtypes)]
        + [pltpu.SemaphoreType.DMA((len(shapes),))],
        compiler_params=pltpu.CompilerParams(vmem_limit_bytes=VMEM_LIMIT),
        cost_estimate=pl.CostEstimate(flops=0, bytes_accessed=1024, transcendentals=0),
        name="combine",
    )(bits, *arrays)


class Share:
    def __init__(self, gives, kepts, late=False):
        self.bits = lax.axis_size("batch").bit_length() - 1
        self.order = list(range(self.bits))
        if late:
            self.order = self.order[:1] + self.order[2:] + self.order[1:2]
        self.give = [self.shaped(one) for one in gives]
        self.kepts = [self.shaped(one) for one in kepts]
        self.gots = []

    def shaped(self, value):
        return value.reshape((2,) * (self.bits - 1) + value.shape[1:])

    def source(self, array, columns, passed):
        turn = len(self.gots)
        picks = []
        for bit in reversed(range(self.bits)):
            place = self.order.index(bit)
            if place >= passed:
                picks.append((bit, True) if place < turn else (bit, False) if place == turn else None)
        return array, columns, picks

    def parts(self, windows=None):
        parts, column = [], 0
        for i, (kept, got) in enumerate(zip(self.kepts, self.gots[0])):
            sources = [self.source(kept, None, 1), self.source(got, None, 1)]
            columns = None if len(self.kepts) == 1 else (column, column + kept.shape[-1])
            for age, later in enumerate(self.gots[1:]):
                sources.append(self.source(later, columns, age + 2))
            parts.append((None if windows is None else windows[i], sources))
            column = column + kept.shape[-1]
        return parts

    def item(self):
        return self.parts(), None, LOW if len(self.gots) < self.bits else FULL

    def finished(self):
        return len(self.gots) == self.bits

    def send(self):
        bit = self.order[len(self.gots)]
        count = lax.axis_size("batch")
        self.got = jax.tree.map(
            lambda one: lax.ppermute(one, "batch", [(i, i ^ (1 << bit)) for i in range(count)]), self.give)

    def land(self):
        self.gots = self.gots + [self.got]


class Total:
    def __init__(self, value):
        self.bits = lax.axis_size("batch").bit_length() - 1
        self.give, self.passed = value, 0

    def item(self):
        return [(None, [(self.give, None, ()), (self.got, None, ())])], None, FULL

    def finished(self):
        return self.passed == self.bits

    def send(self):
        count = lax.axis_size("batch")
        self.got = lax.ppermute(self.give, "batch", [(i, i ^ (1 << self.passed)) for i in range(count)])

    def land(self):
        self.passed = self.passed + 1


class Flow:
    def __init__(self):
        self.index = lax.axis_index("batch")
        count = lax.axis_size("batch").bit_length() - 1
        self.bits = jnp.stack([(self.index >> bit) & 1 for bit in range(count)]).astype(jnp.int32)
        self.away = []

    def send(self, *shares):
        for s in shares:
            s.send()
        self.away = self.away + list(shares)

    def land(self, shares, values=(), others=()):
        values = sync(values, *[(s, "got") for s in shares], *[(s, "give") for s in others])
        for s in shares:
            s.land()
        self.away = [s for s in self.away if s not in shares]
        return values

    def prepare(self, *shares):
        outs = combine(self.bits, [s.item() for s in shares])
        for s, out in zip(shares, outs):
            if s.finished():
                s.total = out
            else:
                s.give = out

    def turn(self, shares, values=(), more=(), hold=()):
        self.land(shares)
        self.prepare(*shares)
        going = [s for s in shares if not s.finished()]
        done = [s for s in shares if s.finished()]
        values, totals = sync((values, [s.total for s in done]), *[(s, "give") for s in going + list(more)])
        for s, total in zip(done, totals):
            s.total = total
        self.send(*[s for s in going if s not in hold], *more)
        return values

    def drain(self):
        while self.away:
            self.turn(list(self.away))


def placed(block):
    return block.T[None]


def body(stream_in, char_ids, char_lengths, mask_pos, cotangent, *params):
    weights = tuple(p.reshape(p.shape[1:]) if p.ndim > 2 else p for p in params)
    (qkv_w, qvb, out_w, out_b, gain, shift, up_w, up_b, down_w, down_b, table, win, bin_, wrec,
     brec, mw, mb, cw, cb) = weights
    section = lax.axis_index("section")
    sections = lax.axis_size("section")
    batch = lax.axis_size("batch")
    seqs, length, _, width = stream_in.shape
    rows = seqs * length
    count = seqs * char_ids.shape[1]
    hidden = wrec.shape[0]
    ends = jnp.cumsum(char_lengths, axis=-1)
    spots = jnp.arange(char_ids.shape[1], dtype=jnp.int32)
    token_of = jnp.sum((ends[:, None, :] <= spots[:, None]).astype(jnp.int32), axis=-1)
    token_of = in_blocks(token_of + length * jnp.arange(seqs, dtype=jnp.int32)[:, None])
    places = (token_of[:, None], token_of[None, :], in_blocks(char_ids)[:, None],
              char_lengths.reshape(-1, 1).astype(FULL))
    streams = stream_in.transpose(2, 0, 1, 3).reshape(2, rows, width)
    sub, char = streams[0], streams[1]
    ident = (in_blocks(char_ids)[:, None] == jnp.arange(table.shape[0], dtype=jnp.int32)).astype(LOW)

    def onward(pair):
        route = [(i, i + 1) for i in range(sections - 1)]
        a = lax.ppermute(pair[0], "section", route)
        a, b = lax.optimization_barrier((a, pair[1]))
        return a, lax.ppermute(b, "section", route)

    def back(value):
        return lax.ppermute(value, "section", [(i + 1, i) for i in range(sections - 1)])

    first, second, third = layer_forward(seqs, False, sub, char, places, weights)
    got = onward((third[0], third[1]))
    sub = jnp.where(section == 0, sub, got[0])
    char = jnp.where(section == 0, char, got[1])
    first, second, third = layer_forward(seqs, True, sub, char, places, weights)
    _, qkv, prob, att, res1, first_low, pre, act, res2 = first
    _, charin, r, z, n, rn, state, prev = second
    out_sub, out_char, mpre, joined, second_low, pooled_low, res3, res4 = third
    joined_all = lax.all_gather(joined, "batch")
    tokc, tokr, idc, counts = places
    grid = spread_cotangent(cotangent, mask_pos, length)

    d_res2, d_pooled = merge_backward(length, None, grid[0], grid[1], res3, res4, mpre, mw, cw, gain, res2)
    d_res1, = ffn_backward(None, d_res2, pre, res1, up_w, down_w, gain)
    d_sub, = attention_backward(seqs, None, d_res1, qkv, prob, qkv_w, out_w)
    d_char, = gru_backward(None, d_pooled, counts, tokc, tokr, r, z, n, rn, state, win, wrec)
    last = section == sections - 1
    g_sub = jnp.where(last, grid[0], back(d_sub).astype(FULL))
    g_char = jnp.where(last, grid[1], back(d_char).astype(FULL))

    flow = Flow()
    wide, lead = act.shape[1], batch // 2
    chunk, tall = width // batch, 3 * width // batch

    def split(outs, count, blocks):
        gives, kepts = blocks.finish(outs[count:])
        return list(outs[:count]), [([give], [kept]) for give, kept in zip(gives, kepts)]

    up_chunk, part = wide // batch, width // 3
    blocks = Blocks(flow.bits, lead, [
        (chunk, 2 * width, [(0, 0, chunk, 0, lead, 0, 0, width, 0, 0),
                            (0, width, chunk, 0, lead, 1, 0, width, 0, width)]),
        (chunk, wide, [(1, 0, chunk, 0, lead, 2, 0, wide, 0, 0)])],
        [(2 * width, rows), (width, rows)], [second_low, pooled_low, act])
    (d_res2, d_pooled, d_conv, small1), (merge, down) = split(merge_backward(
        length, blocks, g_sub, g_char, res3, res4, mpre, mw, cw, gain, res2), 4, blocks)
    merge, down = Share(*merge, True), Share(*down)
    d_conv = d_conv.reshape(batch, -1, rows)

    flow.send(down, merge)
    d_cols = lax.all_to_all(d_conv, "batch", 0, 0, tiled=True)
    d_pooled = flow.turn([down, merge], d_pooled)
    spot, few, halfway = width + hidden, table.shape[0] // 2, (width + hidden + table.shape[0] // 2) // 2
    way = [(1, 0, tall, 0, lead // 2, 1, 0, hidden, 0, width - halfway),
           (1, 0, tall, lead // 2, lead, 1, hidden, 2 * hidden, 0, width - halfway)]
    blocks = Blocks(flow.bits, lead, [
        (tall, halfway, [(0, 0, tall, 0, lead, 0, 0, halfway, 0, 0)]),
        (tall, halfway, [(0, 0, tall, 0, lead, 0, halfway, width, 0, 0), *way,
                         (2, 0, chunk, 0, lead, 2, 0, few, 0, spot - halfway),
                         (2, 0, chunk, 0, lead, 2, few, 2 * few, chunk, spot - halfway)])],
        [(3 * width, count), (3 * width, count), (width, count)], [charin, prev, ident])
    outs, d_cols, joined_all = flow.land([down, merge], (
        gru_backward(blocks, d_pooled, counts, tokc, tokr, r, z, n, rn, state, win, wrec), d_cols, joined_all))
    (d_char, small4), (char, char_more) = split(outs, 2, blocks)
    char, char_more = Share(*char), Share(*char_more)

    flow.send(char, char_more)
    flow.land([char, char_more])
    flow.prepare(char, char_more, down)
    d_res2 = flow.land((), d_res2, [char, char_more, down])
    flow.send(char, down)
    blocks = Blocks(flow.bits, lead, [
        (up_chunk, width // 2, [(0, 0, up_chunk, 0, lead, 0, 0, width // 2, 0, 0)]),
        (up_chunk, width // 2, [(0, 0, up_chunk, 0, lead, 0, width // 2, width, 0, 0)])],
        [(wide, rows)], [first_low])
    outs = flow.land([char, down], ffn_backward(blocks, d_res2, pre, res1, up_w, down_w, gain))
    (d_res1, small2), (up, up_more) = split(outs, 2, blocks)
    ups = Share(up[0] + up_more[0], up[1] + up_more[1])

    flow.send(ups)
    flow.land([ups])
    flow.prepare(ups, merge, char)
    d_res1 = flow.land((), d_res1, [ups, merge, char])
    flow.send(char_more, merge, char)
    split_at = (width + part) // 2
    blocks = Blocks(flow.bits, lead, [
        (tall, split_at, [(0, 0, tall, 0, lead, 0, 0, split_at, 0, 0)]),
        (tall, split_at, [(0, 0, tall, 0, lead, 0, split_at, width, 0, 0),
                          (1, 0, chunk, 0, lead, 1, 0, part, 0, width - split_at),
                          (1, 0, chunk, 0, lead, 1, part, 2 * part, chunk, width - split_at),
                          (1, 0, chunk, 0, lead, 1, 2 * part, width, 2 * chunk, width - split_at)])],
        [(3 * width, rows), (width, rows)], [sub, att])
    outs = flow.land([char_more, merge, char],
                     attention_backward(seqs, blocks, d_res1, qkv, prob, qkv_w, out_w))
    (d_sub, small3), (head, head_more) = split(outs, 2, blocks)
    head, head_more = Share(*head), Share(*head_more)

    small = Total(jnp.concatenate([small1, small2, small3, small4], 0))
    flow.send(ups, head, head_more, small)
    going = [s for s in (char, char_more, merge, down) if not s.finished()]
    flow.prepare(char, char_more, merge, down)
    flow.land([head, head_more, small], (), going)
    flow.send(*going)
    flow.prepare(head, head_more, small)
    joined_all, d_cols = flow.land((), (joined_all, d_cols), [head, head_more, small])
    conv = conv_grad(length, joined_all, d_cols)
    others = list(flow.away)
    conv, streams = flow.turn(others, (conv, (d_sub, d_char, out_sub, out_char)), [head, head_more, small])
    d_sub, d_char, out_sub, out_char = streams
    ends_out = jnp.where(section == 0, jnp.stack([d_sub, d_char], 1), jnp.stack([out_sub, out_char], 1))
    ends_out = ends_out.reshape(1, seqs, length, 2, width)
    ends_out = flow.turn([s for s in flow.away if s is not head_more], ends_out)
    flow.drain()
    small = small.total

    b = lax.axis_index("batch")

    def pieces(*which):
        part = width // batch
        mine = lax.dynamic_slice_in_dim(small, b * part, part, 1)
        return jnp.concatenate([mine[i:i + 1] for i in which], 0)

    def piece(start, count):
        part = count * width // batch
        line = small[start:start + count].reshape(1, count * width)
        return lax.dynamic_slice_in_dim(line, b * part, part, 1)

    return (
        ends_out,
        placed(jnp.concatenate([head.total, head_more.total[:, :width - split_at]], 1)),
        pieces(24, 25)[None],
        placed(jnp.concatenate([head_more.total[i * chunk:(i + 1) * chunk, width - split_at:] for i in range(3)], 1)),
        pieces(20),
        pieces(21, 9, 4, 5)[None],
        pieces(22, 10, 6, 7)[None],
        placed(ups.total),
        piece(16, 4),
        placed(down.total),
        pieces(8),
        placed(jnp.concatenate([char_more.total[i * chunk:(i + 1) * chunk, spot - halfway:] for i in range(2)], 1)),
        placed(jnp.concatenate([char.total, char_more.total[:, :width - halfway]], 1)),
        piece(32, 3),
        placed(char_more.total[:, width - halfway:spot - halfway]),
        piece(35, 3),
        merge.total.reshape(chunk, 2, width).transpose(1, 2, 0)[None],
        pieces(2, 3)[None],
        conv.transpose(0, 2, 1)[None],
        piece(0, 2),
    )


def solution(mesh):
    by = P("batch")
    part = P("section")

    def columns(rank):
        return P(*(["section"] + [None] * (rank - 2) + ["batch"]))

    return jax.shard_map(
        body,
        mesh=mesh,
        in_specs=(by,) * 5 + (part,) * 19,
        out_specs=(P("section", "batch"),) + tuple(
            columns(rank) for rank in (3, 3, 3, 2, 3, 3, 3, 2, 3, 2, 3, 3, 2, 3, 2, 4, 3, 4, 2)),
        check_vma=False,
    )
```

```python
import functools
import math

import jax
import jax.numpy as jnp
from jax import lax
from jax.experimental import pallas as pl
from jax.experimental.pallas import tpu as pltpu
from jax.sharding import PartitionSpec as P

HEAD = 64
BLOCK_CH = 8
EPSILON = 1e-05
LOW = jnp.bfloat16
FULL = jnp.float32
VMEM_LIMIT = 63 * 1024 * 1024


def dot(left, right):
    return lax.dot_general(left, right, (((1,), (0,)), ((), ())), preferred_element_type=FULL)


def dot_nt(left, right):
    return lax.dot_general(left, right, (((1,), (1,)), ((), ())), preferred_element_type=FULL)


def dot_tn(left, right):
    return lax.dot_general(left, right, (((0,), (0,)), ((), ())), preferred_element_type=FULL)


def norm_parts(values):
    row_mean = jnp.mean(values, axis=-1, keepdims=True)
    centered = values - row_mean
    row_var = jnp.mean(centered * centered, axis=-1, keepdims=True)
    inverse = lax.rsqrt(row_var + EPSILON)
    return centered * inverse, inverse


def norm(values, gain, shift):
    return norm_parts(values)[0] * gain + shift


def norm_back(values, gain, grad):
    unit, inverse = norm_parts(values)
    scaled = grad * gain
    first = jnp.mean(scaled, axis=-1, keepdims=True)
    second = jnp.mean(scaled * unit, axis=-1, keepdims=True)
    return inverse * (scaled - first - unit * second), unit


GELU_A = 0.7978845608028654
GELU_B = 0.044715


def gelu(x):
    return 0.5 * x * (1.0 + jnp.tanh(GELU_A * (x + GELU_B * x * x * x)))


def gelu_both(x):
    square = x * x
    bent = jnp.tanh(GELU_A * (x + GELU_B * square * x))
    gate = 0.5 * (1.0 + bent)
    return x * gate, gate + 0.5 * x * (1.0 - bent * bent) * (GELU_A * (1.0 + 3.0 * GELU_B * square))


def sigmoid(x):
    return 0.5 * jnp.tanh(0.5 * x) + 0.5


def column_sum(values):
    return jnp.sum(values, axis=0, keepdims=True)


class Stream:
    def __init__(self, pairs, sems, first=None):
        self.copies = [
            pltpu.make_async_copy(src, dst, sems.at[i]) for i, (src, dst) in enumerate(pairs)
        ]
        self.started, self.waited = 0, set()
        self.start(len(pairs) if first is None else first)

    def start(self, count=None):
        upto = len(self.copies) if count is None else self.started + count
        for copy in self.copies[self.started:upto]:
            copy.start()
        self.started = upto

    def need(self, *which):
        for i in which:
            if i not in self.waited:
                self.waited.add(i)
                self.copies[i].wait()


class Loaded:
    def need(self, *which):
        pass


def chunks(src, dst, axis, size):
    total = src.shape[axis]
    parts = []
    for start in range(0, total, size):
        index = [slice(None)] * len(src.shape)
        index[axis] = pl.ds(start, min(size, total - start))
        parts.append((src.at[tuple(index)], dst.at[tuple(index)]))
    return parts


def fill(out, near, terms):
    lead, chunk, columns = out.shape
    part = [term[9] for term in terms if term[8] > 0]
    if part:
        out[:, :, part[0]:] = jnp.zeros((lead, chunk, columns - part[0]), LOW)
    for d_y, base, height, start, stop, x, first, last, row, column in terms:
        d = jnp.concatenate([
            d_y[pl.ds(pl.multiple_of(base + (2 * i + near) * height, 16), height), :]
            for i in range(start, stop)], axis=0)
        step = min(last - first, 768)
        for at in range(first, last, step):
            value = dot(d, x[:, at:at + step]).astype(LOW)
            lanes = slice(column + at - first, column + at - first + step)
            out[start:stop, row:row + height, lanes] = value.reshape(stop - start, height, step)


def fill_plain(shape, near, terms):
    out = jnp.zeros(shape, LOW)
    for d_y, base, height, start, stop, x, first, last, row, column in terms:
        count = stop - start
        d = d_y[base + 2 * start * height:base + 2 * stop * height].reshape(count, 2, height, -1)
        d = lax.dynamic_slice_in_dim(d, near, 1, 1).reshape(count * height, -1)
        value = dot(d, x[:, first:last]).astype(LOW).reshape(count, height, last - first)
        out = lax.dynamic_update_slice(out, value, (start, row, column))
    return out


def named(plan, d_ys, xs):
    return [(d_ys[d],) + rest[:4] + (xs[rest[4]],) + rest[5:] for d, *rest in map(tuple, plan)
            for rest in [tuple(rest)]]


class Blocks:
    def __init__(self, bits, count, plans, d_shapes, xs):
        self.bits, self.count, self.plans, self.d_shapes, self.xs = bits, count, plans, d_shapes, xs
        self.inside = all(plan[0] % 16 == 0 for plan in plans)

    def shapes(self):
        return [sds((self.count, plan[0], plan[1]), LOW) for plan in self.plans]

    def outs(self):
        return self.shapes() * 2 if self.inside else [sds(shape, LOW) for shape in self.d_shapes]

    def scratch(self):
        return [pltpu.VMEM(shape, LOW) for shape in self.d_shapes] if self.inside else []

    def inputs(self):
        return [self.bits] + (self.xs if self.inside else [])

    def split(self, refs):
        if not self.inside:
            return refs[:len(self.d_shapes)], lambda bits_ref, xs: None
        results, d_ys = refs[:2 * len(self.plans)], refs[2 * len(self.plans):]

        def make(bits_ref, xs):
            near = bits_ref[0]
            for own in range(2):
                for i, plan in enumerate(self.plans):
                    result = results[own * len(self.plans) + i]
                    fill(result, near if own else 1 - near, named(plan[2], d_ys, xs))
                    done(result)

        return d_ys, make

    def finish(self, results):
        if self.inside:
            return results[:len(self.plans)], results[len(self.plans):]
        near = self.bits[0]
        return tuple([fill_plain(shape.shape, which, named(plan[2], results, self.xs))
                      for shape, plan in zip(self.shapes(), self.plans)] for which in (1 - near, near))


def any_spec():
    return pl.BlockSpec(memory_space=pl.ANY)


def vmem_spec():
    return pl.BlockSpec(memory_space=pltpu.VMEM)


def sds(shape, dtype):
    return jax.ShapeDtypeStruct(shape, dtype)


def rest_of(blocks, count):
    return [] if blocks is None else list(range(count + 1, count + len(blocks.inputs())))


class Late:
    def __init__(self, ref, copy):
        self.ref, self.copy, self.shape = ref, copy, ref.shape

    def __getitem__(self, index):
        if self.copy is not None:
            self.copy.wait()
            self.copy = None
        return self.ref[index]


class Early:
    def __init__(self, ref, copy):
        self.ref, self.copy, self.shape, self.started = ref, copy, ref.shape, False

    def __getitem__(self, index):
        return self.ref[index]

    def __setitem__(self, index, value):
        self.ref[index] = value

    def done(self):
        if not self.started:
            self.copy.start()
            self.started = True


def done(*refs):
    for ref in refs:
        if isinstance(ref, Early):
            ref.done()


class Job:
    def __init__(self, kernel, outs, ins, streamed, scratch, flops, copies, blocks=None, late=(), after=()):
        self.scalar, self.after = -1, after
        if blocks is not None:
            ins, outs = list(ins) + blocks.inputs(), list(outs) + blocks.outs()
            scratch = blocks.scratch() + list(scratch)
            self.scalar = len(ins) - len(blocks.inputs())
        self.kernel, self.ins, self.outs, self.flops, self.late = kernel, ins, outs, flops, late
        self.streamed = set(streamed) | set(late)
        self.early = [i for i, o in enumerate(outs) if o.size * o.dtype.itemsize > 200000]
        self.scratch = list(scratch) + [pltpu.SemaphoreType.DMA((copies,))]
        self.buffers = [pltpu.VMEM(ins[i].shape, ins[i].dtype) for i in late]
        self.buffers = self.buffers + [pltpu.VMEM(outs[i].shape, outs[i].dtype) for i in self.early]
        self.buffers = self.buffers + [pltpu.SemaphoreType.DMA((max(len(late), 1),)),
                                       pltpu.SemaphoreType.DMA((max(len(self.early), 1),))]

    def in_specs(self):
        return [any_spec() if i in self.streamed else pl.BlockSpec(memory_space=pltpu.SMEM) if i == self.scalar
                else vmem_spec() for i in range(len(self.ins))]

    def out_specs(self):
        return [any_spec() if i in self.early else vmem_spec() for i in range(len(self.outs))]

    def begin(self, ins, outs, scratch, buffers):
        ins, outs = list(ins), list(outs)
        held, (in_sems, out_sems) = buffers[:-2], buffers[-2:]
        for n, i in enumerate(self.late):
            copy = pltpu.make_async_copy(ins[i], held[n], in_sems.at[n])
            copy.start()
            ins[i] = Late(held[n], copy)
        for n, i in enumerate(self.early):
            buffer = held[len(self.late) + n]
            outs[i] = Early(buffer, pltpu.make_async_copy(buffer, outs[i], out_sems.at[n]))
        self.lates = [ins[i] for i in self.late]
        self.earlies = [outs[i] for i in self.early]
        self.results = outs
        return self.kernel(*[job.results[0] for job in self.after], *ins, *outs, *scratch)

    def end(self):
        for late in self.lates:
            if late.copy is not None:
                late.copy.wait()
        for early in self.earlies:
            early.done()
        for early in self.earlies:
            early.copy.wait()


def together_kernel(jobs, pace, *refs):
    groups, at = [], 0
    for kind in ("ins", "outs", "scratch", "buffers"):
        group = []
        for job in jobs:
            count = len(getattr(job, kind))
            group.append(refs[at:at + count])
            at = at + count
        groups.append(group)
    running, last = [], []
    for n, job in enumerate(jobs):
        steps = job.begin(*[group[n] for group in groups])
        next(steps)
        (last if job.after else running).append((steps, pace[n]))
    while running or last:
        if not running:
            running, last = last, []
        left = []
        for steps, count in running:
            if all(next(steps, True) is None for _ in range(count)):
                left.append((steps, count))
        running = left
    for job in jobs:
        job.end()


def run(name, *jobs, pace=(1, 1, 1)):
    ins = [a for job in jobs for a in job.ins]
    outs = [o for job in jobs for o in job.outs]
    moved = sum(a.size * a.dtype.itemsize for a in ins) + sum(o.size * o.dtype.itemsize for o in outs)
    results = pl.pallas_call(
        functools.partial(together_kernel, jobs, pace),
        out_shape=outs,
        in_specs=[spec for job in jobs for spec in job.in_specs()],
        out_specs=[spec for job in jobs for spec in job.out_specs()],
        scratch_shapes=[s for job in jobs for s in job.scratch] + [s for job in jobs for s in job.buffers],
        compiler_params=pltpu.CompilerParams(vmem_limit_bytes=VMEM_LIMIT),
        cost_estimate=pl.CostEstimate(flops=sum(job.flops for job in jobs), bytes_accessed=moved,
                                      transcendentals=0),
        name=name,
    )(*ins)
    split = []
    for job in jobs:
        split.append(results[:len(job.outs)])
        results = results[len(job.outs):]
    return split[0] if len(jobs) == 1 else split


def attention_forward_kernel(seqs, save, s_ref, qkv_hbm, qvb_ref, qkv_ref, prob_ref, att_ref, wqkv, sems):
    width = s_ref.shape[1]
    length = s_ref.shape[0] // seqs
    w = Stream(chunks(qkv_hbm, wqkv, 1, width), sems)
    yield
    for part in range(3):
        w.need(part)
        if part > 0:
            yield
        cols = slice(part * width, (part + 1) * width)
        y = dot(s_ref[...], wqkv[:, cols])
        if part == 0:
            y = (y + qvb_ref[0:1, :]) * HEAD ** -0.5
        elif part == 2:
            y = y + qvb_ref[1:2, :]
        qkv_ref[:, cols] = y.astype(LOW)
    done(qkv_ref)
    lanes = lax.broadcasted_iota(jnp.int32, (length, 2 * HEAD), 1)
    even = lanes < HEAD
    for seq in range(seqs):
        rows = slice(seq * length, (seq + 1) * length)
        for pair in range(width // (2 * HEAD)):
            lo = pair * 2 * HEAD
            q = qkv_ref[rows, lo:lo + 2 * HEAD]
            k = qkv_ref[rows, width + lo:width + lo + 2 * HEAD]
            v = qkv_ref[rows, 2 * width + lo:2 * width + lo + 2 * HEAD]
            zero = jnp.zeros_like(q)
            probs = []
            for half in range(2):
                mask = even if half == 0 else ~even
                scores = dot_nt(jnp.where(mask, q, zero), k)
                peak = jnp.max(scores, axis=-1, keepdims=True)
                e = jnp.exp(scores - peak)
                prob = (e / jnp.sum(e, axis=-1, keepdims=True)).astype(LOW)
                probs.append(prob)
                if save:
                    at = (seq * (width // HEAD) + 2 * pair + half) * length
                    prob_ref[at:at + length, :] = prob
            both = jnp.concatenate(probs, axis=1)
            vv = jnp.concatenate([jnp.where(even, v, zero), jnp.where(even, zero, v)], axis=0)
            att_ref[rows, lo:lo + 2 * HEAD] = dot(both, vv).astype(LOW)
            yield
    done(prob_ref, att_ref)


def ffn_forward_kernel(save, s_ref, att_ref, out_hbm, outb_ref, gain_ref, shift_ref, up_hbm, upb_ref,
                       down_hbm, downb_ref, after_ref, *rest):
    if save:
        res1_ref, first_ref, pre_ref, act_ref, res2_ref, wout, wup, wdown, sems = rest
    else:
        wout, wup, wdown, sems = rest
    width, wide = s_ref.shape[1], wup.shape[1]
    pairs = zip(chunks(up_hbm, wup, 1, width), chunks(down_hbm, wdown, 0, width))
    w = Stream(chunks(out_hbm, wout, 1, width) + [one for pair in pairs for one in pair], sems)
    yield
    w.need(0)
    res1 = s_ref[...].astype(FULL) + dot(att_ref[...], wout[...]) + outb_ref[...]
    after = norm(res1, gain_ref[0:1, :], shift_ref[0:1, :])
    low = after.astype(LOW)
    if save:
        res1_ref[...] = res1
        first_ref[...] = low
        done(res1_ref, first_ref)
    total = after + downb_ref[...]
    for part in range(wide // width):
        yield
        w.need(1 + 2 * part, 2 + 2 * part)
        cols = slice(part * width, (part + 1) * width)
        pre = dot(low, wup[:, cols]) + upb_ref[:, cols]
        if save:
            act, slope = gelu_both(pre)
            act = act.astype(LOW)
            pre_ref[:, cols] = slope.astype(LOW)
            act_ref[:, cols] = act
        else:
            act = gelu(pre).astype(LOW)
        total = total + dot(act, wdown[cols, :])
    if save:
        res2_ref[...] = total
        done(pre_ref, act_ref, res2_ref)
    after_ref[...] = norm(total, gain_ref[1:2, :], shift_ref[1:2, :])


def sub_forward_kernel(seqs, s_ref, qkv_hbm, qvb_ref, out_hbm, outb_ref, gain_ref, shift_ref, up_hbm, upb_ref,
                       down_hbm, downb_ref, after_ref, wqkv, qkv_ref, att_ref, att_sems, wout, wup, wdown, sems):
    attention = attention_forward_kernel(seqs, False, s_ref, qkv_hbm, qvb_ref, qkv_ref, None, att_ref, wqkv,
                                         att_sems)
    ffn = ffn_forward_kernel(False, s_ref, att_ref, out_hbm, outb_ref, gain_ref, shift_ref, up_hbm, upb_ref,
                             down_hbm, downb_ref, after_ref, wout, wup, wdown, sems)
    next(attention)
    yield
    next(ffn)
    yield from attention
    yield from ffn


def attention_forward(seqs, s, qkv_w, qvb):
    rows, width = s.shape
    length = rows // seqs
    outs = [sds((rows, 3 * width), LOW), sds((seqs * (width // HEAD) * length, length), LOW),
            sds((rows, width), LOW)]
    return Job(functools.partial(attention_forward_kernel, seqs, True), outs, [s, qkv_w, qvb], {1},
               [pltpu.VMEM(qkv_w.shape, LOW)], 2 * rows * qkv_w.size, 3)


def ffn_forward(s, att, out_w, out_b, gain, shift, up_w, up_b, down_w, down_b):
    rows, width = s.shape
    wide = up_w.shape[1]
    outs = [sds((rows, width), FULL), sds((rows, width), FULL), sds((rows, width), LOW),
            sds((rows, wide), LOW), sds((rows, wide), LOW), sds((rows, width), FULL)]
    weights = (out_w, up_w, down_w)
    return Job(functools.partial(ffn_forward_kernel, True), outs,
               [s, att, out_w, out_b, gain, shift, up_w, up_b, down_w, down_b], {2, 6, 8},
               [pltpu.VMEM(one.shape, LOW) for one in weights], 2 * rows * sum(one.size for one in weights),
               1 + 2 * (wide // width))


def sub_forward(seqs, s, qkv_w, qvb, out_w, out_b, gain, shift, up_w, up_b, down_w, down_b):
    rows, width = s.shape
    weights = (qkv_w, out_w, up_w, down_w)
    scratch = [pltpu.VMEM(qkv_w.shape, LOW), pltpu.VMEM((rows, 3 * width), LOW), pltpu.VMEM((rows, width), LOW),
               pltpu.SemaphoreType.DMA((3,))] + [pltpu.VMEM(one.shape, LOW) for one in weights[1:]]
    return Job(functools.partial(sub_forward_kernel, seqs), [sds((rows, width), FULL)],
               [s, qkv_w, qvb, out_w, out_b, gain, shift, up_w, up_b, down_w, down_b], {1, 3, 7, 9}, scratch,
               2 * rows * sum(one.size for one in weights), 1 + 2 * (up_w.shape[1] // width))


def gru_forward_kernel(save, c_ref, tokc_ref, tokr_ref, idc_ref, count_ref, table_hbm, win_hbm,
                       bin_ref, wrec_hbm, brec_ref, *rest):
    if save:
        (pooled_ref, charin_ref, r_ref, z_ref, to_n_ref, to_z_ref, to_r_ref, prev_ref,
         table, win, wrec, gate, low_state, sems) = rest
    else:
        pooled_ref, table, win, wrec, gate, low_state, charin_ref, sems = rest
    rows, width = c_ref.shape
    count = tokc_ref.shape[0]
    hidden = wrec.shape[0]
    w = Stream([(table_hbm, table)] + chunks(win_hbm, win, 1, width)
               + chunks(wrec_hbm, wrec, 1, 3 * hidden), sems)
    yield
    token = (tokc_ref[...] == lax.broadcasted_iota(jnp.int32, (count, rows), 1))
    ident = (idc_ref[...] == lax.broadcasted_iota(jnp.int32, (count, table.shape[0]), 1))
    w.need(0)
    x = dot(token.astype(FULL).astype(LOW), c_ref[...]) + dot(ident.astype(FULL).astype(LOW), table[...])
    charin_ref[...] = x.astype(LOW)
    done(charin_ref)
    for part in range(3):
        yield
        w.need(1 + part)
        cols = slice(part * width, (part + 1) * width)
        gate[:, cols] = dot(charin_ref[...], win[:, cols]) + bin_ref[:, cols]
    lanes = count // BLOCK_CH
    state = [None, None]
    w.need(4, 5)
    for turn in range(BLOCK_CH):
        yield
        for way in range(2):
            at = turn if way == 0 else BLOCK_CH - 1 - turn
            here = slice(at * lanes, (at + 1) * lanes)
            base = way * 3 * hidden
            out = slice(way * hidden, (way + 1) * hidden)
            bias = brec_ref[:, base:base + 3 * hidden]
            g = gate[here, base:base + 3 * hidden]
            if turn == 0:
                rec_n = jnp.broadcast_to(bias[:, 2 * hidden:], (lanes, hidden))
                rz = g[:, :2 * hidden] + bias[:, :2 * hidden]
                if save:
                    prev_ref[here, out] = jnp.zeros((lanes, hidden), LOW)
            else:
                low = state[way].astype(LOW)
                if save:
                    prev_ref[here, out] = low
                rec = dot(low, wrec[:, base:base + 3 * hidden]) + bias
                rec_n = rec[:, 2 * hidden:]
                rz = g[:, :2 * hidden] + rec[:, :2 * hidden]
            rz = sigmoid(rz)
            r, z = rz[:, :hidden], rz[:, hidden:]
            n = jnp.tanh(g[:, 2 * hidden:] + r * rec_n)
            new = (1.0 - z) * n
            before = state[way]
            if turn > 0:
                new = new + z * before
            state[way] = new
            low_state[here, out] = new.astype(LOW)
            if save:
                r_ref[here, out] = r.astype(LOW)
                z_ref[here, out] = z.astype(LOW)
                to_n_ref[here, out] = ((1.0 - z) * (1.0 - n * n)).astype(LOW)
                change = -n if turn == 0 else before - n
                to_z_ref[here, out] = (change * (z * (1.0 - z))).astype(LOW)
                to_r_ref[here, out] = (rec_n * (r * (1.0 - r))).astype(LOW)
    if save:
        done(r_ref, z_ref, to_n_ref, to_z_ref, to_r_ref, prev_ref)
    yield
    spread = (tokr_ref[...] == lax.broadcasted_iota(jnp.int32, (rows, count), 0))
    pooled = dot(spread.astype(FULL).astype(LOW), low_state[...])
    pooled_ref[...] = pooled / count_ref[...]


def gru_forward(save, c, tokc, tokr, idc, counts, table, win, bin_, wrec, brec):
    rows, width = c.shape
    count = tokc.shape[0]
    outs = [sds((rows, width), FULL)]
    scratch = [pltpu.VMEM(a.shape, LOW) for a in (table, win, wrec)]
    scratch = scratch + [pltpu.VMEM((count, win.shape[1]), FULL), pltpu.VMEM((count, width), LOW)]
    if save:
        outs = outs + [sds((count, width), LOW)] * 7
    else:
        scratch = scratch + [pltpu.VMEM((count, width), LOW)]
    return Job(functools.partial(gru_forward_kernel, save), outs,
                [c, tokc, tokr, idc, counts, table, win, bin_, wrec, brec],
                {5, 6, 8}, scratch, 2 * count * (win.size + wrec.size) + 2 * count * width * (2 * rows + table.shape[0]), 6)


def shift_rows(values, by, length):
    rows, width = values.shape
    zero = jnp.zeros((1, width), values.dtype)
    pos = lax.broadcasted_iota(jnp.int32, (rows, 1), 0) % length
    if by == 1:
        moved = jnp.concatenate([zero, values[:-1]], axis=0)
        return jnp.where(pos == 0, 0.0, moved)
    moved = jnp.concatenate([values[1:], zero], axis=0)
    return jnp.where(pos == length - 1, 0.0, moved)


def join_kernel(save, pooled_ref, after_ref, mw_hbm, mb_ref, joined_ref, *rest):
    if save:
        pre_ref, second_ref, poollow_ref, mw, sems = rest
    else:
        mw, sems = rest
    width = after_ref.shape[1]
    w = Stream(chunks(mw_hbm, mw, 0, 1), sems)
    yield
    w.need(0, 1)
    for side in range(2):
        cols = slice(side * width, (side + 1) * width)
        low = (after_ref if side == 0 else pooled_ref)[...].astype(LOW)
        pre = dot(low, mw[side]) + mb_ref[side:side + 1, :]
        if save:
            (second_ref if side == 0 else poollow_ref)[...] = low
            value, slope = gelu_both(pre)
            pre_ref[:, cols] = slope.astype(LOW)
        else:
            value = gelu(pre)
        joined_ref[:, cols] = value.astype(LOW)


def join(save, pooled, after, mw, mb):
    rows, width = pooled.outs[0].shape
    outs = [sds((rows, 2 * width), LOW)]
    if save:
        outs = outs * 2 + [sds((rows, width), LOW)] * 2
    return Job(functools.partial(join_kernel, save), outs, [mw, mb], {0}, [pltpu.VMEM(mw.shape, LOW)],
               2 * rows * mw.size, 2, after=(pooled, after))


def merge_forward_kernel(length, save, after_ref, pooled_ref, joined_ref, cw_hbm, cb_ref, gain_ref, shift_ref,
                         sub_ref, char_ref, *rest):
    if save:
        res3_ref, res4_ref, cw, sems = rest
    else:
        cw, sems = rest
    width = after_ref.shape[1]
    w = Stream([pair for k in (1, 0, 2) for pair in chunks(cw_hbm.at[k], cw.at[k], 0, width)], sems)
    yield
    joined = joined_ref[...]
    total = cb_ref[...]
    for place, k in enumerate((1, 0, 2)):
        moved = joined if k == 1 else shift_rows(joined.astype(FULL), 1 - k, length).astype(LOW)
        for half in range(2):
            w.need(2 * place + half)
            rows = slice(half * width, (half + 1) * width)
            total = total + dot(moved[:, rows], cw[k, rows, :])
    res3 = after_ref[...] + total[:, :width]
    res4 = pooled_ref[...] + total[:, width:]
    if save:
        res3_ref[...] = res3
        res4_ref[...] = res4
        done(res3_ref, res4_ref)
    sub_ref[...] = norm(res3, gain_ref[2:3, :], shift_ref[2:3, :]).astype(LOW)
    char_ref[...] = norm(res4, gain_ref[3:4, :], shift_ref[3:4, :]).astype(LOW)


def merge_forward(length, after, pooled, joined, cw, cb, gain, shift):
    rows, width = after.shape
    return Job(functools.partial(merge_forward_kernel, length, False), [sds((rows, width), LOW)] * 2,
               [after, pooled, joined, cw, cb, gain, shift], {3}, [pltpu.VMEM(cw.shape, LOW)],
               2 * rows * cw.size, 6)


def merge_backward_kernel(length, full, gsub_ref, gchar_ref, res3_ref, res4_ref, pre_ref, mw_hbm, cw_hbm,
                          gain_ref, res2_ref, *rest):
    if full:
        xs, rest = rest[:len(full.inputs())], rest[len(full.inputs()):]
        dres2_ref, dpooled_ref, dconv_ref, small_ref, *rest, mw, cw, sems = rest
        (dpre_ref, ddown_ref), make = full.split(rest)
    else:
        dres2_ref, dpooled_ref, mw, cw, sems = rest
    width = res3_ref.shape[1]
    w = Loaded() if sems is None else Stream(chunks(cw_hbm, cw, 0, 1) + chunks(mw_hbm, mw, 0, 1), sems)
    yield
    grads = [gsub_ref[...], gchar_ref[...]]
    d_res, sums = [], []
    for side in range(2):
        d, unit = norm_back((res3_ref, res4_ref)[side][...], gain_ref[2 + side:3 + side, :], grads[side])
        d_res.append(d)
        if full:
            small_ref[4 + side:5 + side, :] = column_sum(grads[side] * unit)
            small_ref[6 + side:7 + side, :] = column_sum(grads[side])
            small_ref[side:side + 1, :] = column_sum(d)
    d_conv = jnp.concatenate(d_res, axis=1)
    if full:
        dconv_ref[...] = d_conv.astype(LOW).T
        done(dconv_ref)
    total, lows = None, []
    for k in range(3):
        moved = d_conv if k == 1 else shift_rows(d_conv, k - 1, length)
        w.need(k)
        term = dot_nt(moved.astype(LOW), cw[k])
        total = term if total is None else total + term
    for half in range(2):
        cols = slice(half * width, (half + 1) * width)
        d_pre = total[:, cols] * pre_ref[:, cols].astype(FULL)
        lows.append(d_pre.astype(LOW))
        if full:
            dpre_ref[cols, :] = lows[-1].T
            sums.append(column_sum(d_pre))
    d_low = jnp.concatenate(lows, axis=1)
    if full:
        for side in range(2):
            small_ref[2 + side:3 + side, :] = sums[side]
    w.need(3, 4)
    d_second = d_res[0] + dot_nt(d_low[:, :width], mw[0])
    d_res2, unit = norm_back(res2_ref[...], gain_ref[1:2, :], d_second)
    dres2_ref[...] = d_res2
    done(dres2_ref)
    dpooled_ref[...] = d_res[1] + dot_nt(d_low[:, width:], mw[1])
    done(dpooled_ref)
    if full:
        ddown_ref[...] = d_res2.astype(LOW).T
        small_ref[8:9, :] = column_sum(d_res2)
        small_ref[9:10, :] = column_sum(d_second * unit)
        small_ref[10:11, :] = column_sum(d_second)
        small_ref[11:16, :] = jnp.zeros((5, width), FULL)
        make(xs[0], xs[1:])


def merge_backward(length, full, gsub, gchar, res3, res4, pre, mw, cw, gain, res2):
    rows, width = res3.shape
    outs = [sds((rows, width), FULL)] * 2
    if full:
        outs = outs + [sds((2 * width, rows), LOW), sds((16, width), FULL)]
    scratch = [pltpu.VMEM(mw.shape, LOW), pltpu.VMEM(cw.shape, LOW)]
    return Job(functools.partial(merge_backward_kernel, length, full), outs,
                [gsub, gchar, res3, res4, pre, mw, cw, gain, res2], {5, 6}, scratch, 2 * rows * (mw.size + cw.size), 5, full,
               [0, 1, 2, 3, 4, 8] + rest_of(full, 9))


def merge_both_kernel(length, after_ref, pooled_ref, joined_ref, mw_hbm, cw_hbm, cb_ref, gain_ref, shift_ref,
                      gsub_ref, gchar_ref, pre_ref, res2_ref, sub_ref, char_ref, res3_ref, res4_ref, dres2_ref,
                      dpooled_ref, mw, mw_sems, cw, sems):
    forward = merge_forward_kernel(length, True, after_ref, pooled_ref, joined_ref, cw_hbm, cb_ref, gain_ref,
                                   shift_ref, sub_ref, char_ref, res3_ref, res4_ref, cw, sems)
    next(forward)
    w = Stream(chunks(mw_hbm, mw, 0, 1), mw_sems)
    yield
    yield from forward
    w.need(0, 1)
    yield from merge_backward_kernel(length, None, gsub_ref, gchar_ref, res3_ref, res4_ref, pre_ref, mw_hbm,
                                     cw_hbm, gain_ref, res2_ref, dres2_ref, dpooled_ref, mw, cw, None)


def merge_both(length, after, pooled, joined, mw, cw, cb, gain, shift, gsub, gchar, pre, res2):
    rows, width = after.shape
    outs = [sds((rows, width), LOW)] * 2 + [sds((rows, width), FULL)] * 4
    scratch = [pltpu.VMEM(mw.shape, LOW), pltpu.SemaphoreType.DMA((2,)), pltpu.VMEM(cw.shape, LOW)]
    return Job(functools.partial(merge_both_kernel, length), outs,
               [after, pooled, joined, mw, cw, cb, gain, shift, gsub, gchar, pre, res2], {3, 4}, scratch,
               4 * rows * (mw.size + cw.size), 6, None, [2, 0, 1, 8, 9, 10, 11])


def ffn_backward_kernel(full, dres2_ref, pre_ref, res1_ref, up_hbm, down_hbm, gain_ref, *rest):
    if full:
        xs, rest = rest[:len(full.inputs())], rest[len(full.inputs()):]
        dres1_ref, small_ref, *rest, wup, wdown, sems = rest
        (dup_ref,), make = full.split(rest)
    else:
        dres1_ref, wup, wdown, sems = rest
    rows, width = dres1_ref.shape
    wide = wup.shape[1]
    parts = wide // width
    pairs = zip(chunks(down_hbm, wdown, 0, width), chunks(up_hbm, wup, 1, width))
    w = Stream([one for pair in pairs for one in pair], sems)
    yield
    d_res2 = dres2_ref[...]
    d_low = d_res2.astype(LOW)
    d_first = d_res2
    for part in range(parts):
        cols = slice(part * width, (part + 1) * width)
        w.need(2 * part, 2 * part + 1)
        d_up = dot_nt(d_low, wdown[cols, :]) * pre_ref[:, cols].astype(FULL)
        up_low = d_up.astype(LOW)
        if full:
            dup_ref[cols, :] = up_low.T
            small_ref[part:part + 1, :] = column_sum(d_up)
        d_first = d_first + dot_nt(up_low, wup[:, cols])
        yield
    d_res1, unit = norm_back(res1_ref[...], gain_ref[0:1, :], d_first)
    dres1_ref[...] = d_res1
    done(dres1_ref)
    if full:
        small_ref[parts:parts + 1, :] = column_sum(d_res1)
        small_ref[parts + 1:parts + 2, :] = column_sum(d_first * unit)
        small_ref[parts + 2:parts + 3, :] = column_sum(d_first)
        small_ref[parts + 3:, :] = jnp.zeros((small_ref.shape[0] - parts - 3, width), FULL)
        make(xs[0], xs[1:])


def ffn_backward(full, dres2, pre, res1, up_w, down_w, gain):
    rows, width = res1.shape
    wide = up_w.shape[1]
    outs = [sds((rows, width), FULL)]
    scratch = [pltpu.VMEM(a.shape, LOW) for a in (up_w, down_w)]
    if full:
        outs = outs + [sds((8, width), FULL)]
    return Job(functools.partial(ffn_backward_kernel, full), outs,
                [dres2, pre, res1, up_w, down_w, gain], {3, 4}, scratch, 2 * rows * (up_w.size + down_w.size), 2 * (wide // width), full,
                [0, 1, 2] + rest_of(full, 6))


def attention_backward_kernel(seqs, full, dres1_ref, qkv_ref, prob_ref, qkv_hbm, out_hbm, *rest):
    if full:
        xs, rest = rest[:len(full.inputs())], rest[len(full.inputs()):]
        dsub_ref, small_ref, *rest, wqkv, wout, datt, dproj_ref, sems = rest
        (dprojt_ref, dbranch_ref), make = full.split(rest)
    else:
        dsub_ref, wqkv, wout, datt, dproj_ref, sems = rest
    rows, width = dsub_ref.shape
    length = rows // seqs
    w = Stream(chunks(out_hbm, wout, 1, width) + chunks(qkv_hbm, wqkv, 1, width), sems)
    yield
    w.need(0, 1, 2, 3)
    branch_low = dres1_ref[...].astype(LOW)
    datt[...] = dot_nt(branch_low, wout[...]).astype(LOW)
    if full:
        dbranch_ref[...] = branch_low.T
    even = lax.broadcasted_iota(jnp.int32, (length, 2 * HEAD), 1) < HEAD
    scale = HEAD ** -0.5
    for pair in range(width // (2 * HEAD)):
        lo = pair * 2 * HEAD
        totals = [0.0, 0.0]
        for seq in range(seqs):
            at_rows = slice(seq * length, (seq + 1) * length)
            q = qkv_ref[at_rows, lo:lo + 2 * HEAD]
            k = qkv_ref[at_rows, width + lo:width + lo + 2 * HEAD]
            v = qkv_ref[at_rows, 2 * width + lo:2 * width + lo + 2 * HEAD]
            da = datt[at_rows, lo:lo + 2 * HEAD]
            zero = jnp.zeros_like(q)

            def halves(x):
                return jnp.where(even, x, zero), jnp.where(even, zero, x)

            da_h = halves(da)
            probs, d_scores = [], []
            for half in range(2):
                at = (seq * (width // HEAD) + 2 * pair + half) * length
                prob = prob_ref[at:at + length, :]
                d_prob = dot_nt(da_h[half], v)
                wide_prob = prob.astype(FULL)
                weighted = wide_prob * d_prob
                d_score = weighted - wide_prob * jnp.sum(weighted, axis=-1, keepdims=True)
                probs.append(prob)
                d_scores.append(d_score.astype(LOW))
            d_v = dot_tn(jnp.concatenate(probs, axis=0), jnp.concatenate(da_h, axis=0))
            d_q = dot(jnp.concatenate(d_scores, axis=1), jnp.concatenate(halves(k), axis=0)) * scale
            d_k = dot_tn(jnp.concatenate(d_scores, axis=0), jnp.concatenate(halves(q), axis=0))
            dproj_ref[at_rows, lo:lo + 2 * HEAD] = d_q.astype(LOW)
            dproj_ref[at_rows, width + lo:width + lo + 2 * HEAD] = d_k.astype(LOW)
            dproj_ref[at_rows, 2 * width + lo:2 * width + lo + 2 * HEAD] = d_v.astype(LOW)
            yield
            if full:
                totals[0] = totals[0] + column_sum(d_q)
                totals[1] = totals[1] + column_sum(d_v)
        if full:
            small_ref[0:1, lo:lo + 2 * HEAD] = totals[0]
            small_ref[1:2, lo:lo + 2 * HEAD] = totals[1]
    total = dres1_ref[...]
    for part in range(3):
        cols = slice(part * width, (part + 1) * width)
        if full:
            dprojt_ref[cols, :] = dproj_ref[:, cols].T
        yield
        total = total + dot_nt(dproj_ref[:, cols], wqkv[:, cols])
    dsub_ref[...] = total.astype(LOW)
    done(dsub_ref)
    if full:
        small_ref[2:8, :] = jnp.zeros((6, width), FULL)
        make(xs[0], xs[1:])


def attention_backward(seqs, full, dres1, qkv, prob, qkv_w, out_w):
    rows, width = dres1.shape
    outs = [sds((rows, width), LOW)]
    scratch = [pltpu.VMEM(a.shape, LOW) for a in (qkv_w, out_w)]
    scratch = scratch + [pltpu.VMEM((rows, width), LOW), pltpu.VMEM((rows, 3 * width), LOW)]
    if full:
        outs = outs + [sds((8, width), FULL)]
    return Job(functools.partial(attention_backward_kernel, seqs, full), outs,
                [dres1, qkv, prob, qkv_w, out_w], {3, 4}, scratch, 2 * rows * (qkv_w.size + out_w.size), 4, full, [0, 1, 2] + rest_of(full, 5))


def gru_backward_kernel(full, dpooled_ref, count_ref, tokc_ref, tokr_ref, r_ref, z_ref, to_n_ref, to_z_ref,
                        to_r_ref, win_hbm, wrec_hbm, *rest):
    if full:
        xs, rest = rest[:len(full.inputs())], rest[len(full.inputs()):]
        dchar_ref, small_ref, *rest, dstate, win, wrec, dgate_ref, drecn_ref, sems = rest
        (dgatet_ref, drect_ref, dchart_ref), make = full.split(rest)
    else:
        dchar_ref, dstate, win, wrec, dgate_ref, sems = rest
    rows, width = dpooled_ref.shape
    count = tokc_ref.shape[0]
    hidden = wrec.shape[0]
    lanes = count // BLOCK_CH
    w = Stream(chunks(wrec_hbm, wrec, 1, 3 * hidden) + chunks(win_hbm, win, 1, width), sems)
    yield
    share = (dpooled_ref[...] / count_ref[...]).astype(LOW)
    token = (tokc_ref[...] == lax.broadcasted_iota(jnp.int32, (count, rows), 1))
    dstate[...] = dot(token.astype(FULL).astype(LOW), share)
    carry = [None, None]
    sums = [[None] * 4, [None] * 4]
    w.need(0, 1)
    for turn in reversed(range(BLOCK_CH)):
        yield
        for way in range(2):
            at = turn if way == 0 else BLOCK_CH - 1 - turn
            here = slice(at * lanes, (at + 1) * lanes)
            base = way * 3 * hidden
            out = slice(way * hidden, (way + 1) * hidden)
            d_h = dstate[here, out]
            if carry[way] is not None:
                d_h = d_h + carry[way]
            d_n = d_h * to_n_ref[here, out].astype(FULL)
            d_z = d_h * to_z_ref[here, out].astype(FULL)
            d_r = d_n * to_r_ref[here, out].astype(FULL)
            d_rec_n = d_n * r_ref[here, out].astype(FULL)
            pieces = (d_r, d_z, d_n, d_rec_n)
            if full:
                for i, piece in enumerate(pieces):
                    one = column_sum(piece)
                    sums[way][i] = one if sums[way][i] is None else sums[way][i] + one
                drecn_ref[here, out] = d_rec_n.astype(LOW)
            low_r, low_z = d_r.astype(LOW), d_z.astype(LOW)
            dgate_ref[here, base:base + hidden] = low_r
            dgate_ref[here, base + hidden:base + 2 * hidden] = low_z
            dgate_ref[here, base + 2 * hidden:base + 3 * hidden] = d_n.astype(LOW)
            if turn > 0:
                d_rec = jnp.concatenate([low_r, low_z, d_rec_n.astype(LOW)], axis=1)
                carry[way] = d_h * z_ref[here, out].astype(FULL) + dot_nt(d_rec, wrec[:, base:base + 3 * hidden])
    if full:
        for way in range(2):
            for i in range(3):
                at = slice((3 * way + i) * hidden, (3 * way + i + 1) * hidden)
                turned = dgate_ref[:, at].T
                dgatet_ref[at, :] = turned
                drect_ref[at, :] = turned if i < 2 else drecn_ref[:, way * hidden:(way + 1) * hidden].T
        small_ref[6:8, :] = jnp.zeros((2, width), FULL)
        for kind in range(2):
            line = [sums[way][i if i < 2 or kind == 0 else 3] for way in range(2) for i in range(3)]
            for i in range(3):
                small_ref[3 * kind + i:3 * kind + i + 1, :] = jnp.concatenate(line[2 * i:2 * i + 2], axis=1)
    total = None
    for part in range(3):
        cols = slice(part * width, (part + 1) * width)
        yield
        w.need(2 + part)
        term = dot_nt(dgate_ref[:, cols], win[:, cols])
        total = term if total is None else total + term
    low = total.astype(LOW)
    if full:
        dchart_ref[...] = low.T
    spread = (tokr_ref[...] == lax.broadcasted_iota(jnp.int32, (rows, count), 0))
    dchar_ref[...] = dot(spread.astype(FULL).astype(LOW), low).astype(LOW)
    done(dchar_ref)
    if full:
        make(xs[0], xs[1:])


def gru_backward(full, dpooled, counts, tokc, tokr, r, z, to_n, to_z, to_r, win, wrec):
    rows, width = dpooled.shape
    count = tokc.shape[0]
    wide = win.shape[1]
    outs = [sds((rows, width), LOW)]
    scratch = [pltpu.VMEM((count, width), FULL), pltpu.VMEM(win.shape, LOW), pltpu.VMEM(wrec.shape, LOW),
               pltpu.VMEM((count, wide), LOW)]
    if full:
        outs = outs + [sds((8, width), FULL)]
        scratch = scratch + [pltpu.VMEM((count, width), LOW)]
    return Job(functools.partial(gru_backward_kernel, full), outs,
                [dpooled, counts, tokc, tokr, r, z, to_n, to_z, to_r, win, wrec], {9, 10}, scratch, 2 * count * (win.size + wrec.size) + 4 * count * rows * width, 5, full,
                [0, 2, 6, 7, 8, 4, 5] + rest_of(full, 11))


def conv_grad_kernel(length, joined_ref, d_ref, out_ref):
    sources, cols, rows = d_ref.shape
    pos = lax.broadcasted_iota(jnp.int32, (cols, rows), 1) % length
    moved = [[], [], []]
    for i in range(sources):
        d = d_ref[i].astype(FULL)
        moved[0].append(jnp.where(pos == length - 1, 0.0, pltpu.roll(d, rows - 1, 1)).astype(LOW))
        moved[1].append(d_ref[i])
        moved[2].append(jnp.where(pos == 0, 0.0, pltpu.roll(d, 1, 1)).astype(LOW))
    moved = jnp.concatenate([jnp.concatenate(one, axis=1) for one in moved], axis=0)
    width = joined_ref.shape[2]
    step = width // 2
    for at in range(0, width, step):
        joined = jnp.concatenate([joined_ref[i, :, at:at + step] for i in range(sources)], axis=0)
        term = dot(moved, joined)

        @pl.when(pl.program_id(0) == 0)
        def _():
            for k in range(3):
                out_ref[k, :, at:at + step] = term[k * cols:(k + 1) * cols]

        @pl.when(pl.program_id(0) > 0)
        def _():
            for k in range(3):
                out_ref[k, :, at:at + step] += term[k * cols:(k + 1) * cols]


def conv_grad(length, joined_all, d_cols):
    sources, rows, width = joined_all.shape
    cols = d_cols.shape[1]
    once = 4
    return pl.pallas_call(
        functools.partial(conv_grad_kernel, length),
        grid=(sources // once,),
        in_specs=[pl.BlockSpec((once, rows, width), lambda i: (i, 0, 0)),
                  pl.BlockSpec((once, cols, rows), lambda i: (i, 0, 0))],
        out_specs=pl.BlockSpec((3, cols, width), lambda i: (0, 0, 0)),
        out_shape=sds((3, cols, width), FULL),
        compiler_params=pltpu.CompilerParams(vmem_limit_bytes=VMEM_LIMIT),
        cost_estimate=pl.CostEstimate(flops=6 * sources * rows * width * cols,
                                      bytes_accessed=2 * joined_all.size, transcendentals=0),
        name="conv_grad",
    )(joined_all, d_cols)


def in_blocks(values):
    return values.reshape(-1, BLOCK_CH).T.reshape(-1)


def layer_forward(seqs, grid, sub, char, places, weights):
    (qkv_w, qvb, out_w, out_b, gain, shift, up_w, up_b, down_w, down_b, table, win, bin_, wrec,
     brec, mw, mb, cw, cb) = weights
    tokc, tokr, idc, counts = places
    second = gru_forward(grid is not None, char, tokc, tokr, idc, counts, table, win, bin_, wrec, brec)
    length = sub.shape[0] // seqs
    if grid is not None:
        heads = run("attention_forward", attention_forward(seqs, sub, qkv_w, qvb))
        first = ffn_forward(sub, heads[2], out_w, out_b, gain, shift, up_w, up_b, down_w, down_b)
        second, first, joined = run("halves_forward_all", second, first, join(True, second, first, mw, mb),
                                    pace=(2, 1, 1))
        third = run("merge_both", merge_both(length, first[0], second[0], joined[0], mw, cw, cb, gain, shift,
                                             *grid, joined[1], first[-1]))
        first = (first[0], *heads, *first[1:])
        third = (*third[:2], joined[1], joined[0], *joined[2:], *third[2:])
    else:
        first = sub_forward(seqs, sub, qkv_w, qvb, out_w, out_b, gain, shift, up_w, up_b, down_w, down_b)
        second, first, joined = run("halves_forward", second, first, join(False, second, first, mw, mb),
                                    pace=(2, 3, 1))
        third = run("merge_forward", merge_forward(length, first[0], second[0], joined[0], cw, cb, gain, shift))
    return first, second, third


def spread_cotangent(cotangent, positions, length):
    seqs, picks = positions.shape
    chosen = (positions[:, :, None] == jnp.arange(length, dtype=jnp.int32)).astype(LOW)
    grid = lax.dot_general(chosen, cotangent.reshape(seqs, picks, -1), (((1,), (1,)), ((0,), (0,))),
                           preferred_element_type=FULL)
    grid = grid.reshape(seqs * length, 2, -1)
    return grid[:, 0], grid[:, 1]


def together(*values):
    return lax.optimization_barrier(values)


def sync(values, *marks):
    fields = [getattr(share, name) for share, name in marks]
    values, fields = lax.optimization_barrier((values, fields))
    for (share, name), field in zip(marks, fields):
        setattr(share, name, field)
    return values


def swap(value, bit):
    count = lax.axis_size("batch")
    return lax.ppermute(value, "batch", [(i, i ^ (1 << bit)) for i in range(count)])


def combine_kernel(plan, count, bits_ref, *refs):
    flat = [source for parts in plan for _, _, _, sources in parts for source in sources]
    sources, outs = refs[:count], refs[count:count + len(plan)]
    held, sems = refs[count + len(plan):-1], refs[-1]
    copies = []
    for i, (at, columns, picks) in enumerate(flat):
        index = tuple(
            slice(None) if pick is None else bits_ref[pick[0]] if pick[1] else 1 - bits_ref[pick[0]]
            for pick in picks)
        if columns is not None:
            index = index + (slice(None), pl.ds(columns[0], columns[1] - columns[0]))
        copies.append(pltpu.make_async_copy(sources[at].at[index], held[i], sems.at[i]))
    for copy in copies:
        copy.start()
    at = 0
    for parts, out in zip(plan, outs):
        for row, column, windows, sources in parts:
            total = None
            for _ in sources:
                copies[at].wait()
                term = held[at][...].astype(FULL)
                total = term if total is None else total + term
                at = at + 1
            total = total.astype(out.dtype)
            if windows is None:
                out[..., column:column + total.shape[-1]] = total
                continue
            for (top, height, left, wide), (to_row, to_column) in windows:
                out[to_row:to_row + height, to_column:to_column + wide] = (
                    total[top:top + height, left:left + wide])


def combine(bits, items):
    plan, arrays, shapes, dtypes, outs = [], [], [], [], []
    for parts, shape, dtype in items:
        planned, column = [], 0
        for windows, sources in parts:
            listed = []
            for array, columns, picks in sources:
                place = next((i for i, other in enumerate(arrays) if other is array), len(arrays))
                if place == len(arrays):
                    arrays.append(array)
                listed.append((place, columns, picks))
                lead = tuple(size for size, pick in zip(array.shape, picks) if pick is None)
                tail = array.shape[len(picks):]
                if columns is not None:
                    tail = tail[:-1] + (columns[1] - columns[0],)
                shapes.append(lead + tail)
                dtypes.append(array.dtype)
            planned.append((0, column, windows, listed))
            column = column + shapes[-1][-1]
        plan.append(planned)
        outs.append(sds(shapes[-1][:-1] + (column,) if shape is None else shape, dtype))
    return pl.pallas_call(
        functools.partial(combine_kernel, plan, len(arrays)),
        out_shape=outs,
        in_specs=[pl.BlockSpec(memory_space=pltpu.SMEM)] + [any_spec() for _ in arrays],
        out_specs=[vmem_spec() for _ in outs],
        scratch_shapes=[pltpu.VMEM(shape, dtype) for shape, dtype in zip(shapes, dtypes)]
        + [pltpu.SemaphoreType.DMA((len(shapes),))],
        compiler_params=pltpu.CompilerParams(vmem_limit_bytes=VMEM_LIMIT),
        cost_estimate=pl.CostEstimate(flops=0, bytes_accessed=1024, transcendentals=0),
        name="combine",
    )(bits, *arrays)


class Share:
    def __init__(self, gives, kepts, late=False):
        self.bits = lax.axis_size("batch").bit_length() - 1
        self.order = list(range(self.bits))
        if late:
            self.order = self.order[:1] + self.order[2:] + self.order[1:2]
        self.give = [self.shaped(one) for one in gives]
        self.kepts = [self.shaped(one) for one in kepts]
        self.gots = []

    def shaped(self, value):
        return value.reshape((2,) * (self.bits - 1) + value.shape[1:])

    def source(self, array, columns, passed):
        turn = len(self.gots)
        picks = []
        for bit in reversed(range(self.bits)):
            place = self.order.index(bit)
            if place >= passed:
                picks.append((bit, True) if place < turn else (bit, False) if place == turn else None)
        return array, columns, picks

    def parts(self, windows=None):
        parts, column = [], 0
        for i, (kept, got) in enumerate(zip(self.kepts, self.gots[0])):
            sources = [self.source(kept, None, 1), self.source(got, None, 1)]
            columns = None if len(self.kepts) == 1 else (column, column + kept.shape[-1])
            for age, later in enumerate(self.gots[1:]):
                sources.append(self.source(later, columns, age + 2))
            parts.append((None if windows is None else windows[i], sources))
            column = column + kept.shape[-1]
        return parts

    def item(self):
        return self.parts(), None, LOW if len(self.gots) < self.bits else FULL

    def finished(self):
        return len(self.gots) == self.bits

    def send(self):
        bit = self.order[len(self.gots)]
        count = lax.axis_size("batch")
        self.got = jax.tree.map(
            lambda one: lax.ppermute(one, "batch", [(i, i ^ (1 << bit)) for i in range(count)]), self.give)

    def land(self):
        self.gots = self.gots + [self.got]


class Total:
    def __init__(self, value):
        self.bits = lax.axis_size("batch").bit_length() - 1
        self.give, self.passed = value, 0

    def item(self):
        return [(None, [(self.give, None, ()), (self.got, None, ())])], None, FULL

    def finished(self):
        return self.passed == self.bits

    def send(self):
        count = lax.axis_size("batch")
        self.got = lax.ppermute(self.give, "batch", [(i, i ^ (1 << self.passed)) for i in range(count)])

    def land(self):
        self.passed = self.passed + 1


class Flow:
    def __init__(self):
        self.index = lax.axis_index("batch")
        count = lax.axis_size("batch").bit_length() - 1
        self.bits = jnp.stack([(self.index >> bit) & 1 for bit in range(count)]).astype(jnp.int32)
        self.away = []

    def send(self, *shares):
        for s in shares:
            s.send()
        self.away = self.away + list(shares)

    def land(self, shares, values=(), others=()):
        values = sync(values, *[(s, "got") for s in shares], *[(s, "give") for s in others])
        for s in shares:
            s.land()
        self.away = [s for s in self.away if s not in shares]
        return values

    def prepare(self, *shares):
        outs = combine(self.bits, [s.item() for s in shares])
        for s, out in zip(shares, outs):
            if s.finished():
                s.total = out
            else:
                s.give = out

    def turn(self, shares, values=(), more=(), hold=()):
        self.land(shares)
        self.prepare(*shares)
        going = [s for s in shares if not s.finished()]
        done = [s for s in shares if s.finished()]
        values, totals = sync((values, [s.total for s in done]), *[(s, "give") for s in going + list(more)])
        for s, total in zip(done, totals):
            s.total = total
        self.send(*[s for s in going if s not in hold], *more)
        return values

    def drain(self):
        while self.away:
            self.turn(list(self.away))


def placed(block):
    return block.T[None]


def body(stream_in, char_ids, char_lengths, mask_pos, cotangent, *params):
    weights = tuple(p.reshape(p.shape[1:]) if p.ndim > 2 else p for p in params)
    (qkv_w, qvb, out_w, out_b, gain, shift, up_w, up_b, down_w, down_b, table, win, bin_, wrec,
     brec, mw, mb, cw, cb) = weights
    section = lax.axis_index("section")
    sections = lax.axis_size("section")
    batch = lax.axis_size("batch")
    seqs, length, _, width = stream_in.shape
    rows = seqs * length
    count = seqs * char_ids.shape[1]
    hidden = wrec.shape[0]
    ends = jnp.cumsum(char_lengths, axis=-1)
    spots = jnp.arange(char_ids.shape[1], dtype=jnp.int32)
    token_of = jnp.sum((ends[:, None, :] <= spots[:, None]).astype(jnp.int32), axis=-1)
    token_of = in_blocks(token_of + length * jnp.arange(seqs, dtype=jnp.int32)[:, None])
    places = (token_of[:, None], token_of[None, :], in_blocks(char_ids)[:, None],
              char_lengths.reshape(-1, 1).astype(FULL))
    streams = stream_in.transpose(2, 0, 1, 3).reshape(2, rows, width)
    sub, char = streams[0], streams[1]
    ident = (in_blocks(char_ids)[:, None] == jnp.arange(table.shape[0], dtype=jnp.int32)).astype(LOW)

    def onward(pair):
        route = [(i, i + 1) for i in range(sections - 1)]
        a = lax.ppermute(pair[0], "section", route)
        a, b = lax.optimization_barrier((a, pair[1]))
        return a, lax.ppermute(b, "section", route)

    def back(value):
        return lax.ppermute(value, "section", [(i + 1, i) for i in range(sections - 1)])

    first, second, third = layer_forward(seqs, None, sub, char, places, weights)
    got = onward((third[0], third[1]))
    sub = jnp.where(section == 0, sub, got[0])
    char = jnp.where(section == 0, char, got[1])
    grid = spread_cotangent(cotangent, mask_pos, length)
    first, second, third = layer_forward(seqs, grid, sub, char, places, weights)
    _, qkv, prob, att, res1, first_low, pre, act, res2 = first
    _, charin, r, z, to_n, to_z, to_r, prev = second
    out_sub, out_char, mpre, joined, second_low, pooled_low, res3, res4, d_res2, d_pooled = third
    joined_all = lax.all_gather(joined, "batch")
    tokc, tokr, idc, counts = places

    (d_char,), (d_res1,) = run(
        "halves_backward", gru_backward(None, d_pooled, counts, tokc, tokr, r, z, to_n, to_z, to_r, win, wrec),
        ffn_backward(None, d_res2, pre, res1, up_w, down_w, gain), pace=(3, 1))
    d_sub, = run("attention_backward", attention_backward(seqs, None, d_res1, qkv, prob, qkv_w, out_w))
    last = section == sections - 1
    g_sub = jnp.where(last, grid[0], back(d_sub).astype(FULL))
    g_char = jnp.where(last, grid[1], back(d_char).astype(FULL))

    flow = Flow()
    wide, lead = act.shape[1], batch // 2
    chunk, tall = width // batch, 3 * width // batch

    def split(outs, count, blocks):
        gives, kepts = blocks.finish(outs[count:])
        return list(outs[:count]), [([give], [kept]) for give, kept in zip(gives, kepts)]

    up_chunk, part = wide // batch, width // 3
    blocks = Blocks(flow.bits, lead, [
        (chunk, 2 * width, [(0, 0, chunk, 0, lead, 0, 0, width, 0, 0),
                            (0, width, chunk, 0, lead, 1, 0, width, 0, width)]),
        (chunk, wide, [(1, 0, chunk, 0, lead, 2, 0, wide, 0, 0)])],
        [(2 * width, rows), (width, rows)], [second_low, pooled_low, act])
    (d_res2, d_pooled, d_conv, small1), (merge, down) = split(run("merge_backward_all", merge_backward(
        length, blocks, g_sub, g_char, res3, res4, mpre, mw, cw, gain, res2)), 4, blocks)
    merge, down = Share(*merge, True), Share(*down)
    d_conv = d_conv.reshape(batch, -1, rows)

    flow.send(down, merge)
    d_cols = lax.all_to_all(d_conv, "batch", 0, 0, tiled=True)
    d_pooled = flow.turn([down, merge], d_pooled)
    spot, few, halfway = width + hidden, table.shape[0] // 2, (width + hidden + table.shape[0] // 2) // 2
    way = [(1, 0, tall, 0, lead // 2, 1, 0, hidden, 0, width - halfway),
           (1, 0, tall, lead // 2, lead, 1, hidden, 2 * hidden, 0, width - halfway)]
    blocks = Blocks(flow.bits, lead, [
        (tall, halfway, [(0, 0, tall, 0, lead, 0, 0, halfway, 0, 0)]),
        (tall, halfway, [(0, 0, tall, 0, lead, 0, halfway, width, 0, 0), *way,
                         (2, 0, chunk, 0, lead, 2, 0, few, 0, spot - halfway),
                         (2, 0, chunk, 0, lead, 2, few, 2 * few, chunk, spot - halfway)])],
        [(3 * width, count), (3 * width, count), (width, count)], [charin, prev, ident])
    outs, d_cols, joined_all = flow.land([down, merge], (
        run("gru_backward_all", gru_backward(
            blocks, d_pooled, counts, tokc, tokr, r, z, to_n, to_z, to_r, win, wrec)), d_cols, joined_all))
    (d_char, small4), (char, char_more) = split(outs, 2, blocks)
    char, char_more = Share(*char), Share(*char_more)

    flow.send(char, char_more)
    flow.land([char, char_more])
    flow.prepare(char, char_more, down)
    d_res2 = flow.land((), d_res2, [char, char_more, down])
    flow.send(char, down)
    blocks = Blocks(flow.bits, lead, [
        (up_chunk, width // 2, [(0, 0, up_chunk, 0, lead, 0, 0, width // 2, 0, 0)]),
        (up_chunk, width // 2, [(0, 0, up_chunk, 0, lead, 0, width // 2, width, 0, 0)])],
        [(wide, rows)], [first_low])
    outs = flow.land([char, down], run("ffn_backward_all", ffn_backward(
        blocks, d_res2, pre, res1, up_w, down_w, gain)))
    (d_res1, small2), (up, up_more) = split(outs, 2, blocks)
    ups = Share(up[0] + up_more[0], up[1] + up_more[1])

    flow.send(ups)
    flow.land([ups])
    flow.prepare(ups, merge, char)
    d_res1 = flow.land((), d_res1, [ups, merge, char])
    flow.send(char_more, merge, char)
    split_at = (width + part) // 2
    blocks = Blocks(flow.bits, lead, [
        (tall, split_at, [(0, 0, tall, 0, lead, 0, 0, split_at, 0, 0)]),
        (tall, split_at, [(0, 0, tall, 0, lead, 0, split_at, width, 0, 0),
                          (1, 0, chunk, 0, lead, 1, 0, part, 0, width - split_at),
                          (1, 0, chunk, 0, lead, 1, part, 2 * part, chunk, width - split_at),
                          (1, 0, chunk, 0, lead, 1, 2 * part, width, 2 * chunk, width - split_at)])],
        [(3 * width, rows), (width, rows)], [sub, att])
    outs = flow.land([char_more, merge, char],
                     run("attention_backward_all", attention_backward(
                         seqs, blocks, d_res1, qkv, prob, qkv_w, out_w)))
    (d_sub, small3), (head, head_more) = split(outs, 2, blocks)
    head, head_more = Share(*head), Share(*head_more)

    small = Total(jnp.concatenate([small1, small2, small3, small4], 0))
    flow.send(ups, head, head_more, small)
    going = [s for s in (char, char_more, merge, down) if not s.finished()]
    flow.prepare(char, char_more, merge, down)
    flow.land([head, head_more, small], (), going)
    flow.send(*going)
    flow.prepare(head, head_more, small)
    joined_all, d_cols = flow.land((), (joined_all, d_cols), [head, head_more, small])
    conv = conv_grad(length, joined_all, d_cols)
    others = list(flow.away)
    conv, streams = flow.turn(others, (conv, (d_sub, d_char, out_sub, out_char)), [head, head_more, small])
    d_sub, d_char, out_sub, out_char = streams
    ends_out = jnp.where(section == 0, jnp.stack([d_sub, d_char], 1), jnp.stack([out_sub, out_char], 1))
    ends_out = ends_out.reshape(1, seqs, length, 2, width)
    ends_out = flow.turn([s for s in flow.away if s is not head_more], ends_out)
    flow.drain()
    small = small.total

    b = lax.axis_index("batch")

    def pieces(*which):
        part = width // batch
        mine = lax.dynamic_slice_in_dim(small, b * part, part, 1)
        return jnp.concatenate([mine[i:i + 1] for i in which], 0)

    def piece(start, count):
        part = count * width // batch
        line = small[start:start + count].reshape(1, count * width)
        return lax.dynamic_slice_in_dim(line, b * part, part, 1)

    return (
        ends_out,
        placed(jnp.concatenate([head.total, head_more.total[:, :width - split_at]], 1)),
        pieces(24, 25)[None],
        placed(jnp.concatenate([head_more.total[i * chunk:(i + 1) * chunk, width - split_at:] for i in range(3)], 1)),
        pieces(20),
        pieces(21, 9, 4, 5)[None],
        pieces(22, 10, 6, 7)[None],
        placed(ups.total),
        piece(16, 4),
        placed(down.total),
        pieces(8),
        placed(jnp.concatenate([char_more.total[i * chunk:(i + 1) * chunk, spot - halfway:] for i in range(2)], 1)),
        placed(jnp.concatenate([char.total, char_more.total[:, :width - halfway]], 1)),
        piece(32, 3),
        placed(char_more.total[:, width - halfway:spot - halfway]),
        piece(35, 3),
        merge.total.reshape(chunk, 2, width).transpose(1, 2, 0)[None],
        pieces(2, 3)[None],
        conv.transpose(0, 2, 1)[None],
        piece(0, 2),
    )


def solution(mesh):
    by = P("batch")
    part = P("section")

    def columns(rank):
        return P(*(["section"] + [None] * (rank - 2) + ["batch"]))

    return jax.shard_map(
        body,
        mesh=mesh,
        in_specs=(by,) * 5 + (part,) * 19,
        out_specs=(P("section", "batch"),) + tuple(
            columns(rank) for rank in (3, 3, 3, 2, 3, 3, 3, 2, 3, 2, 3, 3, 2, 3, 2, 4, 3, 4, 2)),
        check_vma=False,
    )
```

```python
import functools
import math

import jax
import jax.numpy as jnp
from jax import lax
from jax.experimental import pallas as pl
from jax.experimental.pallas import tpu as pltpu
from jax.sharding import PartitionSpec as P

HEAD = 64
BLOCK_CH = 8
EPSILON = 1e-05
LOW = jnp.bfloat16
FULL = jnp.float32
VMEM_LIMIT = 63 * 1024 * 1024


def dot(left, right):
    return lax.dot_general(left, right, (((1,), (0,)), ((), ())), preferred_element_type=FULL)


def dot_nt(left, right):
    return lax.dot_general(left, right, (((1,), (1,)), ((), ())), preferred_element_type=FULL)


def dot_tn(left, right):
    return lax.dot_general(left, right, (((0,), (0,)), ((), ())), preferred_element_type=FULL)


def norm_parts(values):
    row_mean = jnp.mean(values, axis=-1, keepdims=True)
    centered = values - row_mean
    row_var = jnp.mean(centered * centered, axis=-1, keepdims=True)
    inverse = lax.rsqrt(row_var + EPSILON)
    return centered * inverse, inverse


def norm(values, gain, shift):
    return norm_parts(values)[0] * gain + shift


def norm_back(values, gain, grad):
    unit, inverse = norm_parts(values)
    scaled = grad * gain
    first = jnp.mean(scaled, axis=-1, keepdims=True)
    second = jnp.mean(scaled * unit, axis=-1, keepdims=True)
    return inverse * (scaled - first - unit * second), unit


GELU_A = 0.7978845608028654
GELU_B = 0.044715


def gelu(x):
    return 0.5 * x * (1.0 + jnp.tanh(GELU_A * (x + GELU_B * x * x * x)))


def gelu_both(x):
    square = x * x
    bent = jnp.tanh(GELU_A * (x + GELU_B * square * x))
    gate = 0.5 * (1.0 + bent)
    return x * gate, gate + 0.5 * x * (1.0 - bent * bent) * (GELU_A * (1.0 + 3.0 * GELU_B * square))


def sigmoid(x):
    return 0.5 * jnp.tanh(0.5 * x) + 0.5


def column_sum(values):
    return jnp.sum(values, axis=0, keepdims=True)


class Stream:
    def __init__(self, pairs, sems, first=None):
        self.copies = [
            pltpu.make_async_copy(src, dst, sems.at[i]) for i, (src, dst) in enumerate(pairs)
        ]
        self.started, self.waited = 0, set()
        self.start(len(pairs) if first is None else first)

    def start(self, count=None):
        upto = len(self.copies) if count is None else self.started + count
        for copy in self.copies[self.started:upto]:
            copy.start()
        self.started = upto

    def need(self, *which):
        for i in which:
            if i not in self.waited:
                self.waited.add(i)
                self.copies[i].wait()


class Loaded:
    def need(self, *which):
        pass


def chunks(src, dst, axis, size):
    total = src.shape[axis]
    parts = []
    for start in range(0, total, size):
        index = [slice(None)] * len(src.shape)
        index[axis] = pl.ds(start, min(size, total - start))
        parts.append((src.at[tuple(index)], dst.at[tuple(index)]))
    return parts


def fill(out, near, terms):
    lead, chunk, columns = out.shape
    part = [term[9] for term in terms if term[8] > 0]
    if part:
        out[:, :, part[0]:] = jnp.zeros((lead, chunk, columns - part[0]), LOW)
    for d_y, base, height, start, stop, x, first, last, row, column in terms:
        d = jnp.concatenate([
            d_y[pl.ds(pl.multiple_of(base + (2 * i + near) * height, 16), height), :]
            for i in range(start, stop)], axis=0)
        step = min(last - first, 768)
        for at in range(first, last, step):
            value = dot(d, x[:, at:at + step]).astype(LOW)
            lanes = slice(column + at - first, column + at - first + step)
            out[start:stop, row:row + height, lanes] = value.reshape(stop - start, height, step)


def fill_plain(shape, near, terms):
    out = jnp.zeros(shape, LOW)
    for d_y, base, height, start, stop, x, first, last, row, column in terms:
        count = stop - start
        d = d_y[base + 2 * start * height:base + 2 * stop * height].reshape(count, 2, height, -1)
        d = lax.dynamic_slice_in_dim(d, near, 1, 1).reshape(count * height, -1)
        value = dot(d, x[:, first:last]).astype(LOW).reshape(count, height, last - first)
        out = lax.dynamic_update_slice(out, value, (start, row, column))
    return out


def named(plan, d_ys, xs):
    return [(d_ys[d],) + rest[:4] + (xs[rest[4]],) + rest[5:] for d, *rest in map(tuple, plan)
            for rest in [tuple(rest)]]


class Blocks:
    def __init__(self, bits, count, plans, d_shapes, xs):
        self.bits, self.count, self.plans, self.d_shapes, self.xs = bits, count, plans, d_shapes, xs
        self.inside = all(plan[0] % 16 == 0 for plan in plans)
        self.last = bits.shape[0] - 1

    def shapes(self):
        return [sds((self.count, plan[0], plan[1]), LOW) for plan in self.plans]

    def outs(self):
        return self.shapes() * 2 if self.inside else [sds(shape, LOW) for shape in self.d_shapes]

    def scratch(self):
        return [pltpu.VMEM(shape, LOW) for shape in self.d_shapes] if self.inside else []

    def inputs(self):
        return [self.bits] + (self.xs if self.inside else [])

    def split(self, refs):
        if not self.inside:
            return refs[:len(self.d_shapes)], lambda bits_ref, xs: None
        results, d_ys = refs[:2 * len(self.plans)], refs[2 * len(self.plans):]

        def make(bits_ref, xs):
            near = bits_ref[0]
            for own in range(2):
                for i, plan in enumerate(self.plans):
                    result = results[own * len(self.plans) + i]
                    fill(result, near if own else 1 - near, named(plan[2], d_ys, xs))
                    done(result)

        return d_ys, make

    def finish(self, results):
        if self.inside:
            return results[:len(self.plans)], results[len(self.plans):]
        near = self.bits[0]
        return tuple([fill_plain(shape.shape, which, named(plan[2], results, self.xs))
                      for shape, plan in zip(self.shapes(), self.plans)] for which in (1 - near, near))


def any_spec():
    return pl.BlockSpec(memory_space=pl.ANY)


def vmem_spec():
    return pl.BlockSpec(memory_space=pltpu.VMEM)


def sds(shape, dtype):
    return jax.ShapeDtypeStruct(shape, dtype)


def rest_of(blocks, count):
    return [] if blocks is None else list(range(count + 1, count + len(blocks.inputs())))


class Late:
    def __init__(self, ref, copy):
        self.ref, self.copy, self.shape = ref, copy, ref.shape

    def __getitem__(self, index):
        if self.copy is not None:
            self.copy.wait()
            self.copy = None
        return self.ref[index]


class Early:
    def __init__(self, ref, copy):
        self.ref, self.copy, self.shape, self.started = ref, copy, ref.shape, False

    def __getitem__(self, index):
        return self.ref[index]

    def __setitem__(self, index, value):
        self.ref[index] = value

    def done(self):
        if not self.started:
            self.copy.start()
            self.started = True


def done(*refs):
    for ref in refs:
        if isinstance(ref, Early):
            ref.done()


class Job:
    def __init__(self, kernel, outs, ins, streamed, scratch, flops, copies, blocks=None, late=(), after=()):
        self.scalar, self.after = -1, after
        if blocks is not None:
            ins, outs = list(ins) + blocks.inputs(), list(outs) + blocks.outs()
            scratch = blocks.scratch() + list(scratch)
            self.scalar = len(ins) - len(blocks.inputs())
        self.kernel, self.ins, self.outs, self.flops, self.late = kernel, ins, outs, flops, late
        self.streamed = set(streamed) | set(late)
        self.early = [i for i, o in enumerate(outs) if o.size * o.dtype.itemsize > 200000]
        self.scratch = list(scratch) + [pltpu.SemaphoreType.DMA((copies,))]
        self.buffers = [pltpu.VMEM(ins[i].shape, ins[i].dtype) for i in late]
        self.buffers = self.buffers + [pltpu.VMEM(outs[i].shape, outs[i].dtype) for i in self.early]
        self.buffers = self.buffers + [pltpu.SemaphoreType.DMA((max(len(late), 1),)),
                                       pltpu.SemaphoreType.DMA((max(len(self.early), 1),))]

    def in_specs(self):
        return [any_spec() if i in self.streamed else pl.BlockSpec(memory_space=pltpu.SMEM) if i == self.scalar
                else vmem_spec() for i in range(len(self.ins))]

    def out_specs(self):
        return [any_spec() if i in self.early else vmem_spec() for i in range(len(self.outs))]

    def begin(self, ins, outs, scratch, buffers):
        ins, outs = list(ins), list(outs)
        held, (in_sems, out_sems) = buffers[:-2], buffers[-2:]
        for n, i in enumerate(self.late):
            copy = pltpu.make_async_copy(ins[i], held[n], in_sems.at[n])
            copy.start()
            ins[i] = Late(held[n], copy)
        for n, i in enumerate(self.early):
            buffer = held[len(self.late) + n]
            outs[i] = Early(buffer, pltpu.make_async_copy(buffer, outs[i], out_sems.at[n]))
        self.lates = [ins[i] for i in self.late]
        self.earlies = [outs[i] for i in self.early]
        self.results = outs
        return self.kernel(*[job.results[0] for job in self.after], *ins, *outs, *scratch)

    def end(self):
        for late in self.lates:
            if late.copy is not None:
                late.copy.wait()
        for early in self.earlies:
            early.done()
        for early in self.earlies:
            early.copy.wait()


def together_kernel(jobs, pace, *refs):
    groups, at = [], 0
    for kind in ("ins", "outs", "scratch", "buffers"):
        group = []
        for job in jobs:
            count = len(getattr(job, kind))
            group.append(refs[at:at + count])
            at = at + count
        groups.append(group)
    running, last = [], []
    for n, job in enumerate(jobs):
        steps = job.begin(*[group[n] for group in groups])
        next(steps)
        (last if job.after else running).append((steps, pace[n]))
    while running or last:
        if not running:
            running, last = last[:1], last[1:]
        left = []
        for steps, count in running:
            if all(next(steps, True) is None for _ in range(count)):
                left.append((steps, count))
        running = left
    for job in jobs:
        job.end()


def run(name, *jobs, pace=(1, 1, 1)):
    ins = [a for job in jobs for a in job.ins]
    outs = [o for job in jobs for o in job.outs]
    moved = sum(a.size * a.dtype.itemsize for a in ins) + sum(o.size * o.dtype.itemsize for o in outs)
    results = pl.pallas_call(
        functools.partial(together_kernel, jobs, pace),
        out_shape=outs,
        in_specs=[spec for job in jobs for spec in job.in_specs()],
        out_specs=[spec for job in jobs for spec in job.out_specs()],
        scratch_shapes=[s for job in jobs for s in job.scratch] + [s for job in jobs for s in job.buffers],
        compiler_params=pltpu.CompilerParams(vmem_limit_bytes=VMEM_LIMIT),
        cost_estimate=pl.CostEstimate(flops=sum(job.flops for job in jobs), bytes_accessed=moved,
                                      transcendentals=0),
        name=name,
    )(*ins)
    split = []
    for job in jobs:
        split.append(results[:len(job.outs)])
        results = results[len(job.outs):]
    return split[0] if len(jobs) == 1 else split


def attention_forward_kernel(seqs, save, s_ref, qkv_hbm, qvb_ref, qkv_ref, prob_ref, att_ref, wqkv, sems):
    width = s_ref.shape[1]
    length = s_ref.shape[0] // seqs
    w = Stream(chunks(qkv_hbm, wqkv, 1, width), sems)
    yield
    for part in range(3):
        w.need(part)
        if part > 0:
            yield
        cols = slice(part * width, (part + 1) * width)
        y = dot(s_ref[...], wqkv[:, cols])
        if part == 0:
            y = (y + qvb_ref[0:1, :]) * HEAD ** -0.5
        elif part == 2:
            y = y + qvb_ref[1:2, :]
        qkv_ref[:, cols] = y.astype(LOW)
    done(qkv_ref)
    lanes = lax.broadcasted_iota(jnp.int32, (length, 2 * HEAD), 1)
    even = lanes < HEAD
    for seq in range(seqs):
        rows = slice(seq * length, (seq + 1) * length)
        for pair in range(width // (2 * HEAD)):
            lo = pair * 2 * HEAD
            q = qkv_ref[rows, lo:lo + 2 * HEAD]
            k = qkv_ref[rows, width + lo:width + lo + 2 * HEAD]
            v = qkv_ref[rows, 2 * width + lo:2 * width + lo + 2 * HEAD]
            zero = jnp.zeros_like(q)
            probs = []
            for half in range(2):
                mask = even if half == 0 else ~even
                scores = dot_nt(jnp.where(mask, q, zero), k)
                peak = jnp.max(scores, axis=-1, keepdims=True)
                e = jnp.exp(scores - peak)
                prob = (e / jnp.sum(e, axis=-1, keepdims=True)).astype(LOW)
                probs.append(prob)
                if save:
                    at = (seq * (width // HEAD) + 2 * pair + half) * length
                    prob_ref[at:at + length, :] = prob
            both = jnp.concatenate(probs, axis=1)
            vv = jnp.concatenate([jnp.where(even, v, zero), jnp.where(even, zero, v)], axis=0)
            att_ref[rows, lo:lo + 2 * HEAD] = dot(both, vv).astype(LOW)
            yield
    done(prob_ref, att_ref)


def ffn_forward_kernel(save, s_ref, att_ref, out_hbm, outb_ref, gain_ref, shift_ref, up_hbm, upb_ref,
                       down_hbm, downb_ref, after_ref, *rest):
    if save:
        res1_ref, first_ref, pre_ref, act_ref, res2_ref, wout, wup, wdown, sems = rest
    else:
        wout, wup, wdown, sems = rest
    width, wide = s_ref.shape[1], wup.shape[1]
    pairs = zip(chunks(up_hbm, wup, 1, width), chunks(down_hbm, wdown, 0, width))
    w = Stream(chunks(out_hbm, wout, 1, width) + [one for pair in pairs for one in pair], sems)
    yield
    w.need(0)
    res1 = s_ref[...].astype(FULL) + dot(att_ref[...], wout[...]) + outb_ref[...]
    after = norm(res1, gain_ref[0:1, :], shift_ref[0:1, :])
    low = after.astype(LOW)
    if save:
        res1_ref[...] = res1
        first_ref[...] = low
        done(res1_ref, first_ref)
    total = after + downb_ref[...]
    for part in range(wide // width):
        yield
        w.need(1 + 2 * part, 2 + 2 * part)
        cols = slice(part * width, (part + 1) * width)
        pre = dot(low, wup[:, cols]) + upb_ref[:, cols]
        if save:
            act, slope = gelu_both(pre)
            act = act.astype(LOW)
            pre_ref[:, cols] = slope.astype(LOW)
            act_ref[:, cols] = act
        else:
            act = gelu(pre).astype(LOW)
        total = total + dot(act, wdown[cols, :])
    if save:
        res2_ref[...] = total
        done(pre_ref, act_ref, res2_ref)
    after_ref[...] = norm(total, gain_ref[1:2, :], shift_ref[1:2, :])


def sub_forward_kernel(seqs, s_ref, qkv_hbm, qvb_ref, out_hbm, outb_ref, gain_ref, shift_ref, up_hbm, upb_ref,
                       down_hbm, downb_ref, after_ref, wqkv, qkv_ref, att_ref, att_sems, wout, wup, wdown, sems):
    attention = attention_forward_kernel(seqs, False, s_ref, qkv_hbm, qvb_ref, qkv_ref, None, att_ref, wqkv,
                                         att_sems)
    ffn = ffn_forward_kernel(False, s_ref, att_ref, out_hbm, outb_ref, gain_ref, shift_ref, up_hbm, upb_ref,
                             down_hbm, downb_ref, after_ref, wout, wup, wdown, sems)
    next(attention)
    yield
    next(ffn)
    yield from attention
    yield from ffn


def attention_forward(seqs, s, qkv_w, qvb):
    rows, width = s.shape
    length = rows // seqs
    outs = [sds((rows, 3 * width), LOW), sds((seqs * (width // HEAD) * length, length), LOW),
            sds((rows, width), LOW)]
    return Job(functools.partial(attention_forward_kernel, seqs, True), outs, [s, qkv_w, qvb], {1},
               [pltpu.VMEM(qkv_w.shape, LOW)], 2 * rows * qkv_w.size, 3)


def ffn_forward(s, att, out_w, out_b, gain, shift, up_w, up_b, down_w, down_b):
    rows, width = s.shape
    wide = up_w.shape[1]
    outs = [sds((rows, width), FULL), sds((rows, width), FULL), sds((rows, width), LOW),
            sds((rows, wide), LOW), sds((rows, wide), LOW), sds((rows, width), FULL)]
    weights = (out_w, up_w, down_w)
    return Job(functools.partial(ffn_forward_kernel, True), outs,
               [s, att, out_w, out_b, gain, shift, up_w, up_b, down_w, down_b], {2, 6, 8},
               [pltpu.VMEM(one.shape, LOW) for one in weights], 2 * rows * sum(one.size for one in weights),
               1 + 2 * (wide // width))


def sub_forward(seqs, s, qkv_w, qvb, out_w, out_b, gain, shift, up_w, up_b, down_w, down_b):
    rows, width = s.shape
    weights = (qkv_w, out_w, up_w, down_w)
    scratch = [pltpu.VMEM(qkv_w.shape, LOW), pltpu.VMEM((rows, 3 * width), LOW), pltpu.VMEM((rows, width), LOW),
               pltpu.SemaphoreType.DMA((3,))] + [pltpu.VMEM(one.shape, LOW) for one in weights[1:]]
    return Job(functools.partial(sub_forward_kernel, seqs), [sds((rows, width), FULL)],
               [s, qkv_w, qvb, out_w, out_b, gain, shift, up_w, up_b, down_w, down_b], {1, 3, 7, 9}, scratch,
               2 * rows * sum(one.size for one in weights), 1 + 2 * (up_w.shape[1] // width))


def gru_forward_kernel(save, c_ref, tokc_ref, tokr_ref, idc_ref, count_ref, table_hbm, win_hbm,
                       bin_ref, wrec_hbm, brec_ref, *rest):
    if save:
        (pooled_ref, charin_ref, r_ref, z_ref, to_n_ref, to_z_ref, to_r_ref, prev_ref,
         table, win, wrec, gate, low_state, sems) = rest
    else:
        pooled_ref, table, win, wrec, gate, low_state, charin_ref, sems = rest
    rows, width = c_ref.shape
    count = tokc_ref.shape[0]
    hidden = wrec.shape[0]
    w = Stream([(table_hbm, table)] + chunks(win_hbm, win, 1, width)
               + chunks(wrec_hbm, wrec, 1, 3 * hidden), sems)
    yield
    token = (tokc_ref[...] == lax.broadcasted_iota(jnp.int32, (count, rows), 1))
    ident = (idc_ref[...] == lax.broadcasted_iota(jnp.int32, (count, table.shape[0]), 1))
    w.need(0)
    x = dot(token.astype(FULL).astype(LOW), c_ref[...]) + dot(ident.astype(FULL).astype(LOW), table[...])
    charin_ref[...] = x.astype(LOW)
    done(charin_ref)
    for part in range(3):
        yield
        w.need(1 + part)
        cols = slice(part * width, (part + 1) * width)
        gate[:, cols] = dot(charin_ref[...], win[:, cols]) + bin_ref[:, cols]
    lanes = count // BLOCK_CH
    state = [None, None]
    w.need(4, 5)
    for turn in range(BLOCK_CH):
        yield
        for way in range(2):
            at = turn if way == 0 else BLOCK_CH - 1 - turn
            here = slice(at * lanes, (at + 1) * lanes)
            base = way * 3 * hidden
            out = slice(way * hidden, (way + 1) * hidden)
            bias = brec_ref[:, base:base + 3 * hidden]
            g = gate[here, base:base + 3 * hidden]
            if turn == 0:
                rec_n = jnp.broadcast_to(bias[:, 2 * hidden:], (lanes, hidden))
                rz = g[:, :2 * hidden] + bias[:, :2 * hidden]
                if save:
                    prev_ref[here, out] = jnp.zeros((lanes, hidden), LOW)
            else:
                low = state[way].astype(LOW)
                if save:
                    prev_ref[here, out] = low
                rec = dot(low, wrec[:, base:base + 3 * hidden]) + bias
                rec_n = rec[:, 2 * hidden:]
                rz = g[:, :2 * hidden] + rec[:, :2 * hidden]
            rz = sigmoid(rz)
            r, z = rz[:, :hidden], rz[:, hidden:]
            n = jnp.tanh(g[:, 2 * hidden:] + r * rec_n)
            new = (1.0 - z) * n
            before = state[way]
            if turn > 0:
                new = new + z * before
            state[way] = new
            low_state[here, out] = new.astype(LOW)
            if save:
                r_ref[here, out] = r.astype(LOW)
                z_ref[here, out] = z.astype(LOW)
                to_n_ref[here, out] = ((1.0 - z) * (1.0 - n * n)).astype(LOW)
                change = -n if turn == 0 else before - n
                to_z_ref[here, out] = (change * (z * (1.0 - z))).astype(LOW)
                to_r_ref[here, out] = (rec_n * (r * (1.0 - r))).astype(LOW)
    if save:
        done(r_ref, z_ref, to_n_ref, to_z_ref, to_r_ref, prev_ref)
    yield
    spread = (tokr_ref[...] == lax.broadcasted_iota(jnp.int32, (rows, count), 0))
    pooled = dot(spread.astype(FULL).astype(LOW), low_state[...])
    pooled_ref[...] = pooled / count_ref[...]


def gru_forward(save, c, tokc, tokr, idc, counts, table, win, bin_, wrec, brec):
    rows, width = c.shape
    count = tokc.shape[0]
    outs = [sds((rows, width), FULL)]
    scratch = [pltpu.VMEM(a.shape, LOW) for a in (table, win, wrec)]
    scratch = scratch + [pltpu.VMEM((count, win.shape[1]), FULL), pltpu.VMEM((count, width), LOW)]
    if save:
        outs = outs + [sds((count, width), LOW)] * 7
    else:
        scratch = scratch + [pltpu.VMEM((count, width), LOW)]
    return Job(functools.partial(gru_forward_kernel, save), outs,
                [c, tokc, tokr, idc, counts, table, win, bin_, wrec, brec],
                {5, 6, 8}, scratch, 2 * count * (win.size + wrec.size) + 2 * count * width * (2 * rows + table.shape[0]), 6)


def shift_rows(values, by, length):
    rows, width = values.shape
    zero = jnp.zeros((1, width), values.dtype)
    pos = lax.broadcasted_iota(jnp.int32, (rows, 1), 0) % length
    if by == 1:
        moved = jnp.concatenate([zero, values[:-1]], axis=0)
        return jnp.where(pos == 0, 0.0, moved)
    moved = jnp.concatenate([values[1:], zero], axis=0)
    return jnp.where(pos == length - 1, 0.0, moved)


def join_kernel(save, pooled_ref, after_ref, mw_hbm, mb_ref, joined_ref, *rest):
    if save:
        pre_ref, second_ref, poollow_ref, mw, sems = rest
    else:
        mw, sems = rest
    width = after_ref.shape[1]
    w = Stream(chunks(mw_hbm, mw, 0, 1), sems)
    yield
    w.need(0, 1)
    for side in range(2):
        cols = slice(side * width, (side + 1) * width)
        low = (after_ref if side == 0 else pooled_ref)[...].astype(LOW)
        pre = dot(low, mw[side]) + mb_ref[side:side + 1, :]
        if save:
            (second_ref if side == 0 else poollow_ref)[...] = low
            value, slope = gelu_both(pre)
            pre_ref[:, cols] = slope.astype(LOW)
        else:
            value = gelu(pre)
        joined_ref[:, cols] = value.astype(LOW)


def join(save, pooled, after, mw, mb):
    rows, width = pooled.outs[0].shape
    outs = [sds((rows, 2 * width), LOW)]
    if save:
        outs = outs * 2 + [sds((rows, width), LOW)] * 2
    return Job(functools.partial(join_kernel, save), outs, [mw, mb], {0}, [pltpu.VMEM(mw.shape, LOW)],
               2 * rows * mw.size, 2, after=(pooled, after))


def merge_forward_kernel(length, save, after_ref, pooled_ref, joined_ref, cw_hbm, cb_ref, gain_ref, shift_ref,
                         sub_ref, char_ref, *rest):
    if save:
        res3_ref, res4_ref, cw, sems = rest
    else:
        cw, sems = rest
    width = after_ref.shape[1]
    w = Stream([pair for k in (1, 0, 2) for pair in chunks(cw_hbm.at[k], cw.at[k], 0, width)], sems)
    yield
    joined = joined_ref[...]
    total = cb_ref[...]
    for place, k in enumerate((1, 0, 2)):
        moved = joined if k == 1 else shift_rows(joined.astype(FULL), 1 - k, length).astype(LOW)
        for half in range(2):
            w.need(2 * place + half)
            rows = slice(half * width, (half + 1) * width)
            total = total + dot(moved[:, rows], cw[k, rows, :])
    res3 = after_ref[...] + total[:, :width]
    res4 = pooled_ref[...] + total[:, width:]
    if save:
        res3_ref[...] = res3
        res4_ref[...] = res4
        done(res3_ref, res4_ref)
    sub_ref[...] = norm(res3, gain_ref[2:3, :], shift_ref[2:3, :]).astype(LOW)
    char_ref[...] = norm(res4, gain_ref[3:4, :], shift_ref[3:4, :]).astype(LOW)


def merge_forward(length, after, pooled, joined, cw, cb, gain, shift):
    rows, width = after.outs[0].shape
    return Job(functools.partial(merge_forward_kernel, length, False), [sds((rows, width), LOW)] * 2,
               [cw, cb, gain, shift], {0}, [pltpu.VMEM(cw.shape, LOW)],
               2 * rows * cw.size, 6, after=(after, pooled, joined))


def merge_backward_kernel(length, full, gsub_ref, gchar_ref, res3_ref, res4_ref, pre_ref, mw_hbm, cw_hbm,
                          gain_ref, res2_ref, *rest):
    if full:
        psub_ref, pchar_ref, *rest = rest
        xs, rest = rest[:len(full.inputs())], rest[len(full.inputs()):]
        dres2_ref, dpooled_ref, dconv_ref, small_ref, *rest, mw, cw, sems = rest
        (dpre_ref, ddown_ref), make = full.split(rest)
    else:
        dres2_ref, dpooled_ref, mw, cw, sems = rest
    width = res3_ref.shape[1]
    w = Loaded() if sems is None else Stream(chunks(cw_hbm, cw, 0, 1) + chunks(mw_hbm, mw, 0, 1), sems)
    yield
    grads = [gsub_ref[...], gchar_ref[...]]
    if full:
        last = xs[0][full.last] > 0
        grads = [jnp.where(last, grad, ref[...].astype(FULL))
                 for grad, ref in zip(grads, (psub_ref, pchar_ref))]
    d_res, sums = [], []
    for side in range(2):
        d, unit = norm_back((res3_ref, res4_ref)[side][...], gain_ref[2 + side:3 + side, :], grads[side])
        d_res.append(d)
        if full:
            small_ref[4 + side:5 + side, :] = column_sum(grads[side] * unit)
            small_ref[6 + side:7 + side, :] = column_sum(grads[side])
            small_ref[side:side + 1, :] = column_sum(d)
    d_conv = jnp.concatenate(d_res, axis=1)
    if full:
        dconv_ref[...] = d_conv.astype(LOW).T
        done(dconv_ref)
    total, lows = None, []
    for k in range(3):
        moved = d_conv if k == 1 else shift_rows(d_conv, k - 1, length)
        w.need(k)
        term = dot_nt(moved.astype(LOW), cw[k])
        total = term if total is None else total + term
    for half in range(2):
        cols = slice(half * width, (half + 1) * width)
        d_pre = total[:, cols] * pre_ref[:, cols].astype(FULL)
        lows.append(d_pre.astype(LOW))
        if full:
            dpre_ref[cols, :] = lows[-1].T
            sums.append(column_sum(d_pre))
    d_low = jnp.concatenate(lows, axis=1)
    if full:
        for side in range(2):
            small_ref[2 + side:3 + side, :] = sums[side]
    w.need(3, 4)
    d_second = d_res[0] + dot_nt(d_low[:, :width], mw[0])
    d_res2, unit = norm_back(res2_ref[...], gain_ref[1:2, :], d_second)
    dres2_ref[...] = d_res2
    done(dres2_ref)
    dpooled_ref[...] = d_res[1] + dot_nt(d_low[:, width:], mw[1])
    done(dpooled_ref)
    if full:
        ddown_ref[...] = d_res2.astype(LOW).T
        small_ref[8:9, :] = column_sum(d_res2)
        small_ref[9:10, :] = column_sum(d_second * unit)
        small_ref[10:11, :] = column_sum(d_second)
        small_ref[11:16, :] = jnp.zeros((5, width), FULL)
        make(xs[0], xs[1:])


def merge_backward(length, full, gsub, gchar, res3, res4, pre, mw, cw, gain, res2, passed):
    rows, width = res3.shape
    outs = [sds((rows, width), FULL)] * 2
    if full:
        outs = outs + [sds((2 * width, rows), LOW), sds((16, width), FULL)]
    scratch = [pltpu.VMEM(mw.shape, LOW), pltpu.VMEM(cw.shape, LOW)]
    return Job(functools.partial(merge_backward_kernel, length, full), outs,
                [gsub, gchar, res3, res4, pre, mw, cw, gain, res2, *passed], {5, 6}, scratch, 2 * rows * (mw.size + cw.size), 5, full,
               [0, 1, 9, 10, 2, 3, 4, 8] + rest_of(full, 11))


def merge_both_kernel(length, after_ref, pooled_ref, joined_ref, mw_hbm, cw_hbm, cb_ref, gain_ref, shift_ref,
                      gsub_ref, gchar_ref, pre_ref, res2_ref, sub_ref, char_ref, res3_ref, res4_ref, dres2_ref,
                      dpooled_ref, mw, mw_sems, cw, sems):
    forward = merge_forward_kernel(length, True, after_ref, pooled_ref, joined_ref, cw_hbm, cb_ref, gain_ref,
                                   shift_ref, sub_ref, char_ref, res3_ref, res4_ref, cw, sems)
    next(forward)
    w = Stream(chunks(mw_hbm, mw, 0, 1), mw_sems)
    yield
    yield from forward
    w.need(0, 1)
    yield from merge_backward_kernel(length, None, gsub_ref, gchar_ref, res3_ref, res4_ref, pre_ref, mw_hbm,
                                     cw_hbm, gain_ref, res2_ref, dres2_ref, dpooled_ref, mw, cw, None)


def merge_both(length, after, pooled, joined, mw, cw, cb, gain, shift, gsub, gchar, pre, res2):
    rows, width = after.shape
    outs = [sds((rows, width), LOW)] * 2 + [sds((rows, width), FULL)] * 4
    scratch = [pltpu.VMEM(mw.shape, LOW), pltpu.SemaphoreType.DMA((2,)), pltpu.VMEM(cw.shape, LOW)]
    return Job(functools.partial(merge_both_kernel, length), outs,
               [after, pooled, joined, mw, cw, cb, gain, shift, gsub, gchar, pre, res2], {3, 4}, scratch,
               4 * rows * (mw.size + cw.size), 6, None, [2, 0, 1, 8, 9, 10, 11])


def ffn_backward_kernel(full, dres2_ref, pre_ref, res1_ref, up_hbm, down_hbm, gain_ref, *rest):
    if full:
        xs, rest = rest[:len(full.inputs())], rest[len(full.inputs()):]
        dres1_ref, small_ref, *rest, wup, wdown, sems = rest
        (dup_ref,), make = full.split(rest)
    else:
        dres1_ref, wup, wdown, sems = rest
    rows, width = dres1_ref.shape
    wide = wup.shape[1]
    parts = wide // width
    pairs = zip(chunks(down_hbm, wdown, 0, width), chunks(up_hbm, wup, 1, width))
    w = Stream([one for pair in pairs for one in pair], sems)
    yield
    d_res2 = dres2_ref[...]
    d_low = d_res2.astype(LOW)
    d_first = d_res2
    for part in range(parts):
        cols = slice(part * width, (part + 1) * width)
        w.need(2 * part, 2 * part + 1)
        d_up = dot_nt(d_low, wdown[cols, :]) * pre_ref[:, cols].astype(FULL)
        up_low = d_up.astype(LOW)
        if full:
            dup_ref[cols, :] = up_low.T
            small_ref[part:part + 1, :] = column_sum(d_up)
        d_first = d_first + dot_nt(up_low, wup[:, cols])
        yield
    d_res1, unit = norm_back(res1_ref[...], gain_ref[0:1, :], d_first)
    dres1_ref[...] = d_res1
    done(dres1_ref)
    if full:
        small_ref[parts:parts + 1, :] = column_sum(d_res1)
        small_ref[parts + 1:parts + 2, :] = column_sum(d_first * unit)
        small_ref[parts + 2:parts + 3, :] = column_sum(d_first)
        small_ref[parts + 3:, :] = jnp.zeros((small_ref.shape[0] - parts - 3, width), FULL)
        make(xs[0], xs[1:])


def ffn_backward(full, dres2, pre, res1, up_w, down_w, gain):
    rows, width = res1.shape
    wide = up_w.shape[1]
    outs = [sds((rows, width), FULL)]
    scratch = [pltpu.VMEM(a.shape, LOW) for a in (up_w, down_w)]
    if full:
        outs = outs + [sds((8, width), FULL)]
    return Job(functools.partial(ffn_backward_kernel, full), outs,
                [dres2, pre, res1, up_w, down_w, gain], {3, 4}, scratch, 2 * rows * (up_w.size + down_w.size), 2 * (wide // width), full,
                [0, 1, 2] + rest_of(full, 6))


def attention_backward_kernel(seqs, full, dres1_ref, qkv_ref, prob_ref, qkv_hbm, out_hbm, *rest):
    if full:
        xs, rest = rest[:len(full.inputs())], rest[len(full.inputs()):]
        dsub_ref, small_ref, *rest, wqkv, wout, datt, dproj_ref, sems = rest
        (dprojt_ref, dbranch_ref), make = full.split(rest)
    else:
        dsub_ref, wqkv, wout, datt, dproj_ref, sems = rest
    rows, width = dsub_ref.shape
    length = rows // seqs
    w = Stream(chunks(out_hbm, wout, 1, width) + chunks(qkv_hbm, wqkv, 1, width), sems)
    yield
    w.need(0, 1, 2, 3)
    branch_low = dres1_ref[...].astype(LOW)
    datt[...] = dot_nt(branch_low, wout[...]).astype(LOW)
    if full:
        dbranch_ref[...] = branch_low.T
    even = lax.broadcasted_iota(jnp.int32, (length, 2 * HEAD), 1) < HEAD
    scale = HEAD ** -0.5
    for pair in range(width // (2 * HEAD)):
        lo = pair * 2 * HEAD
        totals = [0.0, 0.0]
        for seq in range(seqs):
            at_rows = slice(seq * length, (seq + 1) * length)
            q = qkv_ref[at_rows, lo:lo + 2 * HEAD]
            k = qkv_ref[at_rows, width + lo:width + lo + 2 * HEAD]
            v = qkv_ref[at_rows, 2 * width + lo:2 * width + lo + 2 * HEAD]
            da = datt[at_rows, lo:lo + 2 * HEAD]
            zero = jnp.zeros_like(q)

            def halves(x):
                return jnp.where(even, x, zero), jnp.where(even, zero, x)

            da_h = halves(da)
            probs, d_scores = [], []
            for half in range(2):
                at = (seq * (width // HEAD) + 2 * pair + half) * length
                prob = prob_ref[at:at + length, :]
                d_prob = dot_nt(da_h[half], v)
                wide_prob = prob.astype(FULL)
                weighted = wide_prob * d_prob
                d_score = weighted - wide_prob * jnp.sum(weighted, axis=-1, keepdims=True)
                probs.append(prob)
                d_scores.append(d_score.astype(LOW))
            d_v = dot_tn(jnp.concatenate(probs, axis=0), jnp.concatenate(da_h, axis=0))
            d_q = dot(jnp.concatenate(d_scores, axis=1), jnp.concatenate(halves(k), axis=0)) * scale
            d_k = dot_tn(jnp.concatenate(d_scores, axis=0), jnp.concatenate(halves(q), axis=0))
            dproj_ref[at_rows, lo:lo + 2 * HEAD] = d_q.astype(LOW)
            dproj_ref[at_rows, width + lo:width + lo + 2 * HEAD] = d_k.astype(LOW)
            dproj_ref[at_rows, 2 * width + lo:2 * width + lo + 2 * HEAD] = d_v.astype(LOW)
            yield
            if full:
                totals[0] = totals[0] + column_sum(d_q)
                totals[1] = totals[1] + column_sum(d_v)
        if full:
            small_ref[0:1, lo:lo + 2 * HEAD] = totals[0]
            small_ref[1:2, lo:lo + 2 * HEAD] = totals[1]
    total = dres1_ref[...]
    for part in range(3):
        cols = slice(part * width, (part + 1) * width)
        if full:
            dprojt_ref[cols, :] = dproj_ref[:, cols].T
        yield
        total = total + dot_nt(dproj_ref[:, cols], wqkv[:, cols])
    dsub_ref[...] = total.astype(LOW)
    done(dsub_ref)
    if full:
        small_ref[2:8, :] = jnp.zeros((6, width), FULL)
        make(xs[0], xs[1:])


def attention_backward(seqs, full, dres1, qkv, prob, qkv_w, out_w):
    rows, width = dres1.shape
    outs = [sds((rows, width), LOW)]
    scratch = [pltpu.VMEM(a.shape, LOW) for a in (qkv_w, out_w)]
    scratch = scratch + [pltpu.VMEM((rows, width), LOW), pltpu.VMEM((rows, 3 * width), LOW)]
    if full:
        outs = outs + [sds((8, width), FULL)]
    return Job(functools.partial(attention_backward_kernel, seqs, full), outs,
                [dres1, qkv, prob, qkv_w, out_w], {3, 4}, scratch, 2 * rows * (qkv_w.size + out_w.size), 4, full, [0, 1, 2] + rest_of(full, 5))


def gru_backward_kernel(full, dpooled_ref, count_ref, tokc_ref, tokr_ref, r_ref, z_ref, to_n_ref, to_z_ref,
                        to_r_ref, win_hbm, wrec_hbm, *rest):
    if full:
        xs, rest = rest[:len(full.inputs())], rest[len(full.inputs()):]
        dchar_ref, small_ref, *rest, dstate, win, wrec, dgate_ref, drecn_ref, sems = rest
        (dgatet_ref, drect_ref, dchart_ref), make = full.split(rest)
    else:
        dchar_ref, dstate, win, wrec, dgate_ref, sems = rest
    rows, width = dpooled_ref.shape
    count = tokc_ref.shape[0]
    hidden = wrec.shape[0]
    lanes = count // BLOCK_CH
    w = Stream(chunks(wrec_hbm, wrec, 1, 3 * hidden) + chunks(win_hbm, win, 1, width), sems)
    yield
    share = (dpooled_ref[...] / count_ref[...]).astype(LOW)
    token = (tokc_ref[...] == lax.broadcasted_iota(jnp.int32, (count, rows), 1))
    dstate[...] = dot(token.astype(FULL).astype(LOW), share)
    carry = [None, None]
    sums = [[None] * 4, [None] * 4]
    w.need(0, 1)
    for turn in reversed(range(BLOCK_CH)):
        yield
        for way in range(2):
            at = turn if way == 0 else BLOCK_CH - 1 - turn
            here = slice(at * lanes, (at + 1) * lanes)
            base = way * 3 * hidden
            out = slice(way * hidden, (way + 1) * hidden)
            d_h = dstate[here, out]
            if carry[way] is not None:
                d_h = d_h + carry[way]
            d_n = d_h * to_n_ref[here, out].astype(FULL)
            d_z = d_h * to_z_ref[here, out].astype(FULL)
            d_r = d_n * to_r_ref[here, out].astype(FULL)
            d_rec_n = d_n * r_ref[here, out].astype(FULL)
            pieces = (d_r, d_z, d_n, d_rec_n)
            if full:
                for i, piece in enumerate(pieces):
                    one = column_sum(piece)
                    sums[way][i] = one if sums[way][i] is None else sums[way][i] + one
                drecn_ref[here, out] = d_rec_n.astype(LOW)
            low_r, low_z = d_r.astype(LOW), d_z.astype(LOW)
            dgate_ref[here, base:base + hidden] = low_r
            dgate_ref[here, base + hidden:base + 2 * hidden] = low_z
            dgate_ref[here, base + 2 * hidden:base + 3 * hidden] = d_n.astype(LOW)
            if turn > 0:
                d_rec = jnp.concatenate([low_r, low_z, d_rec_n.astype(LOW)], axis=1)
                carry[way] = d_h * z_ref[here, out].astype(FULL) + dot_nt(d_rec, wrec[:, base:base + 3 * hidden])
    if full:
        for way in range(2):
            for i in range(3):
                at = slice((3 * way + i) * hidden, (3 * way + i + 1) * hidden)
                turned = dgate_ref[:, at].T
                dgatet_ref[at, :] = turned
                drect_ref[at, :] = turned if i < 2 else drecn_ref[:, way * hidden:(way + 1) * hidden].T
        small_ref[6:8, :] = jnp.zeros((2, width), FULL)
        for kind in range(2):
            line = [sums[way][i if i < 2 or kind == 0 else 3] for way in range(2) for i in range(3)]
            for i in range(3):
                small_ref[3 * kind + i:3 * kind + i + 1, :] = jnp.concatenate(line[2 * i:2 * i + 2], axis=1)
    total = None
    for part in range(3):
        cols = slice(part * width, (part + 1) * width)
        yield
        w.need(2 + part)
        term = dot_nt(dgate_ref[:, cols], win[:, cols])
        total = term if total is None else total + term
    low = total.astype(LOW)
    if full:
        dchart_ref[...] = low.T
    spread = (tokr_ref[...] == lax.broadcasted_iota(jnp.int32, (rows, count), 0))
    dchar_ref[...] = dot(spread.astype(FULL).astype(LOW), low).astype(LOW)
    done(dchar_ref)
    if full:
        make(xs[0], xs[1:])


def gru_backward(full, dpooled, counts, tokc, tokr, r, z, to_n, to_z, to_r, win, wrec):
    rows, width = dpooled.shape
    count = tokc.shape[0]
    wide = win.shape[1]
    outs = [sds((rows, width), LOW)]
    scratch = [pltpu.VMEM((count, width), FULL), pltpu.VMEM(win.shape, LOW), pltpu.VMEM(wrec.shape, LOW),
               pltpu.VMEM((count, wide), LOW)]
    if full:
        outs = outs + [sds((8, width), FULL)]
        scratch = scratch + [pltpu.VMEM((count, width), LOW)]
    return Job(functools.partial(gru_backward_kernel, full), outs,
                [dpooled, counts, tokc, tokr, r, z, to_n, to_z, to_r, win, wrec], {9, 10}, scratch, 2 * count * (win.size + wrec.size) + 4 * count * rows * width, 5, full,
                [0, 2, 6, 7, 8, 4, 5] + rest_of(full, 11))


def whole_part(values, divisor):
    return jnp.floor((values + 0.5) * (1.0 / divisor))


def places_kernel(lens_ref, ids_ref, tokc_ref, tokr_ref, idc_ref, count_ref, ident_ref):
    seqs, length = lens_ref.shape
    chars = ids_ref.shape[1]
    blocks, total = chars // BLOCK_CH, seqs * chars

    def spots(index):
        turn = whole_part(index, seqs * blocks)
        rest = index - turn * (seqs * blocks)
        seq = whole_part(rest, blocks)
        return seq, (rest - seq * blocks) * BLOCK_CH + turn

    first = lax.broadcasted_iota(jnp.int32, (length, length), 0)
    second = lax.broadcasted_iota(jnp.int32, (length, length), 1)
    upto = (first <= second).astype(FULL).astype(LOW)
    since = (first >= second).astype(FULL).astype(LOW)
    same = (first == second).astype(FULL).astype(LOW)
    down_seq, down_spot = spots(lax.broadcasted_iota(jnp.int32, (total, 1), 0).astype(FULL))
    over_seq, over_spot = spots(lax.broadcasted_iota(jnp.int32, (1, total), 1).astype(FULL))
    wide = lax.broadcasted_iota(jnp.int32, (total, chars), 1).astype(FULL)
    token_down, token_over, ident = 0.0, 0.0, 0.0
    for seq in range(seqs):
        lens = jnp.broadcast_to(lens_ref[seq:seq + 1, :].astype(FULL), (8, length)).astype(LOW)
        ends_over = dot(lens, upto)[0:1, :]
        ends_down = dot_nt(since, lens)[:, 0:1]
        count_ref[seq * length:(seq + 1) * length, :] = dot_nt(same, lens)[:, 0:1]
        here = jnp.sum((ends_over <= down_spot).astype(FULL), axis=1, keepdims=True) + seq * length
        token_down = token_down + jnp.where(down_seq == seq, here, 0.0)
        here = jnp.sum((ends_down <= over_spot).astype(FULL), axis=0, keepdims=True) + seq * length
        token_over = token_over + jnp.where(over_seq == seq, here, 0.0)
        here = jnp.sum(jnp.where(wide == down_spot, ids_ref[seq:seq + 1, :].astype(FULL), 0.0), axis=1,
                       keepdims=True)
        ident = ident + jnp.where(down_seq == seq, here, 0.0)
    tokc_ref[...] = token_down.astype(jnp.int32)
    tokr_ref[...] = token_over.astype(jnp.int32)
    idc_ref[...] = ident.astype(jnp.int32)
    vocab = lax.broadcasted_iota(jnp.int32, ident_ref.shape, 1).astype(FULL)
    ident_ref[...] = (vocab == ident).astype(FULL).astype(LOW)


def places_of(char_lengths, char_ids, vocab):
    seqs, length = char_lengths.shape
    total = char_ids.size
    return pl.pallas_call(
        places_kernel,
        out_shape=[sds((total, 1), jnp.int32), sds((1, total), jnp.int32), sds((total, 1), jnp.int32),
                   sds((seqs * length, 1), FULL), sds((total, vocab), LOW)],
        in_specs=[vmem_spec(), vmem_spec()],
        out_specs=[vmem_spec() for _ in range(5)],
        compiler_params=pltpu.CompilerParams(vmem_limit_bytes=VMEM_LIMIT),
        cost_estimate=pl.CostEstimate(flops=1024, bytes_accessed=1024, transcendentals=0),
        name="places",
    )(char_lengths, char_ids)


def conv_grad_kernel(length, joined_ref, d_ref, out_ref):
    sources, cols, rows = d_ref.shape
    pos = lax.broadcasted_iota(jnp.int32, (cols, rows), 1) % length
    moved = [[], [], []]
    for i in range(sources):
        d = d_ref[i].astype(FULL)
        moved[0].append(jnp.where(pos == length - 1, 0.0, pltpu.roll(d, rows - 1, 1)).astype(LOW))
        moved[1].append(d_ref[i])
        moved[2].append(jnp.where(pos == 0, 0.0, pltpu.roll(d, 1, 1)).astype(LOW))
    moved = jnp.concatenate([jnp.concatenate(one, axis=1) for one in moved], axis=0)
    width = joined_ref.shape[2]
    step = width // 2
    for at in range(0, width, step):
        joined = jnp.concatenate([joined_ref[i, :, at:at + step] for i in range(sources)], axis=0)
        term = dot(moved, joined)

        @pl.when(pl.program_id(0) == 0)
        def _():
            for k in range(3):
                out_ref[k, :, at:at + step] = term[k * cols:(k + 1) * cols]

        @pl.when(pl.program_id(0) > 0)
        def _():
            for k in range(3):
                out_ref[k, :, at:at + step] += term[k * cols:(k + 1) * cols]


def conv_grad(length, joined_all, d_cols):
    sources, rows, width = joined_all.shape
    cols = d_cols.shape[1]
    once = 4
    return pl.pallas_call(
        functools.partial(conv_grad_kernel, length),
        grid=(sources // once,),
        in_specs=[pl.BlockSpec((once, rows, width), lambda i: (i, 0, 0)),
                  pl.BlockSpec((once, cols, rows), lambda i: (i, 0, 0))],
        out_specs=pl.BlockSpec((3, cols, width), lambda i: (0, 0, 0)),
        out_shape=sds((3, cols, width), FULL),
        compiler_params=pltpu.CompilerParams(vmem_limit_bytes=VMEM_LIMIT),
        cost_estimate=pl.CostEstimate(flops=6 * sources * rows * width * cols,
                                      bytes_accessed=2 * joined_all.size, transcendentals=0),
        name="conv_grad",
    )(joined_all, d_cols)


def layer_forward(seqs, grid, sub, char, places, weights):
    (qkv_w, qvb, out_w, out_b, gain, shift, up_w, up_b, down_w, down_b, table, win, bin_, wrec,
     brec, mw, mb, cw, cb) = weights
    tokc, tokr, idc, counts = places
    second = gru_forward(grid is not None, char, tokc, tokr, idc, counts, table, win, bin_, wrec, brec)
    length = sub.shape[0] // seqs
    if grid is not None:
        heads = run("attention_forward", attention_forward(seqs, sub, qkv_w, qvb))
        first = ffn_forward(sub, heads[2], out_w, out_b, gain, shift, up_w, up_b, down_w, down_b)
        second, first, joined = run("halves_forward_all", second, first, join(True, second, first, mw, mb),
                                    pace=(2, 1, 1))
        third = run("merge_both", merge_both(length, first[0], second[0], joined[0], mw, cw, cb, gain, shift,
                                             *grid, joined[1], first[-1]))
        first = (first[0], *heads, *first[1:])
        third = (*third[:2], joined[1], joined[0], *joined[2:], *third[2:])
    else:
        first = sub_forward(seqs, sub, qkv_w, qvb, out_w, out_b, gain, shift, up_w, up_b, down_w, down_b)
        joined = join(False, second, first, mw, mb)
        third = merge_forward(length, first, second, joined, cw, cb, gain, shift)
        second, first, joined, third = run("layer_forward", second, first, joined, third, pace=(2, 3, 1, 1))
    return first, second, third


def spread_cotangent(cotangent, positions, length):
    seqs, picks = positions.shape
    chosen = (positions[:, :, None] == jnp.arange(length, dtype=jnp.int32)).astype(LOW)
    grid = lax.dot_general(chosen, cotangent.reshape(seqs, picks, -1), (((1,), (1,)), ((0,), (0,))),
                           preferred_element_type=FULL)
    grid = grid.reshape(seqs * length, 2, -1)
    return grid[:, 0], grid[:, 1]


def together(*values):
    return lax.optimization_barrier(values)


def sync(values, *marks):
    fields = [getattr(share, name) for share, name in marks]
    values, fields = lax.optimization_barrier((values, fields))
    for (share, name), field in zip(marks, fields):
        setattr(share, name, field)
    return values


def swap(value, bit):
    count = lax.axis_size("batch")
    return lax.ppermute(value, "batch", [(i, i ^ (1 << bit)) for i in range(count)])


def combine_kernel(plan, count, bits_ref, *refs):
    flat = [source for parts in plan for _, _, _, sources in parts for source in sources]
    sources, outs = refs[:count], refs[count:count + len(plan)]
    held, sems = refs[count + len(plan):-1], refs[-1]
    copies = []
    for i, (at, columns, picks) in enumerate(flat):
        index = tuple(
            slice(None) if pick is None else bits_ref[pick[0]] if pick[1] else 1 - bits_ref[pick[0]]
            for pick in picks)
        if columns is not None:
            index = index + (slice(None), pl.ds(columns[0], columns[1] - columns[0]))
        copies.append(pltpu.make_async_copy(sources[at].at[index], held[i], sems.at[i]))
    for copy in copies:
        copy.start()
    at = 0
    for parts, out in zip(plan, outs):
        for row, column, windows, sources in parts:
            total = None
            for _ in sources:
                copies[at].wait()
                term = held[at][...].astype(FULL)
                total = term if total is None else total + term
                at = at + 1
            total = total.astype(out.dtype)
            if windows is None:
                out[..., column:column + total.shape[-1]] = total
                continue
            for (top, height, left, wide), (to_row, to_column) in windows:
                out[to_row:to_row + height, to_column:to_column + wide] = (
                    total[top:top + height, left:left + wide])


def combine(bits, items):
    plan, arrays, shapes, dtypes, outs = [], [], [], [], []
    for parts, shape, dtype in items:
        planned, column = [], 0
        for windows, sources in parts:
            listed = []
            for array, columns, picks in sources:
                place = next((i for i, other in enumerate(arrays) if other is array), len(arrays))
                if place == len(arrays):
                    arrays.append(array)
                listed.append((place, columns, picks))
                lead = tuple(size for size, pick in zip(array.shape, picks) if pick is None)
                tail = array.shape[len(picks):]
                if columns is not None:
                    tail = tail[:-1] + (columns[1] - columns[0],)
                shapes.append(lead + tail)
                dtypes.append(array.dtype)
            planned.append((0, column, windows, listed))
            column = column + shapes[-1][-1]
        plan.append(planned)
        outs.append(sds(shapes[-1][:-1] + (column,) if shape is None else shape, dtype))
    return pl.pallas_call(
        functools.partial(combine_kernel, plan, len(arrays)),
        out_shape=outs,
        in_specs=[pl.BlockSpec(memory_space=pltpu.SMEM)] + [any_spec() for _ in arrays],
        out_specs=[vmem_spec() for _ in outs],
        scratch_shapes=[pltpu.VMEM(shape, dtype) for shape, dtype in zip(shapes, dtypes)]
        + [pltpu.SemaphoreType.DMA((len(shapes),))],
        compiler_params=pltpu.CompilerParams(vmem_limit_bytes=VMEM_LIMIT),
        cost_estimate=pl.CostEstimate(flops=0, bytes_accessed=1024, transcendentals=0),
        name="combine",
    )(bits, *arrays)


class Share:
    def __init__(self, gives, kepts, late=False, rounds=None):
        self.bits = lax.axis_size("batch").bit_length() - 1
        self.order = list(range(self.bits))
        if late:
            self.order = self.order[:1] + self.order[2:] + self.order[1:2]
        self.rounds = self.bits if rounds is None else rounds
        self.give = [self.shaped(one) for one in gives]
        self.kepts = [self.shaped(one) for one in kepts]
        self.gots = []

    def shaped(self, value):
        return value.reshape((2,) * (self.bits - 1) + value.shape[1:])

    def source(self, array, columns, passed):
        turn = len(self.gots)
        picks = []
        for bit in reversed(range(self.bits)):
            place = self.order.index(bit)
            if place >= passed:
                picks.append((bit, True) if place < turn else (bit, False) if place == turn < self.rounds else None)
        return array, columns, picks

    def parts(self, windows=None):
        parts, column = [], 0
        for i, (kept, got) in enumerate(zip(self.kepts, self.gots[0])):
            sources = [self.source(kept, None, 1), self.source(got, None, 1)]
            columns = None if len(self.kepts) == 1 else (column, column + kept.shape[-1])
            for age, later in enumerate(self.gots[1:]):
                sources.append(self.source(later, columns, age + 2))
            parts.append((None if windows is None else windows[i], sources))
            column = column + kept.shape[-1]
        return parts

    def window(self, first, last):
        sources = [(self.kepts[0], 1), (self.gots[0][0], 1)]
        sources = sources + [(later, age + 2) for age, later in enumerate(self.gots[1:])]
        return [self.source(array, (first, last), passed) for array, passed in sources]

    def item(self):
        return self.parts(), None, LOW if len(self.gots) < self.bits else FULL

    def scatter(self, held):
        count = lax.axis_size("batch")
        step = 1 << self.rounds
        groups = [list(range(i, count, step)) for i in range(step)]
        block = held.shape[-2:]
        total = lax.psum_scatter(held.reshape(-1, block[1]), "batch", scatter_dimension=0,
                                 axis_index_groups=groups, tiled=True)
        return total.astype(FULL)

    def finished(self):
        return len(self.gots) == self.rounds

    def send(self):
        bit = self.order[len(self.gots)]
        count = lax.axis_size("batch")
        self.got = jax.tree.map(
            lambda one: lax.ppermute(one, "batch", [(i, i ^ (1 << bit)) for i in range(count)]), self.give)

    def land(self):
        self.gots = self.gots + [self.got]


class Total:
    def __init__(self, value):
        self.bits = lax.axis_size("batch").bit_length() - 1
        self.give, self.passed = value, 0

    def item(self):
        return [(None, [(self.give, None, ()), (self.got, None, ())])], None, FULL

    def finished(self):
        return self.passed == self.bits

    def send(self):
        count = lax.axis_size("batch")
        self.got = lax.ppermute(self.give, "batch", [(i, i ^ (1 << self.passed)) for i in range(count)])

    def land(self):
        self.passed = self.passed + 1


class Flow:
    def __init__(self):
        self.index = lax.axis_index("batch")
        count = lax.axis_size("batch").bit_length() - 1
        last = lax.axis_index("section") == lax.axis_size("section") - 1
        self.bits = jnp.stack([(self.index >> bit) & 1 for bit in range(count)] + [last]).astype(jnp.int32)
        self.away, self.later = [], []

    def send(self, *shares):
        for s in shares:
            s.send()
        self.away = self.away + list(shares)

    def land(self, shares, values=(), others=()):
        values = sync(values, *[(s, "got") for s in shares], *[(s, "give") for s in others])
        for s in shares:
            s.land()
        self.away = [s for s in self.away if s not in shares]
        return values

    def prepare(self, *shares):
        shares = [s for s in shares if not (s in self.later and s.finished())]
        outs = combine(self.bits, [s.item() for s in shares]) if shares else []
        for s, out in zip(shares, outs):
            if not s.finished():
                s.give = out
            elif isinstance(s, Share) and s.rounds < s.bits:
                s.total = s.scatter(out)
            else:
                s.total = out

    def turn(self, shares, values=(), more=(), hold=()):
        self.land(shares)
        self.prepare(*shares)
        going = [s for s in shares if not s.finished()]
        values = sync(values, *[(s, "give") for s in going + list(more)])
        self.send(*[s for s in going if s not in hold], *more)
        return values

    def drain(self):
        while self.away:
            self.turn(list(self.away))


def placed(block):
    return block.T[None]


def body(stream_in, char_ids, char_lengths, mask_pos, cotangent, *params):
    weights = tuple(p.reshape(p.shape[1:]) if p.ndim > 2 else p for p in params)
    (qkv_w, qvb, out_w, out_b, gain, shift, up_w, up_b, down_w, down_b, table, win, bin_, wrec,
     brec, mw, mb, cw, cb) = weights
    section = lax.axis_index("section")
    sections = lax.axis_size("section")
    batch = lax.axis_size("batch")
    seqs, length, _, width = stream_in.shape
    rows = seqs * length
    count = seqs * char_ids.shape[1]
    hidden = wrec.shape[0]
    *places, ident = places_of(char_lengths, char_ids, table.shape[0])
    streams = stream_in.transpose(2, 0, 1, 3).reshape(2, rows, width)
    sub, char = streams[0], streams[1]

    def onward(pair):
        route = [(i, i + 1) for i in range(sections - 1)]
        a = lax.ppermute(pair[0], "section", route)
        a, b = lax.optimization_barrier((a, pair[1]))
        return a, lax.ppermute(b, "section", route)

    def back(value):
        return lax.ppermute(value, "section", [(i + 1, i) for i in range(sections - 1)])

    first, second, third = layer_forward(seqs, None, sub, char, places, weights)
    got = onward((third[0], third[1]))
    grid = spread_cotangent(cotangent, mask_pos, length)
    got_sub, grid = together(got[0], grid)
    got = (got_sub, got[1])
    sub = jnp.where(section == 0, sub, got[0])
    char = jnp.where(section == 0, char, got[1])
    first, second, third = layer_forward(seqs, grid, sub, char, places, weights)
    _, qkv, prob, att, res1, first_low, pre, act, res2 = first
    _, charin, r, z, to_n, to_z, to_r, prev = second
    out_sub, out_char, mpre, joined, second_low, pooled_low, res3, res4, d_res2, d_pooled = third
    joined_all = lax.all_gather(joined, "batch")
    tokc, tokr, idc, counts = places

    (d_char,), (d_res1,) = run(
        "halves_backward", gru_backward(None, d_pooled, counts, tokc, tokr, r, z, to_n, to_z, to_r, win, wrec),
        ffn_backward(None, d_res2, pre, res1, up_w, down_w, gain), pace=(3, 1))
    d_sub, = run("attention_backward", attention_backward(seqs, None, d_res1, qkv, prob, qkv_w, out_w))
    d_sub, passed_char = together(d_sub, back(d_char))
    passed = (back(d_sub), passed_char)

    flow = Flow()
    wide, lead = act.shape[1], batch // 2
    chunk, tall = width // batch, 3 * width // batch

    def split(outs, count, blocks):
        gives, kepts = blocks.finish(outs[count:])
        return list(outs[:count]), [([give], [kept]) for give, kept in zip(gives, kepts)]

    up_chunk, part = wide // batch, width // 3
    blocks = Blocks(flow.bits, lead, [
        (chunk, 2 * width, [(0, 0, chunk, 0, lead, 0, 0, width, 0, 0),
                            (0, width, chunk, 0, lead, 1, 0, width, 0, width)]),
        (chunk, wide, [(1, 0, chunk, 0, lead, 2, 0, wide, 0, 0)])],
        [(2 * width, rows), (width, rows)], [second_low, pooled_low, act])
    (d_res2, d_pooled, d_conv, small1), (merge, down) = split(run("merge_backward_all", merge_backward(
        length, blocks, *grid, res3, res4, mpre, mw, cw, gain, res2, passed)), 4, blocks)
    merge, down = Share(*merge, True), Share(*down)
    d_conv = d_conv.reshape(batch, -1, rows)

    flow.send(down, merge)
    d_cols = lax.all_to_all(d_conv, "batch", 0, 0, tiled=True)
    d_pooled = flow.turn([down, merge], d_pooled)
    spot, few, halfway = width + hidden, table.shape[0] // 2, (width + hidden + table.shape[0] // 2) // 2
    way = [(1, 0, tall, 0, lead // 2, 1, 0, hidden, 0, width - halfway),
           (1, 0, tall, lead // 2, lead, 1, hidden, 2 * hidden, 0, width - halfway)]
    blocks = Blocks(flow.bits, lead, [
        (tall, halfway, [(0, 0, tall, 0, lead, 0, 0, halfway, 0, 0)]),
        (tall, halfway, [(0, 0, tall, 0, lead, 0, halfway, width, 0, 0), *way,
                         (2, 0, chunk, 0, lead, 2, 0, few, 0, spot - halfway),
                         (2, 0, chunk, 0, lead, 2, few, 2 * few, chunk, spot - halfway)])],
        [(3 * width, count), (3 * width, count), (width, count)], [charin, prev, ident])
    outs, d_cols, joined_all = flow.land([down, merge], (
        run("gru_backward_all", gru_backward(
            blocks, d_pooled, counts, tokc, tokr, r, z, to_n, to_z, to_r, win, wrec)), d_cols, joined_all))
    (d_char, small4), (char, char_more) = split(outs, 2, blocks)
    char, char_more = Share(*char), Share(*char_more)

    flow.send(char, char_more)
    flow.land([char, char_more])
    flow.prepare(char, char_more, down)
    d_res2 = flow.land((), d_res2, [char, char_more, down])
    flow.send(char, down)
    blocks = Blocks(flow.bits, lead, [
        (up_chunk, width // 2, [(0, 0, up_chunk, 0, lead, 0, 0, width // 2, 0, 0)]),
        (up_chunk, width // 2, [(0, 0, up_chunk, 0, lead, 0, width // 2, width, 0, 0)])],
        [(wide, rows)], [first_low])
    outs = flow.land([char, down], run("ffn_backward_all", ffn_backward(
        blocks, d_res2, pre, res1, up_w, down_w, gain)))
    (d_res1, small2), (up, up_more) = split(outs, 2, blocks)
    ups = Share(up[0] + up_more[0], up[1] + up_more[1])

    flow.send(ups)
    flow.land([ups])
    flow.prepare(ups, merge, char)
    d_res1 = flow.land((), d_res1, [ups, merge, char])
    flow.send(char_more, merge, char)
    split_at = (width + part) // 2
    blocks = Blocks(flow.bits, lead, [
        (tall, split_at, [(0, 0, tall, 0, lead, 0, 0, split_at, 0, 0)]),
        (tall, split_at, [(0, 0, tall, 0, lead, 0, split_at, width, 0, 0),
                          (1, 0, chunk, 0, lead, 1, 0, part, 0, width - split_at),
                          (1, 0, chunk, 0, lead, 1, part, 2 * part, chunk, width - split_at),
                          (1, 0, chunk, 0, lead, 1, 2 * part, width, 2 * chunk, width - split_at)])],
        [(3 * width, rows), (width, rows)], [sub, att])
    outs = flow.land([char_more, merge, char],
                     run("attention_backward_all", attention_backward(
                         seqs, blocks, d_res1, qkv, prob, qkv_w, out_w)))
    (d_sub, small3), (head, head_more) = split(outs, 2, blocks)
    head, head_more = Share(*head), Share(*head_more)
    flow.later = [head, head_more]

    small = Total(jnp.concatenate([small1, small2, small3, small4], 0))
    flow.send(ups, head, head_more, small)
    going = [s for s in (char, char_more, merge, down) if not s.finished()]
    flow.prepare(char, char_more, merge, down)
    flow.land([head, head_more, small], (), going)
    flow.send(*going)
    flow.prepare(head, head_more, small)
    joined_all, d_cols = flow.land((), (joined_all, d_cols), [head, head_more, small])
    conv = conv_grad(length, joined_all, d_cols)
    others = list(flow.away)
    conv, streams = flow.turn(others, (conv, (d_sub, d_char, out_sub, out_char)), [head, head_more, small])
    d_sub, d_char, out_sub, out_char = streams
    ends_out = jnp.where(section == 0, jnp.stack([d_sub, d_char], 1), jnp.stack([out_sub, out_char], 1))
    ends_out = ends_out.reshape(1, seqs, length, 2, width)
    ends_out = flow.turn([s for s in flow.away if s is not head_more], ends_out)
    flow.drain()
    small, rest = small.total, width - split_at
    heads, outs = combine(flow.bits, [
        ([([((0, tall, 0, split_at), (0, 0))], head.window(0, split_at)),
          ([((0, tall, 0, rest), (0, split_at))], head_more.window(0, rest))], (tall, width), FULL),
        ([([((i * chunk, chunk, 0, part), (0, i * part)) for i in range(3)], head_more.window(rest, split_at))],
         (chunk, width), FULL)])

    b = lax.axis_index("batch")

    def pieces(*which):
        part = width // batch
        mine = lax.dynamic_slice_in_dim(small, b * part, part, 1)
        return jnp.concatenate([mine[i:i + 1] for i in which], 0)

    def piece(start, count):
        part = count * width // batch
        line = small[start:start + count].reshape(1, count * width)
        return lax.dynamic_slice_in_dim(line, b * part, part, 1)

    return (
        ends_out,
        placed(heads),
        pieces(24, 25)[None],
        placed(outs),
        pieces(20),
        pieces(21, 9, 4, 5)[None],
        pieces(22, 10, 6, 7)[None],
        placed(ups.total),
        piece(16, 4),
        placed(down.total),
        pieces(8),
        placed(jnp.concatenate([char_more.total[i * chunk:(i + 1) * chunk, spot - halfway:] for i in range(2)], 1)),
        placed(jnp.concatenate([char.total, char_more.total[:, :width - halfway]], 1)),
        piece(32, 3),
        placed(char_more.total[:, width - halfway:spot - halfway]),
        piece(35, 3),
        merge.total.reshape(chunk, 2, width).transpose(1, 2, 0)[None],
        pieces(2, 3)[None],
        conv.transpose(0, 2, 1)[None],
        piece(0, 2),
    )


def solution(mesh):
    by = P("batch")
    part = P("section")

    def columns(rank):
        return P(*(["section"] + [None] * (rank - 2) + ["batch"]))

    return jax.shard_map(
        body,
        mesh=mesh,
        in_specs=(by,) * 5 + (part,) * 19,
        out_specs=(P("section", "batch"),) + tuple(
            columns(rank) for rank in (3, 3, 3, 2, 3, 3, 3, 2, 3, 2, 3, 3, 2, 3, 2, 4, 3, 4, 2)),
        check_vma=False,
    )
```

```python
import functools
import math

import jax
import jax.numpy as jnp
from jax import lax
from jax.experimental import pallas as pl
from jax.experimental.pallas import tpu as pltpu
from jax.sharding import PartitionSpec as P

HEAD = 64
BLOCK_CH = 8
EPSILON = 1e-05
LOW = jnp.bfloat16
FULL = jnp.float32
VMEM_LIMIT = 63 * 1024 * 1024


def dot(left, right):
    return lax.dot_general(left, right, (((1,), (0,)), ((), ())), preferred_element_type=FULL)


def dot_nt(left, right):
    return lax.dot_general(left, right, (((1,), (1,)), ((), ())), preferred_element_type=FULL)


def dot_tn(left, right):
    return lax.dot_general(left, right, (((0,), (0,)), ((), ())), preferred_element_type=FULL)


def norm_parts(values):
    row_mean = jnp.mean(values, axis=-1, keepdims=True)
    centered = values - row_mean
    row_var = jnp.mean(centered * centered, axis=-1, keepdims=True)
    inverse = lax.rsqrt(row_var + EPSILON)
    return centered * inverse, inverse


def norm(values, gain, shift):
    return norm_parts(values)[0] * gain + shift


def norm_back(values, gain, grad):
    unit, inverse = norm_parts(values)
    scaled = grad * gain
    first = jnp.mean(scaled, axis=-1, keepdims=True)
    second = jnp.mean(scaled * unit, axis=-1, keepdims=True)
    return inverse * (scaled - first - unit * second), unit


GELU_A = 0.7978845608028654
GELU_B = 0.044715


def gelu(x):
    return 0.5 * x * (1.0 + jnp.tanh(GELU_A * (x + GELU_B * x * x * x)))


def gelu_both(x):
    square = x * x
    bent = jnp.tanh(GELU_A * (x + GELU_B * square * x))
    gate = 0.5 * (1.0 + bent)
    return x * gate, gate + 0.5 * x * (1.0 - bent * bent) * (GELU_A * (1.0 + 3.0 * GELU_B * square))


def sigmoid(x):
    return 0.5 * jnp.tanh(0.5 * x) + 0.5


def column_sum(values):
    return jnp.sum(values, axis=0, keepdims=True)


class Stream:
    def __init__(self, pairs, sems, first=None):
        self.copies = [
            pltpu.make_async_copy(src, dst, sems.at[i]) for i, (src, dst) in enumerate(pairs)
        ]
        self.started, self.waited = 0, set()
        self.start(len(pairs) if first is None else first)

    def start(self, count=None):
        upto = len(self.copies) if count is None else self.started + count
        for copy in self.copies[self.started:upto]:
            copy.start()
        self.started = upto

    def need(self, *which):
        for i in which:
            if i not in self.waited:
                self.waited.add(i)
                self.copies[i].wait()


class Loaded:
    def need(self, *which):
        pass


def chunks(src, dst, axis, size):
    total = src.shape[axis]
    parts = []
    for start in range(0, total, size):
        index = [slice(None)] * len(src.shape)
        index[axis] = pl.ds(start, min(size, total - start))
        parts.append((src.at[tuple(index)], dst.at[tuple(index)]))
    return parts


def fill(out, near, terms):
    lead, chunk, columns = out.shape
    part = [term[9] for term in terms if term[8] > 0]
    if part:
        out[:, :, part[0]:] = jnp.zeros((lead, chunk, columns - part[0]), LOW)
    for d_y, base, height, start, stop, x, first, last, row, column in terms:
        d = jnp.concatenate([
            d_y[pl.ds(pl.multiple_of(base + (2 * i + near) * height, 16), height), :]
            for i in range(start, stop)], axis=0)
        step = min(last - first, 768)
        for at in range(first, last, step):
            value = dot(d, x[:, at:at + step]).astype(LOW)
            lanes = slice(column + at - first, column + at - first + step)
            out[start:stop, row:row + height, lanes] = value.reshape(stop - start, height, step)


def fill_plain(shape, near, terms):
    out = jnp.zeros(shape, LOW)
    for d_y, base, height, start, stop, x, first, last, row, column in terms:
        count = stop - start
        d = d_y[base + 2 * start * height:base + 2 * stop * height].reshape(count, 2, height, -1)
        d = lax.dynamic_slice_in_dim(d, near, 1, 1).reshape(count * height, -1)
        value = dot(d, x[:, first:last]).astype(LOW).reshape(count, height, last - first)
        out = lax.dynamic_update_slice(out, value, (start, row, column))
    return out


def named(plan, d_ys, xs):
    return [(d_ys[d],) + rest[:4] + (xs[rest[4]],) + rest[5:] for d, *rest in map(tuple, plan)
            for rest in [tuple(rest)]]


class Blocks:
    def __init__(self, bits, count, plans, d_shapes, xs):
        self.bits, self.count, self.plans, self.d_shapes, self.xs = bits, count, plans, d_shapes, xs
        self.inside = all(plan[0] % 16 == 0 for plan in plans)
        self.last = bits.shape[0] - 1

    def shapes(self):
        return [sds((self.count, plan[0], plan[1]), LOW) for plan in self.plans]

    def outs(self):
        return self.shapes() * 2 if self.inside else [sds(shape, LOW) for shape in self.d_shapes]

    def scratch(self):
        return [pltpu.VMEM(shape, LOW) for shape in self.d_shapes] if self.inside else []

    def inputs(self):
        return [self.bits] + (self.xs if self.inside else [])

    def split(self, refs):
        if not self.inside:
            return refs[:len(self.d_shapes)], lambda bits_ref, xs: None
        results, d_ys = refs[:2 * len(self.plans)], refs[2 * len(self.plans):]

        def make(bits_ref, xs):
            near = bits_ref[0]
            for own in range(2):
                for i, plan in enumerate(self.plans):
                    result = results[own * len(self.plans) + i]
                    fill(result, near if own else 1 - near, named(plan[2], d_ys, xs))
                    done(result)

        return d_ys, make

    def finish(self, results):
        if self.inside:
            return results[:len(self.plans)], results[len(self.plans):]
        near = self.bits[0]
        return tuple([fill_plain(shape.shape, which, named(plan[2], results, self.xs))
                      for shape, plan in zip(self.shapes(), self.plans)] for which in (1 - near, near))


def any_spec():
    return pl.BlockSpec(memory_space=pl.ANY)


def vmem_spec():
    return pl.BlockSpec(memory_space=pltpu.VMEM)


def sds(shape, dtype):
    return jax.ShapeDtypeStruct(shape, dtype)


def rest_of(blocks, count):
    return [] if blocks is None else list(range(count + 1, count + len(blocks.inputs())))


class Late:
    def __init__(self, ref, copy):
        self.ref, self.copy, self.shape = ref, copy, ref.shape

    def __getitem__(self, index):
        if self.copy is not None:
            self.copy.wait()
            self.copy = None
        return self.ref[index]


class Early:
    def __init__(self, ref, copy):
        self.ref, self.copy, self.shape, self.started = ref, copy, ref.shape, False

    def __getitem__(self, index):
        return self.ref[index]

    def __setitem__(self, index, value):
        self.ref[index] = value

    def done(self):
        if not self.started:
            self.copy.start()
            self.started = True


def done(*refs):
    for ref in refs:
        if isinstance(ref, Early):
            ref.done()


class Job:
    def __init__(self, kernel, outs, ins, streamed, scratch, flops, copies, blocks=None, late=(), after=()):
        self.scalar, self.after = -1, after
        if blocks is not None:
            ins, outs = list(ins) + blocks.inputs(), list(outs) + blocks.outs()
            scratch = blocks.scratch() + list(scratch)
            self.scalar = len(ins) - len(blocks.inputs())
        self.kernel, self.ins, self.outs, self.flops, self.late = kernel, ins, outs, flops, late
        self.streamed = set(streamed) | set(late)
        self.early = [i for i, o in enumerate(outs) if o.size * o.dtype.itemsize > 200000]
        self.scratch = list(scratch) + [pltpu.SemaphoreType.DMA((copies,))]
        self.buffers = [pltpu.VMEM(ins[i].shape, ins[i].dtype) for i in late]
        self.buffers = self.buffers + [pltpu.VMEM(outs[i].shape, outs[i].dtype) for i in self.early]
        self.buffers = self.buffers + [pltpu.SemaphoreType.DMA((max(len(late), 1),)),
                                       pltpu.SemaphoreType.DMA((max(len(self.early), 1),))]

    def in_specs(self):
        return [any_spec() if i in self.streamed else pl.BlockSpec(memory_space=pltpu.SMEM) if i == self.scalar
                else vmem_spec() for i in range(len(self.ins))]

    def out_specs(self):
        return [any_spec() if i in self.early else vmem_spec() for i in range(len(self.outs))]

    def begin(self, ins, outs, scratch, buffers):
        ins, outs = list(ins), list(outs)
        held, (in_sems, out_sems) = buffers[:-2], buffers[-2:]
        for n, i in enumerate(self.late):
            copy = pltpu.make_async_copy(ins[i], held[n], in_sems.at[n])
            copy.start()
            ins[i] = Late(held[n], copy)
        for n, i in enumerate(self.early):
            buffer = held[len(self.late) + n]
            outs[i] = Early(buffer, pltpu.make_async_copy(buffer, outs[i], out_sems.at[n]))
        self.lates = [ins[i] for i in self.late]
        self.earlies = [outs[i] for i in self.early]
        self.results = outs
        return self.kernel(*[job.results[0] for job in self.after], *ins, *outs, *scratch)

    def end(self):
        for late in self.lates:
            if late.copy is not None:
                late.copy.wait()
        for early in self.earlies:
            early.done()
        for early in self.earlies:
            early.copy.wait()


def together_kernel(jobs, pace, *refs):
    groups, at = [], 0
    for kind in ("ins", "outs", "scratch", "buffers"):
        group = []
        for job in jobs:
            count = len(getattr(job, kind))
            group.append(refs[at:at + count])
            at = at + count
        groups.append(group)
    running, last = [], []
    for n, job in enumerate(jobs):
        steps = job.begin(*[group[n] for group in groups])
        next(steps)
        (last if job.after else running).append((steps, pace[n]))
    while running or last:
        if not running:
            running, last = last[:1], last[1:]
        left = []
        for steps, count in running:
            if all(next(steps, True) is None for _ in range(count)):
                left.append((steps, count))
        running = left
    for job in jobs:
        job.end()


def run(name, *jobs, pace=(1, 1, 1)):
    ins = [a for job in jobs for a in job.ins]
    outs = [o for job in jobs for o in job.outs]
    moved = sum(a.size * a.dtype.itemsize for a in ins) + sum(o.size * o.dtype.itemsize for o in outs)
    results = pl.pallas_call(
        functools.partial(together_kernel, jobs, pace),
        out_shape=outs,
        in_specs=[spec for job in jobs for spec in job.in_specs()],
        out_specs=[spec for job in jobs for spec in job.out_specs()],
        scratch_shapes=[s for job in jobs for s in job.scratch] + [s for job in jobs for s in job.buffers],
        compiler_params=pltpu.CompilerParams(vmem_limit_bytes=VMEM_LIMIT),
        cost_estimate=pl.CostEstimate(flops=sum(job.flops for job in jobs), bytes_accessed=moved,
                                      transcendentals=0),
        name=name,
    )(*ins)
    split = []
    for job in jobs:
        split.append(results[:len(job.outs)])
        results = results[len(job.outs):]
    return split[0] if len(jobs) == 1 else split


def attention_forward_kernel(seqs, save, s_ref, qkv_hbm, qvb_ref, qkv_ref, prob_ref, att_ref, wqkv, sems):
    width = s_ref.shape[1]
    length = s_ref.shape[0] // seqs
    w = Stream(chunks(qkv_hbm, wqkv, 1, width), sems)
    yield
    for part in range(3):
        w.need(part)
        if part > 0:
            yield
        cols = slice(part * width, (part + 1) * width)
        y = dot(s_ref[...], wqkv[:, cols])
        if part == 0:
            y = (y + qvb_ref[0:1, :]) * HEAD ** -0.5
        elif part == 2:
            y = y + qvb_ref[1:2, :]
        qkv_ref[:, cols] = y.astype(LOW)
    done(qkv_ref)
    lanes = lax.broadcasted_iota(jnp.int32, (length, 2 * HEAD), 1)
    even = lanes < HEAD
    for seq in range(seqs):
        rows = slice(seq * length, (seq + 1) * length)
        for pair in range(width // (2 * HEAD)):
            lo = pair * 2 * HEAD
            q = qkv_ref[rows, lo:lo + 2 * HEAD]
            k = qkv_ref[rows, width + lo:width + lo + 2 * HEAD]
            v = qkv_ref[rows, 2 * width + lo:2 * width + lo + 2 * HEAD]
            zero = jnp.zeros_like(q)
            probs = []
            for half in range(2):
                mask = even if half == 0 else ~even
                scores = dot_nt(jnp.where(mask, q, zero), k)
                peak = jnp.max(scores, axis=-1, keepdims=True)
                e = jnp.exp(scores - peak)
                prob = (e / jnp.sum(e, axis=-1, keepdims=True)).astype(LOW)
                probs.append(prob)
                if save:
                    at = (seq * (width // HEAD) + 2 * pair + half) * length
                    prob_ref[at:at + length, :] = prob
            both = jnp.concatenate(probs, axis=1)
            vv = jnp.concatenate([jnp.where(even, v, zero), jnp.where(even, zero, v)], axis=0)
            att_ref[rows, lo:lo + 2 * HEAD] = dot(both, vv).astype(LOW)
            yield
    done(prob_ref, att_ref)


def ffn_forward_kernel(save, s_ref, att_ref, out_hbm, outb_ref, gain_ref, shift_ref, up_hbm, upb_ref,
                       down_hbm, downb_ref, after_ref, *rest):
    if save:
        res1_ref, first_ref, pre_ref, act_ref, res2_ref, wout, wup, wdown, sems = rest
    else:
        wout, wup, wdown, sems = rest
    width, wide = s_ref.shape[1], wup.shape[1]
    pairs = zip(chunks(up_hbm, wup, 1, width), chunks(down_hbm, wdown, 0, width))
    w = Stream(chunks(out_hbm, wout, 1, width) + [one for pair in pairs for one in pair], sems)
    yield
    w.need(0)
    res1 = s_ref[...].astype(FULL) + dot(att_ref[...], wout[...]) + outb_ref[...]
    after = norm(res1, gain_ref[0:1, :], shift_ref[0:1, :])
    low = after.astype(LOW)
    if save:
        res1_ref[...] = res1
        first_ref[...] = low
        done(res1_ref, first_ref)
    total = after + downb_ref[...]
    for part in range(wide // width):
        yield
        w.need(1 + 2 * part, 2 + 2 * part)
        cols = slice(part * width, (part + 1) * width)
        pre = dot(low, wup[:, cols]) + upb_ref[:, cols]
        if save:
            act, slope = gelu_both(pre)
            act = act.astype(LOW)
            pre_ref[:, cols] = slope.astype(LOW)
            act_ref[:, cols] = act
        else:
            act = gelu(pre).astype(LOW)
        total = total + dot(act, wdown[cols, :])
    if save:
        res2_ref[...] = total
        done(pre_ref, act_ref, res2_ref)
    after_ref[...] = norm(total, gain_ref[1:2, :], shift_ref[1:2, :])


def sub_forward_kernel(seqs, s_ref, qkv_hbm, qvb_ref, out_hbm, outb_ref, gain_ref, shift_ref, up_hbm, upb_ref,
                       down_hbm, downb_ref, after_ref, wqkv, qkv_ref, att_ref, att_sems, wout, wup, wdown, sems):
    attention = attention_forward_kernel(seqs, False, s_ref, qkv_hbm, qvb_ref, qkv_ref, None, att_ref, wqkv,
                                         att_sems)
    ffn = ffn_forward_kernel(False, s_ref, att_ref, out_hbm, outb_ref, gain_ref, shift_ref, up_hbm, upb_ref,
                             down_hbm, downb_ref, after_ref, wout, wup, wdown, sems)
    next(attention)
    yield
    next(ffn)
    yield from attention
    yield from ffn


def attention_forward(seqs, s, qkv_w, qvb):
    rows, width = s.shape
    length = rows // seqs
    outs = [sds((rows, 3 * width), LOW), sds((seqs * (width // HEAD) * length, length), LOW),
            sds((rows, width), LOW)]
    return Job(functools.partial(attention_forward_kernel, seqs, True), outs, [s, qkv_w, qvb], {1},
               [pltpu.VMEM(qkv_w.shape, LOW)], 2 * rows * qkv_w.size, 3)


def ffn_forward(s, att, out_w, out_b, gain, shift, up_w, up_b, down_w, down_b):
    rows, width = s.shape
    wide = up_w.shape[1]
    outs = [sds((rows, width), FULL), sds((rows, width), FULL), sds((rows, width), LOW),
            sds((rows, wide), LOW), sds((rows, wide), LOW), sds((rows, width), FULL)]
    weights = (out_w, up_w, down_w)
    return Job(functools.partial(ffn_forward_kernel, True), outs,
               [s, att, out_w, out_b, gain, shift, up_w, up_b, down_w, down_b], {2, 6, 8},
               [pltpu.VMEM(one.shape, LOW) for one in weights], 2 * rows * sum(one.size for one in weights),
               1 + 2 * (wide // width))


def sub_forward(seqs, s, qkv_w, qvb, out_w, out_b, gain, shift, up_w, up_b, down_w, down_b):
    rows, width = s.shape
    weights = (qkv_w, out_w, up_w, down_w)
    scratch = [pltpu.VMEM(qkv_w.shape, LOW), pltpu.VMEM((rows, 3 * width), LOW), pltpu.VMEM((rows, width), LOW),
               pltpu.SemaphoreType.DMA((3,))] + [pltpu.VMEM(one.shape, LOW) for one in weights[1:]]
    return Job(functools.partial(sub_forward_kernel, seqs), [sds((rows, width), FULL)],
               [s, qkv_w, qvb, out_w, out_b, gain, shift, up_w, up_b, down_w, down_b], {1, 3, 7, 9}, scratch,
               2 * rows * sum(one.size for one in weights), 1 + 2 * (up_w.shape[1] // width))


def gru_forward_kernel(save, c_ref, tokc_ref, tokr_ref, idc_ref, count_ref, table_hbm, win_hbm,
                       bin_ref, wrec_hbm, brec_ref, *rest):
    if save:
        (pooled_ref, charin_ref, r_ref, z_ref, to_n_ref, to_z_ref, to_r_ref, prev_ref,
         table, win, wrec, gate, low_state, sems) = rest
    else:
        pooled_ref, table, win, wrec, gate, low_state, charin_ref, sems = rest
    rows, width = c_ref.shape
    count = tokc_ref.shape[0]
    hidden = wrec.shape[0]
    w = Stream([(table_hbm, table)] + chunks(win_hbm, win, 1, width)
               + chunks(wrec_hbm, wrec, 1, 3 * hidden), sems)
    yield
    token = (tokc_ref[...] == lax.broadcasted_iota(jnp.int32, (count, rows), 1))
    ident = (idc_ref[...] == lax.broadcasted_iota(jnp.int32, (count, table.shape[0]), 1))
    w.need(0)
    x = dot(token.astype(FULL).astype(LOW), c_ref[...]) + dot(ident.astype(FULL).astype(LOW), table[...])
    charin_ref[...] = x.astype(LOW)
    done(charin_ref)
    for part in range(3):
        yield
        w.need(1 + part)
        cols = slice(part * width, (part + 1) * width)
        gate[:, cols] = dot(charin_ref[...], win[:, cols]) + bin_ref[:, cols]
    lanes = count // BLOCK_CH
    state = [None, None]
    w.need(4, 5)
    for turn in range(BLOCK_CH):
        yield
        for way in range(2):
            at = turn if way == 0 else BLOCK_CH - 1 - turn
            here = slice(at * lanes, (at + 1) * lanes)
            base = way * 3 * hidden
            out = slice(way * hidden, (way + 1) * hidden)
            bias = brec_ref[:, base:base + 3 * hidden]
            g = gate[here, base:base + 3 * hidden]
            if turn == 0:
                rec_n = jnp.broadcast_to(bias[:, 2 * hidden:], (lanes, hidden))
                rz = g[:, :2 * hidden] + bias[:, :2 * hidden]
                if save:
                    prev_ref[here, out] = jnp.zeros((lanes, hidden), LOW)
            else:
                low = state[way].astype(LOW)
                if save:
                    prev_ref[here, out] = low
                rec = dot(low, wrec[:, base:base + 3 * hidden]) + bias
                rec_n = rec[:, 2 * hidden:]
                rz = g[:, :2 * hidden] + rec[:, :2 * hidden]
            rz = sigmoid(rz)
            r, z = rz[:, :hidden], rz[:, hidden:]
            n = jnp.tanh(g[:, 2 * hidden:] + r * rec_n)
            new = (1.0 - z) * n
            before = state[way]
            if turn > 0:
                new = new + z * before
            state[way] = new
            low_state[here, out] = new.astype(LOW)
            if save:
                r_ref[here, out] = r.astype(LOW)
                z_ref[here, out] = z.astype(LOW)
                to_n_ref[here, out] = ((1.0 - z) * (1.0 - n * n)).astype(LOW)
                change = -n if turn == 0 else before - n
                to_z_ref[here, out] = (change * (z * (1.0 - z))).astype(LOW)
                to_r_ref[here, out] = (rec_n * (r * (1.0 - r))).astype(LOW)
    if save:
        done(r_ref, z_ref, to_n_ref, to_z_ref, to_r_ref, prev_ref)
    yield
    spread = (tokr_ref[...] == lax.broadcasted_iota(jnp.int32, (rows, count), 0))
    pooled = dot(spread.astype(FULL).astype(LOW), low_state[...])
    pooled_ref[...] = pooled / count_ref[...]


def gru_forward(save, c, tokc, tokr, idc, counts, table, win, bin_, wrec, brec):
    rows, width = c.shape
    count = tokc.shape[0]
    outs = [sds((rows, width), FULL)]
    scratch = [pltpu.VMEM(a.shape, LOW) for a in (table, win, wrec)]
    scratch = scratch + [pltpu.VMEM((count, win.shape[1]), FULL), pltpu.VMEM((count, width), LOW)]
    if save:
        outs = outs + [sds((count, width), LOW)] * 7
    else:
        scratch = scratch + [pltpu.VMEM((count, width), LOW)]
    return Job(functools.partial(gru_forward_kernel, save), outs,
                [c, tokc, tokr, idc, counts, table, win, bin_, wrec, brec],
                {5, 6, 8}, scratch, 2 * count * (win.size + wrec.size) + 2 * count * width * (2 * rows + table.shape[0]), 6)


def shift_rows(values, by, length):
    rows, width = values.shape
    zero = jnp.zeros((1, width), values.dtype)
    pos = lax.broadcasted_iota(jnp.int32, (rows, 1), 0) % length
    if by == 1:
        moved = jnp.concatenate([zero, values[:-1]], axis=0)
        return jnp.where(pos == 0, 0.0, moved)
    moved = jnp.concatenate([values[1:], zero], axis=0)
    return jnp.where(pos == length - 1, 0.0, moved)


def join_kernel(save, pooled_ref, after_ref, mw_hbm, mb_ref, joined_ref, *rest):
    if save:
        pre_ref, second_ref, poollow_ref, mw, sems = rest
    else:
        mw, sems = rest
    width = after_ref.shape[1]
    w = Stream(chunks(mw_hbm, mw, 0, 1), sems)
    yield
    w.need(0, 1)
    for side in range(2):
        cols = slice(side * width, (side + 1) * width)
        low = (after_ref if side == 0 else pooled_ref)[...].astype(LOW)
        pre = dot(low, mw[side]) + mb_ref[side:side + 1, :]
        if save:
            (second_ref if side == 0 else poollow_ref)[...] = low
            value, slope = gelu_both(pre)
            pre_ref[:, cols] = slope.astype(LOW)
        else:
            value = gelu(pre)
        joined_ref[:, cols] = value.astype(LOW)


def join(save, pooled, after, mw, mb):
    rows, width = pooled.outs[0].shape
    outs = [sds((rows, 2 * width), LOW)]
    if save:
        outs = outs * 2 + [sds((rows, width), LOW)] * 2
    return Job(functools.partial(join_kernel, save), outs, [mw, mb], {0}, [pltpu.VMEM(mw.shape, LOW)],
               2 * rows * mw.size, 2, after=(pooled, after))


def merge_forward_kernel(length, save, after_ref, pooled_ref, joined_ref, cw_hbm, cb_ref, gain_ref, shift_ref,
                         sub_ref, char_ref, *rest):
    if save:
        res3_ref, res4_ref, cw, sems = rest
    else:
        cw, sems = rest
    width = after_ref.shape[1]
    w = Stream([pair for k in (1, 0, 2) for pair in chunks(cw_hbm.at[k], cw.at[k], 0, width)], sems)
    yield
    joined = joined_ref[...]
    total = cb_ref[...]
    for place, k in enumerate((1, 0, 2)):
        moved = joined if k == 1 else shift_rows(joined.astype(FULL), 1 - k, length).astype(LOW)
        for half in range(2):
            w.need(2 * place + half)
            rows = slice(half * width, (half + 1) * width)
            total = total + dot(moved[:, rows], cw[k, rows, :])
    res3 = after_ref[...] + total[:, :width]
    res4 = pooled_ref[...] + total[:, width:]
    if save:
        res3_ref[...] = res3
        res4_ref[...] = res4
        done(res3_ref, res4_ref)
    sub_ref[...] = norm(res3, gain_ref[2:3, :], shift_ref[2:3, :]).astype(LOW)
    char_ref[...] = norm(res4, gain_ref[3:4, :], shift_ref[3:4, :]).astype(LOW)


def merge_forward(length, after, pooled, joined, cw, cb, gain, shift):
    rows, width = after.outs[0].shape
    return Job(functools.partial(merge_forward_kernel, length, False), [sds((rows, width), LOW)] * 2,
               [cw, cb, gain, shift], {0}, [pltpu.VMEM(cw.shape, LOW)],
               2 * rows * cw.size, 6, after=(after, pooled, joined))


def merge_backward_kernel(length, full, gsub_ref, gchar_ref, res3_ref, res4_ref, pre_ref, mw_hbm, cw_hbm,
                          gain_ref, res2_ref, *rest):
    if full:
        psub_ref, pchar_ref, *rest = rest
        xs, rest = rest[:len(full.inputs())], rest[len(full.inputs()):]
        dres2_ref, dpooled_ref, dconv_ref, small_ref, *rest, mw, cw, sems = rest
        (dpre_ref, ddown_ref), make = full.split(rest)
    else:
        dres2_ref, dpooled_ref, mw, cw, sems = rest
    width = res3_ref.shape[1]
    w = Loaded() if sems is None else Stream(chunks(cw_hbm, cw, 0, 1) + chunks(mw_hbm, mw, 0, 1), sems)
    yield
    grads = [gsub_ref[...], gchar_ref[...]]
    if full:
        last = xs[0][full.last] > 0
        grads = [jnp.where(last, grad, ref[...].astype(FULL))
                 for grad, ref in zip(grads, (psub_ref, pchar_ref))]
    d_res, sums = [], []
    for side in range(2):
        d, unit = norm_back((res3_ref, res4_ref)[side][...], gain_ref[2 + side:3 + side, :], grads[side])
        d_res.append(d)
        if full:
            small_ref[4 + side:5 + side, :] = column_sum(grads[side] * unit)
            small_ref[6 + side:7 + side, :] = column_sum(grads[side])
            small_ref[side:side + 1, :] = column_sum(d)
    d_conv = jnp.concatenate(d_res, axis=1)
    if full:
        dconv_ref[...] = d_conv.astype(LOW).T
        done(dconv_ref)
    total, lows = None, []
    for k in range(3):
        moved = d_conv if k == 1 else shift_rows(d_conv, k - 1, length)
        w.need(k)
        term = dot_nt(moved.astype(LOW), cw[k])
        total = term if total is None else total + term
    for half in range(2):
        cols = slice(half * width, (half + 1) * width)
        d_pre = total[:, cols] * pre_ref[:, cols].astype(FULL)
        lows.append(d_pre.astype(LOW))
        if full:
            dpre_ref[cols, :] = lows[-1].T
            sums.append(column_sum(d_pre))
    d_low = jnp.concatenate(lows, axis=1)
    if full:
        for side in range(2):
            small_ref[2 + side:3 + side, :] = sums[side]
    w.need(3, 4)
    d_second = d_res[0] + dot_nt(d_low[:, :width], mw[0])
    d_res2, unit = norm_back(res2_ref[...], gain_ref[1:2, :], d_second)
    dres2_ref[...] = d_res2
    done(dres2_ref)
    dpooled_ref[...] = d_res[1] + dot_nt(d_low[:, width:], mw[1])
    done(dpooled_ref)
    if full:
        ddown_ref[...] = d_res2.astype(LOW).T
        small_ref[8:9, :] = column_sum(d_res2)
        small_ref[9:10, :] = column_sum(d_second * unit)
        small_ref[10:11, :] = column_sum(d_second)
        small_ref[11:16, :] = jnp.zeros((5, width), FULL)
        make(xs[0], xs[1:])


def merge_backward(length, full, gsub, gchar, res3, res4, pre, mw, cw, gain, res2, passed):
    rows, width = res3.shape
    outs = [sds((rows, width), FULL)] * 2
    if full:
        outs = outs + [sds((2 * width, rows), LOW), sds((16, width), FULL)]
    scratch = [pltpu.VMEM(mw.shape, LOW), pltpu.VMEM(cw.shape, LOW)]
    return Job(functools.partial(merge_backward_kernel, length, full), outs,
                [gsub, gchar, res3, res4, pre, mw, cw, gain, res2, *passed], {5, 6}, scratch, 2 * rows * (mw.size + cw.size), 5, full,
               [0, 1, 9, 10, 2, 3, 4, 8] + rest_of(full, 11))


def merge_both_kernel(length, after_ref, pooled_ref, joined_ref, mw_hbm, cw_hbm, cb_ref, gain_ref, shift_ref,
                      gsub_ref, gchar_ref, pre_ref, res2_ref, sub_ref, char_ref, res3_ref, res4_ref, dres2_ref,
                      dpooled_ref, mw, mw_sems, cw, sems):
    forward = merge_forward_kernel(length, True, after_ref, pooled_ref, joined_ref, cw_hbm, cb_ref, gain_ref,
                                   shift_ref, sub_ref, char_ref, res3_ref, res4_ref, cw, sems)
    next(forward)
    w = Stream(chunks(mw_hbm, mw, 0, 1), mw_sems)
    yield
    yield from forward
    w.need(0, 1)
    yield from merge_backward_kernel(length, None, gsub_ref, gchar_ref, res3_ref, res4_ref, pre_ref, mw_hbm,
                                     cw_hbm, gain_ref, res2_ref, dres2_ref, dpooled_ref, mw, cw, None)


def merge_both(length, after, pooled, joined, mw, cw, cb, gain, shift, gsub, gchar, pre, res2):
    rows, width = after.shape
    outs = [sds((rows, width), LOW)] * 2 + [sds((rows, width), FULL)] * 4
    scratch = [pltpu.VMEM(mw.shape, LOW), pltpu.SemaphoreType.DMA((2,)), pltpu.VMEM(cw.shape, LOW)]
    return Job(functools.partial(merge_both_kernel, length), outs,
               [after, pooled, joined, mw, cw, cb, gain, shift, gsub, gchar, pre, res2], {3, 4}, scratch,
               4 * rows * (mw.size + cw.size), 6, None, [2, 0, 1, 8, 9, 10, 11])


def ffn_backward_kernel(full, dres2_ref, pre_ref, res1_ref, up_hbm, down_hbm, gain_ref, *rest):
    if full:
        xs, rest = rest[:len(full.inputs())], rest[len(full.inputs()):]
        dres1_ref, small_ref, *rest, wup, wdown, sems = rest
        (dup_ref,), make = full.split(rest)
    else:
        dres1_ref, wup, wdown, sems = rest
    rows, width = dres1_ref.shape
    wide = wup.shape[1]
    parts = wide // width
    pairs = zip(chunks(down_hbm, wdown, 0, width), chunks(up_hbm, wup, 1, width))
    w = Stream([one for pair in pairs for one in pair], sems)
    yield
    d_res2 = dres2_ref[...]
    d_low = d_res2.astype(LOW)
    d_first = d_res2
    for part in range(parts):
        cols = slice(part * width, (part + 1) * width)
        w.need(2 * part, 2 * part + 1)
        d_up = dot_nt(d_low, wdown[cols, :]) * pre_ref[:, cols].astype(FULL)
        up_low = d_up.astype(LOW)
        if full:
            dup_ref[cols, :] = up_low.T
            small_ref[part:part + 1, :] = column_sum(d_up)
        d_first = d_first + dot_nt(up_low, wup[:, cols])
        yield
    d_res1, unit = norm_back(res1_ref[...], gain_ref[0:1, :], d_first)
    dres1_ref[...] = d_res1
    done(dres1_ref)
    if full:
        small_ref[parts:parts + 1, :] = column_sum(d_res1)
        small_ref[parts + 1:parts + 2, :] = column_sum(d_first * unit)
        small_ref[parts + 2:parts + 3, :] = column_sum(d_first)
        small_ref[parts + 3:, :] = jnp.zeros((small_ref.shape[0] - parts - 3, width), FULL)
        make(xs[0], xs[1:])


def ffn_backward(full, dres2, pre, res1, up_w, down_w, gain):
    rows, width = res1.shape
    wide = up_w.shape[1]
    outs = [sds((rows, width), FULL)]
    scratch = [pltpu.VMEM(a.shape, LOW) for a in (up_w, down_w)]
    if full:
        outs = outs + [sds((8, width), FULL)]
    return Job(functools.partial(ffn_backward_kernel, full), outs,
                [dres2, pre, res1, up_w, down_w, gain], {3, 4}, scratch, 2 * rows * (up_w.size + down_w.size), 2 * (wide // width), full,
                [0, 1, 2] + rest_of(full, 6))


def attention_backward_kernel(seqs, full, dres1_ref, qkv_ref, prob_ref, qkv_hbm, out_hbm, *rest):
    if full:
        xs, rest = rest[:len(full.inputs())], rest[len(full.inputs()):]
        dsub_ref, small_ref, *rest, wqkv, wout, datt, dproj_ref, sems = rest
        (dprojt_ref, dbranch_ref), make = full.split(rest)
    else:
        dsub_ref, wqkv, wout, datt, dproj_ref, sems = rest
    rows, width = dsub_ref.shape
    length = rows // seqs
    w = Stream(chunks(out_hbm, wout, 1, width) + chunks(qkv_hbm, wqkv, 1, width), sems)
    yield
    w.need(0, 1, 2, 3)
    branch_low = dres1_ref[...].astype(LOW)
    datt[...] = dot_nt(branch_low, wout[...]).astype(LOW)
    if full:
        dbranch_ref[...] = branch_low.T
    even = lax.broadcasted_iota(jnp.int32, (length, 2 * HEAD), 1) < HEAD
    scale = HEAD ** -0.5
    for pair in range(width // (2 * HEAD)):
        lo = pair * 2 * HEAD
        totals = [0.0, 0.0]
        for seq in range(seqs):
            at_rows = slice(seq * length, (seq + 1) * length)
            q = qkv_ref[at_rows, lo:lo + 2 * HEAD]
            k = qkv_ref[at_rows, width + lo:width + lo + 2 * HEAD]
            v = qkv_ref[at_rows, 2 * width + lo:2 * width + lo + 2 * HEAD]
            da = datt[at_rows, lo:lo + 2 * HEAD]
            zero = jnp.zeros_like(q)

            def halves(x):
                return jnp.where(even, x, zero), jnp.where(even, zero, x)

            da_h = halves(da)
            probs, d_scores = [], []
            for half in range(2):
                at = (seq * (width // HEAD) + 2 * pair + half) * length
                prob = prob_ref[at:at + length, :]
                d_prob = dot_nt(da_h[half], v)
                wide_prob = prob.astype(FULL)
                weighted = wide_prob * d_prob
                d_score = weighted - wide_prob * jnp.sum(weighted, axis=-1, keepdims=True)
                probs.append(prob)
                d_scores.append(d_score.astype(LOW))
            d_v = dot_tn(jnp.concatenate(probs, axis=0), jnp.concatenate(da_h, axis=0))
            d_q = dot(jnp.concatenate(d_scores, axis=1), jnp.concatenate(halves(k), axis=0)) * scale
            d_k = dot_tn(jnp.concatenate(d_scores, axis=0), jnp.concatenate(halves(q), axis=0))
            dproj_ref[at_rows, lo:lo + 2 * HEAD] = d_q.astype(LOW)
            dproj_ref[at_rows, width + lo:width + lo + 2 * HEAD] = d_k.astype(LOW)
            dproj_ref[at_rows, 2 * width + lo:2 * width + lo + 2 * HEAD] = d_v.astype(LOW)
            yield
            if full:
                totals[0] = totals[0] + column_sum(d_q)
                totals[1] = totals[1] + column_sum(d_v)
        if full:
            small_ref[0:1, lo:lo + 2 * HEAD] = totals[0]
            small_ref[1:2, lo:lo + 2 * HEAD] = totals[1]
    total = dres1_ref[...]
    for part in range(3):
        cols = slice(part * width, (part + 1) * width)
        if full:
            dprojt_ref[cols, :] = dproj_ref[:, cols].T
        yield
        total = total + dot_nt(dproj_ref[:, cols], wqkv[:, cols])
    dsub_ref[...] = total.astype(LOW)
    done(dsub_ref)
    if full:
        small_ref[2:8, :] = jnp.zeros((6, width), FULL)
        make(xs[0], xs[1:])


def attention_backward(seqs, full, dres1, qkv, prob, qkv_w, out_w):
    rows, width = dres1.shape
    outs = [sds((rows, width), LOW)]
    scratch = [pltpu.VMEM(a.shape, LOW) for a in (qkv_w, out_w)]
    scratch = scratch + [pltpu.VMEM((rows, width), LOW), pltpu.VMEM((rows, 3 * width), LOW)]
    if full:
        outs = outs + [sds((8, width), FULL)]
    return Job(functools.partial(attention_backward_kernel, seqs, full), outs,
                [dres1, qkv, prob, qkv_w, out_w], {3, 4}, scratch, 2 * rows * (qkv_w.size + out_w.size), 4, full, [0, 1, 2] + rest_of(full, 5))


def gru_backward_kernel(full, dpooled_ref, count_ref, tokc_ref, tokr_ref, r_ref, z_ref, to_n_ref, to_z_ref,
                        to_r_ref, win_hbm, wrec_hbm, *rest):
    if full:
        xs, rest = rest[:len(full.inputs())], rest[len(full.inputs()):]
        dchar_ref, small_ref, *rest, dstate, win, wrec, dgate_ref, drecn_ref, sems = rest
        (dgatet_ref, drect_ref, dchart_ref), make = full.split(rest)
    else:
        dchar_ref, dstate, win, wrec, dgate_ref, sems = rest
    rows, width = dpooled_ref.shape
    count = tokc_ref.shape[0]
    hidden = wrec.shape[0]
    lanes = count // BLOCK_CH
    w = Stream(chunks(wrec_hbm, wrec, 1, 3 * hidden) + chunks(win_hbm, win, 1, width), sems)
    yield
    share = (dpooled_ref[...] / count_ref[...]).astype(LOW)
    token = (tokc_ref[...] == lax.broadcasted_iota(jnp.int32, (count, rows), 1))
    dstate[...] = dot(token.astype(FULL).astype(LOW), share)
    carry = [None, None]
    sums = [[None] * 4, [None] * 4]
    w.need(0, 1)
    for turn in reversed(range(BLOCK_CH)):
        yield
        for way in range(2):
            at = turn if way == 0 else BLOCK_CH - 1 - turn
            here = slice(at * lanes, (at + 1) * lanes)
            base = way * 3 * hidden
            out = slice(way * hidden, (way + 1) * hidden)
            d_h = dstate[here, out]
            if carry[way] is not None:
                d_h = d_h + carry[way]
            d_n = d_h * to_n_ref[here, out].astype(FULL)
            d_z = d_h * to_z_ref[here, out].astype(FULL)
            d_r = d_n * to_r_ref[here, out].astype(FULL)
            d_rec_n = d_n * r_ref[here, out].astype(FULL)
            pieces = (d_r, d_z, d_n, d_rec_n)
            if full:
                for i, piece in enumerate(pieces):
                    one = column_sum(piece)
                    sums[way][i] = one if sums[way][i] is None else sums[way][i] + one
                drecn_ref[here, out] = d_rec_n.astype(LOW)
            low_r, low_z = d_r.astype(LOW), d_z.astype(LOW)
            dgate_ref[here, base:base + hidden] = low_r
            dgate_ref[here, base + hidden:base + 2 * hidden] = low_z
            dgate_ref[here, base + 2 * hidden:base + 3 * hidden] = d_n.astype(LOW)
            if turn > 0:
                d_rec = jnp.concatenate([low_r, low_z, d_rec_n.astype(LOW)], axis=1)
                carry[way] = d_h * z_ref[here, out].astype(FULL) + dot_nt(d_rec, wrec[:, base:base + 3 * hidden])
    if full:
        for way in range(2):
            for i in range(3):
                at = slice((3 * way + i) * hidden, (3 * way + i + 1) * hidden)
                turned = dgate_ref[:, at].T
                dgatet_ref[at, :] = turned
                drect_ref[at, :] = turned if i < 2 else drecn_ref[:, way * hidden:(way + 1) * hidden].T
        small_ref[6:8, :] = jnp.zeros((2, width), FULL)
        for kind in range(2):
            line = [sums[way][i if i < 2 or kind == 0 else 3] for way in range(2) for i in range(3)]
            for i in range(3):
                small_ref[3 * kind + i:3 * kind + i + 1, :] = jnp.concatenate(line[2 * i:2 * i + 2], axis=1)
    total = None
    for part in range(3):
        cols = slice(part * width, (part + 1) * width)
        yield
        w.need(2 + part)
        term = dot_nt(dgate_ref[:, cols], win[:, cols])
        total = term if total is None else total + term
    low = total.astype(LOW)
    if full:
        dchart_ref[...] = low.T
    spread = (tokr_ref[...] == lax.broadcasted_iota(jnp.int32, (rows, count), 0))
    dchar_ref[...] = dot(spread.astype(FULL).astype(LOW), low).astype(LOW)
    done(dchar_ref)
    if full:
        make(xs[0], xs[1:])


def gru_backward(full, dpooled, counts, tokc, tokr, r, z, to_n, to_z, to_r, win, wrec):
    rows, width = dpooled.shape
    count = tokc.shape[0]
    wide = win.shape[1]
    outs = [sds((rows, width), LOW)]
    scratch = [pltpu.VMEM((count, width), FULL), pltpu.VMEM(win.shape, LOW), pltpu.VMEM(wrec.shape, LOW),
               pltpu.VMEM((count, wide), LOW)]
    if full:
        outs = outs + [sds((8, width), FULL)]
        scratch = scratch + [pltpu.VMEM((count, width), LOW)]
    return Job(functools.partial(gru_backward_kernel, full), outs,
                [dpooled, counts, tokc, tokr, r, z, to_n, to_z, to_r, win, wrec], {9, 10}, scratch, 2 * count * (win.size + wrec.size) + 4 * count * rows * width, 5, full,
                [0, 2, 6, 7, 8, 4, 5] + rest_of(full, 11))


def whole_part(values, divisor):
    return jnp.floor((values + 0.5) * (1.0 / divisor))


def places_kernel(lens_ref, ids_ref, tokc_ref, tokr_ref, idc_ref, count_ref, ident_ref):
    seqs, length = lens_ref.shape
    chars = ids_ref.shape[1]
    blocks, total = chars // BLOCK_CH, seqs * chars

    def spots(index):
        turn = whole_part(index, seqs * blocks)
        rest = index - turn * (seqs * blocks)
        seq = whole_part(rest, blocks)
        return seq, (rest - seq * blocks) * BLOCK_CH + turn

    first = lax.broadcasted_iota(jnp.int32, (length, length), 0)
    second = lax.broadcasted_iota(jnp.int32, (length, length), 1)
    upto = (first <= second).astype(FULL).astype(LOW)
    since = (first >= second).astype(FULL).astype(LOW)
    same = (first == second).astype(FULL).astype(LOW)
    down_seq, down_spot = spots(lax.broadcasted_iota(jnp.int32, (total, 1), 0).astype(FULL))
    over_seq, over_spot = spots(lax.broadcasted_iota(jnp.int32, (1, total), 1).astype(FULL))
    wide = lax.broadcasted_iota(jnp.int32, (total, chars), 1).astype(FULL)
    token_down, token_over, ident = 0.0, 0.0, 0.0
    for seq in range(seqs):
        lens = jnp.broadcast_to(lens_ref[seq:seq + 1, :].astype(FULL), (8, length)).astype(LOW)
        ends_over = dot(lens, upto)[0:1, :]
        ends_down = dot_nt(since, lens)[:, 0:1]
        count_ref[seq * length:(seq + 1) * length, :] = dot_nt(same, lens)[:, 0:1]
        here = jnp.sum((ends_over <= down_spot).astype(FULL), axis=1, keepdims=True) + seq * length
        token_down = token_down + jnp.where(down_seq == seq, here, 0.0)
        here = jnp.sum((ends_down <= over_spot).astype(FULL), axis=0, keepdims=True) + seq * length
        token_over = token_over + jnp.where(over_seq == seq, here, 0.0)
        here = jnp.sum(jnp.where(wide == down_spot, ids_ref[seq:seq + 1, :].astype(FULL), 0.0), axis=1,
                       keepdims=True)
        ident = ident + jnp.where(down_seq == seq, here, 0.0)
    tokc_ref[...] = token_down.astype(jnp.int32)
    tokr_ref[...] = token_over.astype(jnp.int32)
    idc_ref[...] = ident.astype(jnp.int32)
    vocab = lax.broadcasted_iota(jnp.int32, ident_ref.shape, 1).astype(FULL)
    ident_ref[...] = (vocab == ident).astype(FULL).astype(LOW)


def places_of(char_lengths, char_ids, vocab):
    seqs, length = char_lengths.shape
    total = char_ids.size
    return pl.pallas_call(
        places_kernel,
        out_shape=[sds((total, 1), jnp.int32), sds((1, total), jnp.int32), sds((total, 1), jnp.int32),
                   sds((seqs * length, 1), FULL), sds((total, vocab), LOW)],
        in_specs=[vmem_spec(), vmem_spec()],
        out_specs=[vmem_spec() for _ in range(5)],
        compiler_params=pltpu.CompilerParams(vmem_limit_bytes=VMEM_LIMIT),
        cost_estimate=pl.CostEstimate(flops=1024, bytes_accessed=1024, transcendentals=0),
        name="places",
    )(char_lengths, char_ids)


def conv_grad_kernel(length, joined_ref, d_ref, out_ref):
    sources, cols, rows = d_ref.shape
    pos = lax.broadcasted_iota(jnp.int32, (cols, rows), 1) % length
    moved = [[], [], []]
    for i in range(sources):
        d = d_ref[i].astype(FULL)
        moved[0].append(jnp.where(pos == length - 1, 0.0, pltpu.roll(d, rows - 1, 1)).astype(LOW))
        moved[1].append(d_ref[i])
        moved[2].append(jnp.where(pos == 0, 0.0, pltpu.roll(d, 1, 1)).astype(LOW))
    moved = jnp.concatenate([jnp.concatenate(one, axis=1) for one in moved], axis=0)
    width = joined_ref.shape[2]
    step = width // 2
    for at in range(0, width, step):
        joined = jnp.concatenate([joined_ref[i, :, at:at + step] for i in range(sources)], axis=0)
        term = dot(moved, joined)

        @pl.when(pl.program_id(0) == 0)
        def _():
            for k in range(3):
                out_ref[k, :, at:at + step] = term[k * cols:(k + 1) * cols]

        @pl.when(pl.program_id(0) > 0)
        def _():
            for k in range(3):
                out_ref[k, :, at:at + step] += term[k * cols:(k + 1) * cols]


def conv_grad(length, joined_all, d_cols):
    sources, rows, width = joined_all.shape
    cols = d_cols.shape[1]
    once = 4
    return pl.pallas_call(
        functools.partial(conv_grad_kernel, length),
        grid=(sources // once,),
        in_specs=[pl.BlockSpec((once, rows, width), lambda i: (i, 0, 0)),
                  pl.BlockSpec((once, cols, rows), lambda i: (i, 0, 0))],
        out_specs=pl.BlockSpec((3, cols, width), lambda i: (0, 0, 0)),
        out_shape=sds((3, cols, width), FULL),
        compiler_params=pltpu.CompilerParams(vmem_limit_bytes=VMEM_LIMIT),
        cost_estimate=pl.CostEstimate(flops=6 * sources * rows * width * cols,
                                      bytes_accessed=2 * joined_all.size, transcendentals=0),
        name="conv_grad",
    )(joined_all, d_cols)


def layer_forward(seqs, grid, sub, char, places, weights):
    (qkv_w, qvb, out_w, out_b, gain, shift, up_w, up_b, down_w, down_b, table, win, bin_, wrec,
     brec, mw, mb, cw, cb) = weights
    tokc, tokr, idc, counts = places
    second = gru_forward(grid is not None, char, tokc, tokr, idc, counts, table, win, bin_, wrec, brec)
    length = sub.shape[0] // seqs
    if grid is not None:
        heads = run("attention_forward", attention_forward(seqs, sub, qkv_w, qvb))
        first = ffn_forward(sub, heads[2], out_w, out_b, gain, shift, up_w, up_b, down_w, down_b)
        second, first, joined = run("halves_forward_all", second, first, join(True, second, first, mw, mb),
                                    pace=(3, 1, 1))
        third = run("merge_both", merge_both(length, first[0], second[0], joined[0], mw, cw, cb, gain, shift,
                                             *grid, joined[1], first[-1]))
        first = (first[0], *heads, *first[1:])
        third = (*third[:2], joined[1], joined[0], *joined[2:], *third[2:])
    else:
        first = sub_forward(seqs, sub, qkv_w, qvb, out_w, out_b, gain, shift, up_w, up_b, down_w, down_b)
        joined = join(False, second, first, mw, mb)
        third = merge_forward(length, first, second, joined, cw, cb, gain, shift)
        second, first, joined, third = run("layer_forward", second, first, joined, third, pace=(30, 1, 1, 1))
    return first, second, third


def spread_cotangent(cotangent, positions, length):
    seqs, picks = positions.shape
    chosen = (positions[:, :, None] == jnp.arange(length, dtype=jnp.int32)).astype(LOW)
    grid = lax.dot_general(chosen, cotangent.reshape(seqs, picks, -1), (((1,), (1,)), ((0,), (0,))),
                           preferred_element_type=FULL)
    grid = grid.reshape(seqs * length, 2, -1)
    return grid[:, 0], grid[:, 1]


def together(*values):
    return lax.optimization_barrier(values)


def sync(values, *marks):
    fields = [getattr(share, name) for share, name in marks]
    values, fields = lax.optimization_barrier((values, fields))
    for (share, name), field in zip(marks, fields):
        setattr(share, name, field)
    return values


def swap(value, bit):
    count = lax.axis_size("batch")
    return lax.ppermute(value, "batch", [(i, i ^ (1 << bit)) for i in range(count)])


def combine_kernel(plan, count, bits_ref, *refs):
    flat = [source for parts in plan for _, _, _, sources in parts for source in sources]
    sources, results = refs[:count], refs[count:count + len(plan)]
    held, outs = refs[count + len(plan):-2 - len(plan)], refs[-2 - len(plan):-2]
    sems, out_sems = refs[-2:]
    stored = [pltpu.make_async_copy(out, result, out_sems.at[i])
              for i, (out, result) in enumerate(zip(outs, results))]
    copies = []
    for i, (at, columns, picks) in enumerate(flat):
        index = tuple(
            slice(None) if pick is None else bits_ref[pick[0]] if pick[1] else 1 - bits_ref[pick[0]]
            for pick in picks)
        if columns is not None:
            index = index + (slice(None), pl.ds(columns[0], columns[1] - columns[0]))
        copies.append(pltpu.make_async_copy(sources[at].at[index], held[i], sems.at[i]))
    for copy in copies:
        copy.start()
    at = 0
    for parts, out, store in zip(plan, outs, stored):
        for row, column, windows, sources in parts:
            total = None
            for _ in sources:
                copies[at].wait()
                term = held[at][...].astype(FULL)
                total = term if total is None else total + term
                at = at + 1
            total = total.astype(out.dtype)
            if windows is None:
                out[..., column:column + total.shape[-1]] = total
                continue
            for (top, height, left, wide), (to_row, to_column) in windows:
                out[to_row:to_row + height, to_column:to_column + wide] = (
                    total[top:top + height, left:left + wide])
        store.start()
    for store in stored:
        store.wait()


def combine(bits, items):
    plan, arrays, shapes, dtypes, outs = [], [], [], [], []
    for parts, shape, dtype in items:
        planned, column = [], 0
        for windows, sources in parts:
            listed = []
            for array, columns, picks in sources:
                place = next((i for i, other in enumerate(arrays) if other is array), len(arrays))
                if place == len(arrays):
                    arrays.append(array)
                listed.append((place, columns, picks))
                lead = tuple(size for size, pick in zip(array.shape, picks) if pick is None)
                tail = array.shape[len(picks):]
                if columns is not None:
                    tail = tail[:-1] + (columns[1] - columns[0],)
                shapes.append(lead + tail)
                dtypes.append(array.dtype)
            planned.append((0, column, windows, listed))
            column = column + shapes[-1][-1]
        plan.append(planned)
        outs.append(sds(shapes[-1][:-1] + (column,) if shape is None else shape, dtype))
    return pl.pallas_call(
        functools.partial(combine_kernel, plan, len(arrays)),
        out_shape=outs,
        in_specs=[pl.BlockSpec(memory_space=pltpu.SMEM)] + [any_spec() for _ in arrays],
        out_specs=[any_spec() for _ in outs],
        scratch_shapes=[pltpu.VMEM(shape, dtype) for shape, dtype in zip(shapes, dtypes)]
        + [pltpu.VMEM(out.shape, out.dtype) for out in outs]
        + [pltpu.SemaphoreType.DMA((len(shapes),)), pltpu.SemaphoreType.DMA((len(outs),))],
        compiler_params=pltpu.CompilerParams(vmem_limit_bytes=VMEM_LIMIT),
        cost_estimate=pl.CostEstimate(flops=0, bytes_accessed=1024, transcendentals=0),
        name="combine",
    )(bits, *arrays)


class Share:
    def __init__(self, gives, kepts, late=False, rounds=None):
        self.bits = lax.axis_size("batch").bit_length() - 1
        self.order = list(range(self.bits))
        if late:
            self.order = self.order[:1] + self.order[2:] + self.order[1:2]
        self.rounds = self.bits if rounds is None else rounds
        self.give = [self.shaped(one) for one in gives]
        self.kepts = [self.shaped(one) for one in kepts]
        self.gots = []

    def shaped(self, value):
        return value.reshape((2,) * (self.bits - 1) + value.shape[1:])

    def source(self, array, columns, passed):
        turn = len(self.gots)
        picks = []
        for bit in reversed(range(self.bits)):
            place = self.order.index(bit)
            if place >= passed:
                picks.append((bit, True) if place < turn else (bit, False) if place == turn < self.rounds else None)
        return array, columns, picks

    def parts(self, windows=None):
        parts, column = [], 0
        for i, (kept, got) in enumerate(zip(self.kepts, self.gots[0])):
            sources = [self.source(kept, None, 1), self.source(got, None, 1)]
            columns = None if len(self.kepts) == 1 else (column, column + kept.shape[-1])
            for age, later in enumerate(self.gots[1:]):
                sources.append(self.source(later, columns, age + 2))
            parts.append((None if windows is None else windows[i], sources))
            column = column + kept.shape[-1]
        return parts

    def window(self, first, last):
        sources = [(self.kepts[0], 1), (self.gots[0][0], 1)]
        sources = sources + [(later, age + 2) for age, later in enumerate(self.gots[1:])]
        return [self.source(array, (first, last), passed) for array, passed in sources]

    def item(self):
        return self.parts(), None, LOW if len(self.gots) < self.bits else FULL

    def scatter(self, held):
        count = lax.axis_size("batch")
        step = 1 << self.rounds
        groups = [list(range(i, count, step)) for i in range(step)]
        block = held.shape[-2:]
        total = lax.psum_scatter(held.reshape(-1, block[1]), "batch", scatter_dimension=0,
                                 axis_index_groups=groups, tiled=True)
        return total.astype(FULL)

    def finished(self):
        return len(self.gots) == self.rounds

    def send(self):
        bit = self.order[len(self.gots)]
        count = lax.axis_size("batch")
        self.got = jax.tree.map(
            lambda one: lax.ppermute(one, "batch", [(i, i ^ (1 << bit)) for i in range(count)]), self.give)

    def land(self):
        self.gots = self.gots + [self.got]


class Total:
    def __init__(self, value):
        self.bits = lax.axis_size("batch").bit_length() - 1
        self.give, self.passed = value, 0

    def item(self):
        return [(None, [(self.give, None, ()), (self.got, None, ())])], None, FULL

    def finished(self):
        return self.passed == self.bits

    def send(self):
        count = lax.axis_size("batch")
        self.got = lax.ppermute(self.give, "batch", [(i, i ^ (1 << self.passed)) for i in range(count)])

    def land(self):
        self.passed = self.passed + 1


class Flow:
    def __init__(self):
        self.index = lax.axis_index("batch")
        count = lax.axis_size("batch").bit_length() - 1
        last = lax.axis_index("section") == lax.axis_size("section") - 1
        self.bits = jnp.stack([(self.index >> bit) & 1 for bit in range(count)] + [last]).astype(jnp.int32)
        self.away, self.later = [], []

    def send(self, *shares):
        for s in shares:
            s.send()
        self.away = self.away + list(shares)

    def land(self, shares, values=(), others=()):
        values = sync(values, *[(s, "got") for s in shares], *[(s, "give") for s in others])
        for s in shares:
            s.land()
        self.away = [s for s in self.away if s not in shares]
        return values

    def prepare(self, *shares):
        shares = [s for s in shares if not (s in self.later and s.finished())]
        outs = combine(self.bits, [s.item() for s in shares]) if shares else []
        for s, out in zip(shares, outs):
            if not s.finished():
                s.give = out
            elif isinstance(s, Share) and s.rounds < s.bits:
                s.total = s.scatter(out)
            else:
                s.total = out

    def turn(self, shares, values=(), more=(), hold=()):
        self.land(shares)
        self.prepare(*shares)
        going = [s for s in shares if not s.finished()]
        values = sync(values, *[(s, "give") for s in going + list(more)])
        self.send(*[s for s in going if s not in hold], *more)
        return values

    def drain(self):
        while self.away:
            self.turn(list(self.away))


def placed(block):
    return block.T[None]


def body(stream_in, char_ids, char_lengths, mask_pos, cotangent, *params):
    weights = tuple(p.reshape(p.shape[1:]) if p.ndim > 2 else p for p in params)
    (qkv_w, qvb, out_w, out_b, gain, shift, up_w, up_b, down_w, down_b, table, win, bin_, wrec,
     brec, mw, mb, cw, cb) = weights
    section = lax.axis_index("section")
    sections = lax.axis_size("section")
    batch = lax.axis_size("batch")
    seqs, length, _, width = stream_in.shape
    rows = seqs * length
    count = seqs * char_ids.shape[1]
    hidden = wrec.shape[0]
    *places, ident = places_of(char_lengths, char_ids, table.shape[0])
    streams = stream_in.transpose(2, 0, 1, 3).reshape(2, rows, width)
    sub, char = streams[0], streams[1]

    def onward(pair):
        route = [(i, i + 1) for i in range(sections - 1)]
        a = lax.ppermute(pair[0], "section", route)
        a, b = lax.optimization_barrier((a, pair[1]))
        return a, lax.ppermute(b, "section", route)

    def back(value):
        return lax.ppermute(value, "section", [(i + 1, i) for i in range(sections - 1)])

    first, second, third = layer_forward(seqs, None, sub, char, places, weights)
    got = onward((third[0], third[1]))
    grid = spread_cotangent(cotangent, mask_pos, length)
    got_sub, grid = together(got[0], grid)
    got = (got_sub, got[1])
    sub = jnp.where(section == 0, sub, got[0])
    char = jnp.where(section == 0, char, got[1])
    first, second, third = layer_forward(seqs, grid, sub, char, places, weights)
    _, qkv, prob, att, res1, first_low, pre, act, res2 = first
    _, charin, r, z, to_n, to_z, to_r, prev = second
    out_sub, out_char, mpre, joined, second_low, pooled_low, res3, res4, d_res2, d_pooled = third
    joined_all = lax.all_gather(joined, "batch")
    tokc, tokr, idc, counts = places

    (d_char,), (d_res1,) = run(
        "halves_backward", gru_backward(None, d_pooled, counts, tokc, tokr, r, z, to_n, to_z, to_r, win, wrec),
        ffn_backward(None, d_res2, pre, res1, up_w, down_w, gain), pace=(1, 1))
    d_sub, = run("attention_backward", attention_backward(seqs, None, d_res1, qkv, prob, qkv_w, out_w))
    d_sub, passed_char = together(d_sub, back(d_char))
    passed = (back(d_sub), passed_char)

    flow = Flow()
    wide, lead = act.shape[1], batch // 2
    chunk, tall = width // batch, 3 * width // batch

    def split(outs, count, blocks):
        gives, kepts = blocks.finish(outs[count:])
        return list(outs[:count]), [([give], [kept]) for give, kept in zip(gives, kepts)]

    up_chunk, part = wide // batch, width // 3
    blocks = Blocks(flow.bits, lead, [
        (chunk, 2 * width, [(0, 0, chunk, 0, lead, 0, 0, width, 0, 0),
                            (0, width, chunk, 0, lead, 1, 0, width, 0, width)]),
        (chunk, wide, [(1, 0, chunk, 0, lead, 2, 0, wide, 0, 0)])],
        [(2 * width, rows), (width, rows)], [second_low, pooled_low, act])
    (d_res2, d_pooled, d_conv, small1), (merge, down) = split(run("merge_backward_all", merge_backward(
        length, blocks, *grid, res3, res4, mpre, mw, cw, gain, res2, passed)), 4, blocks)
    merge, down = Share(*merge, True), Share(*down)
    d_conv = d_conv.reshape(batch, -1, rows)

    flow.send(down, merge)
    d_cols = lax.all_to_all(d_conv, "batch", 0, 0, tiled=True)
    d_pooled = flow.turn([down, merge], d_pooled)
    spot, few, halfway = width + hidden, table.shape[0] // 2, (width + hidden + table.shape[0] // 2) // 2
    way = [(1, 0, tall, 0, lead // 2, 1, 0, hidden, 0, width - halfway),
           (1, 0, tall, lead // 2, lead, 1, hidden, 2 * hidden, 0, width - halfway)]
    blocks = Blocks(flow.bits, lead, [
        (tall, halfway, [(0, 0, tall, 0, lead, 0, 0, halfway, 0, 0)]),
        (tall, halfway, [(0, 0, tall, 0, lead, 0, halfway, width, 0, 0), *way,
                         (2, 0, chunk, 0, lead, 2, 0, few, 0, spot - halfway),
                         (2, 0, chunk, 0, lead, 2, few, 2 * few, chunk, spot - halfway)])],
        [(3 * width, count), (3 * width, count), (width, count)], [charin, prev, ident])
    outs, d_cols, joined_all = flow.land([down, merge], (
        run("gru_backward_all", gru_backward(
            blocks, d_pooled, counts, tokc, tokr, r, z, to_n, to_z, to_r, win, wrec)), d_cols, joined_all))
    (d_char, small4), (char, char_more) = split(outs, 2, blocks)
    char, char_more = Share(*char), Share(*char_more)

    flow.send(char, char_more)
    flow.land([char, char_more])
    flow.prepare(char, char_more, down)
    d_res2 = flow.land((), d_res2, [char, char_more, down])
    flow.send(char, down)
    blocks = Blocks(flow.bits, lead, [
        (up_chunk, width // 2, [(0, 0, up_chunk, 0, lead, 0, 0, width // 2, 0, 0)]),
        (up_chunk, width // 2, [(0, 0, up_chunk, 0, lead, 0, width // 2, width, 0, 0)])],
        [(wide, rows)], [first_low])
    outs = flow.land([char, down], run("ffn_backward_all", ffn_backward(
        blocks, d_res2, pre, res1, up_w, down_w, gain)))
    (d_res1, small2), (up, up_more) = split(outs, 2, blocks)
    ups = Share(up[0] + up_more[0], up[1] + up_more[1])

    flow.send(ups)
    flow.land([ups])
    flow.prepare(ups, merge, char)
    d_res1 = flow.land((), d_res1, [ups, merge, char])
    flow.send(char_more, merge, char)
    split_at = (width + part) // 2
    blocks = Blocks(flow.bits, lead, [
        (tall, split_at, [(0, 0, tall, 0, lead, 0, 0, split_at, 0, 0)]),
        (tall, split_at, [(0, 0, tall, 0, lead, 0, split_at, width, 0, 0),
                          (1, 0, chunk, 0, lead, 1, 0, part, 0, width - split_at),
                          (1, 0, chunk, 0, lead, 1, part, 2 * part, chunk, width - split_at),
                          (1, 0, chunk, 0, lead, 1, 2 * part, width, 2 * chunk, width - split_at)])],
        [(3 * width, rows), (width, rows)], [sub, att])
    outs = flow.land([char_more, merge, char],
                     run("attention_backward_all", attention_backward(
                         seqs, blocks, d_res1, qkv, prob, qkv_w, out_w)))
    (d_sub, small3), (head, head_more) = split(outs, 2, blocks)
    head, head_more = Share(*head), Share(*head_more)
    flow.later = [head, head_more]

    small = Total(jnp.concatenate([small1, small2, small3, small4], 0))
    flow.send(ups, head, head_more, small)
    going = [s for s in (char, char_more, merge, down) if not s.finished()]
    flow.prepare(char, char_more, merge, down)
    flow.land([head, head_more, small], (), going)
    flow.send(*going)
    flow.prepare(head, head_more, small)
    joined_all, d_cols = flow.land((), (joined_all, d_cols), [head, head_more, small])
    conv = conv_grad(length, joined_all, d_cols)
    others = list(flow.away)
    conv, streams = flow.turn(others, (conv, (d_sub, d_char, out_sub, out_char)), [head, head_more, small])
    d_sub, d_char, out_sub, out_char = streams
    ends_out = jnp.where(section == 0, jnp.stack([d_sub, d_char], 1), jnp.stack([out_sub, out_char], 1))
    ends_out = ends_out.reshape(1, seqs, length, 2, width)
    ends_out = flow.turn([s for s in flow.away if s is not head_more], ends_out)
    flow.drain()
    small, rest = small.total, width - split_at
    heads, outs = combine(flow.bits, [
        ([([((0, tall, 0, split_at), (0, 0))], head.window(0, split_at)),
          ([((0, tall, 0, rest), (0, split_at))], head_more.window(0, rest))], (tall, width), FULL),
        ([([((i * chunk, chunk, 0, part), (0, i * part)) for i in range(3)], head_more.window(rest, split_at))],
         (chunk, width), FULL)])

    b = lax.axis_index("batch")

    def pieces(*which):
        part = width // batch
        mine = lax.dynamic_slice_in_dim(small, b * part, part, 1)
        return jnp.concatenate([mine[i:i + 1] for i in which], 0)

    def piece(start, count):
        part = count * width // batch
        line = small[start:start + count].reshape(1, count * width)
        return lax.dynamic_slice_in_dim(line, b * part, part, 1)

    return (
        ends_out,
        placed(heads),
        pieces(24, 25)[None],
        placed(outs),
        pieces(20),
        pieces(21, 9, 4, 5)[None],
        pieces(22, 10, 6, 7)[None],
        placed(ups.total),
        piece(16, 4),
        placed(down.total),
        pieces(8),
        placed(jnp.concatenate([char_more.total[i * chunk:(i + 1) * chunk, spot - halfway:] for i in range(2)], 1)),
        placed(jnp.concatenate([char.total, char_more.total[:, :width - halfway]], 1)),
        piece(32, 3),
        placed(char_more.total[:, width - halfway:spot - halfway]),
        piece(35, 3),
        merge.total.reshape(chunk, 2, width).transpose(1, 2, 0)[None],
        pieces(2, 3)[None],
        conv.transpose(0, 2, 1)[None],
        piece(0, 2),
    )


def solution(mesh):
    by = P("batch")
    part = P("section")

    def columns(rank):
        return P(*(["section"] + [None] * (rank - 2) + ["batch"]))

    return jax.shard_map(
        body,
        mesh=mesh,
        in_specs=(by,) * 5 + (part,) * 19,
        out_specs=(P("section", "batch"),) + tuple(
            columns(rank) for rank in (3, 3, 3, 2, 3, 3, 3, 2, 3, 2, 3, 3, 2, 3, 2, 4, 3, 4, 2)),
        check_vma=False,
    )
```

```python
import functools
import math

import jax
import jax.numpy as jnp
from jax import lax
from jax.experimental import pallas as pl
from jax.experimental.pallas import tpu as pltpu
from jax.sharding import PartitionSpec as P

HEAD = 64
BLOCK_CH = 8
EPSILON = 1e-05
LOW = jnp.bfloat16
FULL = jnp.float32
VMEM_LIMIT = 63 * 1024 * 1024


def dot(left, right):
    return lax.dot_general(left, right, (((1,), (0,)), ((), ())), preferred_element_type=FULL)


def dot_nt(left, right):
    return lax.dot_general(left, right, (((1,), (1,)), ((), ())), preferred_element_type=FULL)


def dot_tn(left, right):
    return lax.dot_general(left, right, (((0,), (0,)), ((), ())), preferred_element_type=FULL)


def norm_parts(values):
    row_mean = jnp.mean(values, axis=-1, keepdims=True)
    centered = values - row_mean
    row_var = jnp.mean(centered * centered, axis=-1, keepdims=True)
    inverse = lax.rsqrt(row_var + EPSILON)
    return centered * inverse, inverse


def norm(values, gain, shift):
    return norm_parts(values)[0] * gain + shift


def norm_back(values, gain, grad):
    unit, inverse = norm_parts(values)
    scaled = grad * gain
    first = jnp.mean(scaled, axis=-1, keepdims=True)
    second = jnp.mean(scaled * unit, axis=-1, keepdims=True)
    return inverse * (scaled - first - unit * second), unit


GELU_A = 0.7978845608028654
GELU_B = 0.044715


def gelu(x):
    return 0.5 * x * (1.0 + jnp.tanh(GELU_A * (x + GELU_B * x * x * x)))


def gelu_both(x):
    square = x * x
    bent = jnp.tanh(GELU_A * (x + GELU_B * square * x))
    gate = 0.5 * (1.0 + bent)
    return x * gate, gate + 0.5 * x * (1.0 - bent * bent) * (GELU_A * (1.0 + 3.0 * GELU_B * square))


def sigmoid(x):
    return 0.5 * jnp.tanh(0.5 * x) + 0.5


def column_sum(values):
    return jnp.sum(values, axis=0, keepdims=True)


class Stream:
    def __init__(self, pairs, sems, first=None):
        self.copies = [
            pltpu.make_async_copy(src, dst, sems.at[i]) for i, (src, dst) in enumerate(pairs)
        ]
        self.started, self.waited = 0, set()
        self.start(len(pairs) if first is None else first)

    def start(self, count=None):
        upto = len(self.copies) if count is None else self.started + count
        for copy in self.copies[self.started:upto]:
            copy.start()
        self.started = upto

    def need(self, *which):
        for i in which:
            if i not in self.waited:
                self.waited.add(i)
                self.copies[i].wait()


class Loaded:
    def need(self, *which):
        pass


def chunks(src, dst, axis, size):
    total = src.shape[axis]
    parts = []
    for start in range(0, total, size):
        index = [slice(None)] * len(src.shape)
        index[axis] = pl.ds(start, min(size, total - start))
        parts.append((src.at[tuple(index)], dst.at[tuple(index)]))
    return parts


def fill(out, near, terms):
    lead, chunk, columns = out.shape
    part = [term[9] for term in terms if term[8] > 0]
    if part:
        out[:, :, part[0]:] = jnp.zeros((lead, chunk, columns - part[0]), LOW)
    for d_y, base, height, start, stop, x, first, last, row, column in terms:
        d = jnp.concatenate([
            d_y[pl.ds(pl.multiple_of(base + (2 * i + near) * height, 16), height), :]
            for i in range(start, stop)], axis=0)
        step = min(last - first, 768)
        for at in range(first, last, step):
            value = dot(d, x[:, at:at + step]).astype(LOW)
            lanes = slice(column + at - first, column + at - first + step)
            out[start:stop, row:row + height, lanes] = value.reshape(stop - start, height, step)


def fill_plain(shape, near, terms):
    out = jnp.zeros(shape, LOW)
    for d_y, base, height, start, stop, x, first, last, row, column in terms:
        count = stop - start
        d = d_y[base + 2 * start * height:base + 2 * stop * height].reshape(count, 2, height, -1)
        d = lax.dynamic_slice_in_dim(d, near, 1, 1).reshape(count * height, -1)
        value = dot(d, x[:, first:last]).astype(LOW).reshape(count, height, last - first)
        out = lax.dynamic_update_slice(out, value, (start, row, column))
    return out


def named(plan, d_ys, xs):
    return [(d_ys[d],) + rest[:4] + (xs[rest[4]],) + rest[5:] for d, *rest in map(tuple, plan)
            for rest in [tuple(rest)]]


class Blocks:
    def __init__(self, bits, count, plans, d_shapes, xs):
        self.bits, self.count, self.plans, self.d_shapes, self.xs = bits, count, plans, d_shapes, xs
        self.inside = all(plan[0] % 16 == 0 for plan in plans)
        self.last = bits.shape[0] - 1

    def shapes(self):
        return [sds((self.count, plan[0], plan[1]), LOW) for plan in self.plans]

    def outs(self):
        return self.shapes() * 2 if self.inside else [sds(shape, LOW) for shape in self.d_shapes]

    def scratch(self):
        return [pltpu.VMEM(shape, LOW) for shape in self.d_shapes] if self.inside else []

    def inputs(self):
        return [self.bits] + (self.xs if self.inside else [])

    def split(self, refs):
        if not self.inside:
            return refs[:len(self.d_shapes)], lambda bits_ref, xs: None
        results, d_ys = refs[:2 * len(self.plans)], refs[2 * len(self.plans):]

        def make(bits_ref, xs):
            near = bits_ref[0]
            for own in range(2):
                for i, plan in enumerate(self.plans):
                    result = results[own * len(self.plans) + i]
                    fill(result, near if own else 1 - near, named(plan[2], d_ys, xs))
                    done(result)

        return d_ys, make

    def finish(self, results):
        if self.inside:
            return results[:len(self.plans)], results[len(self.plans):]
        near = self.bits[0]
        return tuple([fill_plain(shape.shape, which, named(plan[2], results, self.xs))
                      for shape, plan in zip(self.shapes(), self.plans)] for which in (1 - near, near))


def any_spec():
    return pl.BlockSpec(memory_space=pl.ANY)


def vmem_spec():
    return pl.BlockSpec(memory_space=pltpu.VMEM)


def sds(shape, dtype):
    return jax.ShapeDtypeStruct(shape, dtype)


def rest_of(blocks, count):
    return [] if blocks is None else list(range(count + 1, count + len(blocks.inputs())))


class Late:
    def __init__(self, ref, copy):
        self.ref, self.copy, self.shape = ref, copy, ref.shape

    def __getitem__(self, index):
        if self.copy is not None:
            self.copy.wait()
            self.copy = None
        return self.ref[index]


class Early:
    def __init__(self, ref, copy):
        self.ref, self.copy, self.shape, self.started = ref, copy, ref.shape, False

    def __getitem__(self, index):
        return self.ref[index]

    def __setitem__(self, index, value):
        self.ref[index] = value

    def done(self):
        if not self.started:
            self.copy.start()
            self.started = True


def done(*refs):
    for ref in refs:
        if isinstance(ref, Early):
            ref.done()


class Job:
    def __init__(self, kernel, outs, ins, streamed, scratch, flops, copies, blocks=None, late=(), after=()):
        self.scalar, self.after = -1, after
        if blocks is not None:
            ins, outs = list(ins) + blocks.inputs(), list(outs) + blocks.outs()
            scratch = blocks.scratch() + list(scratch)
            self.scalar = len(ins) - len(blocks.inputs())
        self.kernel, self.ins, self.outs, self.flops, self.late = kernel, ins, outs, flops, late
        self.streamed = set(streamed) | set(late)
        self.early = [i for i, o in enumerate(outs) if o.size * o.dtype.itemsize > 200000]
        self.scratch = list(scratch) + [pltpu.SemaphoreType.DMA((copies,))]
        self.buffers = [pltpu.VMEM(ins[i].shape, ins[i].dtype) for i in late]
        self.buffers = self.buffers + [pltpu.VMEM(outs[i].shape, outs[i].dtype) for i in self.early]
        self.buffers = self.buffers + [pltpu.SemaphoreType.DMA((max(len(late), 1),)),
                                       pltpu.SemaphoreType.DMA((max(len(self.early), 1),))]

    def in_specs(self):
        return [any_spec() if i in self.streamed else pl.BlockSpec(memory_space=pltpu.SMEM) if i == self.scalar
                else vmem_spec() for i in range(len(self.ins))]

    def out_specs(self):
        return [any_spec() if i in self.early else vmem_spec() for i in range(len(self.outs))]

    def begin(self, ins, outs, scratch, buffers):
        ins, outs = list(ins), list(outs)
        held, (in_sems, out_sems) = buffers[:-2], buffers[-2:]
        for n, i in enumerate(self.late):
            copy = pltpu.make_async_copy(ins[i], held[n], in_sems.at[n])
            copy.start()
            ins[i] = Late(held[n], copy)
        for n, i in enumerate(self.early):
            buffer = held[len(self.late) + n]
            outs[i] = Early(buffer, pltpu.make_async_copy(buffer, outs[i], out_sems.at[n]))
        self.lates = [ins[i] for i in self.late]
        self.earlies = [outs[i] for i in self.early]
        self.results = outs
        return self.kernel(*[job.results[0] for job in self.after], *ins, *outs, *scratch)

    def end(self):
        for late in self.lates:
            if late.copy is not None:
                late.copy.wait()
        for early in self.earlies:
            early.done()
        for early in self.earlies:
            early.copy.wait()


def together_kernel(jobs, pace, *refs):
    groups, at = [], 0
    for kind in ("ins", "outs", "scratch", "buffers"):
        group = []
        for job in jobs:
            count = len(getattr(job, kind))
            group.append(refs[at:at + count])
            at = at + count
        groups.append(group)
    running, last = [], []
    for n, job in enumerate(jobs):
        steps = job.begin(*[group[n] for group in groups])
        next(steps)
        (last if job.after else running).append((steps, pace[n]))
    while running or last:
        if not running:
            running, last = last[:1], last[1:]
        left = []
        for steps, count in running:
            if all(next(steps, True) is None for _ in range(count)):
                left.append((steps, count))
        running = left
    for job in jobs:
        job.end()


def run(name, *jobs, pace=(1, 1, 1)):
    ins = [a for job in jobs for a in job.ins]
    outs = [o for job in jobs for o in job.outs]
    moved = sum(a.size * a.dtype.itemsize for a in ins) + sum(o.size * o.dtype.itemsize for o in outs)
    results = pl.pallas_call(
        functools.partial(together_kernel, jobs, pace),
        out_shape=outs,
        in_specs=[spec for job in jobs for spec in job.in_specs()],
        out_specs=[spec for job in jobs for spec in job.out_specs()],
        scratch_shapes=[s for job in jobs for s in job.scratch] + [s for job in jobs for s in job.buffers],
        compiler_params=pltpu.CompilerParams(vmem_limit_bytes=VMEM_LIMIT),
        cost_estimate=pl.CostEstimate(flops=sum(job.flops for job in jobs), bytes_accessed=moved,
                                      transcendentals=0),
        name=name,
    )(*ins)
    split = []
    for job in jobs:
        split.append(results[:len(job.outs)])
        results = results[len(job.outs):]
    return split[0] if len(jobs) == 1 else split


def attention_forward_kernel(seqs, save, s_ref, qkv_hbm, qvb_ref, qkv_ref, prob_ref, att_ref, wqkv, sems):
    width = s_ref.shape[1]
    length = s_ref.shape[0] // seqs
    w = Stream(chunks(qkv_hbm, wqkv, 1, width), sems)
    yield
    for part in range(3):
        w.need(part)
        if part > 0:
            yield
        cols = slice(part * width, (part + 1) * width)
        y = dot(s_ref[...], wqkv[:, cols])
        if part == 0:
            y = (y + qvb_ref[0:1, :]) * HEAD ** -0.5
        elif part == 2:
            y = y + qvb_ref[1:2, :]
        qkv_ref[:, cols] = y.astype(LOW)
    done(qkv_ref)
    lanes = lax.broadcasted_iota(jnp.int32, (length, 2 * HEAD), 1)
    even = lanes < HEAD
    for seq in range(seqs):
        rows = slice(seq * length, (seq + 1) * length)
        for pair in range(width // (2 * HEAD)):
            lo = pair * 2 * HEAD
            q = qkv_ref[rows, lo:lo + 2 * HEAD]
            k = qkv_ref[rows, width + lo:width + lo + 2 * HEAD]
            v = qkv_ref[rows, 2 * width + lo:2 * width + lo + 2 * HEAD]
            zero = jnp.zeros_like(q)
            probs = []
            for half in range(2):
                mask = even if half == 0 else ~even
                scores = dot_nt(jnp.where(mask, q, zero), k)
                peak = jnp.max(scores, axis=-1, keepdims=True)
                e = jnp.exp(scores - peak)
                prob = (e / jnp.sum(e, axis=-1, keepdims=True)).astype(LOW)
                probs.append(prob)
                if save:
                    at = (seq * (width // HEAD) + 2 * pair + half) * length
                    prob_ref[at:at + length, :] = prob
            both = jnp.concatenate(probs, axis=1)
            vv = jnp.concatenate([jnp.where(even, v, zero), jnp.where(even, zero, v)], axis=0)
            att_ref[rows, lo:lo + 2 * HEAD] = dot(both, vv).astype(LOW)
            yield
    done(prob_ref, att_ref)


def ffn_forward_kernel(save, s_ref, att_ref, out_hbm, outb_ref, gain_ref, shift_ref, up_hbm, upb_ref,
                       down_hbm, downb_ref, after_ref, *rest):
    if save:
        res1_ref, first_ref, pre_ref, act_ref, res2_ref, wout, wup, wdown, sems = rest
    else:
        wout, wup, wdown, sems = rest
    width, wide = s_ref.shape[1], wup.shape[1]
    pairs = zip(chunks(up_hbm, wup, 1, width), chunks(down_hbm, wdown, 0, width))
    w = Stream(chunks(out_hbm, wout, 1, width) + [one for pair in pairs for one in pair], sems)
    yield
    w.need(0)
    res1 = s_ref[...].astype(FULL) + dot(att_ref[...], wout[...]) + outb_ref[...]
    after = norm(res1, gain_ref[0:1, :], shift_ref[0:1, :])
    low = after.astype(LOW)
    if save:
        res1_ref[...] = res1
        first_ref[...] = low
        done(res1_ref, first_ref)
    total = after + downb_ref[...]
    for part in range(wide // width):
        yield
        w.need(1 + 2 * part, 2 + 2 * part)
        cols = slice(part * width, (part + 1) * width)
        pre = dot(low, wup[:, cols]) + upb_ref[:, cols]
        if save:
            act, slope = gelu_both(pre)
            act = act.astype(LOW)
            pre_ref[:, cols] = slope.astype(LOW)
            act_ref[:, cols] = act
        else:
            act = gelu(pre).astype(LOW)
        total = total + dot(act, wdown[cols, :])
    if save:
        res2_ref[...] = total
        done(pre_ref, act_ref, res2_ref)
    after_ref[...] = norm(total, gain_ref[1:2, :], shift_ref[1:2, :])


def sub_forward_kernel(seqs, s_ref, qkv_hbm, qvb_ref, out_hbm, outb_ref, gain_ref, shift_ref, up_hbm, upb_ref,
                       down_hbm, downb_ref, after_ref, wqkv, qkv_ref, att_ref, att_sems, wout, wup, wdown, sems):
    attention = attention_forward_kernel(seqs, False, s_ref, qkv_hbm, qvb_ref, qkv_ref, None, att_ref, wqkv,
                                         att_sems)
    ffn = ffn_forward_kernel(False, s_ref, att_ref, out_hbm, outb_ref, gain_ref, shift_ref, up_hbm, upb_ref,
                             down_hbm, downb_ref, after_ref, wout, wup, wdown, sems)
    next(attention)
    yield
    next(ffn)
    yield from attention
    yield from ffn


def attention_forward(seqs, s, qkv_w, qvb):
    rows, width = s.shape
    length = rows // seqs
    outs = [sds((rows, 3 * width), LOW), sds((seqs * (width // HEAD) * length, length), LOW),
            sds((rows, width), LOW)]
    return Job(functools.partial(attention_forward_kernel, seqs, True), outs, [s, qkv_w, qvb], {1},
               [pltpu.VMEM(qkv_w.shape, LOW)], 2 * rows * qkv_w.size, 3)


def ffn_forward(s, att, out_w, out_b, gain, shift, up_w, up_b, down_w, down_b):
    rows, width = s.shape
    wide = up_w.shape[1]
    outs = [sds((rows, width), FULL), sds((rows, width), FULL), sds((rows, width), LOW),
            sds((rows, wide), LOW), sds((rows, wide), LOW), sds((rows, width), FULL)]
    weights = (out_w, up_w, down_w)
    return Job(functools.partial(ffn_forward_kernel, True), outs,
               [s, att, out_w, out_b, gain, shift, up_w, up_b, down_w, down_b], {2, 6, 8},
               [pltpu.VMEM(one.shape, LOW) for one in weights], 2 * rows * sum(one.size for one in weights),
               1 + 2 * (wide // width))


def sub_forward(seqs, s, qkv_w, qvb, out_w, out_b, gain, shift, up_w, up_b, down_w, down_b):
    rows, width = s.shape
    weights = (qkv_w, out_w, up_w, down_w)
    scratch = [pltpu.VMEM(qkv_w.shape, LOW), pltpu.VMEM((rows, 3 * width), LOW), pltpu.VMEM((rows, width), LOW),
               pltpu.SemaphoreType.DMA((3,))] + [pltpu.VMEM(one.shape, LOW) for one in weights[1:]]
    return Job(functools.partial(sub_forward_kernel, seqs), [sds((rows, width), FULL)],
               [s, qkv_w, qvb, out_w, out_b, gain, shift, up_w, up_b, down_w, down_b], {1, 3, 7, 9}, scratch,
               2 * rows * sum(one.size for one in weights), 1 + 2 * (up_w.shape[1] // width))


def gru_forward_kernel(save, c_ref, tokc_ref, tokr_ref, idc_ref, count_ref, table_hbm, win_hbm,
                       bin_ref, wrec_hbm, brec_ref, *rest):
    if save:
        (pooled_ref, charin_ref, r_ref, z_ref, to_n_ref, to_z_ref, to_r_ref, prev_ref,
         table, win, wrec, gate, low_state, sems) = rest
    else:
        pooled_ref, table, win, wrec, gate, low_state, charin_ref, sems = rest
    rows, width = c_ref.shape
    count = tokc_ref.shape[0]
    hidden = wrec.shape[0]
    w = Stream([(table_hbm, table)] + chunks(win_hbm, win, 1, width)
               + chunks(wrec_hbm, wrec, 1, 3 * hidden), sems)
    yield
    token = (tokc_ref[...] == lax.broadcasted_iota(jnp.int32, (count, rows), 1))
    ident = (idc_ref[...] == lax.broadcasted_iota(jnp.int32, (count, table.shape[0]), 1))
    w.need(0)
    x = dot(token.astype(FULL).astype(LOW), c_ref[...]) + dot(ident.astype(FULL).astype(LOW), table[...])
    charin_ref[...] = x.astype(LOW)
    done(charin_ref)
    for part in range(3):
        yield
        w.need(1 + part)
        cols = slice(part * width, (part + 1) * width)
        gate[:, cols] = dot(charin_ref[...], win[:, cols]) + bin_ref[:, cols]
    lanes = count // BLOCK_CH
    state = [None, None]
    w.need(4, 5)
    for turn in range(BLOCK_CH):
        yield
        for way in range(2):
            at = turn if way == 0 else BLOCK_CH - 1 - turn
            here = slice(at * lanes, (at + 1) * lanes)
            base = way * 3 * hidden
            out = slice(way * hidden, (way + 1) * hidden)
            bias = brec_ref[:, base:base + 3 * hidden]
            g = gate[here, base:base + 3 * hidden]
            if turn == 0:
                rec_n = jnp.broadcast_to(bias[:, 2 * hidden:], (lanes, hidden))
                rz = g[:, :2 * hidden] + bias[:, :2 * hidden]
                if save:
                    prev_ref[here, out] = jnp.zeros((lanes, hidden), LOW)
            else:
                low = state[way].astype(LOW)
                if save:
                    prev_ref[here, out] = low
                rec = dot(low, wrec[:, base:base + 3 * hidden]) + bias
                rec_n = rec[:, 2 * hidden:]
                rz = g[:, :2 * hidden] + rec[:, :2 * hidden]
            rz = sigmoid(rz)
            r, z = rz[:, :hidden], rz[:, hidden:]
            n = jnp.tanh(g[:, 2 * hidden:] + r * rec_n)
            new = (1.0 - z) * n
            before = state[way]
            if turn > 0:
                new = new + z * before
            state[way] = new
            low_state[here, out] = new.astype(LOW)
            if save:
                r_ref[here, out] = r.astype(LOW)
                z_ref[here, out] = z.astype(LOW)
                to_n_ref[here, out] = ((1.0 - z) * (1.0 - n * n)).astype(LOW)
                change = -n if turn == 0 else before - n
                to_z_ref[here, out] = (change * (z * (1.0 - z))).astype(LOW)
                to_r_ref[here, out] = (rec_n * (r * (1.0 - r))).astype(LOW)
    if save:
        done(r_ref, z_ref, to_n_ref, to_z_ref, to_r_ref, prev_ref)
    yield
    spread = (tokr_ref[...] == lax.broadcasted_iota(jnp.int32, (rows, count), 0))
    pooled = dot(spread.astype(FULL).astype(LOW), low_state[...])
    pooled_ref[...] = pooled / count_ref[...]


def gru_forward(save, c, tokc, tokr, idc, counts, table, win, bin_, wrec, brec):
    rows, width = c.shape
    count = tokc.shape[0]
    outs = [sds((rows, width), FULL)]
    scratch = [pltpu.VMEM(a.shape, LOW) for a in (table, win, wrec)]
    scratch = scratch + [pltpu.VMEM((count, win.shape[1]), FULL), pltpu.VMEM((count, width), LOW)]
    if save:
        outs = outs + [sds((count, width), LOW)] * 7
    else:
        scratch = scratch + [pltpu.VMEM((count, width), LOW)]
    return Job(functools.partial(gru_forward_kernel, save), outs,
                [c, tokc, tokr, idc, counts, table, win, bin_, wrec, brec],
                {5, 6, 8}, scratch, 2 * count * (win.size + wrec.size) + 2 * count * width * (2 * rows + table.shape[0]), 6)


def shift_rows(values, by, length):
    rows, width = values.shape
    zero = jnp.zeros((1, width), values.dtype)
    pos = lax.broadcasted_iota(jnp.int32, (rows, 1), 0) % length
    if by == 1:
        moved = jnp.concatenate([zero, values[:-1]], axis=0)
        return jnp.where(pos == 0, 0.0, moved)
    moved = jnp.concatenate([values[1:], zero], axis=0)
    return jnp.where(pos == length - 1, 0.0, moved)


def join_kernel(save, pooled_ref, after_ref, mw_hbm, mb_ref, joined_ref, *rest):
    if save:
        pre_ref, second_ref, poollow_ref, mw, sems = rest
    else:
        mw, sems = rest
    width = after_ref.shape[1]
    w = Stream(chunks(mw_hbm, mw, 0, 1), sems)
    yield
    w.need(0, 1)
    for side in range(2):
        cols = slice(side * width, (side + 1) * width)
        low = (after_ref if side == 0 else pooled_ref)[...].astype(LOW)
        pre = dot(low, mw[side]) + mb_ref[side:side + 1, :]
        if save:
            (second_ref if side == 0 else poollow_ref)[...] = low
            value, slope = gelu_both(pre)
            pre_ref[:, cols] = slope.astype(LOW)
        else:
            value = gelu(pre)
        joined_ref[:, cols] = value.astype(LOW)


def join(save, pooled, after, mw, mb):
    rows, width = pooled.outs[0].shape
    outs = [sds((rows, 2 * width), LOW)]
    if save:
        outs = outs * 2 + [sds((rows, width), LOW)] * 2
    return Job(functools.partial(join_kernel, save), outs, [mw, mb], {0}, [pltpu.VMEM(mw.shape, LOW)],
               2 * rows * mw.size, 2, after=(pooled, after))


def merge_forward_kernel(length, save, after_ref, pooled_ref, joined_ref, cw_hbm, cb_ref, gain_ref, shift_ref,
                         sub_ref, char_ref, *rest):
    if save:
        res3_ref, res4_ref, cw, sems = rest
    else:
        cw, sems = rest
    width = after_ref.shape[1]
    w = Stream([pair for k in (1, 0, 2) for pair in chunks(cw_hbm.at[k], cw.at[k], 0, width)], sems)
    yield
    joined = joined_ref[...]
    total = cb_ref[...]
    for place, k in enumerate((1, 0, 2)):
        moved = joined if k == 1 else shift_rows(joined.astype(FULL), 1 - k, length).astype(LOW)
        for half in range(2):
            w.need(2 * place + half)
            rows = slice(half * width, (half + 1) * width)
            total = total + dot(moved[:, rows], cw[k, rows, :])
    res3 = after_ref[...] + total[:, :width]
    res4 = pooled_ref[...] + total[:, width:]
    if save:
        res3_ref[...] = res3
        res4_ref[...] = res4
        done(res3_ref, res4_ref)
    sub_ref[...] = norm(res3, gain_ref[2:3, :], shift_ref[2:3, :]).astype(LOW)
    char_ref[...] = norm(res4, gain_ref[3:4, :], shift_ref[3:4, :]).astype(LOW)


def merge_forward(length, after, pooled, joined, cw, cb, gain, shift):
    rows, width = after.outs[0].shape
    return Job(functools.partial(merge_forward_kernel, length, False), [sds((rows, width), LOW)] * 2,
               [cw, cb, gain, shift], {0}, [pltpu.VMEM(cw.shape, LOW)],
               2 * rows * cw.size, 6, after=(after, pooled, joined))


def merge_backward_kernel(length, full, gsub_ref, gchar_ref, res3_ref, res4_ref, pre_ref, mw_hbm, cw_hbm,
                          gain_ref, res2_ref, *rest):
    if full:
        psub_ref, pchar_ref, *rest = rest
        xs, rest = rest[:len(full.inputs())], rest[len(full.inputs()):]
        dres2_ref, dpooled_ref, dconv_ref, small_ref, *rest, mw, cw, sems = rest
        (dpre_ref, ddown_ref), make = full.split(rest)
    else:
        dres2_ref, dpooled_ref, mw, cw, sems = rest
    width = res3_ref.shape[1]
    w = Loaded() if sems is None else Stream(chunks(cw_hbm, cw, 0, 1) + chunks(mw_hbm, mw, 0, 1), sems)
    yield
    grads = [gsub_ref[...], gchar_ref[...]]
    if full:
        last = xs[0][full.last] > 0
        grads = [jnp.where(last, grad, ref[...].astype(FULL))
                 for grad, ref in zip(grads, (psub_ref, pchar_ref))]
    d_res, sums = [], []
    for side in range(2):
        d, unit = norm_back((res3_ref, res4_ref)[side][...], gain_ref[2 + side:3 + side, :], grads[side])
        d_res.append(d)
        if full:
            small_ref[4 + side:5 + side, :] = column_sum(grads[side] * unit)
            small_ref[6 + side:7 + side, :] = column_sum(grads[side])
            small_ref[side:side + 1, :] = column_sum(d)
    d_conv = jnp.concatenate(d_res, axis=1)
    if full:
        dconv_ref[...] = d_conv.astype(LOW).T
        done(dconv_ref)
    total, lows = None, []
    for k in range(3):
        moved = d_conv if k == 1 else shift_rows(d_conv, k - 1, length)
        w.need(k)
        term = dot_nt(moved.astype(LOW), cw[k])
        total = term if total is None else total + term
    for half in range(2):
        cols = slice(half * width, (half + 1) * width)
        d_pre = total[:, cols] * pre_ref[:, cols].astype(FULL)
        lows.append(d_pre.astype(LOW))
        if full:
            dpre_ref[cols, :] = lows[-1].T
            sums.append(column_sum(d_pre))
    d_low = jnp.concatenate(lows, axis=1)
    if full:
        for side in range(2):
            small_ref[2 + side:3 + side, :] = sums[side]
    w.need(3, 4)
    d_second = d_res[0] + dot_nt(d_low[:, :width], mw[0])
    d_res2, unit = norm_back(res2_ref[...], gain_ref[1:2, :], d_second)
    dres2_ref[...] = d_res2
    done(dres2_ref)
    dpooled_ref[...] = d_res[1] + dot_nt(d_low[:, width:], mw[1])
    done(dpooled_ref)
    if full:
        ddown_ref[...] = d_res2.astype(LOW).T
        small_ref[8:9, :] = column_sum(d_res2)
        small_ref[9:10, :] = column_sum(d_second * unit)
        small_ref[10:11, :] = column_sum(d_second)
        small_ref[11:16, :] = jnp.zeros((5, width), FULL)
        make(xs[0], xs[1:])


def merge_backward(length, full, gsub, gchar, res3, res4, pre, mw, cw, gain, res2, passed):
    rows, width = res3.shape
    outs = [sds((rows, width), FULL)] * 2
    if full:
        outs = outs + [sds((2 * width, rows), LOW), sds((16, width), FULL)]
    scratch = [pltpu.VMEM(mw.shape, LOW), pltpu.VMEM(cw.shape, LOW)]
    return Job(functools.partial(merge_backward_kernel, length, full), outs,
                [gsub, gchar, res3, res4, pre, mw, cw, gain, res2, *passed], {5, 6}, scratch, 2 * rows * (mw.size + cw.size), 5, full,
               [0, 1, 9, 10, 2, 3, 4, 8] + rest_of(full, 11))


def merge_both_kernel(length, after_ref, pooled_ref, joined_ref, mw_hbm, cw_hbm, cb_ref, gain_ref, shift_ref,
                      gsub_ref, gchar_ref, pre_ref, res2_ref, sub_ref, char_ref, res3_ref, res4_ref, dres2_ref,
                      dpooled_ref, mw, mw_sems, cw, sems):
    forward = merge_forward_kernel(length, True, after_ref, pooled_ref, joined_ref, cw_hbm, cb_ref, gain_ref,
                                   shift_ref, sub_ref, char_ref, res3_ref, res4_ref, cw, sems)
    next(forward)
    w = Stream(chunks(mw_hbm, mw, 0, 1), mw_sems)
    yield
    yield from forward
    w.need(0, 1)
    yield from merge_backward_kernel(length, None, gsub_ref, gchar_ref, res3_ref, res4_ref, pre_ref, mw_hbm,
                                     cw_hbm, gain_ref, res2_ref, dres2_ref, dpooled_ref, mw, cw, None)


def merge_both(length, after, pooled, joined, mw, cw, cb, gain, shift, gsub, gchar, pre, res2):
    rows, width = after.shape
    outs = [sds((rows, width), LOW)] * 2 + [sds((rows, width), FULL)] * 4
    scratch = [pltpu.VMEM(mw.shape, LOW), pltpu.SemaphoreType.DMA((2,)), pltpu.VMEM(cw.shape, LOW)]
    return Job(functools.partial(merge_both_kernel, length), outs,
               [after, pooled, joined, mw, cw, cb, gain, shift, gsub, gchar, pre, res2], {3, 4}, scratch,
               4 * rows * (mw.size + cw.size), 6, None, [2, 0, 1, 8, 9, 10, 11])


def ffn_backward_kernel(full, dres2_ref, pre_ref, res1_ref, up_hbm, down_hbm, gain_ref, *rest):
    if full:
        xs, rest = rest[:len(full.inputs())], rest[len(full.inputs()):]
        dres1_ref, small_ref, *rest, wup, wdown, sems = rest
        (dup_ref,), make = full.split(rest)
    else:
        dres1_ref, wup, wdown, sems = rest
    rows, width = dres1_ref.shape
    wide = wup.shape[1]
    parts = wide // width
    pairs = zip(chunks(down_hbm, wdown, 0, width), chunks(up_hbm, wup, 1, width))
    w = Stream([one for pair in pairs for one in pair], sems)
    yield
    d_res2 = dres2_ref[...]
    d_low = d_res2.astype(LOW)
    d_first = d_res2
    for part in range(parts):
        cols = slice(part * width, (part + 1) * width)
        w.need(2 * part, 2 * part + 1)
        d_up = dot_nt(d_low, wdown[cols, :]) * pre_ref[:, cols].astype(FULL)
        up_low = d_up.astype(LOW)
        if full:
            dup_ref[cols, :] = up_low.T
            small_ref[part:part + 1, :] = column_sum(d_up)
        d_first = d_first + dot_nt(up_low, wup[:, cols])
        yield
    d_res1, unit = norm_back(res1_ref[...], gain_ref[0:1, :], d_first)
    dres1_ref[...] = d_res1
    done(dres1_ref)
    if full:
        small_ref[parts:parts + 1, :] = column_sum(d_res1)
        small_ref[parts + 1:parts + 2, :] = column_sum(d_first * unit)
        small_ref[parts + 2:parts + 3, :] = column_sum(d_first)
        small_ref[parts + 3:, :] = jnp.zeros((small_ref.shape[0] - parts - 3, width), FULL)
        make(xs[0], xs[1:])


def ffn_backward(full, dres2, pre, res1, up_w, down_w, gain):
    rows, width = res1.shape
    wide = up_w.shape[1]
    outs = [sds((rows, width), FULL)]
    scratch = [pltpu.VMEM(a.shape, LOW) for a in (up_w, down_w)]
    if full:
        outs = outs + [sds((8, width), FULL)]
    return Job(functools.partial(ffn_backward_kernel, full), outs,
                [dres2, pre, res1, up_w, down_w, gain], {3, 4}, scratch, 2 * rows * (up_w.size + down_w.size), 2 * (wide // width), full,
                [0, 1, 2] + rest_of(full, 6))


def attention_backward_kernel(seqs, full, dres1_ref, qkv_ref, prob_ref, qkv_hbm, out_hbm, *rest):
    if full:
        xs, rest = rest[:len(full.inputs())], rest[len(full.inputs()):]
        dsub_ref, small_ref, *rest, wqkv, wout, datt, dproj_ref, sems = rest
        (dprojt_ref, dbranch_ref), make = full.split(rest)
    else:
        dsub_ref, wqkv, wout, datt, dproj_ref, sems = rest
    rows, width = dsub_ref.shape
    length = rows // seqs
    w = Stream(chunks(out_hbm, wout, 1, width) + chunks(qkv_hbm, wqkv, 1, width), sems)
    yield
    w.need(0, 1, 2, 3)
    branch_low = dres1_ref[...].astype(LOW)
    datt[...] = dot_nt(branch_low, wout[...]).astype(LOW)
    if full:
        dbranch_ref[...] = branch_low.T
    even = lax.broadcasted_iota(jnp.int32, (length, 2 * HEAD), 1) < HEAD
    scale = HEAD ** -0.5
    for pair in range(width // (2 * HEAD)):
        lo = pair * 2 * HEAD
        totals = [0.0, 0.0]
        for seq in range(seqs):
            at_rows = slice(seq * length, (seq + 1) * length)
            q = qkv_ref[at_rows, lo:lo + 2 * HEAD]
            k = qkv_ref[at_rows, width + lo:width + lo + 2 * HEAD]
            v = qkv_ref[at_rows, 2 * width + lo:2 * width + lo + 2 * HEAD]
            da = datt[at_rows, lo:lo + 2 * HEAD]
            zero = jnp.zeros_like(q)

            def halves(x):
                return jnp.where(even, x, zero), jnp.where(even, zero, x)

            da_h = halves(da)
            probs, d_scores = [], []
            for half in range(2):
                at = (seq * (width // HEAD) + 2 * pair + half) * length
                prob = prob_ref[at:at + length, :]
                d_prob = dot_nt(da_h[half], v)
                wide_prob = prob.astype(FULL)
                weighted = wide_prob * d_prob
                d_score = weighted - wide_prob * jnp.sum(weighted, axis=-1, keepdims=True)
                probs.append(prob)
                d_scores.append(d_score.astype(LOW))
            d_v = dot_tn(jnp.concatenate(probs, axis=0), jnp.concatenate(da_h, axis=0))
            d_q = dot(jnp.concatenate(d_scores, axis=1), jnp.concatenate(halves(k), axis=0)) * scale
            d_k = dot_tn(jnp.concatenate(d_scores, axis=0), jnp.concatenate(halves(q), axis=0))
            dproj_ref[at_rows, lo:lo + 2 * HEAD] = d_q.astype(LOW)
            dproj_ref[at_rows, width + lo:width + lo + 2 * HEAD] = d_k.astype(LOW)
            dproj_ref[at_rows, 2 * width + lo:2 * width + lo + 2 * HEAD] = d_v.astype(LOW)
            yield
            if full:
                totals[0] = totals[0] + column_sum(d_q)
                totals[1] = totals[1] + column_sum(d_v)
        if full:
            small_ref[0:1, lo:lo + 2 * HEAD] = totals[0]
            small_ref[1:2, lo:lo + 2 * HEAD] = totals[1]
    total = dres1_ref[...]
    for part in range(3):
        cols = slice(part * width, (part + 1) * width)
        if full:
            dprojt_ref[cols, :] = dproj_ref[:, cols].T
        yield
        total = total + dot_nt(dproj_ref[:, cols], wqkv[:, cols])
    dsub_ref[...] = total.astype(LOW)
    done(dsub_ref)
    if full:
        small_ref[2:8, :] = jnp.zeros((6, width), FULL)
        make(xs[0], xs[1:])


def attention_backward(seqs, full, dres1, qkv, prob, qkv_w, out_w):
    rows, width = dres1.shape
    outs = [sds((rows, width), LOW)]
    scratch = [pltpu.VMEM(a.shape, LOW) for a in (qkv_w, out_w)]
    scratch = scratch + [pltpu.VMEM((rows, width), LOW), pltpu.VMEM((rows, 3 * width), LOW)]
    if full:
        outs = outs + [sds((8, width), FULL)]
    return Job(functools.partial(attention_backward_kernel, seqs, full), outs,
                [dres1, qkv, prob, qkv_w, out_w], {3, 4}, scratch, 2 * rows * (qkv_w.size + out_w.size), 4, full, [0, 1, 2] + rest_of(full, 5))


def gru_backward_kernel(full, dpooled_ref, count_ref, tokc_ref, tokr_ref, r_ref, z_ref, to_n_ref, to_z_ref,
                        to_r_ref, win_hbm, wrec_hbm, *rest):
    if full:
        xs, rest = rest[:len(full.inputs())], rest[len(full.inputs()):]
        dchar_ref, small_ref, *rest, dstate, win, wrec, dgate_ref, drecn_ref, sems = rest
        (dgatet_ref, drect_ref, dchart_ref), make = full.split(rest)
    else:
        dchar_ref, dstate, win, wrec, dgate_ref, sems = rest
    rows, width = dpooled_ref.shape
    count = tokc_ref.shape[0]
    hidden = wrec.shape[0]
    lanes = count // BLOCK_CH
    w = Stream(chunks(wrec_hbm, wrec, 1, 3 * hidden) + chunks(win_hbm, win, 1, width), sems)
    yield
    share = (dpooled_ref[...] / count_ref[...]).astype(LOW)
    token = (tokc_ref[...] == lax.broadcasted_iota(jnp.int32, (count, rows), 1))
    dstate[...] = dot(token.astype(FULL).astype(LOW), share)
    carry = [None, None]
    sums = [[None] * 4, [None] * 4]
    w.need(0, 1)
    for turn in reversed(range(BLOCK_CH)):
        yield
        for way in range(2):
            at = turn if way == 0 else BLOCK_CH - 1 - turn
            here = slice(at * lanes, (at + 1) * lanes)
            base = way * 3 * hidden
            out = slice(way * hidden, (way + 1) * hidden)
            d_h = dstate[here, out]
            if carry[way] is not None:
                d_h = d_h + carry[way]
            d_n = d_h * to_n_ref[here, out].astype(FULL)
            d_z = d_h * to_z_ref[here, out].astype(FULL)
            d_r = d_n * to_r_ref[here, out].astype(FULL)
            d_rec_n = d_n * r_ref[here, out].astype(FULL)
            pieces = (d_r, d_z, d_n, d_rec_n)
            if full:
                for i, piece in enumerate(pieces):
                    one = column_sum(piece)
                    sums[way][i] = one if sums[way][i] is None else sums[way][i] + one
                drecn_ref[here, out] = d_rec_n.astype(LOW)
            low_r, low_z = d_r.astype(LOW), d_z.astype(LOW)
            dgate_ref[here, base:base + hidden] = low_r
            dgate_ref[here, base + hidden:base + 2 * hidden] = low_z
            dgate_ref[here, base + 2 * hidden:base + 3 * hidden] = d_n.astype(LOW)
            if turn > 0:
                d_rec = jnp.concatenate([low_r, low_z, d_rec_n.astype(LOW)], axis=1)
                carry[way] = d_h * z_ref[here, out].astype(FULL) + dot_nt(d_rec, wrec[:, base:base + 3 * hidden])
    if full:
        for way in range(2):
            for i in range(3):
                at = slice((3 * way + i) * hidden, (3 * way + i + 1) * hidden)
                turned = dgate_ref[:, at].T
                dgatet_ref[at, :] = turned
                drect_ref[at, :] = turned if i < 2 else drecn_ref[:, way * hidden:(way + 1) * hidden].T
        small_ref[6:8, :] = jnp.zeros((2, width), FULL)
        for kind in range(2):
            line = [sums[way][i if i < 2 or kind == 0 else 3] for way in range(2) for i in range(3)]
            for i in range(3):
                small_ref[3 * kind + i:3 * kind + i + 1, :] = jnp.concatenate(line[2 * i:2 * i + 2], axis=1)
    total = None
    for part in range(3):
        cols = slice(part * width, (part + 1) * width)
        yield
        w.need(2 + part)
        term = dot_nt(dgate_ref[:, cols], win[:, cols])
        total = term if total is None else total + term
    low = total.astype(LOW)
    if full:
        dchart_ref[...] = low.T
    spread = (tokr_ref[...] == lax.broadcasted_iota(jnp.int32, (rows, count), 0))
    dchar_ref[...] = dot(spread.astype(FULL).astype(LOW), low).astype(LOW)
    done(dchar_ref)
    if full:
        make(xs[0], xs[1:])


def gru_backward(full, dpooled, counts, tokc, tokr, r, z, to_n, to_z, to_r, win, wrec):
    rows, width = dpooled.shape
    count = tokc.shape[0]
    wide = win.shape[1]
    outs = [sds((rows, width), LOW)]
    scratch = [pltpu.VMEM((count, width), FULL), pltpu.VMEM(win.shape, LOW), pltpu.VMEM(wrec.shape, LOW),
               pltpu.VMEM((count, wide), LOW)]
    if full:
        outs = outs + [sds((8, width), FULL)]
        scratch = scratch + [pltpu.VMEM((count, width), LOW)]
    return Job(functools.partial(gru_backward_kernel, full), outs,
                [dpooled, counts, tokc, tokr, r, z, to_n, to_z, to_r, win, wrec], {9, 10}, scratch, 2 * count * (win.size + wrec.size) + 4 * count * rows * width, 5, full,
                [0, 2, 6, 7, 8, 4, 5] + rest_of(full, 11))


def whole_part(values, divisor):
    return jnp.floor((values + 0.5) * (1.0 / divisor))


def places_kernel(lens_ref, ids_ref, tokc_ref, tokr_ref, idc_ref, count_ref, ident_ref):
    seqs, length = lens_ref.shape
    chars = ids_ref.shape[1]
    blocks, total = chars // BLOCK_CH, seqs * chars

    def spots(index):
        turn = whole_part(index, seqs * blocks)
        rest = index - turn * (seqs * blocks)
        seq = whole_part(rest, blocks)
        return seq, (rest - seq * blocks) * BLOCK_CH + turn

    first = lax.broadcasted_iota(jnp.int32, (length, length), 0)
    second = lax.broadcasted_iota(jnp.int32, (length, length), 1)
    upto = (first <= second).astype(FULL).astype(LOW)
    since = (first >= second).astype(FULL).astype(LOW)
    same = (first == second).astype(FULL).astype(LOW)
    down_seq, down_spot = spots(lax.broadcasted_iota(jnp.int32, (total, 1), 0).astype(FULL))
    over_seq, over_spot = spots(lax.broadcasted_iota(jnp.int32, (1, total), 1).astype(FULL))
    wide = lax.broadcasted_iota(jnp.int32, (total, chars), 1).astype(FULL)
    token_down, token_over, ident = 0.0, 0.0, 0.0
    for seq in range(seqs):
        lens = jnp.broadcast_to(lens_ref[seq:seq + 1, :].astype(FULL), (8, length)).astype(LOW)
        ends_over = dot(lens, upto)[0:1, :]
        ends_down = dot_nt(since, lens)[:, 0:1]
        count_ref[seq * length:(seq + 1) * length, :] = dot_nt(same, lens)[:, 0:1]
        here = jnp.sum((ends_over <= down_spot).astype(FULL), axis=1, keepdims=True) + seq * length
        token_down = token_down + jnp.where(down_seq == seq, here, 0.0)
        here = jnp.sum((ends_down <= over_spot).astype(FULL), axis=0, keepdims=True) + seq * length
        token_over = token_over + jnp.where(over_seq == seq, here, 0.0)
        here = jnp.sum(jnp.where(wide == down_spot, ids_ref[seq:seq + 1, :].astype(FULL), 0.0), axis=1,
                       keepdims=True)
        ident = ident + jnp.where(down_seq == seq, here, 0.0)
    tokc_ref[...] = token_down.astype(jnp.int32)
    tokr_ref[...] = token_over.astype(jnp.int32)
    idc_ref[...] = ident.astype(jnp.int32)
    vocab = lax.broadcasted_iota(jnp.int32, ident_ref.shape, 1).astype(FULL)
    ident_ref[...] = (vocab == ident).astype(FULL).astype(LOW)


def places_of(char_lengths, char_ids, vocab):
    seqs, length = char_lengths.shape
    total = char_ids.size
    return pl.pallas_call(
        places_kernel,
        out_shape=[sds((total, 1), jnp.int32), sds((1, total), jnp.int32), sds((total, 1), jnp.int32),
                   sds((seqs * length, 1), FULL), sds((total, vocab), LOW)],
        in_specs=[vmem_spec(), vmem_spec()],
        out_specs=[vmem_spec() for _ in range(5)],
        compiler_params=pltpu.CompilerParams(vmem_limit_bytes=VMEM_LIMIT),
        cost_estimate=pl.CostEstimate(flops=1024, bytes_accessed=1024, transcendentals=0),
        name="places",
    )(char_lengths, char_ids)


def conv_grad_kernel(length, joined_ref, d_ref, out_ref):
    sources, cols, rows = d_ref.shape
    pos = lax.broadcasted_iota(jnp.int32, (cols, rows), 1) % length
    moved = [[], [], []]
    for i in range(sources):
        d = d_ref[i].astype(FULL)
        moved[0].append(jnp.where(pos == length - 1, 0.0, pltpu.roll(d, rows - 1, 1)).astype(LOW))
        moved[1].append(d_ref[i])
        moved[2].append(jnp.where(pos == 0, 0.0, pltpu.roll(d, 1, 1)).astype(LOW))
    moved = jnp.concatenate([jnp.concatenate(one, axis=1) for one in moved], axis=0)
    width = joined_ref.shape[2]
    step = width // 2
    for at in range(0, width, step):
        joined = jnp.concatenate([joined_ref[i, :, at:at + step] for i in range(sources)], axis=0)
        term = dot(moved, joined)

        @pl.when(pl.program_id(0) == 0)
        def _():
            for k in range(3):
                out_ref[k, :, at:at + step] = term[k * cols:(k + 1) * cols]

        @pl.when(pl.program_id(0) > 0)
        def _():
            for k in range(3):
                out_ref[k, :, at:at + step] += term[k * cols:(k + 1) * cols]


def conv_grad(length, joined_all, d_cols):
    sources, rows, width = joined_all.shape
    cols = d_cols.shape[1]
    once = 4
    return pl.pallas_call(
        functools.partial(conv_grad_kernel, length),
        grid=(sources // once,),
        in_specs=[pl.BlockSpec((once, rows, width), lambda i: (i, 0, 0)),
                  pl.BlockSpec((once, cols, rows), lambda i: (i, 0, 0))],
        out_specs=pl.BlockSpec((3, cols, width), lambda i: (0, 0, 0)),
        out_shape=sds((3, cols, width), FULL),
        compiler_params=pltpu.CompilerParams(vmem_limit_bytes=VMEM_LIMIT),
        cost_estimate=pl.CostEstimate(flops=6 * sources * rows * width * cols,
                                      bytes_accessed=2 * joined_all.size, transcendentals=0),
        name="conv_grad",
    )(joined_all, d_cols)


def layer_forward(seqs, grid, sub, char, places, weights):
    (qkv_w, qvb, out_w, out_b, gain, shift, up_w, up_b, down_w, down_b, table, win, bin_, wrec,
     brec, mw, mb, cw, cb) = weights
    tokc, tokr, idc, counts = places
    second = gru_forward(grid is not None, char, tokc, tokr, idc, counts, table, win, bin_, wrec, brec)
    length = sub.shape[0] // seqs
    if grid is not None:
        heads = run("attention_forward", attention_forward(seqs, sub, qkv_w, qvb))
        first = ffn_forward(sub, heads[2], out_w, out_b, gain, shift, up_w, up_b, down_w, down_b)
        second, first, joined = run("halves_forward_all", second, first, join(True, second, first, mw, mb),
                                    pace=(3, 1, 1))
        third = run("merge_both", merge_both(length, first[0], second[0], joined[0], mw, cw, cb, gain, shift,
                                             *grid, joined[1], first[-1]))
        first = (first[0], *heads, *first[1:])
        third = (*third[:2], joined[1], joined[0], *joined[2:], *third[2:])
    else:
        first = sub_forward(seqs, sub, qkv_w, qvb, out_w, out_b, gain, shift, up_w, up_b, down_w, down_b)
        joined = join(False, second, first, mw, mb)
        third = merge_forward(length, first, second, joined, cw, cb, gain, shift)
        second, first, joined, third = run("layer_forward", second, first, joined, third, pace=(30, 1, 1, 1))
    return first, second, third


def spread_cotangent(cotangent, positions, length):
    seqs, picks = positions.shape
    chosen = (positions[:, :, None] == jnp.arange(length, dtype=jnp.int32)).astype(LOW)
    grid = lax.dot_general(chosen, cotangent.reshape(seqs, picks, -1), (((1,), (1,)), ((0,), (0,))),
                           preferred_element_type=FULL)
    grid = grid.reshape(seqs * length, 2, -1)
    return grid[:, 0], grid[:, 1]


def together(*values):
    return lax.optimization_barrier(values)


def sync(values, *marks):
    fields = [getattr(share, name) for share, name in marks]
    values, fields = lax.optimization_barrier((values, fields))
    for (share, name), field in zip(marks, fields):
        setattr(share, name, field)
    return values


def swap(value, bit):
    count = lax.axis_size("batch")
    return lax.ppermute(value, "batch", [(i, i ^ (1 << bit)) for i in range(count)])


def combine_kernel(plan, count, bits_ref, *refs):
    flat = [source for parts in plan for _, _, _, sources in parts for source in sources]
    sources, results = refs[:count], refs[count:count + len(plan)]
    held, outs = refs[count + len(plan):-2 - len(plan)], refs[-2 - len(plan):-2]
    sems, out_sems = refs[-2:]
    stored = [pltpu.make_async_copy(out, result, out_sems.at[i])
              for i, (out, result) in enumerate(zip(outs, results))]
    copies = []
    for i, (at, columns, picks) in enumerate(flat):
        index = tuple(
            slice(None) if pick is None else bits_ref[pick[0]] if pick[1] else 1 - bits_ref[pick[0]]
            for pick in picks)
        if columns is not None:
            index = index + (slice(None), pl.ds(columns[0], columns[1] - columns[0]))
        copies.append(pltpu.make_async_copy(sources[at].at[index], held[i], sems.at[i]))
    for copy in copies:
        copy.start()
    at = 0
    for parts, out, store in zip(plan, outs, stored):
        for row, column, windows, sources in parts:
            total = None
            for _ in sources:
                copies[at].wait()
                term = held[at][...].astype(FULL)
                total = term if total is None else total + term
                at = at + 1
            total = total.astype(out.dtype)
            if windows is None:
                out[..., column:column + total.shape[-1]] = total
                continue
            for (top, height, left, wide), (to_row, to_column) in windows:
                out[to_row:to_row + height, to_column:to_column + wide] = (
                    total[top:top + height, left:left + wide])
        store.start()
    for store in stored:
        store.wait()


def combine(bits, items):
    plan, arrays, shapes, dtypes, outs = [], [], [], [], []
    for parts, shape, dtype in items:
        planned, column = [], 0
        for windows, sources in parts:
            listed = []
            for array, columns, picks in sources:
                place = next((i for i, other in enumerate(arrays) if other is array), len(arrays))
                if place == len(arrays):
                    arrays.append(array)
                listed.append((place, columns, picks))
                lead = tuple(size for size, pick in zip(array.shape, picks) if pick is None)
                tail = array.shape[len(picks):]
                if columns is not None:
                    tail = tail[:-1] + (columns[1] - columns[0],)
                shapes.append(lead + tail)
                dtypes.append(array.dtype)
            planned.append((0, column, windows, listed))
            column = column + shapes[-1][-1]
        plan.append(planned)
        outs.append(sds(shapes[-1][:-1] + (column,) if shape is None else shape, dtype))
    return pl.pallas_call(
        functools.partial(combine_kernel, plan, len(arrays)),
        out_shape=outs,
        in_specs=[pl.BlockSpec(memory_space=pltpu.SMEM)] + [any_spec() for _ in arrays],
        out_specs=[any_spec() for _ in outs],
        scratch_shapes=[pltpu.VMEM(shape, dtype) for shape, dtype in zip(shapes, dtypes)]
        + [pltpu.VMEM(out.shape, out.dtype) for out in outs]
        + [pltpu.SemaphoreType.DMA((len(shapes),)), pltpu.SemaphoreType.DMA((len(outs),))],
        compiler_params=pltpu.CompilerParams(vmem_limit_bytes=VMEM_LIMIT),
        cost_estimate=pl.CostEstimate(flops=0, bytes_accessed=1024, transcendentals=0),
        name="combine",
    )(bits, *arrays)


class Share:
    def __init__(self, gives, kepts, late=False, rounds=None):
        self.bits = lax.axis_size("batch").bit_length() - 1
        self.order = list(range(self.bits))
        if late:
            self.order = self.order[:1] + self.order[2:] + self.order[1:2]
        self.rounds = self.bits if rounds is None else rounds
        self.give = [self.shaped(one) for one in gives]
        self.kepts = [self.shaped(one) for one in kepts]
        self.gots = []

    def shaped(self, value):
        return value.reshape((2,) * (self.bits - 1) + value.shape[1:])

    def source(self, array, columns, passed):
        turn = len(self.gots)
        picks = []
        for bit in reversed(range(self.bits)):
            place = self.order.index(bit)
            if place >= passed:
                picks.append((bit, True) if place < turn else (bit, False) if place == turn < self.rounds else None)
        return array, columns, picks

    def parts(self, windows=None):
        parts, column = [], 0
        for i, (kept, got) in enumerate(zip(self.kepts, self.gots[0])):
            sources = [self.source(kept, None, 1), self.source(got, None, 1)]
            columns = None if len(self.kepts) == 1 else (column, column + kept.shape[-1])
            for age, later in enumerate(self.gots[1:]):
                sources.append(self.source(later, columns, age + 2))
            parts.append((None if windows is None else windows[i], sources))
            column = column + kept.shape[-1]
        return parts

    def window(self, first, last):
        sources = [(self.kepts[0], 1), (self.gots[0][0], 1)]
        sources = sources + [(later, age + 2) for age, later in enumerate(self.gots[1:])]
        return [self.source(array, (first, last), passed) for array, passed in sources]

    def item(self):
        return self.parts(), None, LOW if len(self.gots) < self.bits else FULL

    def scatter(self, held):
        count = lax.axis_size("batch")
        step = 1 << self.rounds
        groups = [list(range(i, count, step)) for i in range(step)]
        block = held.shape[-2:]
        total = lax.psum_scatter(held.reshape(-1, block[1]), "batch", scatter_dimension=0,
                                 axis_index_groups=groups, tiled=True)
        return total.astype(FULL)

    def finished(self):
        return len(self.gots) == self.rounds

    def send(self):
        bit = self.order[len(self.gots)]
        count = lax.axis_size("batch")
        self.got = jax.tree.map(
            lambda one: lax.ppermute(one, "batch", [(i, i ^ (1 << bit)) for i in range(count)]), self.give)

    def land(self):
        self.gots = self.gots + [self.got]


class Total:
    def __init__(self, value):
        self.bits = lax.axis_size("batch").bit_length() - 1
        self.give, self.passed = value, 0

    def item(self):
        return [(None, [(self.give, None, ()), (self.got, None, ())])], None, FULL

    def finished(self):
        return self.passed == self.bits

    def send(self):
        count = lax.axis_size("batch")
        self.got = lax.ppermute(self.give, "batch", [(i, i ^ (1 << self.passed)) for i in range(count)])

    def land(self):
        self.passed = self.passed + 1


class Flow:
    def __init__(self):
        self.index = lax.axis_index("batch")
        count = lax.axis_size("batch").bit_length() - 1
        last = lax.axis_index("section") == lax.axis_size("section") - 1
        self.bits = jnp.stack([(self.index >> bit) & 1 for bit in range(count)] + [last]).astype(jnp.int32)
        self.away, self.later = [], []

    def send(self, *shares):
        for s in shares:
            s.send()
        self.away = self.away + list(shares)

    def land(self, shares, values=(), others=()):
        values = sync(values, *[(s, "got") for s in shares], *[(s, "give") for s in others])
        for s in shares:
            s.land()
        self.away = [s for s in self.away if s not in shares]
        return values

    def prepare(self, *shares):
        shares = [s for s in shares if not (s in self.later and s.finished())]
        outs = combine(self.bits, [s.item() for s in shares]) if shares else []
        for s, out in zip(shares, outs):
            if not s.finished():
                s.give = out
            elif isinstance(s, Share) and s.rounds < s.bits:
                s.total = s.scatter(out)
            else:
                s.total = out

    def turn(self, shares, values=(), more=(), hold=()):
        self.land(shares)
        self.prepare(*shares)
        going = [s for s in shares if not s.finished()]
        values = sync(values, *[(s, "give") for s in going + list(more)])
        self.send(*[s for s in going if s not in hold], *more)
        return values

    def drain(self):
        while self.away:
            self.turn(list(self.away))


def placed(block):
    return block.T[None]


def body(stream_in, char_ids, char_lengths, mask_pos, cotangent, *params):
    weights = tuple(p.reshape(p.shape[1:]) if p.ndim > 2 else p for p in params)
    (qkv_w, qvb, out_w, out_b, gain, shift, up_w, up_b, down_w, down_b, table, win, bin_, wrec,
     brec, mw, mb, cw, cb) = weights
    section = lax.axis_index("section")
    sections = lax.axis_size("section")
    batch = lax.axis_size("batch")
    seqs, length, _, width = stream_in.shape
    rows = seqs * length
    count = seqs * char_ids.shape[1]
    hidden = wrec.shape[0]
    *places, ident = places_of(char_lengths, char_ids, table.shape[0])
    streams = stream_in.transpose(2, 0, 1, 3).reshape(2, rows, width)
    sub, char = streams[0], streams[1]

    def onward(pair):
        route = [(i, i + 1) for i in range(sections - 1)]
        a = lax.ppermute(pair[0], "section", route)
        a, b = lax.optimization_barrier((a, pair[1]))
        return a, lax.ppermute(b, "section", route)

    def back(value):
        return lax.ppermute(value, "section", [(i + 1, i) for i in range(sections - 1)])

    first, second, third = layer_forward(seqs, None, sub, char, places, weights)
    got = onward((third[0], third[1]))
    grid = spread_cotangent(cotangent, mask_pos, length)
    got_sub, grid = together(got[0], grid)
    got = (got_sub, got[1])
    sub = jnp.where(section == 0, sub, got[0])
    char = jnp.where(section == 0, char, got[1])
    first, second, third = layer_forward(seqs, grid, sub, char, places, weights)
    _, qkv, prob, att, res1, first_low, pre, act, res2 = first
    _, charin, r, z, to_n, to_z, to_r, prev = second
    out_sub, out_char, mpre, joined, second_low, pooled_low, res3, res4, d_res2, d_pooled = third
    joined_all = lax.all_gather(joined, "batch")
    tokc, tokr, idc, counts = places

    (d_char,), (d_res1,) = run(
        "halves_backward", gru_backward(None, d_pooled, counts, tokc, tokr, r, z, to_n, to_z, to_r, win, wrec),
        ffn_backward(None, d_res2, pre, res1, up_w, down_w, gain), pace=(1, 1))
    d_sub, = run("attention_backward", attention_backward(seqs, None, d_res1, qkv, prob, qkv_w, out_w))
    d_sub, passed_char = together(d_sub, back(d_char))
    passed = (back(d_sub), passed_char)

    flow = Flow()
    wide, lead = act.shape[1], batch // 2
    chunk, tall = width // batch, 3 * width // batch

    def split(outs, count, blocks):
        gives, kepts = blocks.finish(outs[count:])
        return list(outs[:count]), [([give], [kept]) for give, kept in zip(gives, kepts)]

    up_chunk, part = wide // batch, width // 3
    blocks = Blocks(flow.bits, lead, [
        (chunk, 2 * width, [(0, 0, chunk, 0, lead, 0, 0, width, 0, 0),
                            (0, width, chunk, 0, lead, 1, 0, width, 0, width)]),
        (chunk, wide, [(1, 0, chunk, 0, lead, 2, 0, wide, 0, 0)])],
        [(2 * width, rows), (width, rows)], [second_low, pooled_low, act])
    (d_res2, d_pooled, d_conv, small1), (merge, down) = split(run("merge_backward_all", merge_backward(
        length, blocks, *grid, res3, res4, mpre, mw, cw, gain, res2, passed)), 4, blocks)
    merge, down = Share(*merge, True), Share(*down)
    d_conv = d_conv.reshape(batch, -1, rows)

    flow.send(down, merge)
    d_cols = lax.all_to_all(d_conv, "batch", 0, 0, tiled=True)
    d_pooled = flow.turn([down, merge], d_pooled)
    spot, few, halfway = width + hidden, table.shape[0] // 2, (width + hidden + table.shape[0] // 2) // 2
    way = [(1, 0, tall, 0, lead // 2, 1, 0, hidden, 0, width - halfway),
           (1, 0, tall, lead // 2, lead, 1, hidden, 2 * hidden, 0, width - halfway)]
    blocks = Blocks(flow.bits, lead, [
        (tall, halfway, [(0, 0, tall, 0, lead, 0, 0, halfway, 0, 0)]),
        (tall, halfway, [(0, 0, tall, 0, lead, 0, halfway, width, 0, 0), *way,
                         (2, 0, chunk, 0, lead, 2, 0, few, 0, spot - halfway),
                         (2, 0, chunk, 0, lead, 2, few, 2 * few, chunk, spot - halfway)])],
        [(3 * width, count), (3 * width, count), (width, count)], [charin, prev, ident])
    outs, d_cols, joined_all = flow.land([down, merge], (
        run("gru_backward_all", gru_backward(
            blocks, d_pooled, counts, tokc, tokr, r, z, to_n, to_z, to_r, win, wrec)), d_cols, joined_all))
    (d_char, small4), (char, char_more) = split(outs, 2, blocks)
    char, char_more = Share(*char), Share(*char_more)

    flow.send(char, char_more)
    flow.prepare(down)
    d_res2 = flow.land((), d_res2, [down])
    flow.send(down)
    flow.land([char, char_more])
    flow.prepare(char, char_more)
    d_res2 = flow.land((), d_res2, [char, char_more])
    flow.send(char)
    blocks = Blocks(flow.bits, lead, [
        (up_chunk, width // 2, [(0, 0, up_chunk, 0, lead, 0, 0, width // 2, 0, 0)]),
        (up_chunk, width // 2, [(0, 0, up_chunk, 0, lead, 0, width // 2, width, 0, 0)])],
        [(wide, rows)], [first_low])
    outs = flow.land([char, down], run("ffn_backward_all", ffn_backward(
        blocks, d_res2, pre, res1, up_w, down_w, gain)))
    (d_res1, small2), (up, up_more) = split(outs, 2, blocks)
    ups = Share(up[0] + up_more[0], up[1] + up_more[1])

    flow.send(ups)
    flow.land([ups])
    flow.prepare(ups, merge, char)
    d_res1 = flow.land((), d_res1, [ups, merge, char])
    flow.send(char_more, merge, char)
    split_at = (width + part) // 2
    blocks = Blocks(flow.bits, lead, [
        (tall, split_at, [(0, 0, tall, 0, lead, 0, 0, split_at, 0, 0)]),
        (tall, split_at, [(0, 0, tall, 0, lead, 0, split_at, width, 0, 0),
                          (1, 0, chunk, 0, lead, 1, 0, part, 0, width - split_at),
                          (1, 0, chunk, 0, lead, 1, part, 2 * part, chunk, width - split_at),
                          (1, 0, chunk, 0, lead, 1, 2 * part, width, 2 * chunk, width - split_at)])],
        [(3 * width, rows), (width, rows)], [sub, att])
    outs = flow.land([char_more, merge, char],
                     run("attention_backward_all", attention_backward(
                         seqs, blocks, d_res1, qkv, prob, qkv_w, out_w)))
    (d_sub, small3), (head, head_more) = split(outs, 2, blocks)
    head, head_more = Share(*head), Share(*head_more)
    flow.later = [head, head_more]

    small = Total(jnp.concatenate([small1, small2, small3, small4], 0))
    flow.send(ups, head, head_more, small)
    going = [s for s in (char, char_more, merge, down) if not s.finished()]
    flow.prepare(char, char_more, merge, down)
    flow.land([head, head_more, small], (), going)
    flow.send(*going)
    flow.prepare(head, head_more, small)
    joined_all, d_cols = flow.land((), (joined_all, d_cols), [head, head_more, small])
    conv = conv_grad(length, joined_all, d_cols)
    others = list(flow.away)
    conv, streams = flow.turn(others, (conv, (d_sub, d_char, out_sub, out_char)), [head, head_more, small])
    d_sub, d_char, out_sub, out_char = streams
    ends_out = jnp.where(section == 0, jnp.stack([d_sub, d_char], 1), jnp.stack([out_sub, out_char], 1))
    ends_out = ends_out.reshape(1, seqs, length, 2, width)
    ends_out = flow.turn([s for s in flow.away if s is not head_more], ends_out)
    flow.drain()
    small, rest = small.total, width - split_at
    heads, outs = combine(flow.bits, [
        ([([((0, tall, 0, split_at), (0, 0))], head.window(0, split_at)),
          ([((0, tall, 0, rest), (0, split_at))], head_more.window(0, rest))], (tall, width), FULL),
        ([([((i * chunk, chunk, 0, part), (0, i * part)) for i in range(3)], head_more.window(rest, split_at))],
         (chunk, width), FULL)])

    b = lax.axis_index("batch")

    def pieces(*which):
        part = width // batch
        mine = lax.dynamic_slice_in_dim(small, b * part, part, 1)
        return jnp.concatenate([mine[i:i + 1] for i in which], 0)

    def piece(start, count):
        part = count * width // batch
        line = small[start:start + count].reshape(1, count * width)
        return lax.dynamic_slice_in_dim(line, b * part, part, 1)

    return (
        ends_out,
        placed(heads),
        pieces(24, 25)[None],
        placed(outs),
        pieces(20),
        pieces(21, 9, 4, 5)[None],
        pieces(22, 10, 6, 7)[None],
        placed(ups.total),
        piece(16, 4),
        placed(down.total),
        pieces(8),
        placed(jnp.concatenate([char_more.total[i * chunk:(i + 1) * chunk, spot - halfway:] for i in range(2)], 1)),
        placed(jnp.concatenate([char.total, char_more.total[:, :width - halfway]], 1)),
        piece(32, 3),
        placed(char_more.total[:, width - halfway:spot - halfway]),
        piece(35, 3),
        merge.total.reshape(chunk, 2, width).transpose(1, 2, 0)[None],
        pieces(2, 3)[None],
        conv.transpose(0, 2, 1)[None],
        piece(0, 2),
    )


def solution(mesh):
    by = P("batch")
    part = P("section")

    def columns(rank):
        return P(*(["section"] + [None] * (rank - 2) + ["batch"]))

    return jax.shard_map(
        body,
        mesh=mesh,
        in_specs=(by,) * 5 + (part,) * 19,
        out_specs=(P("section", "batch"),) + tuple(
            columns(rank) for rank in (3, 3, 3, 2, 3, 3, 3, 2, 3, 2, 3, 3, 2, 3, 2, 4, 3, 4, 2)),
        check_vma=False,
    )
```
